32 devices in a mesh: dp: 8 (over z, y), fsdp: 4 (over x, core).
Axes of the slice: x: 2, y: 2, z: 4, core: 2. Of those that a mesh axis runs over, the one named last changes fastest.
Arguments:
- decoder_in: bfloat16 [2, 32, 256, 768], P(None, ('dp', 'fsdp')), may hold values from -6 to 6
- memory: bfloat16 [2, 32, 128, 768], P(None, ('dp', 'fsdp')), may hold values from -6 to 6
- out_grad: bfloat16 [2, 32, 256, 768], P(None, ('dp', 'fsdp')), may hold values from -6 to 6
- lengths: int32 [2, 32], P(None, ('dp', 'fsdp')), may hold values from 32 to 256, as said below
- self_query: bfloat16 [768, 768], P(('dp', 'fsdp')), may hold values from -0.02734375 to 0.02734375
- self_key: bfloat16 [768, 768], P(('dp', 'fsdp')), may hold values from -0.21875 to 0.21875
- self_value: bfloat16 [768, 768], P(('dp', 'fsdp')), may hold values from -0.21875 to 0.21875
- self_out: bfloat16 [768, 768], P(('dp', 'fsdp')), may hold values from -1.75 to 1.75
- cross_query: bfloat16 [768, 768], P(('dp', 'fsdp')), may hold values from -0.02734375 to 0.02734375
- cross_key: bfloat16 [768, 768], P(('dp', 'fsdp')), may hold values from -0.21875 to 0.21875
- cross_value: bfloat16 [768, 768], P(('dp', 'fsdp')), may hold values from -0.21875 to 0.21875
- cross_out: bfloat16 [768, 768], P(('dp', 'fsdp')), may hold values from -3.5 to 3.5
- ff_in: bfloat16 [768, 3072], P(('dp', 'fsdp')), may hold values from -0.21875 to 0.21875
- ff_out: bfloat16 [3072, 768], P(('dp', 'fsdp')), may hold values from -0.109375 to 0.109375
- norm_self: bfloat16 [768], P(('dp', 'fsdp')), may hold values from 0.25 to 1.75
- norm_cross: bfloat16 [768], P(('dp', 'fsdp')), may hold values from 0.25 to 1.75
- norm_ff: bfloat16 [768], P(('dp', 'fsdp')), may hold values from 0.25 to 1.75
- bucket_bias_table: bfloat16 [32, 12], replicated, may hold values from -4 to 4
Outputs:
- layer_out: bfloat16 [2, 32, 256, 768], P(None, ('dp', 'fsdp'))
- input_grad: float32 [2, 32, 256, 768], P(None, ('dp', 'fsdp'))
- memory_grad: float32 [2, 32, 128, 768], P(None, ('dp', 'fsdp'))
- self_query_grad: float32 [768, 768], P(('dp', 'fsdp'))
- self_key_grad: float32 [768, 768], P(('dp', 'fsdp'))
- self_value_grad: float32 [768, 768], P(('dp', 'fsdp'))
- self_out_grad: float32 [768, 768], P(('dp', 'fsdp'))
- cross_query_grad: float32 [768, 768], P(('dp', 'fsdp'))
- cross_key_grad: float32 [768, 768], P(('dp', 'fsdp'))
- cross_value_grad: float32 [768, 768], P(('dp', 'fsdp'))
- cross_out_grad: float32 [768, 768], P(('dp', 'fsdp'))
- ff_in_grad: float32 [768, 3072], P(('dp', 'fsdp'))
- ff_out_grad: float32 [3072, 768], P(('dp', 'fsdp'))
- norm_self_grad: float32 [768], P(('dp', 'fsdp'))
- norm_cross_grad: float32 [768], P(('dp', 'fsdp'))
- norm_ff_grad: float32 [768], P(('dp', 'fsdp'))
- bias_table_grad: float32 [32, 12], replicated
The draws below stay inside these ranges and needn't reach their ends.
Inputs may be any that keep to these rules, and one draw needn't show every extreme that they name: `lengths`: every sequence has 32 to 256 tokens; some sequence of the batch has exactly 256.
All inputs are finite; a program needn't handle non-finite values.
Results may differ from the reference program's by a relative error of at most 0.019.
Values may be sent and summed in bfloat16 or wider, within the bound.
A program may use at most 320 MiB of HBM per device.

```python
import math
import jax
import jax.numpy as jnp
from jax import lax

D = 768
HEADS = 12
HEAD_DIM = 64
FF = 3072
BUCKETS = 32
MAX_DIST = 128
LEN = 256
MIN_LEN = 32
MEM = 128
MICRO = 2
INNER = 768
SEQS = 32


def draw_lengths(key, part):
    first_key, second_key, chosen_key = jax.random.split(key, 3)
    first = jax.random.randint(first_key, (MICRO * SEQS,), MIN_LEN, LEN + 1)
    second = jax.random.randint(second_key, (MICRO * SEQS,), LEN // 2, LEN + 1)
    lengths = jnp.minimum(first, second)
    chosen = jax.random.randint(chosen_key, (), 0, MICRO * SEQS)
    lengths = lengths.at[chosen].set(LEN)
    return lengths.reshape(MICRO, SEQS).astype(jnp.int32)


def block_scale(rng, dims, cuts, smallest, high):
    def one(dim, shards_of):
        draws = jax.random.uniform(jax.random.fold_in(jax.random.fold_in(rng, 6), dim), (shards_of,), jnp.float32, smallest / len(cuts), high / len(cuts))
        return jnp.repeat(jnp.exp(draws), dims[dim] // shards_of).reshape((-1,) + (1,) * (len(dims) - dim - 1))

    gain = one(*cuts[0])
    for cut in cuts[1:]:
        gain = gain * one(*cut)
    return gain


def normal_values(stream_key, extent, spread, most, cuts=(), held_as=jnp.bfloat16):
    values = spread * jax.random.normal(stream_key, extent, jnp.float32)
    if cuts:
        values = values * block_scale(stream_key, extent, cuts, -0.22, 0.18)
    return jnp.clip(values, -most, most).astype(held_as)


def setup_inputs(seed: int = 0) -> dict:
    keys = jax.random.split(jax.random.key(seed), 19)
    decoder_in = normal_values(keys[0], (MICRO, SEQS, LEN, D), 1.0, 6.0, ((1, 32),))
    memory = normal_values(keys[1], (MICRO, SEQS, MEM, D), 1.0, 6.0, ((1, 32),))
    out_grad = normal_values(keys[2], (MICRO, SEQS, LEN, D), 1.0, 6.0, ((1, 32),))
    lengths = draw_lengths(jax.random.fold_in(keys[18], 71), 0)
    self_query = normal_values(keys[4], (D, INNER), (D * HEAD_DIM) ** -0.5, 0.02734375, ((0, 32),))
    self_key = normal_values(keys[5], (D, INNER), D ** -0.5, 0.21875, ((0, 32),))
    self_value = normal_values(keys[6], (D, INNER), D ** -0.5, 0.21875, ((0, 32),))
    self_out = normal_values(keys[7], (INNER, D), (max(INNER // 64, 1)) ** -0.5, 1.75, ((0, 32),))
    cross_query = normal_values(keys[8], (D, INNER), (D * HEAD_DIM) ** -0.5, 0.02734375, ((0, 32),))
    cross_key = normal_values(keys[9], (D, INNER), D ** -0.5, 0.21875, ((0, 32),))
    cross_value = normal_values(keys[10], (D, INNER), D ** -0.5, 0.21875, ((0, 32),))
    cross_out = normal_values(keys[11], (INNER, D), (max(INNER // 256, 1)) ** -0.5, 3.5, ((0, 32),))
    ff_in = normal_values(keys[12], (D, FF), D ** -0.5, 0.21875, ((0, 32),))
    ff_out = normal_values(keys[13], (FF, D), FF ** -0.5, 0.109375, ((0, 32),))
    norm_self = jnp.clip(1.0 + 0.15 * jax.random.normal(keys[14], (D,), jnp.float32), 0.25, 1.75).astype(jnp.bfloat16)
    norm_cross = jnp.clip(1.0 + 0.15 * jax.random.normal(keys[15], (D,), jnp.float32), 0.25, 1.75).astype(jnp.bfloat16)
    norm_ff = jnp.clip(1.0 + 0.15 * jax.random.normal(keys[16], (D,), jnp.float32), 0.25, 1.75).astype(jnp.bfloat16)
    bucket_bias_table = normal_values(keys[17], (BUCKETS, HEADS), 1.0, 4.0)
    return {"decoder_in": decoder_in, "memory": memory, "out_grad": out_grad, "lengths": lengths, "self_query": self_query, "self_key": self_key, "self_value": self_value, "self_out": self_out, "cross_query": cross_query, "cross_key": cross_key, "cross_value": cross_value, "cross_out": cross_out, "ff_in": ff_in, "ff_out": ff_out, "norm_self": norm_self, "norm_cross": norm_cross, "norm_ff": norm_ff, "bucket_bias_table": bucket_bias_table}


EPS = 1e-06
MASKED = -1e+30
TOP_PRECISION = lax.Precision.HIGHEST

@jax.custom_vjp
def low(v):
    return lax.optimization_barrier(v.astype(jnp.bfloat16)).astype(jnp.float32)

@jax.custom_vjp
def low_back(v):
    return v

def low_keep(v):
    return (low(v), None)

def low_pass(kept, grad):
    return (grad,)

def back_keep(v):
    return (v, None)

def back_low(kept, grad):
    return (low(grad),)
low.defvjp(low_keep, low_pass)
low_back.defvjp(back_keep, back_low)

def bucket_onehot(length):
    half_count = BUCKETS // 2
    positions = jnp.arange(length, dtype=jnp.int32)
    distance = jnp.maximum(positions[:, None] - positions[None, :], 0)
    farther = jnp.zeros_like(distance)
    for level in range(1, half_count):
        border = int(math.ceil(half_count * (MAX_DIST / half_count) ** (level / half_count)))
        farther = farther + (distance >= border).astype(jnp.int32)
    bucket = jnp.where(distance < half_count, distance, half_count + farther)
    return (bucket[None] == jnp.arange(BUCKETS, dtype=jnp.int32)[:, None, None]).astype(jnp.float32)

def normalize(vector, gain_row):
    return vector * lax.rsqrt(lax.optimization_barrier(jnp.mean(vector * vector, axis=-1, keepdims=True)) + EPS) * gain_row

def product(operand, weight):
    return jnp.einsum('gtn,nm->gtm', operand, weight, precision=TOP_PRECISION)

def split_heads(matrix):
    return matrix.reshape(matrix.shape[0], matrix.shape[1], HEADS, HEAD_DIM)

def attention(queries, key_rows, values, relative_position_bias, allowed):
    raw_scores = jnp.einsum('gqhe,gkhe->ghqk', split_heads(queries), split_heads(key_rows), precision=TOP_PRECISION)
    scores = jnp.where(allowed, low_back(raw_scores) + relative_position_bias, MASKED)
    attention_weights = low(jax.nn.softmax(scores, axis=-1))
    context = jnp.einsum('ghqk,gkhe->gqhe', attention_weights, split_heads(values), precision=TOP_PRECISION)
    return low(low_back(context.reshape(queries.shape)))

def layer(decoded, memory_rows, valid_rows, allowed, bucket_indicator, params, bucket_bias_values):
    self_query, self_key, self_value, self_out, cross_query, cross_key, cross_value, cross_out, ff_in, ff_out, norm_self, norm_cross, norm_ff = params
    relative_position_bias = jnp.einsum('fsn,fe->esn', bucket_indicator, bucket_bias_values, precision=TOP_PRECISION)
    normed = low(normalize(decoded, norm_self))
    queries = low(low_back(product(normed, self_query)))
    key_rows = low(low_back(product(normed, self_key)))
    values = low(low_back(product(normed, self_value)))
    context = attention(queries, key_rows, values, relative_position_bias, allowed)
    after_self = decoded + low_back(product(context, self_out))
    normed_cross = low(normalize(after_self, norm_cross))
    cross_queries = low(low_back(product(normed_cross, cross_query)))
    memory_keys = low(low_back(product(memory_rows, cross_key)))
    memory_values = low(low_back(product(memory_rows, cross_value)))
    cross_context = attention(cross_queries, memory_keys, memory_values, 0.0, True)
    after_cross = after_self + low_back(product(cross_context, cross_out))
    normed_ff = low(normalize(after_cross, norm_ff))
    hidden = low_back(product(normed_ff, ff_in))
    activated = low(jax.nn.gelu(hidden, approximate=True))
    after_ff = after_cross + low_back(product(activated, ff_out))
    return after_ff * valid_rows

def reference(decoder_in, memory, out_grad, lengths, self_query, self_key, self_value, self_out, cross_query, cross_key, cross_value, cross_out, ff_in, ff_out, norm_self, norm_cross, norm_ff, bucket_bias_table):
    group_size = 8
    seq_count = MICRO * SEQS
    groups = seq_count // group_size
    decoded = decoder_in.reshape(groups, group_size, LEN, D)
    memory_rows = memory.reshape(groups, group_size, MEM, D)
    cotangent = out_grad.reshape(groups, group_size, LEN, D)
    length_rows = lengths.reshape(groups, group_size)
    params = tuple((weight.astype(jnp.float32) for weight in (self_query, self_key, self_value, self_out, cross_query, cross_key, cross_value, cross_out, ff_in, ff_out, norm_self, norm_cross, norm_ff)))
    bucket_bias_values = bucket_bias_table.astype(jnp.float32)
    bucket_indicator = bucket_onehot(LEN)
    positions = jnp.arange(LEN, dtype=jnp.int32)
    causal = positions[:, None] >= positions[None, :]

    def group_step(totals, member):
        group_in, group_memory, group_grad, group_lengths = member
        present = positions[None, :] < group_lengths[:, None]
        valid_rows = present.astype(jnp.float32)[:, :, None]
        allowed = causal[None, None] & present[:, None, None, :]

        def forward(decoded_rows, memory_part, weight_set, bias_part):
            return layer(decoded_rows, memory_part, valid_rows, allowed, bucket_indicator, weight_set, bias_part)
        result, pullback = jax.vjp(forward, group_in.astype(jnp.float32), group_memory.astype(jnp.float32), params, bucket_bias_values)
        grad_input, grad_memory, grad_params, relative_bias_gradient = pullback(group_grad.astype(jnp.float32))
        totals = jax.tree.map(jnp.add, totals, (grad_params, relative_bias_gradient))
        return (totals, (result.astype(jnp.bfloat16), grad_input, grad_memory))
    initial = (tuple((jnp.zeros_like(weight) for weight in params)), jnp.zeros_like(bucket_bias_values))
    (grad_params, relative_bias_gradient), (outputs, grad_inputs, grad_memories) = lax.scan(group_step, initial, (decoded, memory_rows, cotangent, length_rows))
    return (outputs.reshape(MICRO, SEQS, LEN, D), grad_inputs.reshape(MICRO, SEQS, LEN, D), grad_memories.reshape(MICRO, SEQS, MEM, D), grad_params[0], grad_params[1], grad_params[2], grad_params[3], grad_params[4], grad_params[5], grad_params[6], grad_params[7], grad_params[8], grad_params[9], grad_params[10], grad_params[11], grad_params[12], relative_bias_gradient)
```

```python
import math

import jax
import jax.numpy as jnp
from jax import lax
from jax.sharding import PartitionSpec as P

HEADS = 12
BUCKETS = 32
MAX_DIST = 128


EPS = 1e-06
MASKED = -1e30
TOP_PRECISION = lax.Precision.HIGHEST


def bucket_onehot(length):
    half_count = BUCKETS // 2
    positions = jnp.arange(length, dtype=jnp.int32)
    distance = jnp.maximum(positions[:, None] - positions[None, :], 0)
    farther = jnp.zeros_like(distance)
    for level in range(1, half_count):
        border = int(math.ceil(half_count * (MAX_DIST / half_count) ** (level / half_count)))
        farther = farther + (distance >= border).astype(jnp.int32)
    bucket = jnp.where(distance < half_count, distance, half_count + farther)
    return (bucket[None] == jnp.arange(BUCKETS, dtype=jnp.int32)[:, None, None]).astype(jnp.float32)


def normalize(vector, gain_row):
    return vector * lax.rsqrt(jnp.mean(vector * vector, axis=-1, keepdims=True) + EPS) * gain_row


def project(operand, weight):
    return jnp.dot(operand, weight, preferred_element_type=jnp.float32)


def project_back(operand, weight):
    return lax.dot_general(
        operand, weight, (((1,), (1,)), ((), ())), preferred_element_type=jnp.float32
    )


def weight_grad(inputs_rows, grad_rows):
    return lax.dot_general(
        inputs_rows, grad_rows, (((0,), (0,)), ((), ())), preferred_element_type=jnp.float32
    )


def split_heads(matrix):
    return matrix.reshape(matrix.shape[:-1] + (HEADS, matrix.shape[-1] // HEADS))


def head_scores(queries, key_rows):
    return jnp.einsum(
        "gqhe,gkhe->ghqk",
        split_heads(queries),
        split_heads(key_rows),
        preferred_element_type=jnp.float32,
    )


def attend_forward(queries, key_rows, values, relative_position_bias, allowed):
    scores = jnp.where(allowed, head_scores(queries, key_rows) + relative_position_bias, MASKED)
    largest = jnp.max(scores, axis=-1, keepdims=True)
    exponent = jnp.exp(scores - largest)
    row_totals = jnp.sum(exponent, axis=-1, keepdims=True)
    attention_weights = exponent / row_totals
    context = jnp.einsum(
        "ghqk,gkhe->gqhe",
        attention_weights.astype(jnp.bfloat16),
        split_heads(values),
        preferred_element_type=jnp.float32,
    )
    return (context.reshape(queries.shape).astype(jnp.bfloat16), attention_weights)


def attend_backward(queries, key_rows, values, attention_weights, grad_context):
    grad_heads = split_heads(grad_context)
    grad_values = jnp.einsum(
        "ghqk,gqhe->gkhe",
        attention_weights.astype(jnp.bfloat16),
        grad_heads,
        preferred_element_type=jnp.float32,
    )
    grad_weights = jnp.einsum(
        "gqhe,gkhe->ghqk", grad_heads, split_heads(values), preferred_element_type=jnp.float32
    )
    score_gradient = attention_weights * (
        grad_weights - jnp.sum(grad_weights * attention_weights, axis=-1, keepdims=True)
    )
    rounded = score_gradient.astype(jnp.bfloat16)
    grad_queries = jnp.einsum(
        "ghqk,gkhe->gqhe", rounded, split_heads(key_rows), preferred_element_type=jnp.float32
    )
    grad_keys = jnp.einsum(
        "ghqk,gqhe->gkhe", rounded, split_heads(queries), preferred_element_type=jnp.float32
    )
    return (
        grad_queries.reshape(queries.shape).astype(jnp.bfloat16),
        grad_keys.reshape(key_rows.shape).astype(jnp.bfloat16),
        grad_values.reshape(values.shape).astype(jnp.bfloat16),
        score_gradient,
    )


AXES = ("dp", "fsdp")


def rows_of(matrix):
    return matrix.reshape(-1, matrix.shape[-1])


def gather_all(shards):
    width = shards[0].shape[1]
    blocks = []
    for shard in shards:
        if shard.ndim == 1:
            continue
        blocks.append(shard.reshape(-1, width) if shard.shape[1] != width else shard)
    packed = lax.all_gather(jnp.concatenate(blocks, axis=0), AXES, axis=0)
    whole, at = [], 0
    devices = packed.shape[0]
    for shard, block in zip(shards, blocks):
        part = packed[:, at : at + block.shape[0]]
        at += block.shape[0]
        whole.append(part.reshape(devices * shard.shape[0], shard.shape[1]))
    gains = jnp.stack(shards[len(blocks) :])
    gains = lax.all_gather(gains, AXES, axis=1, tiled=True)
    return whole, [gains[k] for k in range(gains.shape[0])]


def scatter_all(grads, shards):
    width = shards[0].shape[1]
    devices = lax.axis_size(AXES)
    blocks = [grad.astype(jnp.bfloat16).reshape(devices, -1, width) for grad in grads]
    summed = lax.psum_scatter(
        jnp.concatenate(blocks, axis=1), AXES, scatter_dimension=0, tiled=False
    ).astype(jnp.float32)
    pieces, at = [], 0
    for block, shard in zip(blocks, shards):
        pieces.append(summed[at : at + block.shape[1]].reshape(shard.shape))
        at += block.shape[1]
    return pieces


def body(decoder_in, memory, out_grad, lengths, *params):
    shards, bucket_bias_table = params[:13], params[13]
    matrices, gains = gather_all(shards)
    (
        self_query,
        self_key,
        self_value,
        self_out,
        cross_query,
        cross_key,
        cross_value,
        cross_out,
        ff_in,
        ff_out,
    ) = matrices
    norm_self, norm_cross, norm_ff = [gain.astype(jnp.float32) for gain in gains]
    micro, seqs, seq_length, width = decoder_in.shape
    groups = micro * seqs
    memory_bf = memory.reshape(groups, memory.shape[2], width)
    grad_bf = out_grad.reshape(groups, seq_length, width)
    group_lengths = lengths.reshape(groups)
    bucket_indicator = bucket_onehot(seq_length)
    relative_position_bias = jnp.einsum(
        "fsn,fe->esn",
        bucket_indicator,
        bucket_bias_table.astype(jnp.float32),
        precision=TOP_PRECISION,
    )
    positions = jnp.arange(seq_length, dtype=jnp.int32)
    causal = positions[:, None] >= positions[None, :]
    present = positions[None, :] < group_lengths[:, None]
    valid_rows = present[:, :, None].astype(jnp.float32)
    allowed = causal[None, None] & present[:, None, None, :]

    def grad_of(inputs, upstream):
        return weight_grad(rows_of(inputs), rows_of(upstream))

    decoded = decoder_in.reshape(groups, seq_length, width).astype(jnp.float32)
    normed = normalize(decoded, norm_self).astype(jnp.bfloat16)
    queries = project(normed, self_query).astype(jnp.bfloat16)
    key_rows = project(normed, self_key).astype(jnp.bfloat16)
    values = project(normed, self_value).astype(jnp.bfloat16)
    context, self_weights = attend_forward(
        queries, key_rows, values, relative_position_bias, allowed
    )
    after_self = decoded + project(context, self_out)
    normed_cross = normalize(after_self, norm_cross).astype(jnp.bfloat16)
    cross_queries = project(normed_cross, cross_query).astype(jnp.bfloat16)
    memory_keys = project(memory_bf, cross_key).astype(jnp.bfloat16)
    memory_values = project(memory_bf, cross_value).astype(jnp.bfloat16)
    cross_context, cross_weights = attend_forward(
        cross_queries, memory_keys, memory_values, 0.0, True
    )
    after_cross = after_self + project(cross_context, cross_out)
    normed_ff = normalize(after_cross, norm_ff).astype(jnp.bfloat16)
    hidden = project(normed_ff, ff_in)
    activated = jax.nn.gelu(hidden, approximate=True).astype(jnp.bfloat16)
    after_ff = after_cross + project(activated, ff_out)
    layer_out = (after_ff * valid_rows).astype(jnp.bfloat16)

    def back(operand, weight):
        return lax.dot_general(
            operand, weight, (((2,), (1,)), ((), ())), preferred_element_type=jnp.float32
        )

    grad_after = grad_bf.astype(jnp.float32) * valid_rows
    grad_branch = grad_after.astype(jnp.bfloat16)
    grad_ff_out = grad_of(activated, grad_branch)
    gelu_pull = jax.vjp(lambda pre_act: jax.nn.gelu(pre_act, approximate=True), hidden)[1]
    grad_hidden = gelu_pull(back(grad_branch, ff_out))[0].astype(jnp.bfloat16)
    grad_ff_in = grad_of(normed_ff, grad_hidden)
    norm_pull = jax.vjp(normalize, after_cross, norm_ff)[1]
    grad_rows, grad_norm_ff = norm_pull(back(grad_hidden, ff_in))
    grad_after = grad_after + grad_rows
    grad_branch = grad_after.astype(jnp.bfloat16)
    grad_cross_out = grad_of(cross_context, grad_branch)
    grad_context = back(grad_branch, cross_out).astype(jnp.bfloat16)
    grad_cross_rows, grad_memory_keys, grad_memory_values, unused = attend_backward(
        cross_queries, memory_keys, memory_values, cross_weights, grad_context
    )
    grad_cross_query = grad_of(normed_cross, grad_cross_rows)
    grad_cross_key = grad_of(memory_bf, grad_memory_keys)
    grad_cross_value = grad_of(memory_bf, grad_memory_values)
    grad_memory = back(grad_memory_keys, cross_key) + back(grad_memory_values, cross_value)
    norm_pull = jax.vjp(normalize, after_self, norm_cross)[1]
    grad_rows, grad_norm_cross = norm_pull(back(grad_cross_rows, cross_query))
    grad_after = grad_after + grad_rows
    grad_branch = grad_after.astype(jnp.bfloat16)
    grad_self_out = grad_of(context, grad_branch)
    grad_context = back(grad_branch, self_out).astype(jnp.bfloat16)
    grad_queries, grad_key_rows, grad_values, score_gradient = attend_backward(
        queries, key_rows, values, self_weights, grad_context
    )
    grad_self_query = grad_of(normed, grad_queries)
    grad_self_key = grad_of(normed, grad_key_rows)
    grad_self_value = grad_of(normed, grad_values)
    grad_normed = (
        back(grad_queries, self_query) + back(grad_key_rows, self_key) + back(grad_values, self_value)
    )
    norm_pull = jax.vjp(normalize, decoded, norm_self)[1]
    grad_rows, grad_norm_self = norm_pull(grad_normed)
    grad_input = grad_after + grad_rows
    bias_grad = jnp.einsum(
        "fgd,ogd->fo", bucket_indicator, jnp.sum(score_gradient, axis=0), precision=TOP_PRECISION
    )
    pieces = scatter_all(
        (
            grad_self_query,
            grad_self_key,
            grad_self_value,
            grad_self_out,
            grad_cross_query,
            grad_cross_key,
            grad_cross_value,
            grad_cross_out,
            grad_ff_in,
            grad_ff_out,
        ),
        shards[:10],
    )
    small = lax.psum(
        jnp.concatenate([grad_norm_self, grad_norm_cross, grad_norm_ff, bias_grad.reshape(-1)]),
        AXES,
    )
    mine = shards[10].shape[0]
    at = lax.axis_index(AXES) * mine
    gains_out = [
        lax.dynamic_slice_in_dim(small[k * width : (k + 1) * width], at, mine) for k in range(3)
    ]
    return (
        layer_out.reshape(decoder_in.shape),
        grad_input.reshape(decoder_in.shape),
        grad_memory.reshape(memory.shape),
        *pieces,
        *gains_out,
        small[3 * width :].reshape(bucket_bias_table.shape),
    )


def solution(mesh):
    return jax.shard_map(
        body,
        mesh=mesh,
        in_specs=(
            P(None, ("dp", "fsdp"), None, None),
            P(None, ("dp", "fsdp"), None, None),
            P(None, ("dp", "fsdp"), None, None),
            P(None, ("dp", "fsdp")),
            P(("dp", "fsdp"), None),
            P(("dp", "fsdp"), None),
            P(("dp", "fsdp"), None),
            P(("dp", "fsdp"), None),
            P(("dp", "fsdp"), None),
            P(("dp", "fsdp"), None),
            P(("dp", "fsdp"), None),
            P(("dp", "fsdp"), None),
            P(("dp", "fsdp"), None),
            P(("dp", "fsdp"), None),
            P(("dp", "fsdp")),
            P(("dp", "fsdp")),
            P(("dp", "fsdp")),
            P(),
        ),
        out_specs=(
            P(None, ("dp", "fsdp"), None, None),
            P(None, ("dp", "fsdp"), None, None),
            P(None, ("dp", "fsdp"), None, None),
            P(("dp", "fsdp"), None),
            P(("dp", "fsdp"), None),
            P(("dp", "fsdp"), None),
            P(("dp", "fsdp"), None),
            P(("dp", "fsdp"), None),
            P(("dp", "fsdp"), None),
            P(("dp", "fsdp"), None),
            P(("dp", "fsdp"), None),
            P(("dp", "fsdp"), None),
            P(("dp", "fsdp"), None),
            P(("dp", "fsdp")),
            P(("dp", "fsdp")),
            P(("dp", "fsdp")),
            P(),
        ),
        check_vma=False,
    )
```

```python
import math

import jax
import jax.numpy as jnp
from jax import lax
from jax.experimental import pallas as pl
from jax.experimental.pallas import tpu as pltpu
from jax.sharding import PartitionSpec as P

HEADS = 12
BUCKETS = 32
MAX_DIST = 128


EPS = 1e-06
MASKED = -1e30
TOP_PRECISION = lax.Precision.HIGHEST


def bucket_onehot(length):
    half_count = BUCKETS // 2
    positions = jnp.arange(length, dtype=jnp.int32)
    distance = jnp.maximum(positions[:, None] - positions[None, :], 0)
    farther = jnp.zeros_like(distance)
    for level in range(1, half_count):
        border = int(math.ceil(half_count * (MAX_DIST / half_count) ** (level / half_count)))
        farther = farther + (distance >= border).astype(jnp.int32)
    bucket = jnp.where(distance < half_count, distance, half_count + farther)
    return (bucket[None] == jnp.arange(BUCKETS, dtype=jnp.int32)[:, None, None]).astype(jnp.float32)


def normalize(vector, gain_row):
    return vector * lax.rsqrt(jnp.mean(vector * vector, axis=-1, keepdims=True) + EPS) * gain_row


def project(operand, weight):
    return jnp.dot(operand, weight, preferred_element_type=jnp.float32)


def project_back(operand, weight):
    return lax.dot_general(
        operand, weight, (((1,), (1,)), ((), ())), preferred_element_type=jnp.float32
    )


def weight_grad(inputs_rows, grad_rows):
    return lax.dot_general(
        inputs_rows, grad_rows, (((0,), (0,)), ((), ())), preferred_element_type=jnp.float32
    )


def split_heads(matrix):
    return matrix.reshape(matrix.shape[:-1] + (HEADS, matrix.shape[-1] // HEADS))


def head_scores(queries, key_rows):
    return jnp.einsum(
        "gqhe,gkhe->ghqk",
        split_heads(queries),
        split_heads(key_rows),
        preferred_element_type=jnp.float32,
    )


def attend_forward(queries, key_rows, values, relative_position_bias, allowed):
    scores = jnp.where(allowed, head_scores(queries, key_rows) + relative_position_bias, MASKED)
    largest = jnp.max(scores, axis=-1, keepdims=True)
    exponent = jnp.exp(scores - largest)
    row_totals = jnp.sum(exponent, axis=-1, keepdims=True)
    attention_weights = exponent / row_totals
    context = jnp.einsum(
        "ghqk,gkhe->gqhe",
        attention_weights.astype(jnp.bfloat16),
        split_heads(values),
        preferred_element_type=jnp.float32,
    )
    return (context.reshape(queries.shape).astype(jnp.bfloat16), attention_weights)


def attend_backward(queries, key_rows, values, attention_weights, grad_context):
    grad_heads = split_heads(grad_context)
    grad_values = jnp.einsum(
        "ghqk,gqhe->gkhe",
        attention_weights.astype(jnp.bfloat16),
        grad_heads,
        preferred_element_type=jnp.float32,
    )
    grad_weights = jnp.einsum(
        "gqhe,gkhe->ghqk", grad_heads, split_heads(values), preferred_element_type=jnp.float32
    )
    score_gradient = attention_weights * (
        grad_weights - jnp.sum(grad_weights * attention_weights, axis=-1, keepdims=True)
    )
    rounded = score_gradient.astype(jnp.bfloat16)
    grad_queries = jnp.einsum(
        "ghqk,gkhe->gqhe", rounded, split_heads(key_rows), preferred_element_type=jnp.float32
    )
    grad_keys = jnp.einsum(
        "ghqk,gqhe->gkhe", rounded, split_heads(queries), preferred_element_type=jnp.float32
    )
    return (
        grad_queries.reshape(queries.shape).astype(jnp.bfloat16),
        grad_keys.reshape(key_rows.shape).astype(jnp.bfloat16),
        grad_values.reshape(values.shape).astype(jnp.bfloat16),
        score_gradient,
    )


AXES = ("dp", "fsdp")


def rows_of(matrix):
    return matrix.reshape(-1, matrix.shape[-1])


def gather_all(shards):
    width = shards[0].shape[1]
    blocks = []
    for shard in shards:
        if shard.ndim == 1:
            continue
        blocks.append(shard.reshape(-1, width) if shard.shape[1] != width else shard)
    packed = lax.all_gather(jnp.concatenate(blocks, axis=0), AXES, axis=0)
    whole, at = [], 0
    devices = packed.shape[0]
    for shard, block in zip(shards, blocks):
        part = packed[:, at : at + block.shape[0]]
        at += block.shape[0]
        whole.append(part.reshape(devices * shard.shape[0], shard.shape[1]))
    gains = jnp.stack(shards[len(blocks) :])
    gains = lax.all_gather(gains, AXES, axis=1, tiled=True)
    return whole, [gains[k] for k in range(gains.shape[0])]


def scatter_all(grads, shards):
    width = shards[0].shape[1]
    devices = lax.axis_size(AXES)
    blocks = [grad.astype(jnp.bfloat16).reshape(devices, -1, width) for grad in grads]
    summed = lax.psum_scatter(
        jnp.concatenate(blocks, axis=1), AXES, scatter_dimension=0, tiled=False
    ).astype(jnp.float32)
    pieces, at = [], 0
    for block, shard in zip(blocks, shards):
        pieces.append(summed[at : at + block.shape[1]].reshape(shard.shape))
        at += block.shape[1]
    return pieces


MESH = pl.DeviceIdType.MESH
GROUPS = 16


def place():
    dp, fsdp = lax.axis_index("dp"), lax.axis_index("fsdp")
    z, y, x, core = dp // 2, dp % 2, fsdp // 2, fsdp % 2
    sibling = (dp, x * 2 + 1 - core)
    over_x = (dp, (1 - x) * 2 + core)
    over_y = (z * 2 + 1 - y, fsdp)
    first = (jnp.where(core == 0, over_x[0], over_y[0]), jnp.where(core == 0, over_x[1], over_y[1]))
    second = (jnp.where(core == 0, over_y[0], over_x[0]), jnp.where(core == 0, over_y[1], over_x[1]))
    along_z = [(((z + k) % 4) * 2 + y, fsdp) for k in (1, 2, 3)]
    own = y * 2 + x
    beside = jnp.where(core == 0, y * 2 + 1 - x, (1 - y) * 2 + x)
    return z, own, beside, core, sibling, first, second, along_z


def greet(partners):
    barrier = pltpu.get_barrier_semaphore()
    for partner in partners:
        pl.semaphore_signal(barrier, inc=1, device_id=partner, device_id_type=MESH)
    pl.semaphore_wait(barrier, len(partners))


def half(core):
    return pl.ds(pl.multiple_of(core * 384, 128), 384)


def gather_kernel(small_ref, tall_ref, gain_ref, wa, wi, wo, gains, sib, gain_in, ss, rs, ss0, rs0):
    z, own, beside, core, sibling, first, second, along_z = place()
    mine, other = half(core), half(1 - core)

    def view(g, zi, yx, cols):
        zs = slice(None) if zi is None else zi
        if g < 8:
            return wa.at[g, zs, yx, :, cols]
        if g < 12:
            return wi.at[g - 8, zs, yx, :, cols]
        return wo.at[zs, yx, pl.ds(48 * (g - 12), 48), cols]

    def whole(g, cols):
        if g < 8:
            return wa.at[g, :, :, :, cols]
        if g < 12:
            return wi.at[g - 8, :, :, :, cols]
        return wo.at[:, :, pl.ds(48 * (g - 12), 48), cols]

    def send(ref, to, g, k, into=None):
        return pltpu.make_async_remote_copy(
            src_ref=ref, dst_ref=ref if into is None else into, send_sem=ss.at[g, k], recv_sem=rs.at[g, k],
            device_id=to, device_id_type=MESH)

    def step_a(g):
        return [send(view(g, z, own, mine), to, g, k) for k, to in enumerate(along_z)]

    def step_b(g):
        return [send(view(g, None, own, mine), first, g, 3)]

    def step_c(g):
        return [send(view(g, None, own, mine), second, g, 4), send(view(g, None, beside, mine), second, g, 5)]

    def step_d(g):
        return [send(whole(g, mine), sibling, g, 6)]

    greet([sibling, first, second] + along_z)
    swap_small = pltpu.make_async_remote_copy(
        src_ref=small_ref.at[:, :, other], dst_ref=sib, send_sem=ss0.at[0], recv_sem=rs0.at[0],
        device_id=sibling, device_id_type=MESH)
    rows = pl.ds(pl.multiple_of(96 * core, 16), 96)
    swap_tall = pltpu.make_async_remote_copy(
        src_ref=tall_ref.at[:, other], dst_ref=wo.at[z, own, rows, other], send_sem=ss0.at[1], recv_sem=rs0.at[1],
        device_id=sibling, device_id_type=MESH)
    def gain_copies(s):
        to = ([sibling], along_z, [first], [second])[s]
        at = (0, 1, 4, 5)[s]
        return [
            pltpu.make_async_remote_copy(
                src_ref=gains, dst_ref=gain_in.at[at + k], send_sem=ss0.at[2 + at + k], recv_sem=rs0.at[2 + at + k],
                device_id=d, device_id_type=MESH)
            for k, d in enumerate(to)
        ]

    def gain_start(s):
        for copy in gain_copies(s):
            copy.start()

    def gain_finish(s):
        for copy in gain_copies(s):
            copy.wait()
        for k in ((0,), (1, 2, 3), (4,), (5,))[s]:
            gains[...] += gain_in[k]

    swap_small.start()
    swap_tall.start()
    gains[...] = gain_ref[...]
    gain_start(0)
    wo[z, own, rows, mine] = tall_ref[:, mine]
    swap_small.wait()
    for u in range(8):
        wa[u, z, own, :, mine] = small_ref[u, :, mine] + sib[u]
    for u in range(4):
        wi[u, z, own, :, mine] = small_ref[8 + u, :, mine] + sib[8 + u]
    swap_tall.wait()

    def step_b1(g):
        return [send(view(g, z, own, mine), first, g, 3)]

    def step_a2(g):
        out = []
        for k, to in enumerate(along_z):
            out.append(send(view(g, z, own, mine), to, g, k))
            out.append(send(view(g, z, beside, mine), to, g, 7 + k))
        return out

    zf = [step_a, step_b, step_c, step_d]
    zs = [step_b1, step_a2, step_c, step_d]
    steps = [zs if g in ZS else zf for g in range(GROUPS)]
    started = [0] * GROUPS
    order = ORDER(GROUPS)
    gain_finish(0)
    gain_start(1)
    stage = 1
    for n, (g, s) in enumerate(order):
        if n in GAIN_AT:
            gain_finish(stage)
            stage += 1
            if stage < 4:
                gain_start(stage)
        assert started[g] == s
        if s:
            for copy in steps[g][s - 1](g):
                copy.wait()
        if s < 4:
            for copy in steps[g][s](g):
                copy.start()
        started[g] = s + 1
    assert all(v == 5 for v in started) and stage == 4


def skew(ahead):
    def order(groups):
        out = []
        for t in range(-max(ahead), groups + 8):
            for s in range(len(ahead)):
                g = t + ahead[s]
                if 0 <= g < groups:
                    out.append((g, s))
        return out
    return order


ZS = (1, 4, 7, 10, 13)
GAIN_AT = (3, 6, 9)
ORDER = skew([6, 4, 2, 1, 0])


def gather_call(small, tall, gain):
    return pl.pallas_call(
        gather_kernel,
        out_shape=(
            jax.ShapeDtypeStruct((8, 4, 4, 48, 768), jnp.bfloat16),
            jax.ShapeDtypeStruct((4, 4, 4, 48, 768), jnp.bfloat16),
            jax.ShapeDtypeStruct((4, 4, 192, 768), jnp.bfloat16),
            jax.ShapeDtypeStruct((16, 768), jnp.bfloat16),
        ),
        in_specs=[pl.BlockSpec(memory_space=pltpu.VMEM)] * 3,
        out_specs=[pl.BlockSpec(memory_space=pltpu.VMEM)] * 4,
        scratch_shapes=[
            pltpu.VMEM((12, 48, 384), jnp.bfloat16),
            pltpu.VMEM((6, 16, 768), jnp.bfloat16),
            pltpu.SemaphoreType.DMA((GROUPS, 10)),
            pltpu.SemaphoreType.DMA((GROUPS, 10)),
            pltpu.SemaphoreType.DMA((8,)),
            pltpu.SemaphoreType.DMA((8,)),
        ],
        compiler_params=pltpu.CompilerParams(collective_id=0, has_side_effects=True, vmem_limit_bytes=56 * 2**20),
    )(small, tall, gain)


def pack(squares, ff_in, ff_out, gains):
    core = lax.axis_index("fsdp") % 2
    units = list(squares) + [ff_in[:, 768 * j : 768 * j + 768] for j in range(4)]
    block = jnp.stack(units)
    low = jnp.pad(block, ((0, 0), (0, 24), (0, 0)))
    high = jnp.pad(block, ((0, 0), (24, 0), (0, 0)))
    at = lax.axis_index(("dp", "fsdp")) * 24
    placed = lax.dynamic_update_slice(jnp.zeros((16, 768), jnp.bfloat16), jnp.stack(gains), (0, at))
    return jnp.where(core == 0, low, high), ff_out, placed


def gather_weights(squares, ff_in, ff_out, gains):
    wa, wi, wo, whole_gains = gather_call(*pack(squares, ff_in, ff_out, gains))
    return (
        [wa[u].reshape(768, 768) for u in range(8)],
        jnp.concatenate([wi[u].reshape(768, 768) for u in range(4)], axis=1),
        wo.reshape(3072, 768),
        [whole_gains[k] for k in range(3)],
    )


ZS2 = (2, 5, 8, 11)
ORDER2 = skew([8, 7, 6, 4, 2, 0])
SMALL_AT = (3, 6, 9, 12)


def scatter_kernel(ga, gi, go, small_ref, small_out, tall_out, acc_small, r0, r1, r2, r3, fa, fo, fa_in, fo_in, small_in, ss, rs, ss0, rs0):
    z, own, beside, core, sibling, first, second, along_z = place()
    mine, other = half(core), half(1 - core)
    diag = 3 - own
    across = 3 - beside
    f32 = jnp.float32

    def block(g, cols):
        if g < 8:
            return ga.at[g, :, :, :, cols]
        if g < 12:
            return gi.at[g - 8, :, :, :, cols]
        return go.at[:, :, pl.ds(48 * (g - 12), 48), cols]

    def send(src, dst, to, g, k):
        return pltpu.make_async_remote_copy(
            src_ref=src, dst_ref=dst, send_sem=ss.at[g, k], recv_sem=rs.at[g, k], device_id=to, device_id_type=MESH)

    def swap(g):
        return [send(block(g, other), r0.at[g], sibling, g, 0)]

    def over_second(g):
        return [send(r0.at[g, :, across], r1.at[g, 0], second, g, 1), send(r0.at[g, :, diag], r1.at[g, 1], second, g, 2)]

    def over_first(g):
        return [send(r0.at[g, :, beside], r2.at[g], first, g, 3)]

    def over_z(g):
        return [send(r0.at[g, (z + k + 1) % 4, own], r3.at[g, 0, k], to, g, 4 + k) for k, to in enumerate(along_z)]

    def over_z2(g):
        return over_z(g) + [
            send(r0.at[g, (z + k + 1) % 4, beside], r3.at[g, 1, k], to, g, 7 + k) for k, to in enumerate(along_z)]

    def over_first1(g):
        return [send(r0.at[g, z, beside], r2.at[g, 0], first, g, 3)]

    def last(g):
        if g < 12:
            rows = pl.ds(pl.multiple_of(24 * (1 - core), 8), 24)
            return [send(fa.at[g, rows], fa_in.at[g], sibling, g, 10)]
        if g == 15:
            return [send(fo.at[pl.ds(2 * (1 - core), 2)], fo_in, sibling, g, 10)]
        return []

    def add0(g):
        r0[g] += block(g, mine)[...]

    def add1(g):
        r0[g, :, own] += r1[g, 0]
        r0[g, :, beside] += r1[g, 1]

    def finish(g, value):
        if g < 12:
            fa[g] = value
        else:
            fo[g - 12] = value

    def add2(g):
        r0[g, :, own] += r2[g]

    def add3(g):
        finish(g, r0[g, z, own].astype(f32) + r3[g, 0, 0].astype(f32) + r3[g, 0, 1].astype(f32) + r3[g, 0, 2].astype(f32))

    def add2z(g):
        for j, yx in enumerate((own, beside)):
            total = r0[g, z, yx].astype(f32) + r3[g, j, 0].astype(f32) + r3[g, j, 1].astype(f32) + r3[g, j, 2].astype(f32)
            r0[g, z, yx] = total.astype(jnp.bfloat16)

    def add3z(g):
        finish(g, r0[g, z, own].astype(f32) + r2[g, 0].astype(f32))

    def write(g):
        if g < 12:
            rows = pl.ds(pl.multiple_of(24 * core, 8), 24)
            small_out[g, :, mine] = fa[g, rows]
            small_out[g, :, other] = fa_in[g]
        elif g == 15:
            tall_out[:, mine] = fo[pl.ds(2 * core, 2)].reshape(96, 384)
            tall_out[:, other] = fo_in[...].reshape(96, 384)

    zf = ([swap, over_second, over_first, over_z, last], [None, add0, add1, add2, add3, write])
    zs = ([swap, over_second, over_z2, over_first1, last], [None, add0, add1, add2z, add3z, write])

    def small_copies(s):
        to = ([sibling], along_z, [first], [second])[s]
        at = (0, 1, 4, 5)[s]
        return [
            pltpu.make_async_remote_copy(
                src_ref=acc_small, dst_ref=small_in.at[at + k], send_sem=ss0.at[at + k], recv_sem=rs0.at[at + k],
                device_id=d, device_id_type=MESH)
            for k, d in enumerate(to)
        ]

    greet([sibling, first, second] + along_z)
    acc_small[...] = small_ref[...]
    for copy in small_copies(0):
        copy.start()
    stage = 0
    for n, (g, s) in enumerate(ORDER2(GROUPS)):
        copies, sums = zs if g in ZS2 else zf
        if s:
            for copy in copies[s - 1](g):
                copy.wait()
            sums[s](g)
        if s < 5:
            for copy in copies[s](g):
                copy.start()
        if n in SMALL_AT:
            for copy in small_copies(stage):
                copy.wait()
            for k in ((0,), (1, 2, 3), (4,), (5,))[stage]:
                acc_small[...] += small_in[k]
            stage += 1
            if stage < 4:
                for copy in small_copies(stage):
                    copy.start()
    small_out_done = stage
    assert small_out_done == 4


def scatter_call(ga, gi, go, small):
    def wrapped(ga, gi, go, small, small_out, tall_out, sum_out, *scratch):
        scatter_kernel(ga, gi, go, small, small_out, tall_out, sum_out, *scratch)

    return pl.pallas_call(
        wrapped,
        out_shape=(
            jax.ShapeDtypeStruct((12, 24, 768), jnp.float32),
            jax.ShapeDtypeStruct((96, 768), jnp.float32),
            jax.ShapeDtypeStruct((8, 768), jnp.float32),
        ),
        in_specs=[pl.BlockSpec(memory_space=pltpu.VMEM)] * 4,
        out_specs=[pl.BlockSpec(memory_space=pltpu.VMEM)] * 3,
        scratch_shapes=[
            pltpu.VMEM((GROUPS, 4, 4, 48, 384), jnp.bfloat16),
            pltpu.VMEM((GROUPS, 2, 4, 48, 384), jnp.bfloat16),
            pltpu.VMEM((GROUPS, 4, 48, 384), jnp.bfloat16),
            pltpu.VMEM((GROUPS, 2, 3, 48, 384), jnp.bfloat16),
            pltpu.VMEM((12, 48, 384), jnp.float32),
            pltpu.VMEM((4, 48, 384), jnp.float32),
            pltpu.VMEM((12, 24, 384), jnp.float32),
            pltpu.VMEM((2, 48, 384), jnp.float32),
            pltpu.VMEM((6, 8, 768), jnp.float32),
            pltpu.SemaphoreType.DMA((GROUPS, 11)),
            pltpu.SemaphoreType.DMA((GROUPS, 11)),
            pltpu.SemaphoreType.DMA((6,)),
            pltpu.SemaphoreType.DMA((6,)),
        ],
        compiler_params=pltpu.CompilerParams(collective_id=1, has_side_effects=True, vmem_limit_bytes=60 * 2**20),
    )(ga, gi, go, small)


def scatter_grads(squares, ff_in, ff_out, small):
    low = jnp.bfloat16
    ga = jnp.stack([s.astype(low).reshape(4, 4, 48, 768) for s in squares])
    gi = jnp.stack([ff_in[:, 768 * j : 768 * j + 768].astype(low).reshape(4, 4, 48, 768) for j in range(4)])
    go = ff_out.astype(low).reshape(4, 4, 192, 768)
    a, b, c = scatter_call(ga, gi, go, small)
    return [a[u] for u in range(8)], jnp.concatenate([a[8 + u] for u in range(4)], axis=1), b, c


def by_kernels(shards):
    return (lax.axis_size("dp"), lax.axis_size("fsdp")) == (8, 4) and shards[0].shape == (24, 768)


def body(decoder_in, memory, out_grad, lengths, *params):
    shards, bucket_bias_table = params[:13], params[13]
    if by_kernels(shards):
        squares, whole_in, whole_out, gains = gather_weights(
            shards[:8], shards[8], shards[9], shards[10:]
        )
        matrices = squares + [whole_in, whole_out]
    else:
        matrices, gains = gather_all(shards)
    (
        self_query,
        self_key,
        self_value,
        self_out,
        cross_query,
        cross_key,
        cross_value,
        cross_out,
        ff_in,
        ff_out,
    ) = matrices
    norm_self, norm_cross, norm_ff = [gain.astype(jnp.float32) for gain in gains]
    micro, seqs, seq_length, width = decoder_in.shape
    groups = micro * seqs
    memory_bf = memory.reshape(groups, memory.shape[2], width)
    grad_bf = out_grad.reshape(groups, seq_length, width)
    group_lengths = lengths.reshape(groups)
    bucket_indicator = bucket_onehot(seq_length)
    relative_position_bias = jnp.einsum(
        "fsn,fe->esn",
        bucket_indicator,
        bucket_bias_table.astype(jnp.float32),
        precision=TOP_PRECISION,
    )
    positions = jnp.arange(seq_length, dtype=jnp.int32)
    causal = positions[:, None] >= positions[None, :]
    present = positions[None, :] < group_lengths[:, None]
    valid_rows = present[:, :, None].astype(jnp.float32)
    allowed = causal[None, None] & present[:, None, None, :]

    def grad_of(inputs, upstream):
        return weight_grad(rows_of(inputs), rows_of(upstream))

    decoded = decoder_in.reshape(groups, seq_length, width).astype(jnp.float32)
    normed = normalize(decoded, norm_self).astype(jnp.bfloat16)
    queries = project(normed, self_query).astype(jnp.bfloat16)
    key_rows = project(normed, self_key).astype(jnp.bfloat16)
    values = project(normed, self_value).astype(jnp.bfloat16)
    context, self_weights = attend_forward(
        queries, key_rows, values, relative_position_bias, allowed
    )
    after_self = decoded + project(context, self_out)
    normed_cross = normalize(after_self, norm_cross).astype(jnp.bfloat16)
    cross_queries = project(normed_cross, cross_query).astype(jnp.bfloat16)
    memory_keys = project(memory_bf, cross_key).astype(jnp.bfloat16)
    memory_values = project(memory_bf, cross_value).astype(jnp.bfloat16)
    cross_context, cross_weights = attend_forward(
        cross_queries, memory_keys, memory_values, 0.0, True
    )
    after_cross = after_self + project(cross_context, cross_out)
    normed_ff = normalize(after_cross, norm_ff).astype(jnp.bfloat16)
    hidden = project(normed_ff, ff_in)
    activated = jax.nn.gelu(hidden, approximate=True).astype(jnp.bfloat16)
    after_ff = after_cross + project(activated, ff_out)
    layer_out = (after_ff * valid_rows).astype(jnp.bfloat16)

    def back(operand, weight):
        return lax.dot_general(
            operand, weight, (((2,), (1,)), ((), ())), preferred_element_type=jnp.float32
        )

    grad_after = grad_bf.astype(jnp.float32) * valid_rows
    grad_branch = grad_after.astype(jnp.bfloat16)
    grad_ff_out = grad_of(activated, grad_branch)
    gelu_pull = jax.vjp(lambda pre_act: jax.nn.gelu(pre_act, approximate=True), hidden)[1]
    grad_hidden = gelu_pull(back(grad_branch, ff_out))[0].astype(jnp.bfloat16)
    grad_ff_in = grad_of(normed_ff, grad_hidden)
    norm_pull = jax.vjp(normalize, after_cross, norm_ff)[1]
    grad_rows, grad_norm_ff = norm_pull(back(grad_hidden, ff_in))
    grad_after = grad_after + grad_rows
    grad_branch = grad_after.astype(jnp.bfloat16)
    grad_cross_out = grad_of(cross_context, grad_branch)
    grad_context = back(grad_branch, cross_out).astype(jnp.bfloat16)
    grad_cross_rows, grad_memory_keys, grad_memory_values, unused = attend_backward(
        cross_queries, memory_keys, memory_values, cross_weights, grad_context
    )
    grad_cross_query = grad_of(normed_cross, grad_cross_rows)
    grad_cross_key = grad_of(memory_bf, grad_memory_keys)
    grad_cross_value = grad_of(memory_bf, grad_memory_values)
    grad_memory = back(grad_memory_keys, cross_key) + back(grad_memory_values, cross_value)
    norm_pull = jax.vjp(normalize, after_self, norm_cross)[1]
    grad_rows, grad_norm_cross = norm_pull(back(grad_cross_rows, cross_query))
    grad_after = grad_after + grad_rows
    grad_branch = grad_after.astype(jnp.bfloat16)
    grad_self_out = grad_of(context, grad_branch)
    grad_context = back(grad_branch, self_out).astype(jnp.bfloat16)
    grad_queries, grad_key_rows, grad_values, score_gradient = attend_backward(
        queries, key_rows, values, self_weights, grad_context
    )
    grad_self_query = grad_of(normed, grad_queries)
    grad_self_key = grad_of(normed, grad_key_rows)
    grad_self_value = grad_of(normed, grad_values)
    grad_normed = (
        back(grad_queries, self_query) + back(grad_key_rows, self_key) + back(grad_values, self_value)
    )
    norm_pull = jax.vjp(normalize, decoded, norm_self)[1]
    grad_rows, grad_norm_self = norm_pull(grad_normed)
    grad_input = grad_after + grad_rows
    bias_grad = jnp.einsum(
        "fgd,ogd->fo", bucket_indicator, jnp.sum(score_gradient, axis=0), precision=TOP_PRECISION
    )
    matrix_grads = (
        grad_self_query,
        grad_self_key,
        grad_self_value,
        grad_self_out,
        grad_cross_query,
        grad_cross_key,
        grad_cross_value,
        grad_cross_out,
        grad_ff_in,
        grad_ff_out,
    )
    small = jnp.concatenate([grad_norm_self, grad_norm_cross, grad_norm_ff, bias_grad.reshape(-1)])
    if by_kernels(shards):
        small = jnp.pad(small, (0, 8 * width - small.shape[0])).reshape(8, width)
        squares, piece_in, piece_out, small = scatter_grads(
            matrix_grads[:8], matrix_grads[8], matrix_grads[9], small
        )
        pieces = squares + [piece_in, piece_out]
        small = small.reshape(-1)
    else:
        pieces = scatter_all(matrix_grads, shards[:10])
        small = lax.psum(small, AXES)
    mine = shards[10].shape[0]
    at = lax.axis_index(AXES) * mine
    gains_out = [
        lax.dynamic_slice_in_dim(small[k * width : (k + 1) * width], at, mine) for k in range(3)
    ]
    return (
        layer_out.reshape(decoder_in.shape),
        grad_input.reshape(decoder_in.shape),
        grad_memory.reshape(memory.shape),
        *pieces,
        *gains_out,
        small[3 * width : 3 * width + bucket_bias_table.size].reshape(bucket_bias_table.shape),
    )


def solution(mesh):
    return jax.shard_map(
        body,
        mesh=mesh,
        in_specs=(
            P(None, ("dp", "fsdp"), None, None),
            P(None, ("dp", "fsdp"), None, None),
            P(None, ("dp", "fsdp"), None, None),
            P(None, ("dp", "fsdp")),
            P(("dp", "fsdp"), None),
            P(("dp", "fsdp"), None),
            P(("dp", "fsdp"), None),
            P(("dp", "fsdp"), None),
            P(("dp", "fsdp"), None),
            P(("dp", "fsdp"), None),
            P(("dp", "fsdp"), None),
            P(("dp", "fsdp"), None),
            P(("dp", "fsdp"), None),
            P(("dp", "fsdp"), None),
            P(("dp", "fsdp")),
            P(("dp", "fsdp")),
            P(("dp", "fsdp")),
            P(),
        ),
        out_specs=(
            P(None, ("dp", "fsdp"), None, None),
            P(None, ("dp", "fsdp"), None, None),
            P(None, ("dp", "fsdp"), None, None),
            P(("dp", "fsdp"), None),
            P(("dp", "fsdp"), None),
            P(("dp", "fsdp"), None),
            P(("dp", "fsdp"), None),
            P(("dp", "fsdp"), None),
            P(("dp", "fsdp"), None),
            P(("dp", "fsdp"), None),
            P(("dp", "fsdp"), None),
            P(("dp", "fsdp"), None),
            P(("dp", "fsdp"), None),
            P(("dp", "fsdp")),
            P(("dp", "fsdp")),
            P(("dp", "fsdp")),
            P(),
        ),
        check_vma=False,
    )
```

```python
import math

import jax
import jax.numpy as jnp
from jax import lax
from jax.experimental import pallas as pl
from jax.experimental.pallas import tpu as pltpu
from jax.sharding import PartitionSpec as P

HEADS = 12
BUCKETS = 32
MAX_DIST = 128


EPS = 1e-06
MASKED = -1e30
TOP_PRECISION = lax.Precision.HIGHEST


def bucket_onehot(length):
    half_count = BUCKETS // 2
    positions = jnp.arange(length, dtype=jnp.int32)
    distance = jnp.maximum(positions[:, None] - positions[None, :], 0)
    farther = jnp.zeros_like(distance)
    for level in range(1, half_count):
        border = int(math.ceil(half_count * (MAX_DIST / half_count) ** (level / half_count)))
        farther = farther + (distance >= border).astype(jnp.int32)
    bucket = jnp.where(distance < half_count, distance, half_count + farther)
    return (bucket[None] == jnp.arange(BUCKETS, dtype=jnp.int32)[:, None, None]).astype(jnp.float32)


def normalize(vector, gain_row):
    return vector * lax.rsqrt(jnp.mean(vector * vector, axis=-1, keepdims=True) + EPS) * gain_row


def project(operand, weight):
    return jnp.dot(operand, weight, preferred_element_type=jnp.float32)


def project_back(operand, weight):
    return lax.dot_general(
        operand, weight, (((1,), (1,)), ((), ())), preferred_element_type=jnp.float32
    )


def weight_grad(inputs_rows, grad_rows):
    return lax.dot_general(
        inputs_rows, grad_rows, (((0,), (0,)), ((), ())), preferred_element_type=jnp.float32
    )


def split_heads(matrix):
    return matrix.reshape(matrix.shape[:-1] + (HEADS, matrix.shape[-1] // HEADS))


def head_scores(queries, key_rows):
    return jnp.einsum(
        "gqhe,gkhe->ghqk",
        split_heads(queries),
        split_heads(key_rows),
        preferred_element_type=jnp.float32,
    )


def attend_forward(queries, key_rows, values, relative_position_bias, allowed):
    scores = jnp.where(allowed, head_scores(queries, key_rows) + relative_position_bias, MASKED)
    largest = jnp.max(scores, axis=-1, keepdims=True)
    exponent = jnp.exp(scores - largest)
    row_totals = jnp.sum(exponent, axis=-1, keepdims=True)
    attention_weights = exponent / row_totals
    context = jnp.einsum(
        "ghqk,gkhe->gqhe",
        attention_weights.astype(jnp.bfloat16),
        split_heads(values),
        preferred_element_type=jnp.float32,
    )
    return (context.reshape(queries.shape).astype(jnp.bfloat16), attention_weights)


def attend_backward(queries, key_rows, values, attention_weights, grad_context):
    grad_heads = split_heads(grad_context)
    grad_values = jnp.einsum(
        "ghqk,gqhe->gkhe",
        attention_weights.astype(jnp.bfloat16),
        grad_heads,
        preferred_element_type=jnp.float32,
    )
    grad_weights = jnp.einsum(
        "gqhe,gkhe->ghqk", grad_heads, split_heads(values), preferred_element_type=jnp.float32
    )
    score_gradient = attention_weights * (
        grad_weights - jnp.sum(grad_weights * attention_weights, axis=-1, keepdims=True)
    )
    rounded = score_gradient.astype(jnp.bfloat16)
    grad_queries = jnp.einsum(
        "ghqk,gkhe->gqhe", rounded, split_heads(key_rows), preferred_element_type=jnp.float32
    )
    grad_keys = jnp.einsum(
        "ghqk,gqhe->gkhe", rounded, split_heads(queries), preferred_element_type=jnp.float32
    )
    return (
        grad_queries.reshape(queries.shape).astype(jnp.bfloat16),
        grad_keys.reshape(key_rows.shape).astype(jnp.bfloat16),
        grad_values.reshape(values.shape).astype(jnp.bfloat16),
        score_gradient,
    )


AXES = ("dp", "fsdp")


def rows_of(matrix):
    return matrix.reshape(-1, matrix.shape[-1])


def gather_all(shards):
    width = shards[0].shape[1]
    blocks = []
    for shard in shards:
        if shard.ndim == 1:
            continue
        blocks.append(shard.reshape(-1, width) if shard.shape[1] != width else shard)
    packed = lax.all_gather(jnp.concatenate(blocks, axis=0), AXES, axis=0)
    whole, at = [], 0
    devices = packed.shape[0]
    for shard, block in zip(shards, blocks):
        part = packed[:, at : at + block.shape[0]]
        at += block.shape[0]
        whole.append(part.reshape(devices * shard.shape[0], shard.shape[1]))
    gains = jnp.stack(shards[len(blocks) :])
    gains = lax.all_gather(gains, AXES, axis=1, tiled=True)
    return whole, [gains[k] for k in range(gains.shape[0])]


def scatter_all(grads, shards):
    width = shards[0].shape[1]
    devices = lax.axis_size(AXES)
    blocks = [grad.astype(jnp.bfloat16).reshape(devices, -1, width) for grad in grads]
    summed = lax.psum_scatter(
        jnp.concatenate(blocks, axis=1), AXES, scatter_dimension=0, tiled=False
    ).astype(jnp.float32)
    pieces, at = [], 0
    for block, shard in zip(blocks, shards):
        pieces.append(summed[at : at + block.shape[1]].reshape(shard.shape))
        at += block.shape[1]
    return pieces


def plain_body(decoder_in, memory, out_grad, lengths, *params):
    shards, bucket_bias_table = params[:13], params[13]
    matrices, gains = gather_all(shards)
    (
        self_query,
        self_key,
        self_value,
        self_out,
        cross_query,
        cross_key,
        cross_value,
        cross_out,
        ff_in,
        ff_out,
    ) = matrices
    norm_self, norm_cross, norm_ff = [gain.astype(jnp.float32) for gain in gains]
    micro, seqs, seq_length, width = decoder_in.shape
    groups = micro * seqs
    memory_bf = memory.reshape(groups, memory.shape[2], width)
    grad_bf = out_grad.reshape(groups, seq_length, width)
    group_lengths = lengths.reshape(groups)
    bucket_indicator = bucket_onehot(seq_length)
    relative_position_bias = jnp.einsum(
        "fsn,fe->esn",
        bucket_indicator,
        bucket_bias_table.astype(jnp.float32),
        precision=TOP_PRECISION,
    )
    positions = jnp.arange(seq_length, dtype=jnp.int32)
    causal = positions[:, None] >= positions[None, :]
    present = positions[None, :] < group_lengths[:, None]
    valid_rows = present[:, :, None].astype(jnp.float32)
    allowed = causal[None, None] & present[:, None, None, :]

    def grad_of(inputs, upstream):
        return weight_grad(rows_of(inputs), rows_of(upstream))

    decoded = decoder_in.reshape(groups, seq_length, width).astype(jnp.float32)
    normed = normalize(decoded, norm_self).astype(jnp.bfloat16)
    queries = project(normed, self_query).astype(jnp.bfloat16)
    key_rows = project(normed, self_key).astype(jnp.bfloat16)
    values = project(normed, self_value).astype(jnp.bfloat16)
    context, self_weights = attend_forward(
        queries, key_rows, values, relative_position_bias, allowed
    )
    after_self = decoded + project(context, self_out)
    normed_cross = normalize(after_self, norm_cross).astype(jnp.bfloat16)
    cross_queries = project(normed_cross, cross_query).astype(jnp.bfloat16)
    memory_keys = project(memory_bf, cross_key).astype(jnp.bfloat16)
    memory_values = project(memory_bf, cross_value).astype(jnp.bfloat16)
    cross_context, cross_weights = attend_forward(
        cross_queries, memory_keys, memory_values, 0.0, True
    )
    after_cross = after_self + project(cross_context, cross_out)
    normed_ff = normalize(after_cross, norm_ff).astype(jnp.bfloat16)
    hidden = project(normed_ff, ff_in)
    activated = jax.nn.gelu(hidden, approximate=True).astype(jnp.bfloat16)
    after_ff = after_cross + project(activated, ff_out)
    layer_out = (after_ff * valid_rows).astype(jnp.bfloat16)

    def back(operand, weight):
        return lax.dot_general(
            operand, weight, (((2,), (1,)), ((), ())), preferred_element_type=jnp.float32
        )

    grad_after = grad_bf.astype(jnp.float32) * valid_rows
    grad_branch = grad_after.astype(jnp.bfloat16)
    grad_ff_out = grad_of(activated, grad_branch)
    gelu_pull = jax.vjp(lambda pre_act: jax.nn.gelu(pre_act, approximate=True), hidden)[1]
    grad_hidden = gelu_pull(back(grad_branch, ff_out))[0].astype(jnp.bfloat16)
    grad_ff_in = grad_of(normed_ff, grad_hidden)
    norm_pull = jax.vjp(normalize, after_cross, norm_ff)[1]
    grad_rows, grad_norm_ff = norm_pull(back(grad_hidden, ff_in))
    grad_after = grad_after + grad_rows
    grad_branch = grad_after.astype(jnp.bfloat16)
    grad_cross_out = grad_of(cross_context, grad_branch)
    grad_context = back(grad_branch, cross_out).astype(jnp.bfloat16)
    grad_cross_rows, grad_memory_keys, grad_memory_values, unused = attend_backward(
        cross_queries, memory_keys, memory_values, cross_weights, grad_context
    )
    grad_cross_query = grad_of(normed_cross, grad_cross_rows)
    grad_cross_key = grad_of(memory_bf, grad_memory_keys)
    grad_cross_value = grad_of(memory_bf, grad_memory_values)
    grad_memory = back(grad_memory_keys, cross_key) + back(grad_memory_values, cross_value)
    norm_pull = jax.vjp(normalize, after_self, norm_cross)[1]
    grad_rows, grad_norm_cross = norm_pull(back(grad_cross_rows, cross_query))
    grad_after = grad_after + grad_rows
    grad_branch = grad_after.astype(jnp.bfloat16)
    grad_self_out = grad_of(context, grad_branch)
    grad_context = back(grad_branch, self_out).astype(jnp.bfloat16)
    grad_queries, grad_key_rows, grad_values, score_gradient = attend_backward(
        queries, key_rows, values, self_weights, grad_context
    )
    grad_self_query = grad_of(normed, grad_queries)
    grad_self_key = grad_of(normed, grad_key_rows)
    grad_self_value = grad_of(normed, grad_values)
    grad_normed = (
        back(grad_queries, self_query) + back(grad_key_rows, self_key) + back(grad_values, self_value)
    )
    norm_pull = jax.vjp(normalize, decoded, norm_self)[1]
    grad_rows, grad_norm_self = norm_pull(grad_normed)
    grad_input = grad_after + grad_rows
    bias_grad = jnp.einsum(
        "fgd,ogd->fo", bucket_indicator, jnp.sum(score_gradient, axis=0), precision=TOP_PRECISION
    )
    pieces = scatter_all(
        (
            grad_self_query,
            grad_self_key,
            grad_self_value,
            grad_self_out,
            grad_cross_query,
            grad_cross_key,
            grad_cross_value,
            grad_cross_out,
            grad_ff_in,
            grad_ff_out,
        ),
        shards[:10],
    )
    small = lax.psum(
        jnp.concatenate([grad_norm_self, grad_norm_cross, grad_norm_ff, bias_grad.reshape(-1)]),
        AXES,
    )
    mine = shards[10].shape[0]
    at = lax.axis_index(AXES) * mine
    gains_out = [
        lax.dynamic_slice_in_dim(small[k * width : (k + 1) * width], at, mine) for k in range(3)
    ]
    return (
        layer_out.reshape(decoder_in.shape),
        grad_input.reshape(decoder_in.shape),
        grad_memory.reshape(memory.shape),
        *pieces,
        *gains_out,
        small[3 * width :].reshape(bucket_bias_table.shape),
    )


MESH = pl.DeviceIdType.MESH
LOW = jnp.bfloat16
WIDE = jnp.float32
GROUPS = 16
WIDTH = 768
ROWS = 512
LENGTH = 256
MEMORY = 128
PAIRS = 6
CURVE = math.sqrt(2.0 / math.pi)


def place():
    dp, fsdp = lax.axis_index("dp"), lax.axis_index("fsdp")
    z, y, x, core = dp // 2, dp % 2, fsdp // 2, fsdp % 2
    sibling = (dp, x * 2 + 1 - core)
    over_x = (dp, (1 - x) * 2 + core)
    over_y = (z * 2 + 1 - y, fsdp)
    first = (jnp.where(core == 0, over_x[0], over_y[0]), jnp.where(core == 0, over_x[1], over_y[1]))
    second = (jnp.where(core == 0, over_y[0], over_x[0]), jnp.where(core == 0, over_y[1], over_x[1]))
    along_z = [(((z + k) % 4) * 2 + y, fsdp) for k in (1, 2, 3)]
    own = y * 2 + x
    beside = jnp.where(core == 0, y * 2 + 1 - x, (1 - y) * 2 + x)
    return z, own, beside, core, sibling, first, second, along_z


def greet(partners):
    barrier = pltpu.get_barrier_semaphore()
    for partner in partners:
        pl.semaphore_signal(barrier, inc=1, device_id=partner, device_id_type=MESH)
    pl.semaphore_wait(barrier, len(partners))


def half(core):
    return pl.ds(pl.multiple_of(core * 384, 128), 384)


def skew(ahead, groups=GROUPS):
    order = []
    for t in range(-max(ahead), groups + 8):
        for s in range(len(ahead)):
            g = t + ahead[s]
            if 0 <= g < groups:
                order.append((g, s))
    return order


def dot(a, b):
    return jnp.dot(a, b, preferred_element_type=WIDE)


def dot_nt(a, b):
    return lax.dot_general(a, b, (((1,), (1,)), ((), ())), preferred_element_type=WIDE)


def dot_tn(a, b):
    return lax.dot_general(a, b, (((0,), (0,)), ((), ())), preferred_element_type=WIDE)


def unit(w, u):
    return w[u].reshape(WIDTH, WIDTH)


def root_scale(value):
    return lax.rsqrt(jnp.mean(value * value, axis=-1, keepdims=True) + EPS)


def bucket_columns(flipped):
    j = lax.broadcasted_iota(jnp.int32, (BUCKETS, LENGTH), 1)
    row = lax.broadcasted_iota(jnp.int32, (BUCKETS, LENGTH), 0)
    n = jnp.where(j == 0, 0, LENGTH - j) if flipped else j
    half_count = BUCKETS // 2
    farther = jnp.zeros_like(n)
    for level in range(1, half_count):
        border = int(math.ceil(half_count * (MAX_DIST / half_count) ** (level / half_count)))
        farther = farther + (n >= border).astype(jnp.int32)
    bucket = jnp.where(n < half_count, n, half_count + farther)
    return (bucket == row).astype(WIDE)


ZS = (1, 4, 7, 10, 13)
AHEAD = (6, 4, 2, 1, 0)
BUDGET = 4.5


def forward_kernel(
    small_ref, tall_ref, gain_ref, x_ref, mem_ref, table_ref, lens_ref,
    w_out, gains_out, normed_out, q_out, k_out, v_out, ctx_out, p_out, after_self_out, ncross_out,
    cq_out, mk_out, mv_out, cctx_out, pc_out, after_cross_out, nff_out, act_out, slope_out, layer_out,
    w, gains, normed, q, k, v, ctx, p, after_self, ncross, cq, mk, mv, cctx, pc, after_cross, nff, act, slope, layer,
    bias, sib, gain_in, ss, rs, ss0, rs0, out_sem,
):
    z, own, beside, core, sibling, first, second, along_z = place()
    mine, other = half(core), half(1 - core)

    def view(g, zi, yx, cols):
        if g < 12:
            return w.at[g, slice(None) if zi is None else zi, yx, :, cols]
        return w.at[pl.ds(12, 4) if zi is None else 12 + zi, yx, g - 12, :, cols]

    def whole(g, cols):
        return w.at[g, :, :, :, cols] if g < 12 else w.at[pl.ds(12, 4), :, g - 12, :, cols]

    def send(ref, to, g, n):
        return pltpu.make_async_remote_copy(
            src_ref=ref, dst_ref=ref, send_sem=ss.at[g, n], recv_sem=rs.at[g, n], device_id=to, device_id_type=MESH)

    def step_a(g):
        return [send(view(g, z, own, mine), to, g, n) for n, to in enumerate(along_z)]

    def step_b(g):
        return [send(view(g, None, own, mine), first, g, 3)]

    def step_c(g):
        return [send(view(g, None, own, mine), second, g, 4), send(view(g, None, beside, mine), second, g, 5)]

    def step_d(g):
        return [send(whole(g, mine), sibling, g, 6)]

    def step_b1(g):
        return [send(view(g, z, own, mine), first, g, 3)]

    def step_a2(g):
        return step_a(g) + [send(view(g, z, beside, mine), to, g, 7 + n) for n, to in enumerate(along_z)]

    def gain_copies(s):
        to = ([sibling], along_z, [first], [second])[s]
        at = (0, 1, 4, 5)[s]
        return [
            pltpu.make_async_remote_copy(
                src_ref=gains, dst_ref=gain_in.at[at + n], send_sem=ss0.at[2 + at + n], recv_sem=rs0.at[2 + at + n],
                device_id=d, device_id_type=MESH)
            for n, d in enumerate(to)
        ]

    def start(copies):
        for copy in copies:
            copy.start()

    def gain_finish(s):
        for copy in gain_copies(s):
            copy.wait()
        for n in ((0,), (1, 2, 3), (4,), (5,))[s]:
            gains[...] += gain_in[n]

    stores = []

    def store(src, dst):
        copy = pltpu.make_async_copy(src, dst, out_sem.at[len(stores)])
        stores.append(copy)
        copy.start()

    def store_unit(g):
        if g < 12:
            store(w.at[g], w_out.at[g])

    def gain(n):
        return gains[n : n + 1, :].astype(WIDE)

    def scale_rows(src, n, dst):
        g = gain(n)

        def chunk(i, c):
            rows = pl.ds(pl.multiple_of(i * 128, 128), 128)
            value = src[rows, :].astype(WIDE)
            dst[rows, :] = (value * root_scale(value) * g).astype(LOW)
            return c

        lax.fori_loop(0, ROWS // 128, chunk, 0)

    def make_bias():
        by_distance = dot(table_ref[...], bucket_columns(True).astype(LOW))
        for h in range(HEADS):
            row = jnp.broadcast_to(by_distance[h : h + 1, :], (LENGTH, LENGTH))
            bias[h] = pltpu.roll(row, 0, 1, stride=1, stride_axis=0)

    def project_into(src, u, dst):
        dst[...] = dot(src[...], unit(w, u)).astype(LOW)

    lane = lax.broadcasted_iota(jnp.int32, (1, 128), 1)
    sides = [lane < 64, lane >= 64]

    def attend(i, queries, keys, vals, keep_p, into, depth, masked):
        s, pair = i // PAIRS, i % PAIRS
        rows = pl.ds(pl.multiple_of(s * LENGTH, LENGTH), LENGTH)
        deep = pl.ds(pl.multiple_of(s * depth, depth), depth)
        cols = pl.ds(pl.multiple_of(pair * 128, 128), 128)
        qp, kp, vp = queries[rows, cols], keys[deep, cols], vals[deep, cols]
        parts = []
        for side in range(2):
            scores = dot_nt(jnp.where(sides[side], qp, jnp.zeros_like(qp)), kp)
            if masked:
                t = lax.broadcasted_iota(jnp.int32, (LENGTH, LENGTH), 0)
                u = lax.broadcasted_iota(jnp.int32, (LENGTH, LENGTH), 1)
                allowed = (u <= t) & (u < lens_ref[s])
                scores = jnp.where(allowed, scores + bias[2 * pair + side], MASKED)
            e = jnp.exp(scores - jnp.max(scores, axis=-1, keepdims=True))
            weights = (e * (1.0 / jnp.sum(e, axis=-1, keepdims=True))).astype(LOW)
            keep_p[rows, pl.ds(pl.multiple_of((2 * pair + side) * depth, 128), depth)] = weights
            parts.append(dot(weights, vp))
        into[rows, cols] = jnp.where(sides[0], parts[0], parts[1]).astype(LOW)

    def self_part(lo, hi):
        def it(i, c):
            attend(i, q, k, v, p, ctx, LENGTH, True)
            return c

        lax.fori_loop(lo, hi, it, 0)

    def cross_part(lo, hi):
        def it(i, c):
            attend(i, cq, mk, mv, pc, cctx, MEMORY, False)
            return c

        lax.fori_loop(lo, hi, it, 0)

    def after_self_part():
        after_self[...] = x_ref[...].astype(WIDE) + dot(ctx[...], unit(w, 3))
        scale_rows(after_self, 1, ncross)

    def after_cross_part():
        after_cross[...] = after_self[...] + dot(cctx[...], unit(w, 7))
        scale_rows(after_cross, 2, nff)

    def hidden_part(j):
        cols = slice(j * WIDTH, (j + 1) * WIDTH)
        for m in range(2):
            rows = slice(m * 256, m * 256 + 256)
            a = dot(nff[rows, :], unit(w, 8 + j))
            sq = a * a
            th = jnp.tanh(a * (CURVE + (CURVE * 0.044715) * sq))
            act[rows, cols] = (0.5 * a * (1.0 + th)).astype(LOW)
            slope[rows, cols] = (
                0.5 * (1.0 + th) + 0.5 * a * (1.0 - th * th) * (CURVE + (3.0 * CURVE * 0.044715) * sq)
            ).astype(LOW)

    def layer_part():
        total = after_cross[...]
        for j in range(4):
            total = total + dot(act[:, j * WIDTH : (j + 1) * WIDTH], unit(w, 12 + j))
        for s in range(2):
            t = lax.broadcasted_iota(jnp.int32, (LENGTH, 1), 0)
            valid = (t < lens_ref[s]).astype(WIDE)
            layer[s * LENGTH : (s + 1) * LENGTH, :] = (total[s * LENGTH : (s + 1) * LENGTH] * valid).astype(LOW)

    pieces = [
        (0, 1.0, lambda: project_into(normed, 0, q)), (0, 0.1, lambda: store(q, q_out)),
        (1, 1.0, lambda: project_into(normed, 1, k)), (1, 0.1, lambda: store(k, k_out)),
        (2, 1.0, lambda: project_into(normed, 2, v)), (2, 0.1, lambda: store(v, v_out)),
        (2, 2.5, lambda: self_part(0, 3)), (2, 2.5, lambda: self_part(3, 6)),
        (2, 2.5, lambda: self_part(6, 9)), (2, 2.5, lambda: self_part(9, 12)),
        (2, 0.1, lambda: store(ctx, ctx_out)), (2, 0.1, lambda: store(p, p_out)),
        (3, 2.0, after_self_part), (3, 0.1, lambda: store(after_self, after_self_out)), (3, 0.1, lambda: store(ncross, ncross_out)),
        (4, 1.0, lambda: project_into(ncross, 4, cq)), (4, 0.1, lambda: store(cq, cq_out)),
        (5, 0.6, lambda: project_into(mem_ref, 5, mk)), (5, 0.1, lambda: store(mk, mk_out)),
        (6, 0.6, lambda: project_into(mem_ref, 6, mv)), (6, 0.1, lambda: store(mv, mv_out)),
        (6, 2.5, lambda: cross_part(0, 4)), (6, 2.5, lambda: cross_part(4, 8)), (6, 2.5, lambda: cross_part(8, 12)),
        (6, 0.1, lambda: store(cctx, cctx_out)), (6, 0.1, lambda: store(pc, pc_out)),
        (7, 2.0, after_cross_part), (7, 0.1, lambda: store(after_cross, after_cross_out)), (7, 0.1, lambda: store(nff, nff_out)),
        (8, 2.0, lambda: hidden_part(0)), (9, 2.0, lambda: hidden_part(1)),
        (10, 2.0, lambda: hidden_part(2)), (11, 2.0, lambda: hidden_part(3)),
        (11, 0.1, lambda: store(act, act_out)), (11, 0.1, lambda: store(slope, slope_out)),
        (15, 4.0, layer_part), (15, 0.1, lambda: store(layer, layer_out)),
    ]

    greet([sibling, first, second] + along_z)
    swap_small = pltpu.make_async_remote_copy(
        src_ref=small_ref.at[:, :, other], dst_ref=sib, send_sem=ss0.at[0], recv_sem=rs0.at[0],
        device_id=sibling, device_id_type=MESH)

    def tall_view(cols):
        return w.at[12 + z, own, pl.ds(2 * core, 2), :, cols]

    swap_tall = pltpu.make_async_remote_copy(
        src_ref=tall_ref.at[:, :, other], dst_ref=tall_view(other), send_sem=ss0.at[1], recv_sem=rs0.at[1],
        device_id=sibling, device_id_type=MESH)
    swap_small.start()
    swap_tall.start()
    gains[...] = gain_ref[...]
    start(gain_copies(0))
    w[12 + z, own, pl.ds(2 * core, 2), :, mine] = tall_ref[:, :, mine]
    swap_small.wait()
    for u in range(12):
        w[u, z, own, :, mine] = small_ref[u, :, mine] + sib[u]
    swap_tall.wait()
    gain_finish(0)
    start(gain_copies(1))

    zf = (step_a, step_b, step_c, step_d)
    zs = (step_b1, step_a2, step_c, step_d)
    stage, done = 1, 0
    for n, (g, s) in enumerate(skew(AHEAD)):
        steps = zs if g in ZS else zf
        if s:
            for copy in steps[s - 1](g):
                copy.wait()
        if s < 4:
            start(steps[s](g))
        if n == 8:
            make_bias()
        if n in (8, 11, 14):
            gain_finish(stage)
            stage += 1
            if stage < 4:
                start(gain_copies(stage))
            else:
                scale_rows(x_ref, 0, normed)
                store(normed, normed_out)
                store(gains, gains_out)
        if s == 4:
            store_unit(g)
            spent = 0.0
            while done < len(pieces) and pieces[done][0] <= g and (spent < BUDGET or g == GROUPS - 1):
                spent += pieces[done][1]
                pieces[done][2]()
                done += 1
            if g == GROUPS - 1:
                store(w.at[pl.ds(12, 4)], w_out.at[pl.ds(12, 4)])
    assert done == len(pieces) and stage == 4
    for copy in stores:
        copy.wait()


FORWARD_OUT = (
    ((16, 4, 4, 48, 768), LOW),
    ((16, 768), LOW),
    ((512, 768), LOW), ((512, 768), LOW), ((512, 768), LOW), ((512, 768), LOW),
    ((512, 768), LOW),
    ((512, 3072), LOW),
    ((512, 768), WIDE),
    ((512, 768), LOW),
    ((512, 768), LOW), ((256, 768), LOW), ((256, 768), LOW), ((512, 768), LOW),
    ((512, 1536), LOW),
    ((512, 768), WIDE),
    ((512, 768), LOW),
    ((512, 3072), LOW), ((512, 3072), LOW),
    ((512, 768), LOW),
)


def forward_call(small, tall, gain, x, mem, table, lens):
    return pl.pallas_call(
        forward_kernel,
        out_shape=tuple(jax.ShapeDtypeStruct(s, t) for s, t in FORWARD_OUT),
        in_specs=[pl.BlockSpec(memory_space=pltpu.VMEM)] * 6 + [pl.BlockSpec(memory_space=pltpu.SMEM)],
        out_specs=[pl.BlockSpec(memory_space=pl.ANY)] * len(FORWARD_OUT),
        scratch_shapes=[pltpu.VMEM(s, t) for s, t in FORWARD_OUT]
        + [
            pltpu.VMEM((HEADS, LENGTH, LENGTH), WIDE),
            pltpu.VMEM((12, 48, 384), LOW),
            pltpu.VMEM((6, 16, 768), LOW),
            pltpu.SemaphoreType.DMA((GROUPS, 10)),
            pltpu.SemaphoreType.DMA((GROUPS, 10)),
            pltpu.SemaphoreType.DMA((8,)),
            pltpu.SemaphoreType.DMA((8,)),
            pltpu.SemaphoreType.DMA((32,)),
        ],
        compiler_params=pltpu.CompilerParams(collective_id=0, has_side_effects=True, vmem_limit_bytes=60 * 2**20),
    )(small, tall, gain, x, mem, table, lens)


def pack(shards):
    core = lax.axis_index("fsdp") % 2
    units = list(shards[:8]) + [shards[8][:, WIDTH * j : WIDTH * (j + 1)] for j in range(4)]
    block = jnp.stack(units)
    low = jnp.pad(block, ((0, 0), (0, 24), (0, 0)))
    high = jnp.pad(block, ((0, 0), (24, 0), (0, 0)))
    at = lax.axis_index(("dp", "fsdp")) * 24
    placed = lax.dynamic_update_slice(jnp.zeros((16, WIDTH), LOW), jnp.stack(shards[10:13]), (0, at))
    return jnp.where(core == 0, low, high), shards[9].reshape(2, 48, WIDTH), placed


def forward(shards, decoder_in, memory, table, lengths):
    small, tall, gain = pack(shards)
    padded = jnp.pad(table.T, ((0, 16 - HEADS), (0, 0)))
    return forward_call(
        small, tall, gain, decoder_in.reshape(ROWS, WIDTH), memory.reshape(2 * MEMORY, WIDTH), padded, lengths.reshape(2)
    )


ZS2 = (2, 5, 8, 11)
ORDER2 = skew((8, 7, 6, 4, 2, 0))
SMALL_AT = (3, 6, 9, 12)


def scatter_kernel(ga, gi, go, small_ref, small_out, tall_out, acc_small, r0, r1, r2, r3, fa, fo, fa_in, fo_in, small_in, ss, rs, ss0, rs0):
    z, own, beside, core, sibling, first, second, along_z = place()
    mine, other = half(core), half(1 - core)
    diag = 3 - own
    across = 3 - beside
    f32 = jnp.float32

    def block(g, cols):
        if g < 8:
            return ga.at[g, :, :, :, cols]
        if g < 12:
            return gi.at[g - 8, :, :, :, cols]
        return go.at[:, :, pl.ds(48 * (g - 12), 48), cols]

    def send(src, dst, to, g, k):
        return pltpu.make_async_remote_copy(
            src_ref=src, dst_ref=dst, send_sem=ss.at[g, k], recv_sem=rs.at[g, k], device_id=to, device_id_type=MESH)

    def swap(g):
        return [send(block(g, other), r0.at[g], sibling, g, 0)]

    def over_second(g):
        return [send(r0.at[g, :, across], r1.at[g, 0], second, g, 1), send(r0.at[g, :, diag], r1.at[g, 1], second, g, 2)]

    def over_first(g):
        return [send(r0.at[g, :, beside], r2.at[g], first, g, 3)]

    def over_z(g):
        return [send(r0.at[g, (z + k + 1) % 4, own], r3.at[g, 0, k], to, g, 4 + k) for k, to in enumerate(along_z)]

    def over_z2(g):
        return over_z(g) + [
            send(r0.at[g, (z + k + 1) % 4, beside], r3.at[g, 1, k], to, g, 7 + k) for k, to in enumerate(along_z)]

    def over_first1(g):
        return [send(r0.at[g, z, beside], r2.at[g, 0], first, g, 3)]

    def last(g):
        if g < 12:
            rows = pl.ds(pl.multiple_of(24 * (1 - core), 8), 24)
            return [send(fa.at[g, rows], fa_in.at[g], sibling, g, 10)]
        if g == 15:
            return [send(fo.at[pl.ds(2 * (1 - core), 2)], fo_in, sibling, g, 10)]
        return []

    def add0(g):
        r0[g] += block(g, mine)[...]

    def add1(g):
        r0[g, :, own] += r1[g, 0]
        r0[g, :, beside] += r1[g, 1]

    def finish(g, value):
        if g < 12:
            fa[g] = value
        else:
            fo[g - 12] = value

    def add2(g):
        r0[g, :, own] += r2[g]

    def add3(g):
        finish(g, r0[g, z, own].astype(f32) + r3[g, 0, 0].astype(f32) + r3[g, 0, 1].astype(f32) + r3[g, 0, 2].astype(f32))

    def add2z(g):
        for j, yx in enumerate((own, beside)):
            total = r0[g, z, yx].astype(f32) + r3[g, j, 0].astype(f32) + r3[g, j, 1].astype(f32) + r3[g, j, 2].astype(f32)
            r0[g, z, yx] = total.astype(jnp.bfloat16)

    def add3z(g):
        finish(g, r0[g, z, own].astype(f32) + r2[g, 0].astype(f32))

    def write(g):
        if g < 12:
            rows = pl.ds(pl.multiple_of(24 * core, 8), 24)
            small_out[g, :, mine] = fa[g, rows]
            small_out[g, :, other] = fa_in[g]
        elif g == 15:
            tall_out[:, mine] = fo[pl.ds(2 * core, 2)].reshape(96, 384)
            tall_out[:, other] = fo_in[...].reshape(96, 384)

    zf = ([swap, over_second, over_first, over_z, last], [None, add0, add1, add2, add3, write])
    zs = ([swap, over_second, over_z2, over_first1, last], [None, add0, add1, add2z, add3z, write])

    def small_copies(s):
        to = ([sibling], along_z, [first], [second])[s]
        at = (0, 1, 4, 5)[s]
        return [
            pltpu.make_async_remote_copy(
                src_ref=acc_small, dst_ref=small_in.at[at + k], send_sem=ss0.at[at + k], recv_sem=rs0.at[at + k],
                device_id=d, device_id_type=MESH)
            for k, d in enumerate(to)
        ]

    greet([sibling, first, second] + along_z)
    acc_small[...] = small_ref[...]
    for copy in small_copies(0):
        copy.start()
    stage = 0
    for n, (g, s) in enumerate(ORDER2):
        copies, sums = zs if g in ZS2 else zf
        if s:
            for copy in copies[s - 1](g):
                copy.wait()
            sums[s](g)
        if s < 5:
            for copy in copies[s](g):
                copy.start()
        if n in SMALL_AT:
            for copy in small_copies(stage):
                copy.wait()
            for k in ((0,), (1, 2, 3), (4,), (5,))[stage]:
                acc_small[...] += small_in[k]
            stage += 1
            if stage < 4:
                for copy in small_copies(stage):
                    copy.start()
    small_out_done = stage
    assert small_out_done == 4


def scatter_call(ga, gi, go, small):
    def wrapped(ga, gi, go, small, small_out, tall_out, sum_out, *scratch):
        scatter_kernel(ga, gi, go, small, small_out, tall_out, sum_out, *scratch)

    return pl.pallas_call(
        wrapped,
        out_shape=(
            jax.ShapeDtypeStruct((12, 24, 768), jnp.float32),
            jax.ShapeDtypeStruct((96, 768), jnp.float32),
            jax.ShapeDtypeStruct((8, 768), jnp.float32),
        ),
        in_specs=[pl.BlockSpec(memory_space=pltpu.VMEM)] * 4,
        out_specs=[pl.BlockSpec(memory_space=pltpu.VMEM)] * 3,
        scratch_shapes=[
            pltpu.VMEM((GROUPS, 4, 4, 48, 384), jnp.bfloat16),
            pltpu.VMEM((GROUPS, 2, 4, 48, 384), jnp.bfloat16),
            pltpu.VMEM((GROUPS, 4, 48, 384), jnp.bfloat16),
            pltpu.VMEM((GROUPS, 2, 3, 48, 384), jnp.bfloat16),
            pltpu.VMEM((12, 48, 384), jnp.float32),
            pltpu.VMEM((4, 48, 384), jnp.float32),
            pltpu.VMEM((12, 24, 384), jnp.float32),
            pltpu.VMEM((2, 48, 384), jnp.float32),
            pltpu.VMEM((6, 8, 768), jnp.float32),
            pltpu.SemaphoreType.DMA((GROUPS, 11)),
            pltpu.SemaphoreType.DMA((GROUPS, 11)),
            pltpu.SemaphoreType.DMA((6,)),
            pltpu.SemaphoreType.DMA((6,)),
        ],
        compiler_params=pltpu.CompilerParams(collective_id=1, has_side_effects=True, vmem_limit_bytes=60 * 2**20),
    )(ga, gi, go, small)


def scatter_grads(squares, ff_in, ff_out, small):
    low = jnp.bfloat16
    ga = jnp.stack([s.astype(low).reshape(4, 4, 48, 768) for s in squares])
    gi = jnp.stack([ff_in[:, 768 * j : 768 * j + 768].astype(low).reshape(4, 4, 48, 768) for j in range(4)])
    go = ff_out.astype(low).reshape(4, 4, 192, 768)
    a, b, c = scatter_call(ga, gi, go, small)
    return [a[u] for u in range(8)], jnp.concatenate([a[8 + u] for u in range(4)], axis=1), b, c


def kernel_body(decoder_in, memory, out_grad, lengths, *params):
    shards, bucket_bias_table = params[:13], params[13]
    (
        whole, gains, normed, queries, key_rows, values, context, self_weights, after_self, normed_cross,
        cross_queries, memory_keys, memory_values, cross_context, cross_weights, after_cross, normed_ff,
        activated, slope, layer_out,
    ) = forward(shards, decoder_in, memory, bucket_bias_table, lengths)
    squares = [whole[u].reshape(WIDTH, WIDTH) for u in range(12)]
    self_query, self_key, self_value, self_out, cross_query, cross_key, cross_value, cross_out = squares[:8]
    ff_in = jnp.concatenate(squares[8:], axis=1)
    ff_out = whole[12:].reshape(4 * WIDTH, WIDTH)
    norm_self, norm_cross, norm_ff = [gains[k].astype(WIDE) for k in range(3)]

    def pairs(matrix):
        return matrix.reshape(2, -1, matrix.shape[-1])

    def by_head(weights):
        weights = pairs(weights).reshape(2, LENGTH, HEADS, -1)
        return weights.transpose(0, 2, 1, 3).astype(WIDE)

    present = jnp.arange(LENGTH)[None, :] < lengths.reshape(2, 1)
    grad_after = (out_grad.reshape(2, LENGTH, WIDTH) * present[:, :, None]).reshape(ROWS, WIDTH).astype(WIDE)
    grad_branch = grad_after.astype(LOW)
    grad_ff_out = weight_grad(activated, grad_branch)
    grad_hidden = (project_back(grad_branch, ff_out) * slope).astype(LOW)
    grad_ff_in = weight_grad(normed_ff, grad_hidden)
    norm_pull = jax.vjp(normalize, after_cross, norm_ff)[1]
    grad_rows, grad_norm_ff = norm_pull(project_back(grad_hidden, ff_in))
    grad_after = grad_after + grad_rows
    grad_branch = grad_after.astype(LOW)
    grad_cross_out = weight_grad(cross_context, grad_branch)
    grad_context = project_back(grad_branch, cross_out).astype(LOW)
    grad_cross_rows, grad_memory_keys, grad_memory_values, unused = attend_backward(
        pairs(cross_queries), pairs(memory_keys), pairs(memory_values), by_head(cross_weights), pairs(grad_context)
    )
    memory_rows = memory.reshape(2 * MEMORY, WIDTH)
    grad_cross_rows, grad_memory_keys, grad_memory_values = [
        rows_of(g) for g in (grad_cross_rows, grad_memory_keys, grad_memory_values)]
    grad_cross_query = weight_grad(normed_cross, grad_cross_rows)
    grad_cross_key = weight_grad(memory_rows, grad_memory_keys)
    grad_cross_value = weight_grad(memory_rows, grad_memory_values)
    grad_memory = project_back(grad_memory_keys, cross_key) + project_back(grad_memory_values, cross_value)
    norm_pull = jax.vjp(normalize, after_self, norm_cross)[1]
    grad_rows, grad_norm_cross = norm_pull(project_back(grad_cross_rows, cross_query))
    grad_after = grad_after + grad_rows
    grad_branch = grad_after.astype(LOW)
    grad_self_out = weight_grad(context, grad_branch)
    grad_context = project_back(grad_branch, self_out).astype(LOW)
    grad_queries, grad_key_rows, grad_values, score_gradient = attend_backward(
        pairs(queries), pairs(key_rows), pairs(values), by_head(self_weights), pairs(grad_context)
    )
    grad_queries, grad_key_rows, grad_values = [rows_of(g) for g in (grad_queries, grad_key_rows, grad_values)]
    grad_normed = (
        project_back(grad_queries, self_query)
        + project_back(grad_key_rows, self_key)
        + project_back(grad_values, self_value)
    )
    norm_pull = jax.vjp(normalize, decoder_in.reshape(ROWS, WIDTH).astype(WIDE), norm_self)[1]
    grad_rows, grad_norm_self = norm_pull(grad_normed)
    grad_input = grad_after + grad_rows
    bias_grad = jnp.einsum(
        "fgd,ogd->fo", bucket_onehot(LENGTH), jnp.sum(score_gradient, axis=0), precision=TOP_PRECISION
    )
    small = jnp.concatenate([grad_norm_self, grad_norm_cross, grad_norm_ff, bias_grad.reshape(-1)])
    small = jnp.pad(small, (0, 8 * WIDTH - small.shape[0])).reshape(8, WIDTH)
    square_pieces, piece_in, piece_out, small = scatter_grads(
        (
            weight_grad(normed, grad_queries),
            weight_grad(normed, grad_key_rows),
            weight_grad(normed, grad_values),
            grad_self_out,
            grad_cross_query,
            grad_cross_key,
            grad_cross_value,
            grad_cross_out,
        ),
        grad_ff_in,
        grad_ff_out,
        small,
    )
    mine = shards[10].shape[0]
    at = lax.axis_index(AXES) * mine
    gains_out = [lax.dynamic_slice_in_dim(small[k], at, mine) for k in range(3)]
    return (
        layer_out.reshape(decoder_in.shape),
        grad_input.reshape(decoder_in.shape),
        grad_memory.reshape(memory.shape),
        *square_pieces,
        piece_in,
        piece_out,
        *gains_out,
        small[3:].reshape(-1)[: bucket_bias_table.size].reshape(bucket_bias_table.shape),
    )


def body(decoder_in, memory, out_grad, lengths, *params):
    sizes = (lax.axis_size("dp"), lax.axis_size("fsdp"))
    if sizes == (8, 4) and decoder_in.shape == (2, 1, LENGTH, WIDTH) and params[0].shape == (24, WIDTH):
        return kernel_body(decoder_in, memory, out_grad, lengths, *params)
    return plain_body(decoder_in, memory, out_grad, lengths, *params)


def solution(mesh):
    return jax.shard_map(
        body,
        mesh=mesh,
        in_specs=(
            P(None, ("dp", "fsdp"), None, None),
            P(None, ("dp", "fsdp"), None, None),
            P(None, ("dp", "fsdp"), None, None),
            P(None, ("dp", "fsdp")),
            P(("dp", "fsdp"), None),
            P(("dp", "fsdp"), None),
            P(("dp", "fsdp"), None),
            P(("dp", "fsdp"), None),
            P(("dp", "fsdp"), None),
            P(("dp", "fsdp"), None),
            P(("dp", "fsdp"), None),
            P(("dp", "fsdp"), None),
            P(("dp", "fsdp"), None),
            P(("dp", "fsdp"), None),
            P(("dp", "fsdp")),
            P(("dp", "fsdp")),
            P(("dp", "fsdp")),
            P(),
        ),
        out_specs=(
            P(None, ("dp", "fsdp"), None, None),
            P(None, ("dp", "fsdp"), None, None),
            P(None, ("dp", "fsdp"), None, None),
            P(("dp", "fsdp"), None),
            P(("dp", "fsdp"), None),
            P(("dp", "fsdp"), None),
            P(("dp", "fsdp"), None),
            P(("dp", "fsdp"), None),
            P(("dp", "fsdp"), None),
            P(("dp", "fsdp"), None),
            P(("dp", "fsdp"), None),
            P(("dp", "fsdp"), None),
            P(("dp", "fsdp"), None),
            P(("dp", "fsdp")),
            P(("dp", "fsdp")),
            P(("dp", "fsdp")),
            P(),
        ),
        check_vma=False,
    )
```

```python
import functools
import math

import jax
import jax.numpy as jnp
from jax import lax
from jax.experimental import pallas as pl
from jax.experimental.pallas import tpu as pltpu
from jax.sharding import PartitionSpec as P

HEADS = 12
BUCKETS = 32
MAX_DIST = 128


EPS = 1e-06
MASKED = -1e30
TOP_PRECISION = lax.Precision.HIGHEST


def bucket_onehot(length):
    half_count = BUCKETS // 2
    positions = jnp.arange(length, dtype=jnp.int32)
    distance = jnp.maximum(positions[:, None] - positions[None, :], 0)
    farther = jnp.zeros_like(distance)
    for level in range(1, half_count):
        border = int(math.ceil(half_count * (MAX_DIST / half_count) ** (level / half_count)))
        farther = farther + (distance >= border).astype(jnp.int32)
    bucket = jnp.where(distance < half_count, distance, half_count + farther)
    return (bucket[None] == jnp.arange(BUCKETS, dtype=jnp.int32)[:, None, None]).astype(jnp.float32)


def normalize(vector, gain_row):
    return vector * lax.rsqrt(jnp.mean(vector * vector, axis=-1, keepdims=True) + EPS) * gain_row


def project(operand, weight):
    return jnp.dot(operand, weight, preferred_element_type=jnp.float32)


def project_back(operand, weight):
    return lax.dot_general(
        operand, weight, (((1,), (1,)), ((), ())), preferred_element_type=jnp.float32
    )


def weight_grad(inputs_rows, grad_rows):
    return lax.dot_general(
        inputs_rows, grad_rows, (((0,), (0,)), ((), ())), preferred_element_type=jnp.float32
    )


def split_heads(matrix):
    return matrix.reshape(matrix.shape[:-1] + (HEADS, matrix.shape[-1] // HEADS))


def head_scores(queries, key_rows):
    return jnp.einsum(
        "gqhe,gkhe->ghqk",
        split_heads(queries),
        split_heads(key_rows),
        preferred_element_type=jnp.float32,
    )


def attend_forward(queries, key_rows, values, relative_position_bias, allowed):
    scores = jnp.where(allowed, head_scores(queries, key_rows) + relative_position_bias, MASKED)
    largest = jnp.max(scores, axis=-1, keepdims=True)
    exponent = jnp.exp(scores - largest)
    row_totals = jnp.sum(exponent, axis=-1, keepdims=True)
    attention_weights = exponent / row_totals
    context = jnp.einsum(
        "ghqk,gkhe->gqhe",
        attention_weights.astype(jnp.bfloat16),
        split_heads(values),
        preferred_element_type=jnp.float32,
    )
    return (context.reshape(queries.shape).astype(jnp.bfloat16), attention_weights)


def attend_backward(queries, key_rows, values, attention_weights, grad_context):
    grad_heads = split_heads(grad_context)
    grad_values = jnp.einsum(
        "ghqk,gqhe->gkhe",
        attention_weights.astype(jnp.bfloat16),
        grad_heads,
        preferred_element_type=jnp.float32,
    )
    grad_weights = jnp.einsum(
        "gqhe,gkhe->ghqk", grad_heads, split_heads(values), preferred_element_type=jnp.float32
    )
    score_gradient = attention_weights * (
        grad_weights - jnp.sum(grad_weights * attention_weights, axis=-1, keepdims=True)
    )
    rounded = score_gradient.astype(jnp.bfloat16)
    grad_queries = jnp.einsum(
        "ghqk,gkhe->gqhe", rounded, split_heads(key_rows), preferred_element_type=jnp.float32
    )
    grad_keys = jnp.einsum(
        "ghqk,gqhe->gkhe", rounded, split_heads(queries), preferred_element_type=jnp.float32
    )
    return (
        grad_queries.reshape(queries.shape).astype(jnp.bfloat16),
        grad_keys.reshape(key_rows.shape).astype(jnp.bfloat16),
        grad_values.reshape(values.shape).astype(jnp.bfloat16),
        score_gradient,
    )


AXES = ("dp", "fsdp")


def rows_of(matrix):
    return matrix.reshape(-1, matrix.shape[-1])


def gather_all(shards):
    width = shards[0].shape[1]
    blocks = []
    for shard in shards:
        if shard.ndim == 1:
            continue
        blocks.append(shard.reshape(-1, width) if shard.shape[1] != width else shard)
    packed = lax.all_gather(jnp.concatenate(blocks, axis=0), AXES, axis=0)
    whole, at = [], 0
    devices = packed.shape[0]
    for shard, block in zip(shards, blocks):
        part = packed[:, at : at + block.shape[0]]
        at += block.shape[0]
        whole.append(part.reshape(devices * shard.shape[0], shard.shape[1]))
    gains = jnp.stack(shards[len(blocks) :])
    gains = lax.all_gather(gains, AXES, axis=1, tiled=True)
    return whole, [gains[k] for k in range(gains.shape[0])]


def scatter_all(grads, shards):
    width = shards[0].shape[1]
    devices = lax.axis_size(AXES)
    blocks = [grad.astype(jnp.bfloat16).reshape(devices, -1, width) for grad in grads]
    summed = lax.psum_scatter(
        jnp.concatenate(blocks, axis=1), AXES, scatter_dimension=0, tiled=False
    ).astype(jnp.float32)
    pieces, at = [], 0
    for block, shard in zip(blocks, shards):
        pieces.append(summed[at : at + block.shape[1]].reshape(shard.shape))
        at += block.shape[1]
    return pieces


def plain_body(decoder_in, memory, out_grad, lengths, *params):
    shards, bucket_bias_table = params[:13], params[13]
    matrices, gains = gather_all(shards)
    (
        self_query,
        self_key,
        self_value,
        self_out,
        cross_query,
        cross_key,
        cross_value,
        cross_out,
        ff_in,
        ff_out,
    ) = matrices
    norm_self, norm_cross, norm_ff = [gain.astype(jnp.float32) for gain in gains]
    micro, seqs, seq_length, width = decoder_in.shape
    groups = micro * seqs
    memory_bf = memory.reshape(groups, memory.shape[2], width)
    grad_bf = out_grad.reshape(groups, seq_length, width)
    group_lengths = lengths.reshape(groups)
    bucket_indicator = bucket_onehot(seq_length)
    relative_position_bias = jnp.einsum(
        "fsn,fe->esn",
        bucket_indicator,
        bucket_bias_table.astype(jnp.float32),
        precision=TOP_PRECISION,
    )
    positions = jnp.arange(seq_length, dtype=jnp.int32)
    causal = positions[:, None] >= positions[None, :]
    present = positions[None, :] < group_lengths[:, None]
    valid_rows = present[:, :, None].astype(jnp.float32)
    allowed = causal[None, None] & present[:, None, None, :]

    def grad_of(inputs, upstream):
        return weight_grad(rows_of(inputs), rows_of(upstream))

    decoded = decoder_in.reshape(groups, seq_length, width).astype(jnp.float32)
    normed = normalize(decoded, norm_self).astype(jnp.bfloat16)
    queries = project(normed, self_query).astype(jnp.bfloat16)
    key_rows = project(normed, self_key).astype(jnp.bfloat16)
    values = project(normed, self_value).astype(jnp.bfloat16)
    context, self_weights = attend_forward(
        queries, key_rows, values, relative_position_bias, allowed
    )
    after_self = decoded + project(context, self_out)
    normed_cross = normalize(after_self, norm_cross).astype(jnp.bfloat16)
    cross_queries = project(normed_cross, cross_query).astype(jnp.bfloat16)
    memory_keys = project(memory_bf, cross_key).astype(jnp.bfloat16)
    memory_values = project(memory_bf, cross_value).astype(jnp.bfloat16)
    cross_context, cross_weights = attend_forward(
        cross_queries, memory_keys, memory_values, 0.0, True
    )
    after_cross = after_self + project(cross_context, cross_out)
    normed_ff = normalize(after_cross, norm_ff).astype(jnp.bfloat16)
    hidden = project(normed_ff, ff_in)
    activated = jax.nn.gelu(hidden, approximate=True).astype(jnp.bfloat16)
    after_ff = after_cross + project(activated, ff_out)
    layer_out = (after_ff * valid_rows).astype(jnp.bfloat16)

    def back(operand, weight):
        return lax.dot_general(
            operand, weight, (((2,), (1,)), ((), ())), preferred_element_type=jnp.float32
        )

    grad_after = grad_bf.astype(jnp.float32) * valid_rows
    grad_branch = grad_after.astype(jnp.bfloat16)
    grad_ff_out = grad_of(activated, grad_branch)
    gelu_pull = jax.vjp(lambda pre_act: jax.nn.gelu(pre_act, approximate=True), hidden)[1]
    grad_hidden = gelu_pull(back(grad_branch, ff_out))[0].astype(jnp.bfloat16)
    grad_ff_in = grad_of(normed_ff, grad_hidden)
    norm_pull = jax.vjp(normalize, after_cross, norm_ff)[1]
    grad_rows, grad_norm_ff = norm_pull(back(grad_hidden, ff_in))
    grad_after = grad_after + grad_rows
    grad_branch = grad_after.astype(jnp.bfloat16)
    grad_cross_out = grad_of(cross_context, grad_branch)
    grad_context = back(grad_branch, cross_out).astype(jnp.bfloat16)
    grad_cross_rows, grad_memory_keys, grad_memory_values, unused = attend_backward(
        cross_queries, memory_keys, memory_values, cross_weights, grad_context
    )
    grad_cross_query = grad_of(normed_cross, grad_cross_rows)
    grad_cross_key = grad_of(memory_bf, grad_memory_keys)
    grad_cross_value = grad_of(memory_bf, grad_memory_values)
    grad_memory = back(grad_memory_keys, cross_key) + back(grad_memory_values, cross_value)
    norm_pull = jax.vjp(normalize, after_self, norm_cross)[1]
    grad_rows, grad_norm_cross = norm_pull(back(grad_cross_rows, cross_query))
    grad_after = grad_after + grad_rows
    grad_branch = grad_after.astype(jnp.bfloat16)
    grad_self_out = grad_of(context, grad_branch)
    grad_context = back(grad_branch, self_out).astype(jnp.bfloat16)
    grad_queries, grad_key_rows, grad_values, score_gradient = attend_backward(
        queries, key_rows, values, self_weights, grad_context
    )
    grad_self_query = grad_of(normed, grad_queries)
    grad_self_key = grad_of(normed, grad_key_rows)
    grad_self_value = grad_of(normed, grad_values)
    grad_normed = (
        back(grad_queries, self_query) + back(grad_key_rows, self_key) + back(grad_values, self_value)
    )
    norm_pull = jax.vjp(normalize, decoded, norm_self)[1]
    grad_rows, grad_norm_self = norm_pull(grad_normed)
    grad_input = grad_after + grad_rows
    bias_grad = jnp.einsum(
        "fgd,ogd->fo", bucket_indicator, jnp.sum(score_gradient, axis=0), precision=TOP_PRECISION
    )
    pieces = scatter_all(
        (
            grad_self_query,
            grad_self_key,
            grad_self_value,
            grad_self_out,
            grad_cross_query,
            grad_cross_key,
            grad_cross_value,
            grad_cross_out,
            grad_ff_in,
            grad_ff_out,
        ),
        shards[:10],
    )
    small = lax.psum(
        jnp.concatenate([grad_norm_self, grad_norm_cross, grad_norm_ff, bias_grad.reshape(-1)]),
        AXES,
    )
    mine = shards[10].shape[0]
    at = lax.axis_index(AXES) * mine
    gains_out = [
        lax.dynamic_slice_in_dim(small[k * width : (k + 1) * width], at, mine) for k in range(3)
    ]
    return (
        layer_out.reshape(decoder_in.shape),
        grad_input.reshape(decoder_in.shape),
        grad_memory.reshape(memory.shape),
        *pieces,
        *gains_out,
        small[3 * width :].reshape(bucket_bias_table.shape),
    )


MESH = pl.DeviceIdType.MESH
LOW = jnp.bfloat16
WIDE = jnp.float32
GROUPS = 16
WIDTH = 768
ROWS = 512
LENGTH = 256
MEMORY = 128
PAIRS = 6
CURVE = math.sqrt(2.0 / math.pi)


def place():
    dp, fsdp = lax.axis_index("dp"), lax.axis_index("fsdp")
    z, y, x, core = dp // 2, dp % 2, fsdp // 2, fsdp % 2
    sibling = (dp, x * 2 + 1 - core)
    over_x = (dp, (1 - x) * 2 + core)
    over_y = (z * 2 + 1 - y, fsdp)
    first = (jnp.where(core == 0, over_x[0], over_y[0]), jnp.where(core == 0, over_x[1], over_y[1]))
    second = (jnp.where(core == 0, over_y[0], over_x[0]), jnp.where(core == 0, over_y[1], over_x[1]))
    along_z = [(((z + k) % 4) * 2 + y, fsdp) for k in (1, 2, 3)]
    own = y * 2 + x
    beside = jnp.where(core == 0, y * 2 + 1 - x, (1 - y) * 2 + x)
    return z, own, beside, core, sibling, first, second, along_z


def greet(partners):
    barrier = pltpu.get_barrier_semaphore()
    for partner in partners:
        pl.semaphore_signal(barrier, inc=1, device_id=partner, device_id_type=MESH)
    pl.semaphore_wait(barrier, len(partners))


def half(core):
    return pl.ds(pl.multiple_of(core * 384, 128), 384)


def skew(ahead, groups=GROUPS):
    order = []
    for t in range(-max(ahead), groups + 8):
        for s in range(len(ahead)):
            g = t + ahead[s]
            if 0 <= g < groups:
                order.append((g, s))
    return order


def dot(a, b):
    return jnp.dot(a, b, preferred_element_type=WIDE)


def dot_nt(a, b):
    return lax.dot_general(a, b, (((1,), (1,)), ((), ())), preferred_element_type=WIDE)


def dot_tn(a, b):
    return lax.dot_general(a, b, (((0,), (0,)), ((), ())), preferred_element_type=WIDE)


def unit(w, u):
    return w[u].reshape(WIDTH, WIDTH)


def root_scale(value):
    return lax.rsqrt(jnp.mean(value * value, axis=-1, keepdims=True) + EPS)


def bucket_columns(flipped):
    j = lax.broadcasted_iota(jnp.int32, (BUCKETS, LENGTH), 1)
    row = lax.broadcasted_iota(jnp.int32, (BUCKETS, LENGTH), 0)
    n = jnp.where(j == 0, 0, LENGTH - j) if flipped else j
    half_count = BUCKETS // 2
    farther = jnp.zeros_like(n)
    for level in range(1, half_count):
        border = int(math.ceil(half_count * (MAX_DIST / half_count) ** (level / half_count)))
        farther = farther + (n >= border).astype(jnp.int32)
    bucket = jnp.where(n < half_count, n, half_count + farther)
    return (bucket == row).astype(WIDE)


ZS = (1, 4, 7, 10, 13)
AHEAD = (6, 4, 2, 1, 0)
BUDGET = 4.5


def forward_kernel(
    small_ref, tall_ref, gain_ref, x_ref, mem_ref, table_ref, lens_ref,
    w_out, gains_out, normed_out, q_out, k_out, v_out, ctx_out, p_out, after_self_out, ncross_out,
    cq_out, mk_out, mv_out, cctx_out, pc_out, after_cross_out, nff_out, act_out, slope_out, layer_out,
    w, gains, normed, q, k, v, ctx, p, after_self, ncross, cq, mk, mv, cctx, pc, after_cross, nff, act, slope, layer,
    bias, sib, gain_in, ss, rs, ss0, rs0, out_sem,
):
    z, own, beside, core, sibling, first, second, along_z = place()
    mine, other = half(core), half(1 - core)

    def view(g, zi, yx, cols):
        if g < 12:
            return w.at[g, slice(None) if zi is None else zi, yx, :, cols]
        return w.at[pl.ds(12, 4) if zi is None else 12 + zi, yx, g - 12, :, cols]

    def whole(g, cols):
        return w.at[g, :, :, :, cols] if g < 12 else w.at[pl.ds(12, 4), :, g - 12, :, cols]

    def send(ref, to, g, n):
        return pltpu.make_async_remote_copy(
            src_ref=ref, dst_ref=ref, send_sem=ss.at[g, n], recv_sem=rs.at[g, n], device_id=to, device_id_type=MESH)

    def step_a(g):
        return [send(view(g, z, own, mine), to, g, n) for n, to in enumerate(along_z)]

    def step_b(g):
        return [send(view(g, None, own, mine), first, g, 3)]

    def step_c(g):
        return [send(view(g, None, own, mine), second, g, 4), send(view(g, None, beside, mine), second, g, 5)]

    def step_d(g):
        return [send(whole(g, mine), sibling, g, 6)]

    def step_b1(g):
        return [send(view(g, z, own, mine), first, g, 3)]

    def step_a2(g):
        return step_a(g) + [send(view(g, z, beside, mine), to, g, 7 + n) for n, to in enumerate(along_z)]

    def gain_copies(s):
        to = ([sibling], along_z, [first], [second])[s]
        at = (0, 1, 4, 5)[s]
        return [
            pltpu.make_async_remote_copy(
                src_ref=gains, dst_ref=gain_in.at[at + n], send_sem=ss0.at[2 + at + n], recv_sem=rs0.at[2 + at + n],
                device_id=d, device_id_type=MESH)
            for n, d in enumerate(to)
        ]

    def start(copies):
        for copy in copies:
            copy.start()

    def gain_finish(s):
        for copy in gain_copies(s):
            copy.wait()
        for n in ((0,), (1, 2, 3), (4,), (5,))[s]:
            gains[...] += gain_in[n]

    stores = []

    def store(src, dst):
        copy = pltpu.make_async_copy(src, dst, out_sem.at[len(stores)])
        stores.append(copy)
        copy.start()

    def store_unit(g):
        if g < 12:
            store(w.at[g], w_out.at[g])

    def gain(n):
        return gains[n : n + 1, :].astype(WIDE)

    def scale_rows(src, n, dst):
        g = gain(n)

        def chunk(i, c):
            rows = pl.ds(pl.multiple_of(i * 128, 128), 128)
            value = src[rows, :].astype(WIDE)
            dst[rows, :] = (value * root_scale(value) * g).astype(LOW)
            return c

        lax.fori_loop(0, ROWS // 128, chunk, 0)

    def make_bias():
        by_distance = dot(table_ref[...], bucket_columns(True).astype(LOW))
        for h in range(HEADS):
            row = jnp.broadcast_to(by_distance[h : h + 1, :], (LENGTH, LENGTH))
            bias[h] = pltpu.roll(row, 0, 1, stride=1, stride_axis=0)

    def project_into(src, u, dst):
        dst[...] = dot(src[...], unit(w, u)).astype(LOW)

    lane = lax.broadcasted_iota(jnp.int32, (1, 128), 1)
    sides = [lane < 64, lane >= 64]

    def attend(i, queries, keys, vals, keep_p, into, depth, masked):
        s, pair = i // PAIRS, i % PAIRS
        rows = pl.ds(pl.multiple_of(s * LENGTH, LENGTH), LENGTH)
        deep = pl.ds(pl.multiple_of(s * depth, depth), depth)
        cols = pl.ds(pl.multiple_of(pair * 128, 128), 128)
        qp, kp, vp = queries[rows, cols], keys[deep, cols], vals[deep, cols]
        parts = []
        for side in range(2):
            scores = dot_nt(jnp.where(sides[side], qp, jnp.zeros_like(qp)), kp)
            if masked:
                t = lax.broadcasted_iota(jnp.int32, (LENGTH, LENGTH), 0)
                u = lax.broadcasted_iota(jnp.int32, (LENGTH, LENGTH), 1)
                allowed = (u <= t) & (u < lens_ref[s])
                scores = jnp.where(allowed, scores + bias[2 * pair + side], MASKED)
            e = jnp.exp(scores - jnp.max(scores, axis=-1, keepdims=True))
            weights = (e * (1.0 / jnp.sum(e, axis=-1, keepdims=True))).astype(LOW)
            keep_p[rows, pl.ds(pl.multiple_of((2 * pair + side) * depth, 128), depth)] = weights
            parts.append(dot(weights, vp))
        into[rows, cols] = jnp.where(sides[0], parts[0], parts[1]).astype(LOW)

    def self_part(lo, hi):
        def it(i, c):
            attend(i, q, k, v, p, ctx, LENGTH, True)
            return c

        lax.fori_loop(lo, hi, it, 0)

    def cross_part(lo, hi):
        def it(i, c):
            attend(i, cq, mk, mv, pc, cctx, MEMORY, False)
            return c

        lax.fori_loop(lo, hi, it, 0)

    def after_self_part():
        after_self[...] = x_ref[...].astype(WIDE) + dot(ctx[...], unit(w, 3))
        scale_rows(after_self, 1, ncross)

    def after_cross_part():
        after_cross[...] = after_self[...] + dot(cctx[...], unit(w, 7))
        scale_rows(after_cross, 2, nff)

    def hidden_part(j):
        cols = slice(j * WIDTH, (j + 1) * WIDTH)
        for m in range(2):
            rows = slice(m * 256, m * 256 + 256)
            a = dot(nff[rows, :], unit(w, 8 + j))
            sq = a * a
            th = jnp.tanh(a * (CURVE + (CURVE * 0.044715) * sq))
            act[rows, cols] = (0.5 * a * (1.0 + th)).astype(LOW)
            slope[rows, cols] = (
                0.5 * (1.0 + th) + 0.5 * a * (1.0 - th * th) * (CURVE + (3.0 * CURVE * 0.044715) * sq)
            ).astype(LOW)

    def layer_part():
        total = after_cross[...]
        for j in range(4):
            total = total + dot(act[:, j * WIDTH : (j + 1) * WIDTH], unit(w, 12 + j))
        for s in range(2):
            t = lax.broadcasted_iota(jnp.int32, (LENGTH, 1), 0)
            valid = (t < lens_ref[s]).astype(WIDE)
            layer[s * LENGTH : (s + 1) * LENGTH, :] = (total[s * LENGTH : (s + 1) * LENGTH] * valid).astype(LOW)

    pieces = [
        (0, 1.0, lambda: project_into(normed, 0, q)), (0, 0.1, lambda: store(q, q_out)),
        (1, 1.0, lambda: project_into(normed, 1, k)), (1, 0.1, lambda: store(k, k_out)),
        (2, 1.0, lambda: project_into(normed, 2, v)), (2, 0.1, lambda: store(v, v_out)),
        (2, 2.5, lambda: self_part(0, 3)), (2, 2.5, lambda: self_part(3, 6)),
        (2, 2.5, lambda: self_part(6, 9)), (2, 2.5, lambda: self_part(9, 12)),
        (2, 0.1, lambda: store(ctx, ctx_out)), (2, 0.1, lambda: store(p, p_out)),
        (3, 2.0, after_self_part), (3, 0.1, lambda: store(after_self, after_self_out)), (3, 0.1, lambda: store(ncross, ncross_out)),
        (4, 1.0, lambda: project_into(ncross, 4, cq)), (4, 0.1, lambda: store(cq, cq_out)),
        (5, 0.6, lambda: project_into(mem_ref, 5, mk)), (5, 0.1, lambda: store(mk, mk_out)),
        (6, 0.6, lambda: project_into(mem_ref, 6, mv)), (6, 0.1, lambda: store(mv, mv_out)),
        (6, 2.5, lambda: cross_part(0, 4)), (6, 2.5, lambda: cross_part(4, 8)), (6, 2.5, lambda: cross_part(8, 12)),
        (6, 0.1, lambda: store(cctx, cctx_out)), (6, 0.1, lambda: store(pc, pc_out)),
        (7, 2.0, after_cross_part), (7, 0.1, lambda: store(after_cross, after_cross_out)), (7, 0.1, lambda: store(nff, nff_out)),
        (8, 2.0, lambda: hidden_part(0)), (9, 2.0, lambda: hidden_part(1)),
        (10, 2.0, lambda: hidden_part(2)), (11, 2.0, lambda: hidden_part(3)),
        (11, 0.1, lambda: store(act, act_out)), (11, 0.1, lambda: store(slope, slope_out)),
        (15, 4.0, layer_part), (15, 0.1, lambda: store(layer, layer_out)),
    ]

    greet([sibling, first, second] + along_z)
    swap_small = pltpu.make_async_remote_copy(
        src_ref=small_ref.at[:, :, other], dst_ref=sib, send_sem=ss0.at[0], recv_sem=rs0.at[0],
        device_id=sibling, device_id_type=MESH)

    def tall_view(cols):
        return w.at[12 + z, own, pl.ds(2 * core, 2), :, cols]

    swap_tall = pltpu.make_async_remote_copy(
        src_ref=tall_ref.at[:, :, other], dst_ref=tall_view(other), send_sem=ss0.at[1], recv_sem=rs0.at[1],
        device_id=sibling, device_id_type=MESH)
    swap_small.start()
    swap_tall.start()
    gains[...] = gain_ref[...]
    start(gain_copies(0))
    w[12 + z, own, pl.ds(2 * core, 2), :, mine] = tall_ref[:, :, mine]
    swap_small.wait()
    for u in range(12):
        w[u, z, own, :, mine] = small_ref[u, :, mine] + sib[u]
    swap_tall.wait()
    gain_finish(0)
    start(gain_copies(1))

    zf = (step_a, step_b, step_c, step_d)
    zs = (step_b1, step_a2, step_c, step_d)
    stage, done = 1, 0
    for n, (g, s) in enumerate(skew(AHEAD)):
        steps = zs if g in ZS else zf
        if s:
            for copy in steps[s - 1](g):
                copy.wait()
        if s < 4:
            start(steps[s](g))
        if n == 8:
            make_bias()
        if n in (8, 11, 14):
            gain_finish(stage)
            stage += 1
            if stage < 4:
                start(gain_copies(stage))
            else:
                scale_rows(x_ref, 0, normed)
                store(normed, normed_out)
                store(gains, gains_out)
        if s == 4:
            store_unit(g)
            spent = 0.0
            while done < len(pieces) and pieces[done][0] <= g and (spent < BUDGET or g == GROUPS - 1):
                spent += pieces[done][1]
                pieces[done][2]()
                done += 1
            if g == GROUPS - 1:
                store(w.at[pl.ds(12, 4)], w_out.at[pl.ds(12, 4)])
    assert done == len(pieces) and stage == 4
    for copy in stores:
        copy.wait()


FORWARD_OUT = (
    ((16, 4, 4, 48, 768), LOW),
    ((16, 768), LOW),
    ((512, 768), LOW), ((512, 768), LOW), ((512, 768), LOW), ((512, 768), LOW),
    ((512, 768), LOW),
    ((512, 3072), LOW),
    ((512, 768), WIDE),
    ((512, 768), LOW),
    ((512, 768), LOW), ((256, 768), LOW), ((256, 768), LOW), ((512, 768), LOW),
    ((512, 1536), LOW),
    ((512, 768), WIDE),
    ((512, 768), LOW),
    ((512, 3072), LOW), ((512, 3072), LOW),
    ((512, 768), LOW),
)


def forward_call(small, tall, gain, x, mem, table, lens):
    return pl.pallas_call(
        forward_kernel,
        out_shape=tuple(jax.ShapeDtypeStruct(s, t) for s, t in FORWARD_OUT),
        in_specs=[pl.BlockSpec(memory_space=pltpu.VMEM)] * 6 + [pl.BlockSpec(memory_space=pltpu.SMEM)],
        out_specs=[pl.BlockSpec(memory_space=pl.ANY)] * len(FORWARD_OUT),
        scratch_shapes=[pltpu.VMEM(s, t) for s, t in FORWARD_OUT]
        + [
            pltpu.VMEM((HEADS, LENGTH, LENGTH), WIDE),
            pltpu.VMEM((12, 48, 384), LOW),
            pltpu.VMEM((6, 16, 768), LOW),
            pltpu.SemaphoreType.DMA((GROUPS, 10)),
            pltpu.SemaphoreType.DMA((GROUPS, 10)),
            pltpu.SemaphoreType.DMA((8,)),
            pltpu.SemaphoreType.DMA((8,)),
            pltpu.SemaphoreType.DMA((32,)),
        ],
        compiler_params=pltpu.CompilerParams(collective_id=0, has_side_effects=True, vmem_limit_bytes=60 * 2**20),
    )(small, tall, gain, x, mem, table, lens)


def pack(shards):
    core = lax.axis_index("fsdp") % 2
    units = list(shards[:8]) + [shards[8][:, WIDTH * j : WIDTH * (j + 1)] for j in range(4)]
    block = jnp.stack(units)
    low = jnp.pad(block, ((0, 0), (0, 24), (0, 0)))
    high = jnp.pad(block, ((0, 0), (24, 0), (0, 0)))
    at = lax.axis_index(("dp", "fsdp")) * 24
    placed = lax.dynamic_update_slice(jnp.zeros((16, WIDTH), LOW), jnp.stack(shards[10:13]), (0, at))
    return jnp.where(core == 0, low, high), shards[9].reshape(2, 48, WIDTH), placed


def forward(shards, decoder_in, memory, table, lengths):
    small, tall, gain = pack(shards)
    padded = jnp.pad(table.T, ((0, 16 - HEADS), (0, 0)))
    return forward_call(
        small, tall, gain, decoder_in.reshape(ROWS, WIDTH), memory.reshape(2 * MEMORY, WIDTH), padded, lengths.reshape(2)
    )


LINE = (12, 13, 14, 15, 8, 9, 10, 11, 7, 4, 5, 6, 3, 0, 1, 2)
USED = (12, 8, 13, 9, 14, 10, 15, 11, 7, 5, 6, 4, 3, 0, 1, 2)
SLOTS = 6
LAGS = (0, 1, 2, 4, 6, 8)
PACE = 4.5
FIRST_Z = (13, 9, 4, 1)


def backward_kernel(
    gains, lens_ref, w_hbm, act_hbm, slope_hbm, nff_hbm, after_cross_hbm, cctx_hbm, ncross_hbm, cq_hbm, mk_hbm, mv_hbm,
    mem_hbm, pc_hbm, after_self_hbm, p_hbm, normed_hbm, q_hbm, k_hbm, v_hbm, ctx_hbm, x_hbm, og_hbm,
    input_out, memory_out, *rest,
):
    pieces_out, rest = rest[:8], rest[8:]
    (
        in_piece_out, out_piece_out, sum_out,
        ring, act, slope, nff, aft, cctx, ncross, cq, mk, mv, mem, pc, x, gl, total, up, ghj, low, gctx, dq, dk, dv,
        dist, grad, r0, r1, r23, fa, fo, fa_in, fo_in, acc, acc_in, ss, rs, ss0, rs0, in_sem, ring_sem, out_sem,
    ) = rest
    z, own, beside, core, sibling, first, second, along_z = place()
    mine, other = half(core), half(1 - core)
    diag, across = 3 - own, 3 - beside

    fetches = {}

    def fetch(name, src, dst):
        copy = pltpu.make_async_copy(src, dst, in_sem.at[len(fetches)])
        fetches[name] = copy
        copy.start()

    def fetched(*names):
        for name in names:
            fetches[name].wait()

    def weight_copy(n):
        return pltpu.make_async_copy(w_hbm.at[USED[n]], ring.at[n % SLOTS], ring_sem.at[n])

    asked, got = [0], [0]

    def ask(n):
        while asked[0] < min(n, GROUPS):
            weight_copy(asked[0]).start()
            asked[0] += 1

    def weight(u):
        n = USED.index(u)
        while got[0] <= n:
            weight_copy(got[0]).wait()
            got[0] += 1
        return ring[n % SLOTS].reshape(WIDTH, WIDTH)

    def send(src, dst, to, g, n):
        return pltpu.make_async_remote_copy(
            src_ref=src, dst_ref=dst, send_sem=ss.at[g, n], recv_sem=rs.at[g, n], device_id=to, device_id_type=MESH)

    def block(g, cols):
        if g < 12:
            return grad.at[LINE.index(g) % 4, :, :, :, cols]
        return grad.at[:, :, g - 12, :, cols]

    def swap(g):
        return [send(block(g, other), r0.at[g], sibling, g, 0)]

    def over_second(g):
        return [send(r0.at[g, :, across], r1.at[g, 0], second, g, 1), send(r0.at[g, :, diag], r1.at[g, 1], second, g, 2)]

    def over_first(g):
        return [send(r0.at[g, :, beside], r23.at[g, pl.ds(0, 4)], first, g, 3)]

    def over_z(g):
        return [send(r0.at[g, (z + n + 1) % 4, own], r23.at[g, 4 + n], to, g, 4 + n) for n, to in enumerate(along_z)]

    def over_z2(g):
        return over_z(g) + [
            send(r0.at[g, (z + n + 1) % 4, beside], r23.at[g, 1 + n], to, g, 7 + n) for n, to in enumerate(along_z)]

    def over_first1(g):
        return [send(r0.at[g, z, beside], r23.at[g, 0], first, g, 3)]

    def last(g):
        if g < 12:
            rows = pl.ds(pl.multiple_of(24 * (1 - core), 8), 24)
            return [send(fa.at[g, rows], fa_in.at[g], sibling, g, 10)]
        if g == 15:
            return [send(fo.at[pl.ds(2 * (1 - core), 2)], fo_in, sibling, g, 10)]
        return []

    def add0(g):
        r0[g] += block(g, mine)[...]

    def add1(g):
        r0[g, :, own] += r1[g, 0]
        r0[g, :, beside] += r1[g, 1]

    def finish(g, value):
        if g < 12:
            fa[g] = value
        else:
            fo[g - 12] = value

    def add2(g):
        r0[g, :, own] += r23[g, 0:4]

    def over(g, yx, at):
        value = r0[g, z, yx].astype(WIDE)
        for n in range(3):
            value = value + r23[g, at + n].astype(WIDE)
        return value

    def add3(g):
        finish(g, over(g, own, 4))

    def add2z(g):
        mid = over(g, own, 4), over(g, beside, 1)
        r0[g, z, own] = mid[0].astype(LOW)
        r0[g, z, beside] = mid[1].astype(LOW)

    def add3z(g):
        finish(g, r0[g, z, own].astype(WIDE) + r23[g, 0].astype(WIDE))

    def write(g):
        rows = pl.ds(pl.multiple_of(24 * core, 8), 24)
        if g < 8:
            pieces_out[g][:, mine] = fa[g, rows]
            pieces_out[g][:, other] = fa_in[g]
        elif g < 12:
            at = WIDTH * (g - 8)
            in_piece_out[:, pl.ds(pl.multiple_of(at + core * 384, 128), 384)] = fa[g, rows]
            in_piece_out[:, pl.ds(pl.multiple_of(at + 384 - core * 384, 128), 384)] = fa_in[g]
        elif g == 15:
            out_piece_out[:, mine] = fo[pl.ds(2 * core, 2)].reshape(96, 384)
            out_piece_out[:, other] = fo_in[...].reshape(96, 384)

    zf = ((swap, over_second, over_first, over_z, last), (None, add0, add1, add2, add3, write))
    zs = ((swap, over_second, over_z2, over_first1, last), (None, add0, add1, add2z, add3z, write))

    def event(g, s):
        copies, sums = zs if g in FIRST_Z else zf
        if s:
            for copy in copies[s - 1](g):
                copy.wait()
            sums[s](g)
        if s < 5:
            for copy in copies[s](g):
                copy.start()

    def acc_copies(s):
        to = ([sibling], along_z, [first], [second])[s]
        at = (0, 1, 4, 5)[s]
        return [
            pltpu.make_async_remote_copy(
                src_ref=acc, dst_ref=acc_in.at[at + n], send_sem=ss0.at[at + n], recv_sem=rs0.at[at + n],
                device_id=d, device_id_type=MESH)
            for n, d in enumerate(to)
        ]

    lane = lax.broadcasted_iota(jnp.int32, (1, 128), 1)
    sides = [lane < 64, lane >= 64]

    def keep(g, value):
        grad[LINE.index(g) % 4] = value.astype(LOW).reshape(4, 4, 48, WIDTH)

    def begin():
        fetched("og")
        for s in range(2):
            rows = slice(s * LENGTH, (s + 1) * LENGTH)
            t = lax.broadcasted_iota(jnp.int32, (LENGTH, 1), 0)
            gl[rows, :] = jnp.where(t < lens_ref[s], gl[rows, :].astype(WIDE), 0.0).astype(LOW)
        fetched("act")

    def out_grad_part(j):
        grad[j] = dot_tn(act[:, j * WIDTH : (j + 1) * WIDTH], gl[...]).astype(LOW).reshape(4, 4, 48, WIDTH)

    def hidden_part(j):
        if j == 0:
            fetched("slope", "nff")
        cols = slice(j * WIDTH, (j + 1) * WIDTH)
        ghj[...] = (dot_nt(gl[...], weight(12 + j)) * slope[:, cols].astype(WIDE)).astype(LOW)
        keep(8 + j, dot_tn(nff[...], ghj[...]))

    def hidden_back(j):
        part = dot_nt(ghj[...], weight(8 + j))
        if j:
            up[...] += part
        else:
            up[...] = part

    def norm_back(value_ref, base_ref, n):
        g = gains[n : n + 1, :].astype(WIDE)

        def chunk(i, carried):
            rows = pl.ds(pl.multiple_of(i * 128, 128), 128)
            value = value_ref[rows, :].astype(WIDE)
            r = root_scale(value)
            unit_rows = value * r
            upstream = up[rows, :]
            weighted = upstream * g
            inner = jnp.mean(weighted * unit_rows, axis=-1, keepdims=True)
            new = base_ref[rows, :].astype(WIDE) + r * (weighted - unit_rows * inner)
            total[rows, :] = new
            low[rows, :] = new.astype(LOW)
            return carried + jnp.sum(upstream * unit_rows, axis=0, keepdims=True)

        acc[n : n + 1, 0:WIDTH] = lax.fori_loop(0, ROWS // 128, chunk, jnp.zeros((1, WIDTH), WIDE))

    def ff_norm_part():
        fetched("after_cross")
        norm_back(aft, gl, 2)
        fetch("p", p_hbm, act)
        fetch("normed", normed_hbm, slope.at[:, 0:768])
        fetch("q", q_hbm, slope.at[:, 768:1536])
        fetch("k", k_hbm, slope.at[:, 1536:2304])
        fetch("v", v_hbm, slope.at[:, 2304:3072])
        fetch("ctx", ctx_hbm, nff)
        fetch("after_self", after_self_hbm, aft)

    def cross_out_part():
        fetched("cctx")
        keep(7, dot_tn(cctx[...], low[...]))
        gctx[...] = dot_nt(low[...], weight(7)).astype(LOW)
        fetched("cq", "mk", "mv", "pc")

    def head_back(weights, gp, qp, kp, vp, side):
        p32 = weights.astype(WIDE)
        pull = dot_nt(jnp.where(sides[side], gp, jnp.zeros_like(gp)), vp)
        slant = p32 * (pull - jnp.sum(pull * p32, axis=-1, keepdims=True))
        rounded = slant.astype(LOW)
        return dot(rounded, kp), dot_tn(rounded, qp), dot_tn(weights, gp), slant

    def joined(low_part, high_part):
        return jnp.where(sides[0], low_part, high_part).astype(LOW)

    def cross_part(lo, hi):
        def it(i, c):
            s, pair = i // PAIRS, i % PAIRS
            rows = pl.ds(pl.multiple_of(s * LENGTH, LENGTH), LENGTH)
            deep = pl.ds(pl.multiple_of(s * MEMORY, MEMORY), MEMORY)
            cols = pl.ds(pl.multiple_of(pair * 128, 128), 128)
            gp, qp, kp, vp = gctx[rows, cols], cq[rows, cols], mk[deep, cols], mv[deep, cols]
            one, two = [
                head_back(pc[rows, pl.ds(pl.multiple_of((2 * pair + side) * MEMORY, 128), MEMORY)], gp, qp, kp, vp, side)
                for side in range(2)
            ]
            dq[rows, cols] = joined(one[0], two[0])
            dk[deep, cols] = joined(one[1], two[1])
            dv[deep, cols] = joined(one[2], two[2])
            return c

        lax.fori_loop(lo, hi, it, 0)

    def cross_query_part():
        fetched("ncross")
        keep(4, dot_tn(ncross[...], dq[...]))

    def cross_key_part():
        fetched("mem")
        keep(5, dot_tn(mem[...], dk[0:256, :]))

    def cross_value_part():
        keep(6, dot_tn(mem[...], dv[0:256, :]))

    def cross_norm_part():
        up[0:256, :] = dot_nt(dk[0:256, :], weight(5)) + dot_nt(dv[0:256, :], weight(6))
        copy = pltpu.make_async_copy(up.at[pl.ds(0, 256)], memory_out, out_sem.at[0])
        copy.start()
        copy.wait()
        up[...] = dot_nt(dq[...], weight(4))
        fetched("after_self")
        norm_back(aft, total, 1)

    def self_out_part():
        fetched("ctx")
        keep(3, dot_tn(nff[...], low[...]))
        gctx[...] = dot_nt(low[...], weight(3)).astype(LOW)
        fetched("p", "q", "k", "v")

    def self_part(lo, hi):
        def it(pair, c):
            cols = pl.ds(pl.multiple_of(pair * 128, 128), 128)
            q_cols = pl.ds(pl.multiple_of(768 + pair * 128, 128), 128)
            k_cols = pl.ds(pl.multiple_of(1536 + pair * 128, 128), 128)
            v_cols = pl.ds(pl.multiple_of(2304 + pair * 128, 128), 128)
            slants = []
            for s in range(2):
                rows = slice(s * LENGTH, (s + 1) * LENGTH)
                gp, qp, kp, vp = gctx[rows, cols], slope[rows, q_cols], slope[rows, k_cols], slope[rows, v_cols]
                one, two = [
                    head_back(act[rows, pl.ds(pl.multiple_of((2 * pair + side) * LENGTH, 256), LENGTH)], gp, qp, kp, vp, side)
                    for side in range(2)
                ]
                dq[rows, cols] = joined(one[0], two[0])
                dk[rows, cols] = joined(one[1], two[1])
                dv[rows, cols] = joined(one[2], two[2])
                slants.append((one[3], two[3]))
            t = lax.broadcasted_iota(jnp.int32, (LENGTH, LENGTH), 0)
            u = lax.broadcasted_iota(jnp.int32, (LENGTH, LENGTH), 1)
            upside = (t + u == LENGTH - 1).astype(LOW)
            for side in range(2):
                both = slants[0][side] + slants[1][side]
                coarse = both.astype(LOW)
                fine = (both - coarse.astype(WIDE)).astype(LOW)
                turned = dot(upside, coarse) + dot(upside, fine)
                rolled = pltpu.roll(turned, 1, 1, stride=1, stride_axis=0)
                dist[pl.ds(2 * pair + side, 1), :] = jnp.sum(rolled, axis=0, keepdims=True)
            return c

        lax.fori_loop(lo, hi, it, 0)

    def self_grads(n):
        fetched(*(["normed"] if n == 0 else []))
        keep(n, dot_tn(slope[:, 0:768], (dq, dk, dv)[n][...]))

    def input_part():
        up[...] = dot_nt(dq[...], weight(0)) + dot_nt(dk[...], weight(1)) + dot_nt(dv[...], weight(2))
        fetched("x")
        norm_back(x, total, 0)
        pltpu.make_async_copy(total, input_out, out_sem.at[1]).start()
        buckets = lax.dot_general(
            dist[...], bucket_columns(True), (((1,), (1,)), ((), ())),
            precision=lax.Precision.HIGHEST, preferred_element_type=WIDE)
        acc[:, WIDTH : WIDTH + BUCKETS] = buckets
        for copy in acc_copies(0):
            copy.start()

    pieces = [(0.5, begin, None, 6)]
    pieces += [(1.0, functools.partial(out_grad_part, j), 12 + j, 6) for j in range(4)]
    for j in range(4):
        pieces += [(2.0, functools.partial(hidden_part, j), 8 + j, 0), (1.0, functools.partial(hidden_back, j), None, 8 + 2 * j)]
    pieces += [
        (1.5, ff_norm_part, None, 0), (1.9, cross_out_part, 7, 15),
        (2.5, lambda: cross_part(0, 4), None, 0), (2.5, lambda: cross_part(4, 8), None, 0), (2.5, lambda: cross_part(8, 12), None, 0),
        (1.0, cross_query_part, 4, 0), (0.5, cross_key_part, 5, 0), (0.5, cross_value_part, 6, 0),
        (4.0, cross_norm_part, None, 16), (2.0, self_out_part, 3, 0),
        (4.0, lambda: self_part(0, 2), None, 0), (4.0, lambda: self_part(2, 4), None, 0), (4.0, lambda: self_part(4, 6), None, 0),
        (1.0, lambda: self_grads(0), 0, 0), (1.0, lambda: self_grads(1), 1, 0), (1.0, lambda: self_grads(2), 2, 0),
        (4.5, input_part, None, 0),
    ]

    acc[...] = jnp.zeros_like(acc)
    dist[...] = jnp.zeros_like(dist)
    fetch("og", og_hbm, gl)
    fetch("act", act_hbm, act)
    ask(2)
    fetch("slope", slope_hbm, slope)
    fetch("nff", nff_hbm, nff)
    fetch("after_cross", after_cross_hbm, aft)
    fetch("cctx", cctx_hbm, cctx)
    fetch("cq", cq_hbm, cq)
    fetch("mk", mk_hbm, mk)
    fetch("mv", mv_hbm, mv)
    fetch("pc", pc_hbm, pc)
    fetch("ncross", ncross_hbm, ncross)
    fetch("mem", mem_hbm, mem)
    fetch("x", x_hbm, x)
    greet([sibling, first, second] + along_z)

    clock, done, made, freed = 0.0, 0, set(), set()

    def run_piece():
        nonlocal clock, done
        cost, what, makes, asks = pieces[done]
        what()
        ask(asks)
        clock += cost
        made.add(makes)
        done += 1

    def may_run():
        makes = pieces[done][2]
        if makes is None or makes >= 12:
            return True
        i = LINE.index(makes)
        return set(LINE[:4]) <= freed if i < 8 else LINE[i - 4] in freed

    stage = None
    for r in range(GROUPS + LAGS[-1]):
        for s in range(1, 6):
            i = r - LAGS[s]
            if 0 <= i < GROUPS:
                event(LINE[i], s)
                if s == 1:
                    freed.add(LINE[i])
        if r < GROUPS:
            needed = set(LINE[:4]) if r < 4 else {LINE[r]}
            while not needed <= made:
                assert may_run()
                run_piece()
            event(LINE[r], 0)
        while done < len(pieces) and clock < PACE * (r + 1) and may_run():
            run_piece()
        if done == len(pieces):
            if stage is None:
                stage = 0
            elif stage < 4:
                for copy in acc_copies(stage):
                    copy.wait()
                for n in ((0,), (1, 2, 3), (4,), (5,))[stage]:
                    acc[...] += acc_in[n]
                stage += 1
                if stage < 4:
                    for copy in acc_copies(stage):
                        copy.start()
    assert done == len(pieces) and stage == 4 and got[0] == GROUPS
    sum_out[...] = acc[...]
    pltpu.make_async_copy(total, input_out, out_sem.at[1]).wait()


BACKWARD_OUT = (
    (((512, 768), WIDE), ((256, 768), WIDE)),
    (((24, 768), WIDE),) * 8 + (((24, 3072), WIDE), ((96, 768), WIDE), ((16, 896), WIDE)),
)


def backward_call(gains, lens, *arrays):
    shape = lambda s: jax.ShapeDtypeStruct(*s)
    vmem = lambda *s: pltpu.VMEM(s, LOW)
    return pl.pallas_call(
        backward_kernel,
        out_shape=tuple(shape(s) for s in BACKWARD_OUT[0] + BACKWARD_OUT[1]),
        in_specs=[pl.BlockSpec(memory_space=pltpu.VMEM), pl.BlockSpec(memory_space=pltpu.SMEM)]
        + [pl.BlockSpec(memory_space=pl.ANY)] * len(arrays),
        out_specs=[pl.BlockSpec(memory_space=pl.ANY)] * 2 + [pl.BlockSpec(memory_space=pltpu.VMEM)] * 11,
        scratch_shapes=[
            vmem(SLOTS, 4, 4, 48, 768),
            vmem(512, 3072), vmem(512, 3072), vmem(512, 768),
            pltpu.VMEM((512, 768), WIDE),
            vmem(512, 768), vmem(512, 768), vmem(512, 768), vmem(256, 768), vmem(256, 768), vmem(256, 768),
            vmem(512, 1536),
            vmem(512, 768), vmem(512, 768),
            pltpu.VMEM((512, 768), WIDE), pltpu.VMEM((512, 768), WIDE),
            vmem(512, 768), vmem(512, 768), vmem(512, 768),
            vmem(512, 768), vmem(512, 768), vmem(512, 768),
            pltpu.VMEM((16, LENGTH), WIDE),
            vmem(4, 4, 4, 48, 768),
            vmem(GROUPS, 4, 4, 48, 384), vmem(GROUPS, 2, 4, 48, 384), vmem(GROUPS, 7, 48, 384),
            pltpu.VMEM((12, 48, 384), WIDE), pltpu.VMEM((4, 48, 384), WIDE),
            pltpu.VMEM((12, 24, 384), WIDE), pltpu.VMEM((2, 48, 384), WIDE),
            pltpu.VMEM((16, 896), WIDE), pltpu.VMEM((6, 16, 896), WIDE),
            pltpu.SemaphoreType.DMA((GROUPS, 11)), pltpu.SemaphoreType.DMA((GROUPS, 11)),
            pltpu.SemaphoreType.DMA((6,)), pltpu.SemaphoreType.DMA((6,)),
            pltpu.SemaphoreType.DMA((24,)), pltpu.SemaphoreType.DMA((GROUPS,)), pltpu.SemaphoreType.DMA((2,)),
        ],
        compiler_params=pltpu.CompilerParams(collective_id=1, has_side_effects=True, vmem_limit_bytes=62 * 2**20),
    )(gains, lens, *arrays)


def layer_kernels(decoder_in, memory, out_grad, lengths, *params):
    shards, table = params[:13], params[13]
    (
        w, gains, normed, q, k, v, ctx, p, after_self, ncross, cq, mk, mv, cctx, pc, after_cross, nff, act, slope, layer,
    ) = forward(shards, decoder_in, memory, table, lengths)
    rows = decoder_in.reshape(ROWS, WIDTH)
    input_grad, memory_grad, *pieces, in_piece, out_piece, small = backward_call(
        gains, lengths.reshape(2), w, act, slope, nff, after_cross, cctx, ncross, cq, mk, mv,
        memory.reshape(2 * MEMORY, WIDTH), pc, after_self, p, normed, q, k, v, ctx, rows, out_grad.reshape(ROWS, WIDTH),
    )
    own_rows = shards[10].shape[0]
    at = lax.axis_index(("dp", "fsdp")) * own_rows
    return (
        layer.reshape(decoder_in.shape),
        input_grad.reshape(decoder_in.shape),
        memory_grad.reshape(memory.shape),
        *pieces,
        in_piece,
        out_piece,
        *[lax.dynamic_slice_in_dim(small[n, :WIDTH], at, own_rows) for n in range(3)],
        small[:HEADS, WIDTH : WIDTH + BUCKETS].T,
    )


def body(decoder_in, memory, out_grad, lengths, *params):
    sizes = (lax.axis_size("dp"), lax.axis_size("fsdp"))
    if sizes == (8, 4) and decoder_in.shape == (2, 1, LENGTH, WIDTH) and params[0].shape == (24, WIDTH):
        return layer_kernels(decoder_in, memory, out_grad, lengths, *params)
    return plain_body(decoder_in, memory, out_grad, lengths, *params)


def solution(mesh):
    return jax.shard_map(
        body,
        mesh=mesh,
        in_specs=(
            P(None, ("dp", "fsdp"), None, None),
            P(None, ("dp", "fsdp"), None, None),
            P(None, ("dp", "fsdp"), None, None),
            P(None, ("dp", "fsdp")),
            P(("dp", "fsdp"), None),
            P(("dp", "fsdp"), None),
            P(("dp", "fsdp"), None),
            P(("dp", "fsdp"), None),
            P(("dp", "fsdp"), None),
            P(("dp", "fsdp"), None),
            P(("dp", "fsdp"), None),
            P(("dp", "fsdp"), None),
            P(("dp", "fsdp"), None),
            P(("dp", "fsdp"), None),
            P(("dp", "fsdp")),
            P(("dp", "fsdp")),
            P(("dp", "fsdp")),
            P(),
        ),
        out_specs=(
            P(None, ("dp", "fsdp"), None, None),
            P(None, ("dp", "fsdp"), None, None),
            P(None, ("dp", "fsdp"), None, None),
            P(("dp", "fsdp"), None),
            P(("dp", "fsdp"), None),
            P(("dp", "fsdp"), None),
            P(("dp", "fsdp"), None),
            P(("dp", "fsdp"), None),
            P(("dp", "fsdp"), None),
            P(("dp", "fsdp"), None),
            P(("dp", "fsdp"), None),
            P(("dp", "fsdp"), None),
            P(("dp", "fsdp"), None),
            P(("dp", "fsdp")),
            P(("dp", "fsdp")),
            P(("dp", "fsdp")),
            P(),
        ),
        check_vma=False,
    )
```

```python
import functools
import math

import jax
import jax.numpy as jnp
from jax import lax
from jax.experimental import pallas as pl
from jax.experimental.pallas import tpu as pltpu
from jax.sharding import PartitionSpec as P

HEADS = 12
BUCKETS = 32
MAX_DIST = 128


EPS = 1e-06
MASKED = -1e30
TOP_PRECISION = lax.Precision.HIGHEST


def bucket_onehot(length):
    half_count = BUCKETS // 2
    positions = jnp.arange(length, dtype=jnp.int32)
    distance = jnp.maximum(positions[:, None] - positions[None, :], 0)
    farther = jnp.zeros_like(distance)
    for level in range(1, half_count):
        border = int(math.ceil(half_count * (MAX_DIST / half_count) ** (level / half_count)))
        farther = farther + (distance >= border).astype(jnp.int32)
    bucket = jnp.where(distance < half_count, distance, half_count + farther)
    return (bucket[None] == jnp.arange(BUCKETS, dtype=jnp.int32)[:, None, None]).astype(jnp.float32)


def normalize(vector, gain_row):
    return vector * lax.rsqrt(jnp.mean(vector * vector, axis=-1, keepdims=True) + EPS) * gain_row


def project(operand, weight):
    return jnp.dot(operand, weight, preferred_element_type=jnp.float32)


def project_back(operand, weight):
    return lax.dot_general(
        operand, weight, (((1,), (1,)), ((), ())), preferred_element_type=jnp.float32
    )


def weight_grad(inputs_rows, grad_rows):
    return lax.dot_general(
        inputs_rows, grad_rows, (((0,), (0,)), ((), ())), preferred_element_type=jnp.float32
    )


def split_heads(matrix):
    return matrix.reshape(matrix.shape[:-1] + (HEADS, matrix.shape[-1] // HEADS))


def head_scores(queries, key_rows):
    return jnp.einsum(
        "gqhe,gkhe->ghqk",
        split_heads(queries),
        split_heads(key_rows),
        preferred_element_type=jnp.float32,
    )


def attend_forward(queries, key_rows, values, relative_position_bias, allowed):
    scores = jnp.where(allowed, head_scores(queries, key_rows) + relative_position_bias, MASKED)
    largest = jnp.max(scores, axis=-1, keepdims=True)
    exponent = jnp.exp(scores - largest)
    row_totals = jnp.sum(exponent, axis=-1, keepdims=True)
    attention_weights = exponent / row_totals
    context = jnp.einsum(
        "ghqk,gkhe->gqhe",
        attention_weights.astype(jnp.bfloat16),
        split_heads(values),
        preferred_element_type=jnp.float32,
    )
    return (context.reshape(queries.shape).astype(jnp.bfloat16), attention_weights)


def attend_backward(queries, key_rows, values, attention_weights, grad_context):
    grad_heads = split_heads(grad_context)
    grad_values = jnp.einsum(
        "ghqk,gqhe->gkhe",
        attention_weights.astype(jnp.bfloat16),
        grad_heads,
        preferred_element_type=jnp.float32,
    )
    grad_weights = jnp.einsum(
        "gqhe,gkhe->ghqk", grad_heads, split_heads(values), preferred_element_type=jnp.float32
    )
    score_gradient = attention_weights * (
        grad_weights - jnp.sum(grad_weights * attention_weights, axis=-1, keepdims=True)
    )
    rounded = score_gradient.astype(jnp.bfloat16)
    grad_queries = jnp.einsum(
        "ghqk,gkhe->gqhe", rounded, split_heads(key_rows), preferred_element_type=jnp.float32
    )
    grad_keys = jnp.einsum(
        "ghqk,gqhe->gkhe", rounded, split_heads(queries), preferred_element_type=jnp.float32
    )
    return (
        grad_queries.reshape(queries.shape).astype(jnp.bfloat16),
        grad_keys.reshape(key_rows.shape).astype(jnp.bfloat16),
        grad_values.reshape(values.shape).astype(jnp.bfloat16),
        score_gradient,
    )


AXES = ("dp", "fsdp")


def rows_of(matrix):
    return matrix.reshape(-1, matrix.shape[-1])


def gather_all(shards):
    width = shards[0].shape[1]
    blocks = []
    for shard in shards:
        if shard.ndim == 1:
            continue
        blocks.append(shard.reshape(-1, width) if shard.shape[1] != width else shard)
    packed = lax.all_gather(jnp.concatenate(blocks, axis=0), AXES, axis=0)
    whole, at = [], 0
    devices = packed.shape[0]
    for shard, block in zip(shards, blocks):
        part = packed[:, at : at + block.shape[0]]
        at += block.shape[0]
        whole.append(part.reshape(devices * shard.shape[0], shard.shape[1]))
    gains = jnp.stack(shards[len(blocks) :])
    gains = lax.all_gather(gains, AXES, axis=1, tiled=True)
    return whole, [gains[k] for k in range(gains.shape[0])]


def scatter_all(grads, shards):
    width = shards[0].shape[1]
    devices = lax.axis_size(AXES)
    blocks = [grad.astype(jnp.bfloat16).reshape(devices, -1, width) for grad in grads]
    summed = lax.psum_scatter(
        jnp.concatenate(blocks, axis=1), AXES, scatter_dimension=0, tiled=False
    ).astype(jnp.float32)
    pieces, at = [], 0
    for block, shard in zip(blocks, shards):
        pieces.append(summed[at : at + block.shape[1]].reshape(shard.shape))
        at += block.shape[1]
    return pieces


def plain_body(decoder_in, memory, out_grad, lengths, *params):
    shards, bucket_bias_table = params[:13], params[13]
    matrices, gains = gather_all(shards)
    (
        self_query,
        self_key,
        self_value,
        self_out,
        cross_query,
        cross_key,
        cross_value,
        cross_out,
        ff_in,
        ff_out,
    ) = matrices
    norm_self, norm_cross, norm_ff = [gain.astype(jnp.float32) for gain in gains]
    micro, seqs, seq_length, width = decoder_in.shape
    groups = micro * seqs
    memory_bf = memory.reshape(groups, memory.shape[2], width)
    grad_bf = out_grad.reshape(groups, seq_length, width)
    group_lengths = lengths.reshape(groups)
    bucket_indicator = bucket_onehot(seq_length)
    relative_position_bias = jnp.einsum(
        "fsn,fe->esn",
        bucket_indicator,
        bucket_bias_table.astype(jnp.float32),
        precision=TOP_PRECISION,
    )
    positions = jnp.arange(seq_length, dtype=jnp.int32)
    causal = positions[:, None] >= positions[None, :]
    present = positions[None, :] < group_lengths[:, None]
    valid_rows = present[:, :, None].astype(jnp.float32)
    allowed = causal[None, None] & present[:, None, None, :]

    def grad_of(inputs, upstream):
        return weight_grad(rows_of(inputs), rows_of(upstream))

    decoded = decoder_in.reshape(groups, seq_length, width).astype(jnp.float32)
    normed = normalize(decoded, norm_self).astype(jnp.bfloat16)
    queries = project(normed, self_query).astype(jnp.bfloat16)
    key_rows = project(normed, self_key).astype(jnp.bfloat16)
    values = project(normed, self_value).astype(jnp.bfloat16)
    context, self_weights = attend_forward(
        queries, key_rows, values, relative_position_bias, allowed
    )
    after_self = decoded + project(context, self_out)
    normed_cross = normalize(after_self, norm_cross).astype(jnp.bfloat16)
    cross_queries = project(normed_cross, cross_query).astype(jnp.bfloat16)
    memory_keys = project(memory_bf, cross_key).astype(jnp.bfloat16)
    memory_values = project(memory_bf, cross_value).astype(jnp.bfloat16)
    cross_context, cross_weights = attend_forward(
        cross_queries, memory_keys, memory_values, 0.0, True
    )
    after_cross = after_self + project(cross_context, cross_out)
    normed_ff = normalize(after_cross, norm_ff).astype(jnp.bfloat16)
    hidden = project(normed_ff, ff_in)
    activated = jax.nn.gelu(hidden, approximate=True).astype(jnp.bfloat16)
    after_ff = after_cross + project(activated, ff_out)
    layer_out = (after_ff * valid_rows).astype(jnp.bfloat16)

    def back(operand, weight):
        return lax.dot_general(
            operand, weight, (((2,), (1,)), ((), ())), preferred_element_type=jnp.float32
        )

    grad_after = grad_bf.astype(jnp.float32) * valid_rows
    grad_branch = grad_after.astype(jnp.bfloat16)
    grad_ff_out = grad_of(activated, grad_branch)
    gelu_pull = jax.vjp(lambda pre_act: jax.nn.gelu(pre_act, approximate=True), hidden)[1]
    grad_hidden = gelu_pull(back(grad_branch, ff_out))[0].astype(jnp.bfloat16)
    grad_ff_in = grad_of(normed_ff, grad_hidden)
    norm_pull = jax.vjp(normalize, after_cross, norm_ff)[1]
    grad_rows, grad_norm_ff = norm_pull(back(grad_hidden, ff_in))
    grad_after = grad_after + grad_rows
    grad_branch = grad_after.astype(jnp.bfloat16)
    grad_cross_out = grad_of(cross_context, grad_branch)
    grad_context = back(grad_branch, cross_out).astype(jnp.bfloat16)
    grad_cross_rows, grad_memory_keys, grad_memory_values, unused = attend_backward(
        cross_queries, memory_keys, memory_values, cross_weights, grad_context
    )
    grad_cross_query = grad_of(normed_cross, grad_cross_rows)
    grad_cross_key = grad_of(memory_bf, grad_memory_keys)
    grad_cross_value = grad_of(memory_bf, grad_memory_values)
    grad_memory = back(grad_memory_keys, cross_key) + back(grad_memory_values, cross_value)
    norm_pull = jax.vjp(normalize, after_self, norm_cross)[1]
    grad_rows, grad_norm_cross = norm_pull(back(grad_cross_rows, cross_query))
    grad_after = grad_after + grad_rows
    grad_branch = grad_after.astype(jnp.bfloat16)
    grad_self_out = grad_of(context, grad_branch)
    grad_context = back(grad_branch, self_out).astype(jnp.bfloat16)
    grad_queries, grad_key_rows, grad_values, score_gradient = attend_backward(
        queries, key_rows, values, self_weights, grad_context
    )
    grad_self_query = grad_of(normed, grad_queries)
    grad_self_key = grad_of(normed, grad_key_rows)
    grad_self_value = grad_of(normed, grad_values)
    grad_normed = (
        back(grad_queries, self_query) + back(grad_key_rows, self_key) + back(grad_values, self_value)
    )
    norm_pull = jax.vjp(normalize, decoded, norm_self)[1]
    grad_rows, grad_norm_self = norm_pull(grad_normed)
    grad_input = grad_after + grad_rows
    bias_grad = jnp.einsum(
        "fgd,ogd->fo", bucket_indicator, jnp.sum(score_gradient, axis=0), precision=TOP_PRECISION
    )
    pieces = scatter_all(
        (
            grad_self_query,
            grad_self_key,
            grad_self_value,
            grad_self_out,
            grad_cross_query,
            grad_cross_key,
            grad_cross_value,
            grad_cross_out,
            grad_ff_in,
            grad_ff_out,
        ),
        shards[:10],
    )
    small = lax.psum(
        jnp.concatenate([grad_norm_self, grad_norm_cross, grad_norm_ff, bias_grad.reshape(-1)]),
        AXES,
    )
    mine = shards[10].shape[0]
    at = lax.axis_index(AXES) * mine
    gains_out = [
        lax.dynamic_slice_in_dim(small[k * width : (k + 1) * width], at, mine) for k in range(3)
    ]
    return (
        layer_out.reshape(decoder_in.shape),
        grad_input.reshape(decoder_in.shape),
        grad_memory.reshape(memory.shape),
        *pieces,
        *gains_out,
        small[3 * width :].reshape(bucket_bias_table.shape),
    )


MESH = pl.DeviceIdType.MESH
LOW = jnp.bfloat16
WIDE = jnp.float32
GROUPS = 16
WIDTH = 768
ROWS = 512
LENGTH = 256
MEMORY = 128
PAIRS = 6
CURVE = math.sqrt(2.0 / math.pi)


def place():
    dp, fsdp = lax.axis_index("dp"), lax.axis_index("fsdp")
    z, y, x, core = dp // 2, dp % 2, fsdp // 2, fsdp % 2
    sibling = (dp, x * 2 + 1 - core)
    over_x = (dp, (1 - x) * 2 + core)
    over_y = (z * 2 + 1 - y, fsdp)
    first = (jnp.where(core == 0, over_x[0], over_y[0]), jnp.where(core == 0, over_x[1], over_y[1]))
    second = (jnp.where(core == 0, over_y[0], over_x[0]), jnp.where(core == 0, over_y[1], over_x[1]))
    along_z = [(((z + k) % 4) * 2 + y, fsdp) for k in (1, 2, 3)]
    own = y * 2 + x
    beside = jnp.where(core == 0, y * 2 + 1 - x, (1 - y) * 2 + x)
    return z, own, beside, core, sibling, first, second, along_z


def greet(partners):
    barrier = pltpu.get_barrier_semaphore()
    for partner in partners:
        pl.semaphore_signal(barrier, inc=1, device_id=partner, device_id_type=MESH)
    pl.semaphore_wait(barrier, len(partners))


def half(core):
    return pl.ds(pl.multiple_of(core * 384, 128), 384)


def skew(ahead, groups=GROUPS):
    order = []
    for t in range(-max(ahead), groups + 8):
        for s in range(len(ahead)):
            g = t + ahead[s]
            if 0 <= g < groups:
                order.append((g, s))
    return order


def dot(a, b):
    return jnp.dot(a, b, preferred_element_type=WIDE)


def dot_nt(a, b):
    return lax.dot_general(a, b, (((1,), (1,)), ((), ())), preferred_element_type=WIDE)


def dot_tn(a, b):
    return lax.dot_general(a, b, (((0,), (0,)), ((), ())), preferred_element_type=WIDE)


def unit(w, u):
    return w[u].reshape(WIDTH, WIDTH)


def root_scale(value):
    return lax.rsqrt(jnp.mean(value * value, axis=-1, keepdims=True) + EPS)


def bucket_columns(flipped):
    j = lax.broadcasted_iota(jnp.int32, (BUCKETS, LENGTH), 1)
    row = lax.broadcasted_iota(jnp.int32, (BUCKETS, LENGTH), 0)
    n = jnp.where(j == 0, 0, LENGTH - j) if flipped else j
    half_count = BUCKETS // 2
    farther = jnp.zeros_like(n)
    for level in range(1, half_count):
        border = int(math.ceil(half_count * (MAX_DIST / half_count) ** (level / half_count)))
        farther = farther + (n >= border).astype(jnp.int32)
    bucket = jnp.where(n < half_count, n, half_count + farther)
    return (bucket == row).astype(WIDE)


ZS = (2, 5, 8, 11, 14)
AHEAD = (8, 6, 3, 1, 0)
BUDGET = 3.0


def forward_kernel(*refs):
    shard_refs, gain_refs = refs[:9], refs[9:12]
    forward_steps(shard_refs, gain_refs, *refs[12:])


def forward_steps(
    shard_refs, gain_refs, tall_ref, x_ref, mem_ref, table_ref, lens_ref,
    w_out, gains_out, normed_out, q_out, k_out, v_out, ctx_out, p_out, after_self_out, ncross_out,
    cq_out, mk_out, mv_out, cctx_out, pc_out, after_cross_out, nff_out, act_out, slope_out, layer_out,
    w, gains, normed, q, k, v, ctx, p, after_self, ncross, cq, mk, mv, cctx, pc, after_cross, nff, act, slope, layer,
    bias, small, sib, gain_in, ss, rs, ss0, rs0, out_sem,
):
    z, own, beside, core, sibling, first, second, along_z = place()
    mine, other = half(core), half(1 - core)

    def view(g, zi, yx, cols):
        if g < 12:
            return w.at[g, slice(None) if zi is None else zi, yx, :, cols]
        return w.at[pl.ds(12, 4) if zi is None else 12 + zi, yx, g - 12, :, cols]

    def whole(g, cols):
        return w.at[g, :, :, :, cols] if g < 12 else w.at[pl.ds(12, 4), :, g - 12, :, cols]

    def send(ref, to, g, n):
        return pltpu.make_async_remote_copy(
            src_ref=ref, dst_ref=ref, send_sem=ss.at[g, n], recv_sem=rs.at[g, n], device_id=to, device_id_type=MESH)

    def step_a(g):
        return [send(view(g, z, own, mine), to, g, n) for n, to in enumerate(along_z)]

    def step_b(g):
        return [send(view(g, None, own, mine), first, g, 3)]

    def step_c(g):
        return [send(view(g, None, own, mine), second, g, 4), send(view(g, None, beside, mine), second, g, 5)]

    def step_d(g):
        return [send(whole(g, mine), sibling, g, 6)]

    def step_b1(g):
        return [send(view(g, z, own, mine), first, g, 3)]

    def step_a2(g):
        return step_a(g) + [send(view(g, z, beside, mine), to, g, 7 + n) for n, to in enumerate(along_z)]

    def gain_copies(s):
        to = ([sibling], along_z, [first], [second])[s]
        at = (0, 1, 4, 5)[s]
        return [
            pltpu.make_async_remote_copy(
                src_ref=gains, dst_ref=gain_in.at[at + n], send_sem=ss0.at[2 + at + n], recv_sem=rs0.at[2 + at + n],
                device_id=d, device_id_type=MESH)
            for n, d in enumerate(to)
        ]

    def start(copies):
        for copy in copies:
            copy.start()

    def gain_finish(s):
        for copy in gain_copies(s):
            copy.wait()
        for n in ((0,), (1, 2, 3), (4,), (5,))[s]:
            gains[...] += gain_in[n]

    stores = []

    def store(src, dst):
        copy = pltpu.make_async_copy(src, dst, out_sem.at[len(stores)])
        stores.append(copy)
        copy.start()

    def store_unit(g):
        if g < 12:
            store(w.at[g], w_out.at[g])

    def gain(n):
        return gains[n : n + 1, :].astype(WIDE)

    def scale_rows(src, n, dst):
        g = gain(n)

        def chunk(i, c):
            rows = pl.ds(pl.multiple_of(i * 128, 128), 128)
            value = src[rows, :].astype(WIDE)
            dst[rows, :] = (value * root_scale(value) * g).astype(LOW)
            return c

        lax.fori_loop(0, ROWS // 128, chunk, 0)

    def make_bias():
        by_distance = dot(table_ref[...], bucket_columns(True).astype(LOW))
        for h in range(HEADS):
            row = jnp.broadcast_to(by_distance[h : h + 1, :], (LENGTH, LENGTH))
            bias[h] = pltpu.roll(row, 0, 1, stride=1, stride_axis=0)

    def project_into(src, u, dst):
        dst[...] = dot(src[...], unit(w, u)).astype(LOW)

    lane = lax.broadcasted_iota(jnp.int32, (1, 128), 1)
    sides = [lane < 64, lane >= 64]

    def attend(i, queries, keys, vals, keep_p, into, depth, masked):
        s, pair = i // PAIRS, i % PAIRS
        rows = pl.ds(pl.multiple_of(s * LENGTH, LENGTH), LENGTH)
        deep = pl.ds(pl.multiple_of(s * depth, depth), depth)
        cols = pl.ds(pl.multiple_of(pair * 128, 128), 128)
        qp, kp, vp = queries[rows, cols], keys[deep, cols], vals[deep, cols]
        parts = []
        for side in range(2):
            scores = dot_nt(jnp.where(sides[side], qp, jnp.zeros_like(qp)), kp)
            if masked:
                t = lax.broadcasted_iota(jnp.int32, (LENGTH, LENGTH), 0)
                u = lax.broadcasted_iota(jnp.int32, (LENGTH, LENGTH), 1)
                allowed = (u <= t) & (u < lens_ref[s])
                scores = jnp.where(allowed, scores + bias[2 * pair + side], MASKED)
            e = jnp.exp(scores - jnp.max(scores, axis=-1, keepdims=True))
            weights = (e * (1.0 / jnp.sum(e, axis=-1, keepdims=True))).astype(LOW)
            keep_p[rows, pl.ds(pl.multiple_of((2 * pair + side) * depth, 128), depth)] = weights
            parts.append(dot(weights, vp))
        into[rows, cols] = jnp.where(sides[0], parts[0], parts[1]).astype(LOW)

    def self_part(lo, hi):
        def it(i, c):
            attend(i, q, k, v, p, ctx, LENGTH, True)
            return c

        lax.fori_loop(lo, hi, it, 0)

    def cross_part(lo, hi):
        def it(i, c):
            attend(i, cq, mk, mv, pc, cctx, MEMORY, False)
            return c

        lax.fori_loop(lo, hi, it, 0)

    def after_self_part():
        after_self[...] = x_ref[...].astype(WIDE) + dot(ctx[...], unit(w, 3))
        scale_rows(after_self, 1, ncross)

    def after_cross_part():
        after_cross[...] = after_self[...] + dot(cctx[...], unit(w, 7))
        scale_rows(after_cross, 2, nff)

    def hidden_part(j):
        cols = slice(j * WIDTH, (j + 1) * WIDTH)
        for m in range(2):
            rows = slice(m * 256, m * 256 + 256)
            a = dot(nff[rows, :], unit(w, 8 + j))
            sq = a * a
            th = jnp.tanh(a * (CURVE + (CURVE * 0.044715) * sq))
            act[rows, cols] = (0.5 * a * (1.0 + th)).astype(LOW)
            slope[rows, cols] = (
                0.5 * (1.0 + th) + 0.5 * a * (1.0 - th * th) * (CURVE + (3.0 * CURVE * 0.044715) * sq)
            ).astype(LOW)

    def layer_part():
        total = after_cross[...]
        for j in range(4):
            total = total + dot(act[:, j * WIDTH : (j + 1) * WIDTH], unit(w, 12 + j))
        for s in range(2):
            t = lax.broadcasted_iota(jnp.int32, (LENGTH, 1), 0)
            valid = (t < lens_ref[s]).astype(WIDE)
            layer[s * LENGTH : (s + 1) * LENGTH, :] = (total[s * LENGTH : (s + 1) * LENGTH] * valid).astype(LOW)

    pieces = [
        (0, 1.0, lambda: project_into(normed, 0, q)), (0, 0.1, lambda: store(q, q_out)),
        (1, 1.0, lambda: project_into(normed, 1, k)), (1, 0.1, lambda: store(k, k_out)),
        (2, 1.0, lambda: project_into(normed, 2, v)), (2, 0.1, lambda: store(v, v_out)),
        (2, 2.5, lambda: self_part(0, 3)), (2, 2.5, lambda: self_part(3, 6)),
        (2, 2.5, lambda: self_part(6, 9)), (2, 2.5, lambda: self_part(9, 12)),
        (2, 0.1, lambda: store(ctx, ctx_out)), (2, 0.1, lambda: store(p, p_out)),
        (3, 2.0, after_self_part), (3, 0.1, lambda: store(after_self, after_self_out)), (3, 0.1, lambda: store(ncross, ncross_out)),
        (4, 1.0, lambda: project_into(ncross, 4, cq)), (4, 0.1, lambda: store(cq, cq_out)),
        (5, 0.6, lambda: project_into(mem_ref, 5, mk)), (5, 0.1, lambda: store(mk, mk_out)),
        (6, 0.6, lambda: project_into(mem_ref, 6, mv)), (6, 0.1, lambda: store(mv, mv_out)),
        (6, 2.5, lambda: cross_part(0, 4)), (6, 2.5, lambda: cross_part(4, 8)), (6, 2.5, lambda: cross_part(8, 12)),
        (6, 0.1, lambda: store(cctx, cctx_out)), (6, 0.1, lambda: store(pc, pc_out)),
        (7, 2.0, after_cross_part), (7, 0.1, lambda: store(after_cross, after_cross_out)), (7, 0.1, lambda: store(nff, nff_out)),
        (8, 2.0, lambda: hidden_part(0)), (9, 2.0, lambda: hidden_part(1)),
        (10, 2.0, lambda: hidden_part(2)), (11, 2.0, lambda: hidden_part(3)),
        (11, 0.1, lambda: store(act, act_out)), (11, 0.1, lambda: store(slope, slope_out)),
        (15, 4.0, layer_part), (15, 0.1, lambda: store(layer, layer_out)),
    ]

    for u in range(12):
        rows = shard_refs[u][...] if u < 8 else shard_refs[8][:, WIDTH * (u - 8) : WIDTH * (u - 7)]
        rows = rows.astype(WIDE)
        none = jnp.zeros_like(rows)
        small[u] = jnp.concatenate(
            [jnp.where(core == 0, rows, none), jnp.where(core == 0, none, rows)], axis=0).astype(LOW)
    offset = (lax.axis_index("dp") * 4 + lax.axis_index("fsdp")) * 24
    spot = (lax.broadcasted_iota(jnp.int32, (24, WIDTH), 1) == lax.broadcasted_iota(jnp.int32, (24, WIDTH), 0) + offset)
    placed = [dot(ref[...], spot.astype(LOW)) for ref in gain_refs]
    gains[...] = jnp.concatenate(placed + [jnp.zeros((13, WIDTH), WIDE)], axis=0).astype(LOW)

    greet([sibling, first, second] + along_z)
    swap_small = pltpu.make_async_remote_copy(
        src_ref=small.at[:, :, other], dst_ref=sib, send_sem=ss0.at[0], recv_sem=rs0.at[0],
        device_id=sibling, device_id_type=MESH)

    def tall_view(cols):
        return w.at[12 + z, own, pl.ds(2 * core, 2), :, cols]

    swap_tall = pltpu.make_async_remote_copy(
        src_ref=tall_ref.at[:, :, other], dst_ref=tall_view(other), send_sem=ss0.at[1], recv_sem=rs0.at[1],
        device_id=sibling, device_id_type=MESH)
    swap_small.start()
    swap_tall.start()
    start(gain_copies(0))
    w[12 + z, own, pl.ds(2 * core, 2), :, mine] = tall_ref[:, :, mine]
    swap_small.wait()
    for u in range(12):
        w[u, z, own, :, mine] = small[u, :, mine] + sib[u]
    swap_tall.wait()
    gain_finish(0)
    start(gain_copies(1))

    zf = (step_a, step_b, step_c, step_d)
    zs = (step_b1, step_a2, step_c, step_d)
    stage, done = 1, 0
    for n, (g, s) in enumerate(skew(AHEAD)):
        steps = zs if g in ZS else zf
        if s:
            for copy in steps[s - 1](g):
                copy.wait()
        if s < 4:
            start(steps[s](g))
        if n == 8:
            make_bias()
        if n in (8, 11, 14):
            gain_finish(stage)
            stage += 1
            if stage < 4:
                start(gain_copies(stage))
            else:
                scale_rows(x_ref, 0, normed)
                store(normed, normed_out)
                store(gains, gains_out)
        if s == 4:
            store_unit(g)
            spent = 0.0
            while done < len(pieces) and pieces[done][0] <= g and (spent < BUDGET or g == GROUPS - 1):
                spent += pieces[done][1]
                pieces[done][2]()
                done += 1
            if g == GROUPS - 1:
                store(w.at[pl.ds(12, 4)], w_out.at[pl.ds(12, 4)])
    assert done == len(pieces) and stage == 4
    for copy in stores:
        copy.wait()


FORWARD_OUT = (
    ((16, 4, 4, 48, 768), LOW),
    ((16, 768), LOW),
    ((512, 768), LOW), ((512, 768), LOW), ((512, 768), LOW), ((512, 768), LOW),
    ((512, 768), LOW),
    ((512, 3072), LOW),
    ((512, 768), WIDE),
    ((512, 768), LOW),
    ((512, 768), LOW), ((256, 768), LOW), ((256, 768), LOW), ((512, 768), LOW),
    ((512, 1536), LOW),
    ((512, 768), WIDE),
    ((512, 768), LOW),
    ((512, 3072), LOW), ((512, 3072), LOW),
    ((512, 768), LOW),
)


def forward_call(*operands):
    return pl.pallas_call(
        forward_kernel,
        out_shape=tuple(jax.ShapeDtypeStruct(s, t) for s, t in FORWARD_OUT),
        in_specs=[pl.BlockSpec(memory_space=pltpu.VMEM)] * 16 + [pl.BlockSpec(memory_space=pltpu.SMEM)],
        out_specs=[pl.BlockSpec(memory_space=pl.ANY)] * len(FORWARD_OUT),
        scratch_shapes=[pltpu.VMEM(s, t) for s, t in FORWARD_OUT]
        + [
            pltpu.VMEM((HEADS, LENGTH, LENGTH), WIDE),
            pltpu.VMEM((12, 48, 768), LOW),
            pltpu.VMEM((12, 48, 384), LOW),
            pltpu.VMEM((6, 16, 768), LOW),
            pltpu.SemaphoreType.DMA((GROUPS, 10)),
            pltpu.SemaphoreType.DMA((GROUPS, 10)),
            pltpu.SemaphoreType.DMA((8,)),
            pltpu.SemaphoreType.DMA((8,)),
            pltpu.SemaphoreType.DMA((32,)),
        ],
        compiler_params=pltpu.CompilerParams(collective_id=0, has_side_effects=True, vmem_limit_bytes=60 * 2**20),
    )(*operands)


def forward(shards, decoder_in, memory, table, lengths):
    return forward_call(
        *shards[:9],
        *[shard.reshape(1, 24) for shard in shards[10:13]],
        shards[9].reshape(2, 48, WIDTH),
        decoder_in.reshape(ROWS, WIDTH),
        memory.reshape(2 * MEMORY, WIDTH),
        table.T,
        lengths.reshape(2),
    )


LINE = (12, 13, 14, 15, 8, 9, 10, 11, 7, 4, 5, 6, 3, 0, 1, 2)
USED = (12, 8, 13, 9, 14, 10, 15, 11, 7, 5, 6, 4, 3, 0, 1, 2)
SLOTS = 6
LAGS = (0, 1, 4, 6, 8, 9)
PACE = 3.5
FIRST_Z = ()


def backward_kernel(
    gains, lens_ref, w_hbm, act_hbm, slope_hbm, nff_hbm, after_cross_hbm, cctx_hbm, ncross_hbm, cq_hbm, mk_hbm, mv_hbm,
    mem_hbm, pc_hbm, after_self_hbm, p_hbm, normed_hbm, q_hbm, k_hbm, v_hbm, ctx_hbm, x_hbm, og_hbm,
    input_out, memory_out, *rest,
):
    pieces_out, rest = rest[:8], rest[8:]
    (
        in_piece_out, out_piece_out, sum_out,
        ring, act, slope, nff, aft, cctx, ncross, cq, mk, mv, mem, pc, x, gl, total, up, ghj, low, gctx, dq, dk, dv,
        dist, grad, r0, r1, r23, fa, fo, fa_in, fo_in, acc, acc_in, ss, rs, ss0, rs0, in_sem, ring_sem, out_sem,
    ) = rest
    z, own, beside, core, sibling, first, second, along_z = place()
    mine, other = half(core), half(1 - core)
    diag, across = 3 - own, 3 - beside

    fetches = {}

    def fetch(name, src, dst):
        copy = pltpu.make_async_copy(src, dst, in_sem.at[len(fetches)])
        fetches[name] = copy
        copy.start()

    def fetched(*names):
        for name in names:
            fetches[name].wait()

    def weight_copy(n):
        return pltpu.make_async_copy(w_hbm.at[USED[n]], ring.at[n % SLOTS], ring_sem.at[n])

    asked, got = [0], [0]

    def ask(n):
        while asked[0] < min(n, GROUPS):
            weight_copy(asked[0]).start()
            asked[0] += 1

    def weight(u):
        n = USED.index(u)
        while got[0] <= n:
            weight_copy(got[0]).wait()
            got[0] += 1
        return ring[n % SLOTS].reshape(WIDTH, WIDTH)

    def send(src, dst, to, g, n):
        return pltpu.make_async_remote_copy(
            src_ref=src, dst_ref=dst, send_sem=ss.at[g, n], recv_sem=rs.at[g, n], device_id=to, device_id_type=MESH)

    def block(g, cols):
        if g < 12:
            return grad.at[LINE.index(g) % 4, :, :, :, cols]
        return grad.at[:, :, g - 12, :, cols]

    def swap(g):
        return [send(block(g, other), r0.at[g], sibling, g, 0)]

    def over_second(g):
        return [send(r0.at[g, :, across], r1.at[g, 0], second, g, 1), send(r0.at[g, :, diag], r1.at[g, 1], second, g, 2)]

    def over_first(g):
        return [send(r0.at[g, :, beside], r23.at[g, pl.ds(0, 4)], first, g, 3)]

    def over_z(g):
        return [send(r0.at[g, (z + n + 1) % 4, own], r23.at[g, 4 + n], to, g, 4 + n) for n, to in enumerate(along_z)]

    def over_z2(g):
        return over_z(g) + [
            send(r0.at[g, (z + n + 1) % 4, beside], r23.at[g, 1 + n], to, g, 7 + n) for n, to in enumerate(along_z)]

    def over_first1(g):
        return [send(r0.at[g, z, beside], r23.at[g, 0], first, g, 3)]

    def last(g):
        if g < 12:
            rows = pl.ds(pl.multiple_of(24 * (1 - core), 8), 24)
            return [send(fa.at[g, rows], fa_in.at[g], sibling, g, 10)]
        if g == 15:
            return [send(fo.at[pl.ds(2 * (1 - core), 2)], fo_in, sibling, g, 10)]
        return []

    def add0(g):
        r0[g] += block(g, mine)[...]

    def add1(g):
        r0[g, :, own] += r1[g, 0]
        r0[g, :, beside] += r1[g, 1]

    def finish(g, value):
        if g < 12:
            fa[g] = value
        else:
            fo[g - 12] = value

    def add2(g):
        r0[g, :, own] += r23[g, 0:4]

    def over(g, yx, at):
        value = r0[g, z, yx].astype(WIDE)
        for n in range(3):
            value = value + r23[g, at + n].astype(WIDE)
        return value

    def add3(g):
        finish(g, over(g, own, 4))

    def add2z(g):
        mid = over(g, own, 4), over(g, beside, 1)
        r0[g, z, own] = mid[0].astype(LOW)
        r0[g, z, beside] = mid[1].astype(LOW)

    def add3z(g):
        finish(g, r0[g, z, own].astype(WIDE) + r23[g, 0].astype(WIDE))

    def write(g):
        rows = pl.ds(pl.multiple_of(24 * core, 8), 24)
        if g < 8:
            pieces_out[g][:, mine] = fa[g, rows]
            pieces_out[g][:, other] = fa_in[g]
        elif g < 12:
            at = WIDTH * (g - 8)
            in_piece_out[:, pl.ds(pl.multiple_of(at + core * 384, 128), 384)] = fa[g, rows]
            in_piece_out[:, pl.ds(pl.multiple_of(at + 384 - core * 384, 128), 384)] = fa_in[g]
        elif g == 15:
            out_piece_out[:, mine] = fo[pl.ds(2 * core, 2)].reshape(96, 384)
            out_piece_out[:, other] = fo_in[...].reshape(96, 384)

    zf = ((swap, over_second, over_first, over_z, last), (None, add0, add1, add2, add3, write))
    zs = ((swap, over_second, over_z2, over_first1, last), (None, add0, add1, add2z, add3z, write))

    def event(g, s):
        copies, sums = zs if g in FIRST_Z else zf
        if s:
            for copy in copies[s - 1](g):
                copy.wait()
            sums[s](g)
        if s < 5:
            for copy in copies[s](g):
                copy.start()

    def acc_copies(s):
        to = ([sibling], along_z, [first], [second])[s]
        at = (0, 1, 4, 5)[s]
        return [
            pltpu.make_async_remote_copy(
                src_ref=acc, dst_ref=acc_in.at[at + n], send_sem=ss0.at[at + n], recv_sem=rs0.at[at + n],
                device_id=d, device_id_type=MESH)
            for n, d in enumerate(to)
        ]

    lane = lax.broadcasted_iota(jnp.int32, (1, 128), 1)
    sides = [lane < 64, lane >= 64]

    def keep(g, value):
        grad[LINE.index(g) % 4] = value.astype(LOW).reshape(4, 4, 48, WIDTH)

    def begin():
        fetched("og")
        for s in range(2):
            rows = slice(s * LENGTH, (s + 1) * LENGTH)
            t = lax.broadcasted_iota(jnp.int32, (LENGTH, 1), 0)
            gl[rows, :] = jnp.where(t < lens_ref[s], gl[rows, :].astype(WIDE), 0.0).astype(LOW)
        fetched("act")

    def out_grad_part(j):
        grad[j] = dot_tn(act[:, j * WIDTH : (j + 1) * WIDTH], gl[...]).astype(LOW).reshape(4, 4, 48, WIDTH)

    def hidden_part(j):
        if j == 0:
            fetched("slope", "nff")
        cols = slice(j * WIDTH, (j + 1) * WIDTH)
        ghj[...] = (dot_nt(gl[...], weight(12 + j)) * slope[:, cols].astype(WIDE)).astype(LOW)
        keep(8 + j, dot_tn(nff[...], ghj[...]))

    def hidden_back(j):
        part = dot_nt(ghj[...], weight(8 + j))
        if j:
            up[...] += part
        else:
            up[...] = part

    def norm_back(value_ref, base_ref, n):
        g = gains[n : n + 1, :].astype(WIDE)

        def chunk(i, carried):
            rows = pl.ds(pl.multiple_of(i * 128, 128), 128)
            value = value_ref[rows, :].astype(WIDE)
            r = root_scale(value)
            unit_rows = value * r
            upstream = up[rows, :]
            weighted = upstream * g
            inner = jnp.mean(weighted * unit_rows, axis=-1, keepdims=True)
            new = base_ref[rows, :].astype(WIDE) + r * (weighted - unit_rows * inner)
            total[rows, :] = new
            low[rows, :] = new.astype(LOW)
            return carried + jnp.sum(upstream * unit_rows, axis=0, keepdims=True)

        acc[n : n + 1, 0:WIDTH] = lax.fori_loop(0, ROWS // 128, chunk, jnp.zeros((1, WIDTH), WIDE))

    def ff_norm_part():
        fetched("after_cross")
        norm_back(aft, gl, 2)
        fetch("p", p_hbm, act)
        fetch("normed", normed_hbm, slope.at[:, 0:768])
        fetch("q", q_hbm, slope.at[:, 768:1536])
        fetch("k", k_hbm, slope.at[:, 1536:2304])
        fetch("v", v_hbm, slope.at[:, 2304:3072])
        fetch("ctx", ctx_hbm, nff)
        fetch("after_self", after_self_hbm, aft)

    def cross_out_part():
        fetched("cctx")
        keep(7, dot_tn(cctx[...], low[...]))
        gctx[...] = dot_nt(low[...], weight(7)).astype(LOW)
        fetched("cq", "mk", "mv", "pc")

    def head_back(weights, gp, qp, kp, vp, side):
        p32 = weights.astype(WIDE)
        pull = dot_nt(jnp.where(sides[side], gp, jnp.zeros_like(gp)), vp)
        slant = p32 * (pull - jnp.sum(pull * p32, axis=-1, keepdims=True))
        rounded = slant.astype(LOW)
        return dot(rounded, kp), dot_tn(rounded, qp), dot_tn(weights, gp), slant

    def joined(low_part, high_part):
        return jnp.where(sides[0], low_part, high_part).astype(LOW)

    def cross_part(lo, hi):
        def it(i, c):
            s, pair = i // PAIRS, i % PAIRS
            rows = pl.ds(pl.multiple_of(s * LENGTH, LENGTH), LENGTH)
            deep = pl.ds(pl.multiple_of(s * MEMORY, MEMORY), MEMORY)
            cols = pl.ds(pl.multiple_of(pair * 128, 128), 128)
            gp, qp, kp, vp = gctx[rows, cols], cq[rows, cols], mk[deep, cols], mv[deep, cols]
            one, two = [
                head_back(pc[rows, pl.ds(pl.multiple_of((2 * pair + side) * MEMORY, 128), MEMORY)], gp, qp, kp, vp, side)
                for side in range(2)
            ]
            dq[rows, cols] = joined(one[0], two[0])
            dk[deep, cols] = joined(one[1], two[1])
            dv[deep, cols] = joined(one[2], two[2])
            return c

        lax.fori_loop(lo, hi, it, 0)

    def cross_query_part():
        fetched("ncross")
        keep(4, dot_tn(ncross[...], dq[...]))

    def cross_key_part():
        fetched("mem")
        keep(5, dot_tn(mem[...], dk[0:256, :]))

    def cross_value_part():
        keep(6, dot_tn(mem[...], dv[0:256, :]))

    def cross_norm_part():
        up[0:256, :] = dot_nt(dk[0:256, :], weight(5)) + dot_nt(dv[0:256, :], weight(6))
        copy = pltpu.make_async_copy(up.at[pl.ds(0, 256)], memory_out, out_sem.at[0])
        copy.start()
        copy.wait()
        up[...] = dot_nt(dq[...], weight(4))
        fetched("after_self")
        norm_back(aft, total, 1)

    def self_out_part():
        fetched("ctx")
        keep(3, dot_tn(nff[...], low[...]))
        gctx[...] = dot_nt(low[...], weight(3)).astype(LOW)
        fetched("p", "q", "k", "v")

    def self_part(lo, hi):
        def it(pair, c):
            cols = pl.ds(pl.multiple_of(pair * 128, 128), 128)
            q_cols = pl.ds(pl.multiple_of(768 + pair * 128, 128), 128)
            k_cols = pl.ds(pl.multiple_of(1536 + pair * 128, 128), 128)
            v_cols = pl.ds(pl.multiple_of(2304 + pair * 128, 128), 128)
            slants = []
            for s in range(2):
                rows = slice(s * LENGTH, (s + 1) * LENGTH)
                gp, qp, kp, vp = gctx[rows, cols], slope[rows, q_cols], slope[rows, k_cols], slope[rows, v_cols]
                one, two = [
                    head_back(act[rows, pl.ds(pl.multiple_of((2 * pair + side) * LENGTH, 256), LENGTH)], gp, qp, kp, vp, side)
                    for side in range(2)
                ]
                dq[rows, cols] = joined(one[0], two[0])
                dk[rows, cols] = joined(one[1], two[1])
                dv[rows, cols] = joined(one[2], two[2])
                slants.append((one[3], two[3]))
            t = lax.broadcasted_iota(jnp.int32, (LENGTH, LENGTH), 0)
            u = lax.broadcasted_iota(jnp.int32, (LENGTH, LENGTH), 1)
            upside = (t + u == LENGTH - 1).astype(LOW)
            for side in range(2):
                both = slants[0][side] + slants[1][side]
                coarse = both.astype(LOW)
                fine = (both - coarse.astype(WIDE)).astype(LOW)
                turned = dot(upside, coarse) + dot(upside, fine)
                rolled = pltpu.roll(turned, 1, 1, stride=1, stride_axis=0)
                dist[pl.ds(2 * pair + side, 1), :] = jnp.sum(rolled, axis=0, keepdims=True)
            return c

        lax.fori_loop(lo, hi, it, 0)

    def self_grads(n):
        fetched(*(["normed"] if n == 0 else []))
        keep(n, dot_tn(slope[:, 0:768], (dq, dk, dv)[n][...]))

    def input_part():
        up[...] = dot_nt(dq[...], weight(0)) + dot_nt(dk[...], weight(1)) + dot_nt(dv[...], weight(2))
        fetched("x")
        norm_back(x, total, 0)
        pltpu.make_async_copy(total, input_out, out_sem.at[1]).start()
        buckets = lax.dot_general(
            dist[...], bucket_columns(True), (((1,), (1,)), ((), ())),
            precision=lax.Precision.HIGHEST, preferred_element_type=WIDE)
        acc[:, WIDTH : WIDTH + BUCKETS] = buckets
        for copy in acc_copies(0):
            copy.start()

    pieces = [(0.5, begin, None, 6)]
    pieces += [(1.0, functools.partial(out_grad_part, j), 12 + j, 6) for j in range(4)]
    for j in range(4):
        pieces += [(2.0, functools.partial(hidden_part, j), 8 + j, 0), (1.0, functools.partial(hidden_back, j), None, 8 + 2 * j)]
    pieces += [
        (1.5, ff_norm_part, None, 0), (1.9, cross_out_part, 7, 15),
        (2.5, lambda: cross_part(0, 4), None, 0), (2.5, lambda: cross_part(4, 8), None, 0), (2.5, lambda: cross_part(8, 12), None, 0),
        (1.0, cross_query_part, 4, 0), (0.5, cross_key_part, 5, 0), (0.5, cross_value_part, 6, 0),
        (4.0, cross_norm_part, None, 16), (2.0, self_out_part, 3, 0),
        (4.0, lambda: self_part(0, 2), None, 0), (4.0, lambda: self_part(2, 4), None, 0), (4.0, lambda: self_part(4, 6), None, 0),
        (1.0, lambda: self_grads(0), 0, 0), (1.0, lambda: self_grads(1), 1, 0), (1.0, lambda: self_grads(2), 2, 0),
        (4.5, input_part, None, 0),
    ]

    acc[...] = jnp.zeros_like(acc)
    dist[...] = jnp.zeros_like(dist)
    fetch("og", og_hbm, gl)
    fetch("act", act_hbm, act)
    ask(2)
    fetch("slope", slope_hbm, slope)
    fetch("nff", nff_hbm, nff)
    fetch("after_cross", after_cross_hbm, aft)
    fetch("cctx", cctx_hbm, cctx)
    fetch("cq", cq_hbm, cq)
    fetch("mk", mk_hbm, mk)
    fetch("mv", mv_hbm, mv)
    fetch("pc", pc_hbm, pc)
    fetch("ncross", ncross_hbm, ncross)
    fetch("mem", mem_hbm, mem)
    fetch("x", x_hbm, x)
    greet([sibling, first, second] + along_z)

    clock, done, made, freed = 0.0, 0, set(), set()

    def run_piece():
        nonlocal clock, done
        cost, what, makes, asks = pieces[done]
        what()
        ask(asks)
        clock += cost
        made.add(makes)
        done += 1

    def may_run():
        makes = pieces[done][2]
        if makes is None or makes >= 12:
            return True
        i = LINE.index(makes)
        return set(LINE[:4]) <= freed if i < 8 else LINE[i - 4] in freed

    stage = None
    for r in range(GROUPS + LAGS[-1]):
        for s in range(1, 6):
            i = r - LAGS[s]
            if 0 <= i < GROUPS:
                event(LINE[i], s)
                if s == 1:
                    freed.add(LINE[i])
        if r < GROUPS:
            needed = set(LINE[:4]) if r < 4 else {LINE[r]}
            while not needed <= made:
                assert may_run()
                run_piece()
            event(LINE[r], 0)
        while done < len(pieces) and clock < PACE * (r + 1) and may_run():
            run_piece()
        if done == len(pieces):
            if stage is None:
                stage = 0
            elif stage < 4:
                for copy in acc_copies(stage):
                    copy.wait()
                for n in ((0,), (1, 2, 3), (4,), (5,))[stage]:
                    acc[...] += acc_in[n]
                stage += 1
                if stage < 4:
                    for copy in acc_copies(stage):
                        copy.start()
    assert done == len(pieces) and stage == 4 and got[0] == GROUPS
    offset = (lax.axis_index("dp") * 4 + lax.axis_index("fsdp")) * 24
    sum_out[:, 0:WIDTH] = pltpu.roll(acc[:, 0:WIDTH], WIDTH - offset, 1)
    sum_out[:, WIDTH:] = acc[:, WIDTH:]
    pltpu.make_async_copy(total, input_out, out_sem.at[1]).wait()


BACKWARD_OUT = (
    (((512, 768), WIDE), ((256, 768), WIDE)),
    (((24, 768), WIDE),) * 8 + (((24, 3072), WIDE), ((96, 768), WIDE), ((16, 896), WIDE)),
)


def backward_call(gains, lens, *arrays):
    shape = lambda s: jax.ShapeDtypeStruct(*s)
    vmem = lambda *s: pltpu.VMEM(s, LOW)
    return pl.pallas_call(
        backward_kernel,
        out_shape=tuple(shape(s) for s in BACKWARD_OUT[0] + BACKWARD_OUT[1]),
        in_specs=[pl.BlockSpec(memory_space=pltpu.VMEM), pl.BlockSpec(memory_space=pltpu.SMEM)]
        + [pl.BlockSpec(memory_space=pl.ANY)] * len(arrays),
        out_specs=[pl.BlockSpec(memory_space=pl.ANY)] * 2 + [pl.BlockSpec(memory_space=pltpu.VMEM)] * 11,
        scratch_shapes=[
            vmem(SLOTS, 4, 4, 48, 768),
            vmem(512, 3072), vmem(512, 3072), vmem(512, 768),
            pltpu.VMEM((512, 768), WIDE),
            vmem(512, 768), vmem(512, 768), vmem(512, 768), vmem(256, 768), vmem(256, 768), vmem(256, 768),
            vmem(512, 1536),
            vmem(512, 768), vmem(512, 768),
            pltpu.VMEM((512, 768), WIDE), pltpu.VMEM((512, 768), WIDE),
            vmem(512, 768), vmem(512, 768), vmem(512, 768),
            vmem(512, 768), vmem(512, 768), vmem(512, 768),
            pltpu.VMEM((16, LENGTH), WIDE),
            vmem(4, 4, 4, 48, 768),
            vmem(GROUPS, 4, 4, 48, 384), vmem(GROUPS, 2, 4, 48, 384), vmem(GROUPS, 7, 48, 384),
            pltpu.VMEM((12, 48, 384), WIDE), pltpu.VMEM((4, 48, 384), WIDE),
            pltpu.VMEM((12, 24, 384), WIDE), pltpu.VMEM((2, 48, 384), WIDE),
            pltpu.VMEM((16, 896), WIDE), pltpu.VMEM((6, 16, 896), WIDE),
            pltpu.SemaphoreType.DMA((GROUPS, 11)), pltpu.SemaphoreType.DMA((GROUPS, 11)),
            pltpu.SemaphoreType.DMA((6,)), pltpu.SemaphoreType.DMA((6,)),
            pltpu.SemaphoreType.DMA((24,)), pltpu.SemaphoreType.DMA((GROUPS,)), pltpu.SemaphoreType.DMA((2,)),
        ],
        compiler_params=pltpu.CompilerParams(collective_id=1, has_side_effects=True, vmem_limit_bytes=62 * 2**20),
    )(gains, lens, *arrays)


def place_kernel(*refs):
    small_ref, arrays = refs[0], refs[1:14]
    outs, held, sems = refs[14:31], refs[31:44], refs[44]
    copies = [pltpu.make_async_copy(src, dst, sems.at[0, n]) for n, (src, dst) in enumerate(zip(arrays, held))]
    for copy in copies:
        copy.start()
    onward = [pltpu.make_async_copy(src, dst, sems.at[1, n]) for n, (src, dst) in enumerate(zip(held, outs))]
    for n in range(3):
        outs[13 + n][...] = small_ref[n : n + 1, 0:24]
    outs[16][...] = small_ref[0:HEADS, WIDTH : WIDTH + BUCKETS]
    for copy, next_copy in zip(copies, onward):
        copy.wait()
        next_copy.start()
    for copy in onward:
        copy.wait()


def place_call(small, *arrays):
    shapes = [jax.ShapeDtypeStruct(a.shape, a.dtype) for a in arrays]
    shapes += [jax.ShapeDtypeStruct((1, 24), WIDE)] * 3 + [jax.ShapeDtypeStruct((HEADS, BUCKETS), WIDE)]
    return pl.pallas_call(
        place_kernel,
        out_shape=tuple(shapes),
        in_specs=[pl.BlockSpec(memory_space=pltpu.VMEM)] + [pl.BlockSpec(memory_space=pl.ANY)] * 13,
        out_specs=[pl.BlockSpec(memory_space=pl.ANY)] * 13 + [pl.BlockSpec(memory_space=pltpu.VMEM)] * 4,
        scratch_shapes=[pltpu.VMEM(a.shape, a.dtype) for a in arrays] + [pltpu.SemaphoreType.DMA((2, 13))],
    )(small, *arrays)


def layer_kernels(decoder_in, memory, out_grad, lengths, *params):
    shards, table = params[:13], params[13]
    (
        w, gains, normed, q, k, v, ctx, p, after_self, ncross, cq, mk, mv, cctx, pc, after_cross, nff, act, slope, layer,
    ) = forward(shards, decoder_in, memory, table, lengths)
    rows = decoder_in.reshape(ROWS, WIDTH)
    input_grad, memory_grad, *pieces, in_piece, out_piece, small = backward_call(
        gains, lengths.reshape(2), w, act, slope, nff, after_cross, cctx, ncross, cq, mk, mv,
        memory.reshape(2 * MEMORY, WIDTH), pc, after_self, p, normed, q, k, v, ctx, rows, out_grad.reshape(ROWS, WIDTH),
    )
    layer, input_grad, memory_grad, *rest = place_call(small, layer, input_grad, memory_grad, *pieces, in_piece, out_piece)
    return (
        layer.reshape(decoder_in.shape),
        input_grad.reshape(decoder_in.shape),
        memory_grad.reshape(memory.shape),
        *rest[:10],
        *[part.reshape(24) for part in rest[10:13]],
        rest[13].T,
    )


def body(decoder_in, memory, out_grad, lengths, *params):
    sizes = (lax.axis_size("dp"), lax.axis_size("fsdp"))
    if sizes == (8, 4) and decoder_in.shape == (2, 1, LENGTH, WIDTH) and params[0].shape == (24, WIDTH):
        return layer_kernels(decoder_in, memory, out_grad, lengths, *params)
    return plain_body(decoder_in, memory, out_grad, lengths, *params)


def solution(mesh):
    return jax.shard_map(
        body,
        mesh=mesh,
        in_specs=(
            P(None, ("dp", "fsdp"), None, None),
            P(None, ("dp", "fsdp"), None, None),
            P(None, ("dp", "fsdp"), None, None),
            P(None, ("dp", "fsdp")),
            P(("dp", "fsdp"), None),
            P(("dp", "fsdp"), None),
            P(("dp", "fsdp"), None),
            P(("dp", "fsdp"), None),
            P(("dp", "fsdp"), None),
            P(("dp", "fsdp"), None),
            P(("dp", "fsdp"), None),
            P(("dp", "fsdp"), None),
            P(("dp", "fsdp"), None),
            P(("dp", "fsdp"), None),
            P(("dp", "fsdp")),
            P(("dp", "fsdp")),
            P(("dp", "fsdp")),
            P(),
        ),
        out_specs=(
            P(None, ("dp", "fsdp"), None, None),
            P(None, ("dp", "fsdp"), None, None),
            P(None, ("dp", "fsdp"), None, None),
            P(("dp", "fsdp"), None),
            P(("dp", "fsdp"), None),
            P(("dp", "fsdp"), None),
            P(("dp", "fsdp"), None),
            P(("dp", "fsdp"), None),
            P(("dp", "fsdp"), None),
            P(("dp", "fsdp"), None),
            P(("dp", "fsdp"), None),
            P(("dp", "fsdp"), None),
            P(("dp", "fsdp"), None),
            P(("dp", "fsdp")),
            P(("dp", "fsdp")),
            P(("dp", "fsdp")),
            P(),
        ),
        check_vma=False,
    )
```

```python
import functools
import math

import jax
import jax.numpy as jnp
from jax import lax
from jax.experimental import pallas as pl
from jax.experimental.pallas import tpu as pltpu
from jax.sharding import PartitionSpec as P

HEADS = 12
BUCKETS = 32
MAX_DIST = 128


EPS = 1e-06
MASKED = -1e30
TOP_PRECISION = lax.Precision.HIGHEST


def bucket_onehot(length):
    half_count = BUCKETS // 2
    positions = jnp.arange(length, dtype=jnp.int32)
    distance = jnp.maximum(positions[:, None] - positions[None, :], 0)
    farther = jnp.zeros_like(distance)
    for level in range(1, half_count):
        border = int(math.ceil(half_count * (MAX_DIST / half_count) ** (level / half_count)))
        farther = farther + (distance >= border).astype(jnp.int32)
    bucket = jnp.where(distance < half_count, distance, half_count + farther)
    return (bucket[None] == jnp.arange(BUCKETS, dtype=jnp.int32)[:, None, None]).astype(jnp.float32)


def normalize(vector, gain_row):
    return vector * lax.rsqrt(jnp.mean(vector * vector, axis=-1, keepdims=True) + EPS) * gain_row


def project(operand, weight):
    return jnp.dot(operand, weight, preferred_element_type=jnp.float32)


def project_back(operand, weight):
    return lax.dot_general(
        operand, weight, (((1,), (1,)), ((), ())), preferred_element_type=jnp.float32
    )


def weight_grad(inputs_rows, grad_rows):
    return lax.dot_general(
        inputs_rows, grad_rows, (((0,), (0,)), ((), ())), preferred_element_type=jnp.float32
    )


def split_heads(matrix):
    return matrix.reshape(matrix.shape[:-1] + (HEADS, matrix.shape[-1] // HEADS))


def head_scores(queries, key_rows):
    return jnp.einsum(
        "gqhe,gkhe->ghqk",
        split_heads(queries),
        split_heads(key_rows),
        preferred_element_type=jnp.float32,
    )


def attend_forward(queries, key_rows, values, relative_position_bias, allowed):
    scores = jnp.where(allowed, head_scores(queries, key_rows) + relative_position_bias, MASKED)
    largest = jnp.max(scores, axis=-1, keepdims=True)
    exponent = jnp.exp(scores - largest)
    row_totals = jnp.sum(exponent, axis=-1, keepdims=True)
    attention_weights = exponent / row_totals
    context = jnp.einsum(
        "ghqk,gkhe->gqhe",
        attention_weights.astype(jnp.bfloat16),
        split_heads(values),
        preferred_element_type=jnp.float32,
    )
    return (context.reshape(queries.shape).astype(jnp.bfloat16), attention_weights)


def attend_backward(queries, key_rows, values, attention_weights, grad_context):
    grad_heads = split_heads(grad_context)
    grad_values = jnp.einsum(
        "ghqk,gqhe->gkhe",
        attention_weights.astype(jnp.bfloat16),
        grad_heads,
        preferred_element_type=jnp.float32,
    )
    grad_weights = jnp.einsum(
        "gqhe,gkhe->ghqk", grad_heads, split_heads(values), preferred_element_type=jnp.float32
    )
    score_gradient = attention_weights * (
        grad_weights - jnp.sum(grad_weights * attention_weights, axis=-1, keepdims=True)
    )
    rounded = score_gradient.astype(jnp.bfloat16)
    grad_queries = jnp.einsum(
        "ghqk,gkhe->gqhe", rounded, split_heads(key_rows), preferred_element_type=jnp.float32
    )
    grad_keys = jnp.einsum(
        "ghqk,gqhe->gkhe", rounded, split_heads(queries), preferred_element_type=jnp.float32
    )
    return (
        grad_queries.reshape(queries.shape).astype(jnp.bfloat16),
        grad_keys.reshape(key_rows.shape).astype(jnp.bfloat16),
        grad_values.reshape(values.shape).astype(jnp.bfloat16),
        score_gradient,
    )


AXES = ("dp", "fsdp")


def rows_of(matrix):
    return matrix.reshape(-1, matrix.shape[-1])


def gather_all(shards):
    width = shards[0].shape[1]
    blocks = []
    for shard in shards:
        if shard.ndim == 1:
            continue
        blocks.append(shard.reshape(-1, width) if shard.shape[1] != width else shard)
    packed = lax.all_gather(jnp.concatenate(blocks, axis=0), AXES, axis=0)
    whole, at = [], 0
    devices = packed.shape[0]
    for shard, block in zip(shards, blocks):
        part = packed[:, at : at + block.shape[0]]
        at += block.shape[0]
        whole.append(part.reshape(devices * shard.shape[0], shard.shape[1]))
    gains = jnp.stack(shards[len(blocks) :])
    gains = lax.all_gather(gains, AXES, axis=1, tiled=True)
    return whole, [gains[k] for k in range(gains.shape[0])]


def scatter_all(grads, shards):
    width = shards[0].shape[1]
    devices = lax.axis_size(AXES)
    blocks = [grad.astype(jnp.bfloat16).reshape(devices, -1, width) for grad in grads]
    summed = lax.psum_scatter(
        jnp.concatenate(blocks, axis=1), AXES, scatter_dimension=0, tiled=False
    ).astype(jnp.float32)
    pieces, at = [], 0
    for block, shard in zip(blocks, shards):
        pieces.append(summed[at : at + block.shape[1]].reshape(shard.shape))
        at += block.shape[1]
    return pieces


def plain_body(decoder_in, memory, out_grad, lengths, *params):
    shards, bucket_bias_table = params[:13], params[13]
    matrices, gains = gather_all(shards)
    (
        self_query,
        self_key,
        self_value,
        self_out,
        cross_query,
        cross_key,
        cross_value,
        cross_out,
        ff_in,
        ff_out,
    ) = matrices
    norm_self, norm_cross, norm_ff = [gain.astype(jnp.float32) for gain in gains]
    micro, seqs, seq_length, width = decoder_in.shape
    groups = micro * seqs
    memory_bf = memory.reshape(groups, memory.shape[2], width)
    grad_bf = out_grad.reshape(groups, seq_length, width)
    group_lengths = lengths.reshape(groups)
    bucket_indicator = bucket_onehot(seq_length)
    relative_position_bias = jnp.einsum(
        "fsn,fe->esn",
        bucket_indicator,
        bucket_bias_table.astype(jnp.float32),
        precision=TOP_PRECISION,
    )
    positions = jnp.arange(seq_length, dtype=jnp.int32)
    causal = positions[:, None] >= positions[None, :]
    present = positions[None, :] < group_lengths[:, None]
    valid_rows = present[:, :, None].astype(jnp.float32)
    allowed = causal[None, None] & present[:, None, None, :]

    def grad_of(inputs, upstream):
        return weight_grad(rows_of(inputs), rows_of(upstream))

    decoded = decoder_in.reshape(groups, seq_length, width).astype(jnp.float32)
    normed = normalize(decoded, norm_self).astype(jnp.bfloat16)
    queries = project(normed, self_query).astype(jnp.bfloat16)
    key_rows = project(normed, self_key).astype(jnp.bfloat16)
    values = project(normed, self_value).astype(jnp.bfloat16)
    context, self_weights = attend_forward(
        queries, key_rows, values, relative_position_bias, allowed
    )
    after_self = decoded + project(context, self_out)
    normed_cross = normalize(after_self, norm_cross).astype(jnp.bfloat16)
    cross_queries = project(normed_cross, cross_query).astype(jnp.bfloat16)
    memory_keys = project(memory_bf, cross_key).astype(jnp.bfloat16)
    memory_values = project(memory_bf, cross_value).astype(jnp.bfloat16)
    cross_context, cross_weights = attend_forward(
        cross_queries, memory_keys, memory_values, 0.0, True
    )
    after_cross = after_self + project(cross_context, cross_out)
    normed_ff = normalize(after_cross, norm_ff).astype(jnp.bfloat16)
    hidden = project(normed_ff, ff_in)
    activated = jax.nn.gelu(hidden, approximate=True).astype(jnp.bfloat16)
    after_ff = after_cross + project(activated, ff_out)
    layer_out = (after_ff * valid_rows).astype(jnp.bfloat16)

    def back(operand, weight):
        return lax.dot_general(
            operand, weight, (((2,), (1,)), ((), ())), preferred_element_type=jnp.float32
        )

    grad_after = grad_bf.astype(jnp.float32) * valid_rows
    grad_branch = grad_after.astype(jnp.bfloat16)
    grad_ff_out = grad_of(activated, grad_branch)
    gelu_pull = jax.vjp(lambda pre_act: jax.nn.gelu(pre_act, approximate=True), hidden)[1]
    grad_hidden = gelu_pull(back(grad_branch, ff_out))[0].astype(jnp.bfloat16)
    grad_ff_in = grad_of(normed_ff, grad_hidden)
    norm_pull = jax.vjp(normalize, after_cross, norm_ff)[1]
    grad_rows, grad_norm_ff = norm_pull(back(grad_hidden, ff_in))
    grad_after = grad_after + grad_rows
    grad_branch = grad_after.astype(jnp.bfloat16)
    grad_cross_out = grad_of(cross_context, grad_branch)
    grad_context = back(grad_branch, cross_out).astype(jnp.bfloat16)
    grad_cross_rows, grad_memory_keys, grad_memory_values, unused = attend_backward(
        cross_queries, memory_keys, memory_values, cross_weights, grad_context
    )
    grad_cross_query = grad_of(normed_cross, grad_cross_rows)
    grad_cross_key = grad_of(memory_bf, grad_memory_keys)
    grad_cross_value = grad_of(memory_bf, grad_memory_values)
    grad_memory = back(grad_memory_keys, cross_key) + back(grad_memory_values, cross_value)
    norm_pull = jax.vjp(normalize, after_self, norm_cross)[1]
    grad_rows, grad_norm_cross = norm_pull(back(grad_cross_rows, cross_query))
    grad_after = grad_after + grad_rows
    grad_branch = grad_after.astype(jnp.bfloat16)
    grad_self_out = grad_of(context, grad_branch)
    grad_context = back(grad_branch, self_out).astype(jnp.bfloat16)
    grad_queries, grad_key_rows, grad_values, score_gradient = attend_backward(
        queries, key_rows, values, self_weights, grad_context
    )
    grad_self_query = grad_of(normed, grad_queries)
    grad_self_key = grad_of(normed, grad_key_rows)
    grad_self_value = grad_of(normed, grad_values)
    grad_normed = (
        back(grad_queries, self_query) + back(grad_key_rows, self_key) + back(grad_values, self_value)
    )
    norm_pull = jax.vjp(normalize, decoded, norm_self)[1]
    grad_rows, grad_norm_self = norm_pull(grad_normed)
    grad_input = grad_after + grad_rows
    bias_grad = jnp.einsum(
        "fgd,ogd->fo", bucket_indicator, jnp.sum(score_gradient, axis=0), precision=TOP_PRECISION
    )
    pieces = scatter_all(
        (
            grad_self_query,
            grad_self_key,
            grad_self_value,
            grad_self_out,
            grad_cross_query,
            grad_cross_key,
            grad_cross_value,
            grad_cross_out,
            grad_ff_in,
            grad_ff_out,
        ),
        shards[:10],
    )
    small = lax.psum(
        jnp.concatenate([grad_norm_self, grad_norm_cross, grad_norm_ff, bias_grad.reshape(-1)]),
        AXES,
    )
    mine = shards[10].shape[0]
    at = lax.axis_index(AXES) * mine
    gains_out = [
        lax.dynamic_slice_in_dim(small[k * width : (k + 1) * width], at, mine) for k in range(3)
    ]
    return (
        layer_out.reshape(decoder_in.shape),
        grad_input.reshape(decoder_in.shape),
        grad_memory.reshape(memory.shape),
        *pieces,
        *gains_out,
        small[3 * width :].reshape(bucket_bias_table.shape),
    )


MESH = pl.DeviceIdType.MESH
LOW = jnp.bfloat16
WIDE = jnp.float32
GROUPS = 16
WIDTH = 768
ROWS = 512
LENGTH = 256
MEMORY = 128
PAIRS = 6
CURVE = math.sqrt(2.0 / math.pi)


def place():
    dp, fsdp = lax.axis_index("dp"), lax.axis_index("fsdp")
    z, y, x, core = dp // 2, dp % 2, fsdp // 2, fsdp % 2
    sibling = (dp, x * 2 + 1 - core)
    over_x = (dp, (1 - x) * 2 + core)
    over_y = (z * 2 + 1 - y, fsdp)
    first = (jnp.where(core == 0, over_x[0], over_y[0]), jnp.where(core == 0, over_x[1], over_y[1]))
    second = (jnp.where(core == 0, over_y[0], over_x[0]), jnp.where(core == 0, over_y[1], over_x[1]))
    along_z = [(((z + k) % 4) * 2 + y, fsdp) for k in (1, 2, 3)]
    own = y * 2 + x
    beside = jnp.where(core == 0, y * 2 + 1 - x, (1 - y) * 2 + x)
    return z, own, beside, core, sibling, first, second, along_z


def greet(partners, meanwhile):
    barrier = pltpu.get_barrier_semaphore()
    for partner in partners:
        pl.semaphore_signal(barrier, inc=1, device_id=partner, device_id_type=MESH)
    meanwhile()
    pl.semaphore_wait(barrier, len(partners))


def half(core):
    return pl.ds(pl.multiple_of(core * 384, 128), 384)


def skew(ahead, groups=GROUPS):
    order = []
    for t in range(-max(ahead), groups + 8):
        for s in range(len(ahead)):
            g = t + ahead[s]
            if 0 <= g < groups:
                order.append((g, s))
    return order


def dot(a, b):
    return jnp.dot(a, b, preferred_element_type=WIDE)


def dot_nt(a, b):
    return lax.dot_general(a, b, (((1,), (1,)), ((), ())), preferred_element_type=WIDE)


def dot_tn(a, b):
    return lax.dot_general(a, b, (((0,), (0,)), ((), ())), preferred_element_type=WIDE)


def unit(w, u):
    return w[u].reshape(WIDTH, WIDTH)


def root_scale(value):
    return lax.rsqrt(jnp.mean(value * value, axis=-1, keepdims=True) + EPS)


def bucket_columns(flipped):
    j = lax.broadcasted_iota(jnp.int32, (BUCKETS, LENGTH), 1)
    row = lax.broadcasted_iota(jnp.int32, (BUCKETS, LENGTH), 0)
    n = jnp.where(j == 0, 0, LENGTH - j) if flipped else j
    half_count = BUCKETS // 2
    farther = jnp.zeros_like(n)
    for level in range(1, half_count):
        border = int(math.ceil(half_count * (MAX_DIST / half_count) ** (level / half_count)))
        farther = farther + (n >= border).astype(jnp.int32)
    bucket = jnp.where(n < half_count, n, half_count + farther)
    return (bucket == row).astype(WIDE)


QUEUE = (0, 1, 2, 3, 4, 5, 6, 7, 12, 13, 14, 15, 8, 9, 10, 11)
ZS = (3, 5, 7, 9, 11, 13, 15)
AHEAD = (9, 8, 6, 3, 1, 0)
GAIN_AT = (8, 11, 14)
BUDGET = 3.0
UNROLL = 1


def forward_kernel(*refs):
    shard_refs, gain_refs = refs[:9], refs[9:12]
    forward_steps(shard_refs, gain_refs, *refs[12:])


def forward_steps(
    shard_refs, gain_refs, tall_ref, x_hbm, mem_hbm, table_ref, lens_ref,
    w_out, gains_out, normed_out, q_out, k_out, v_out, ctx_out, p_out, after_self_out, ncross_out,
    cq_out, mk_out, mv_out, cctx_out, pc_out, after_cross_out, nff_out, act_out, slope_out, layer_out,
    w, gains, normed, q, k, v, ctx, p, after_self, ncross, cq, mk, mv, cctx, pc, after_cross, nff, act, slope, layer,
    x_ref, mem_ref, total, bias, small, sib, gain_in, ss, rs, ss0, rs0, out_sem, in_sem,
):
    z, own, beside, core, sibling, first, second, along_z = place()
    mine, other = half(core), half(1 - core)

    def along_at(zi):
        return (zi * 2 + lax.axis_index("dp") % 2, lax.axis_index("fsdp"))

    def view(g, zi, yx, cols):
        if g < 12:
            return w.at[g, slice(None) if zi is None else zi, yx, :, cols]
        return w.at[pl.ds(12, 4) if zi is None else 12 + zi, yx, g - 12, :, cols]

    def whole(g, cols):
        return w.at[g, :, :, :, cols] if g < 12 else w.at[pl.ds(12, 4), :, g - 12, :, cols]

    def send(ref, to, g, n):
        return pltpu.make_async_remote_copy(
            src_ref=ref, dst_ref=ref, send_sem=ss.at[g, n], recv_sem=rs.at[g, n], device_id=to, device_id_type=MESH)

    inner = (z == 1) | (z == 2)
    far = (z + 2) % 4
    end = along_at(jnp.where(z == 1, 0, 3))

    def z_send(g, block, n):
        yx, at = block
        return send(view(g, z, yx, mine), along_z[n], g, at + n)

    def z_hand_on(g, block):
        yx, at = block
        return send(view(g, far, yx, mine), end, g, 10 + (at > 0))

    def z_start(g, blocks):
        for block in blocks:
            z_send(g, block, 1).start()
            pl.when(z < 3)(lambda: z_send(g, block, 0).start())
            pl.when(z > 0)(lambda: z_send(g, block, 2).start())

    def z_relay(g, blocks):
        @pl.when(inner)
        def _():
            for block in blocks:
                z_send(g, block, 1).wait_recv()
                z_hand_on(g, block).start()

    def z_wait(g, blocks):
        for block in blocks:
            z_send(g, block, 1).wait_send()

            @pl.when(z < 3)
            def _():
                z_send(g, block, 0).wait_send()
                z_send(g, block, 2).wait_recv()

            @pl.when(z > 0)
            def _():
                z_send(g, block, 2).wait_send()
                z_send(g, block, 0).wait_recv()

            @pl.when(inner)
            def _():
                z_hand_on(g, block).wait_send()

            @pl.when(jnp.logical_not(inner))
            def _():
                z_send(g, block, 1).wait_recv()
                z_hand_on(g, block).wait_recv()

    one_block, two_blocks = [(own, 0)], [(own, 0), (beside, 7)]

    def step_b(g):
        return [send(view(g, None, own, mine), first, g, 3)]

    def step_c(g):
        return [send(view(g, None, own, mine), second, g, 4), send(view(g, None, beside, mine), second, g, 5)]

    def step_d(g):
        return [send(whole(g, mine), sibling, g, 6)]

    def step_b1(g):
        return [send(view(g, z, own, mine), first, g, 3)]

    def wait(copies):
        for copy in copies:
            copy.wait()

    def event(g, s, z_second):
        blocks = two_blocks if z_second else one_block
        if s == 0:
            start(step_b1(g)) if z_second else z_start(g, blocks)
        elif s == 1:
            if z_second:
                wait(step_b1(g))
                z_start(g, blocks)
            else:
                z_relay(g, blocks)
        elif s == 2:
            if z_second:
                z_relay(g, blocks)
            else:
                z_wait(g, blocks)
                start(step_b(g))
        elif s == 3:
            z_wait(g, blocks) if z_second else wait(step_b(g))
            start(step_c(g))
        elif s == 4:
            wait(step_c(g))
            start(step_d(g))
        else:
            wait(step_d(g))

    def gain_copies(s):
        to = ([sibling], along_z, [first], [second])[s]
        at = (0, 1, 4, 5)[s]
        return [
            pltpu.make_async_remote_copy(
                src_ref=gains, dst_ref=gain_in.at[at + n], send_sem=ss0.at[2 + at + n], recv_sem=rs0.at[2 + at + n],
                device_id=d, device_id_type=MESH)
            for n, d in enumerate(to)
        ]

    def start(copies):
        for copy in copies:
            copy.start()

    def gain_finish(s):
        for copy in gain_copies(s):
            copy.wait()
        for n in ((0,), (1, 2, 3), (4,), (5,))[s]:
            gains[...] += gain_in[n]

    stores = []

    def store(src, dst):
        copy = pltpu.make_async_copy(src, dst, out_sem.at[len(stores)])
        stores.append(copy)
        copy.start()

    def store_unit(g):
        if g < 12:
            store(w.at[g], w_out.at[g])
        elif g == 15:
            store(w.at[pl.ds(12, 4)], w_out.at[pl.ds(12, 4)])

    def gain(n):
        return gains[n : n + 1, :].astype(WIDE)

    def scale_rows(src, n, dst):
        g = gain(n)

        def chunk(i, c):
            rows = pl.ds(pl.multiple_of(i * 128, 128), 128)
            value = src[rows, :].astype(WIDE)
            dst[rows, :] = (value * root_scale(value) * g).astype(LOW)
            return c

        lax.fori_loop(0, ROWS // 128, chunk, 0)

    def make_bias():
        by_distance = dot(table_ref[...], bucket_columns(True).astype(LOW))
        for h in range(HEADS):
            row = jnp.broadcast_to(by_distance[h : h + 1, :], (LENGTH, LENGTH))
            bias[h] = pltpu.roll(row, 0, 1, stride=1, stride_axis=0)

    def project_into(src, u, dst):
        dst[...] = dot(src[...], unit(w, u)).astype(LOW)

    lane = lax.broadcasted_iota(jnp.int32, (1, 128), 1)
    sides = [lane < 64, lane >= 64]

    def attend(i, queries, keys, vals, keep_p, into, depth, masked):
        s, pair = i // PAIRS, i % PAIRS
        rows = pl.ds(pl.multiple_of(s * LENGTH, LENGTH), LENGTH)
        deep = pl.ds(pl.multiple_of(s * depth, depth), depth)
        cols = pl.ds(pl.multiple_of(pair * 128, 128), 128)
        qp, kp, vp = queries[rows, cols], keys[deep, cols], vals[deep, cols]
        parts = []
        for side in range(2):
            scores = dot_nt(jnp.where(sides[side], qp, jnp.zeros_like(qp)), kp)
            if masked:
                t = lax.broadcasted_iota(jnp.int32, (LENGTH, LENGTH), 0)
                u = lax.broadcasted_iota(jnp.int32, (LENGTH, LENGTH), 1)
                allowed = (u <= t) & (u < lens_ref[s])
                scores = jnp.where(allowed, scores + bias[2 * pair + side], MASKED)
            e = jnp.exp(scores - jnp.max(scores, axis=-1, keepdims=True))
            weights = (e * (1.0 / jnp.sum(e, axis=-1, keepdims=True))).astype(LOW)
            keep_p[rows, pl.ds(pl.multiple_of((2 * pair + side) * depth, 128), depth)] = weights
            parts.append(dot(weights, vp))
        into[rows, cols] = jnp.where(sides[0], parts[0], parts[1]).astype(LOW)

    def self_part(lo, hi):
        def it(i, c):
            attend(i, q, k, v, p, ctx, LENGTH, True)
            return c

        lax.fori_loop(lo, hi, it, 0, unroll=UNROLL)

    def cross_part(lo, hi):
        def it(i, c):
            attend(i, cq, mk, mv, pc, cctx, MEMORY, False)
            return c

        lax.fori_loop(lo, hi, it, 0, unroll=UNROLL)

    def after_self_part():
        after_self[...] = x_ref[...].astype(WIDE) + dot(ctx[...], unit(w, 3))
        scale_rows(after_self, 1, ncross)

    def after_cross_part():
        after_cross[...] = after_self[...] + dot(cctx[...], unit(w, 7))
        scale_rows(after_cross, 2, nff)

    def hidden_part(j):
        cols = slice(j * WIDTH, (j + 1) * WIDTH)
        for m in range(2):
            rows = slice(m * 256, m * 256 + 256)
            a = dot(nff[rows, :], unit(w, 8 + j))
            sq = a * a
            th = jnp.tanh(a * (CURVE + (CURVE * 0.044715) * sq))
            act[rows, cols] = (0.5 * a * (1.0 + th)).astype(LOW)
            slope[rows, cols] = (
                0.5 * (1.0 + th) + 0.5 * a * (1.0 - th * th) * (CURVE + (3.0 * CURVE * 0.044715) * sq)
            ).astype(LOW)
        store(act.at[:, pl.ds(j * WIDTH, WIDTH)], act_out.at[:, pl.ds(j * WIDTH, WIDTH)])
        store(slope.at[:, pl.ds(j * WIDTH, WIDTH)], slope_out.at[:, pl.ds(j * WIDTH, WIDTH)])
        part = dot(act[:, cols], unit(w, 12 + j))
        if j == 0:
            total[...] = after_cross[...] + part
        elif j < 3:
            total[...] += part
        else:
            part = total[...] + part
            for s in range(2):
                rows = slice(s * LENGTH, (s + 1) * LENGTH)
                t = lax.broadcasted_iota(jnp.int32, (LENGTH, 1), 0)
                layer[rows, :] = (part[rows] * (t < lens_ref[s]).astype(WIDE)).astype(LOW)

    pieces = [
        (0, 1.0, lambda: project_into(normed, 0, q)), (0, 0.1, lambda: store(q, q_out)),
        (1, 1.0, lambda: project_into(normed, 1, k)), (1, 0.1, lambda: store(k, k_out)),
        (2, 1.0, lambda: project_into(normed, 2, v)), (2, 0.1, lambda: store(v, v_out)),
        (2, 2.5, lambda: self_part(0, 3)), (2, 2.5, lambda: self_part(3, 6)),
        (2, 2.5, lambda: self_part(6, 9)), (2, 2.5, lambda: self_part(9, 12)),
        (2, 0.1, lambda: store(ctx, ctx_out)), (2, 0.1, lambda: store(p, p_out)),
        (3, 2.0, after_self_part), (3, 0.1, lambda: store(after_self, after_self_out)), (3, 0.1, lambda: store(ncross, ncross_out)),
        (4, 1.0, lambda: project_into(ncross, 4, cq)), (4, 0.1, lambda: store(cq, cq_out)),
        (5, 0.6, lambda: project_into(mem_ref, 5, mk)), (5, 0.1, lambda: store(mk, mk_out)),
        (6, 0.6, lambda: project_into(mem_ref, 6, mv)), (6, 0.1, lambda: store(mv, mv_out)),
        (6, 2.5, lambda: cross_part(0, 4)), (6, 2.5, lambda: cross_part(4, 8)), (6, 2.5, lambda: cross_part(8, 12)),
        (6, 0.1, lambda: store(cctx, cctx_out)), (6, 0.1, lambda: store(pc, pc_out)),
        (7, 2.0, after_cross_part), (7, 0.1, lambda: store(after_cross, after_cross_out)), (7, 0.1, lambda: store(nff, nff_out)),
        (8, 3.0, lambda: hidden_part(0)), (9, 3.0, lambda: hidden_part(1)), (10, 3.0, lambda: hidden_part(2)),
        (11, 3.0, lambda: hidden_part(3)), (11, 0.1, lambda: store(layer, layer_out)),
    ]

    load_x = pltpu.make_async_copy(x_hbm, x_ref, in_sem.at[0])
    load_mem = pltpu.make_async_copy(mem_hbm, mem_ref, in_sem.at[1])

    def prepare():
        load_x.start()
        load_mem.start()
        for u in range(12):
            rows = shard_refs[u][...] if u < 8 else shard_refs[8][:, WIDTH * (u - 8) : WIDTH * (u - 7)]
            rows = rows.astype(WIDE)
            none = jnp.zeros_like(rows)
            small[u] = jnp.concatenate(
                [jnp.where(core == 0, rows, none), jnp.where(core == 0, none, rows)], axis=0).astype(LOW)
        offset = (lax.axis_index("dp") * 4 + lax.axis_index("fsdp")) * 24
        spot = (lax.broadcasted_iota(jnp.int32, (24, WIDTH), 1) == lax.broadcasted_iota(jnp.int32, (24, WIDTH), 0) + offset)
        placed = [dot(ref[...], spot.astype(LOW)) for ref in gain_refs]
        gains[...] = jnp.concatenate(placed + [jnp.zeros((13, WIDTH), WIDE)], axis=0).astype(LOW)

    greet([sibling, first, second] + along_z, prepare)
    swap_small = pltpu.make_async_remote_copy(
        src_ref=small.at[:, :, other], dst_ref=sib, send_sem=ss0.at[0], recv_sem=rs0.at[0],
        device_id=sibling, device_id_type=MESH)

    def tall_view(cols):
        return w.at[12 + z, own, pl.ds(2 * core, 2), :, cols]

    swap_tall = pltpu.make_async_remote_copy(
        src_ref=tall_ref.at[:, :, other], dst_ref=tall_view(other), send_sem=ss0.at[1], recv_sem=rs0.at[1],
        device_id=sibling, device_id_type=MESH)
    swap_small.start()
    swap_tall.start()
    start(gain_copies(0))
    w[12 + z, own, pl.ds(2 * core, 2), :, mine] = tall_ref[:, :, mine]
    swap_small.wait()

    def assemble(u):
        w[u, z, own, :, mine] = small[u, :, mine] + sib[u]

    early = skew(AHEAD)[:2]
    assert all(s == 0 and QUEUE[at] < 12 for at, s in early)
    for at, s in early:
        assemble(QUEUE[at])
        event(QUEUE[at], 0, at in ZS)
    for u in range(12):
        if u not in [QUEUE[at] for at, s in early]:
            assemble(u)
    gain_finish(0)
    start(gain_copies(1))
    swap_tall.wait()
    make_bias()
    load_x.wait()
    load_mem.wait()

    stage, done = 1, 0
    for n, (at, s) in enumerate(skew(AHEAD)):
        g = QUEUE[at]
        if n >= 2:
            event(g, s, at in ZS)
        if n in GAIN_AT:
            gain_finish(stage)
            stage += 1
            if stage < 4:
                start(gain_copies(stage))
            else:
                scale_rows(x_ref, 0, normed)
                store(normed, normed_out)
                store(gains, gains_out)
        if s == 5:
            store_unit(g)
            spent = 0.0
            while done < len(pieces) and QUEUE.index(pieces[done][0]) <= at and (spent < BUDGET or at == GROUPS - 1):
                spent += pieces[done][1]
                pieces[done][2]()
                done += 1
    assert done == len(pieces) and stage == 4
    for copy in stores:
        copy.wait()


FORWARD_OUT = (
    ((16, 4, 4, 48, 768), LOW),
    ((16, 768), LOW),
    ((512, 768), LOW), ((512, 768), LOW), ((512, 768), LOW), ((512, 768), LOW),
    ((512, 768), LOW),
    ((512, 3072), LOW),
    ((512, 768), WIDE),
    ((512, 768), LOW),
    ((512, 768), LOW), ((256, 768), LOW), ((256, 768), LOW), ((512, 768), LOW),
    ((512, 1536), LOW),
    ((512, 768), WIDE),
    ((512, 768), LOW),
    ((512, 3072), LOW), ((512, 3072), LOW),
    ((512, 768), LOW),
)


def forward_call(*operands):
    return pl.pallas_call(
        forward_kernel,
        out_shape=tuple(jax.ShapeDtypeStruct(s, t) for s, t in FORWARD_OUT),
        in_specs=[pl.BlockSpec(memory_space=pltpu.VMEM)] * 13
        + [pl.BlockSpec(memory_space=pl.ANY)] * 2
        + [pl.BlockSpec(memory_space=pltpu.VMEM), pl.BlockSpec(memory_space=pltpu.SMEM)],
        out_specs=[pl.BlockSpec(memory_space=pl.ANY)] * len(FORWARD_OUT),
        scratch_shapes=[pltpu.VMEM(s, t) for s, t in FORWARD_OUT]
        + [
            pltpu.VMEM((ROWS, WIDTH), LOW),
            pltpu.VMEM((2 * MEMORY, WIDTH), LOW),
            pltpu.VMEM((ROWS, WIDTH), WIDE),
            pltpu.VMEM((HEADS, LENGTH, LENGTH), WIDE),
            pltpu.VMEM((12, 48, 768), LOW),
            pltpu.VMEM((12, 48, 384), LOW),
            pltpu.VMEM((6, 16, 768), LOW),
            pltpu.SemaphoreType.DMA((GROUPS, 12)),
            pltpu.SemaphoreType.DMA((GROUPS, 12)),
            pltpu.SemaphoreType.DMA((8,)),
            pltpu.SemaphoreType.DMA((8,)),
            pltpu.SemaphoreType.DMA((40,)),
            pltpu.SemaphoreType.DMA((2,)),
        ],
        compiler_params=pltpu.CompilerParams(collective_id=0, has_side_effects=True, vmem_limit_bytes=60 * 2**20),
    )(*operands)


def forward(shards, decoder_in, memory, table, lengths):
    return forward_call(
        *shards[:9],
        *[shard.reshape(1, 24) for shard in shards[10:13]],
        shards[9].reshape(2, 48, WIDTH),
        decoder_in.reshape(ROWS, WIDTH),
        memory.reshape(2 * MEMORY, WIDTH),
        table.T,
        lengths.reshape(2),
    )


LINE = (12, 13, 14, 15, 8, 9, 10, 11, 7, 4, 5, 6, 3, 0, 1, 2)
USED = (12, 8, 13, 9, 14, 10, 15, 11, 7, 5, 6, 4, 3, 0, 1, 2)
SLOTS = 6
LAGS = (0, 1, 4, 6, 7, 9, 10)
PACE = 3.5
FIRST_Z = ()


def backward_kernel(
    gains, lens_ref, w_hbm, act_hbm, slope_hbm, nff_hbm, after_cross_hbm, cctx_hbm, ncross_hbm, cq_hbm, mk_hbm, mv_hbm,
    mem_hbm, pc_hbm, after_self_hbm, p_hbm, normed_hbm, q_hbm, k_hbm, v_hbm, ctx_hbm, x_hbm, og_hbm,
    input_out, memory_out, *rest,
):
    pieces_out, rest = rest[:8], rest[8:]
    (
        in_piece_out, out_piece_out, sum_out,
        ring, act, slope, nff, aft, cctx, ncross, cq, mk, mv, mem, pc, x, gl, total, up, ghj, low, gctx, dq, dk, dv,
        dist, grad, r0, r1, r23, zsum, fa, fo, fa_in, fo_in, acc, acc_in, ss, rs, ss0, rs0, in_sem, ring_sem, out_sem,
    ) = rest
    z, own, beside, core, sibling, first, second, along_z = place()
    mine, other = half(core), half(1 - core)
    diag, across = 3 - own, 3 - beside

    fetches = {}

    def fetch(name, src, dst):
        copy = pltpu.make_async_copy(src, dst, in_sem.at[len(fetches)])
        fetches[name] = copy
        copy.start()

    def fetched(*names):
        for name in names:
            fetches[name].wait()

    def weight_copy(n):
        return pltpu.make_async_copy(w_hbm.at[USED[n]], ring.at[n % SLOTS], ring_sem.at[n])

    asked, got = [0], [0]

    def ask(n):
        while asked[0] < min(n, GROUPS):
            weight_copy(asked[0]).start()
            asked[0] += 1

    def weight(u):
        n = USED.index(u)
        while got[0] <= n:
            weight_copy(got[0]).wait()
            got[0] += 1
        return ring[n % SLOTS].reshape(WIDTH, WIDTH)

    def send(src, dst, to, g, n):
        return pltpu.make_async_remote_copy(
            src_ref=src, dst_ref=dst, send_sem=ss.at[g, n], recv_sem=rs.at[g, n], device_id=to, device_id_type=MESH)

    def block(g, cols):
        return grad.at[LINE.index(g) % 4, :, :, :, cols]

    def swap(g):
        return [send(block(g, other), r0.at[g], sibling, g, 0)]

    def quarter(ref, g, yx):
        return ref.at[g, :, yx] if g < 12 else ref.at[g, yx]

    def share(g, zi, yx):
        return r0.at[g, zi, yx] if g < 12 else r0.at[12 + zi, yx, g - 12]

    def over_second(g):
        return [
            send(quarter(r0, g, across), r1.at[g, 0], second, g, 1),
            send(quarter(r0, g, diag), r1.at[g, 1], second, g, 2),
        ]

    def over_first(g):
        return [send(quarter(r0, g, beside), r23.at[g, pl.ds(0, 4)], first, g, 3)]

    def over_first1(g):
        return [send(r0.at[g, z, beside], r23.at[g, 0], first, g, 3)]

    inner = (z == 1) | (z == 2)
    far = (z + 2) % 4
    next_in = (jnp.where(z == 0, 1, 2) * 2 + lax.axis_index("dp") % 2, lax.axis_index("fsdp"))

    def z_send(g, block, n):
        yx, at, sem = block
        return send(share(g, (z + n + 1) % 4, yx), r23.at[g, at + n], along_z[n], g, sem + n)

    def z_hand_over(g, block, slot):
        return send(share(g, 3 - z, block[0]), r23.at[g, 7 + slot], next_in, g, 11 + slot)

    def z_start(g, blocks):
        for slot, block in enumerate(blocks):

            @pl.when(jnp.logical_not(inner))
            def _():
                z_hand_over(g, block, slot).start()
                z_send(g, block, 1).start()

            pl.when(z < 3)(lambda: z_send(g, block, 0).start())
            pl.when(z > 0)(lambda: z_send(g, block, 2).start())

    def z_relay(g, blocks):
        @pl.when(inner)
        def _():
            for slot, block in enumerate(blocks):
                z_hand_over(g, block, slot).wait_recv()
                both = share(g, far, block[0])[...].astype(WIDE) + r23[g, 7 + slot].astype(WIDE)
                share(g, far, block[0])[...] = both.astype(LOW)
                z_send(g, block, 1).start()

    def z_wait(g, blocks):
        for slot, block in enumerate(blocks):
            yx, at, sem = block
            z_send(g, block, 1).wait()
            pl.when(jnp.logical_not(inner))(lambda: z_hand_over(g, block, slot).wait_send())
            zsum[slot] = share(g, z, yx)[...].astype(WIDE) + r23[g, at + 1].astype(WIDE)

            @pl.when(z > 0)
            def _():
                z_send(g, block, 2).wait_send()
                z_send(g, block, 0).wait_recv()
                zsum[slot] += r23[g, at].astype(WIDE)

            @pl.when(z < 3)
            def _():
                z_send(g, block, 0).wait_send()
                z_send(g, block, 2).wait_recv()
                zsum[slot] += r23[g, at + 2].astype(WIDE)

    one_block, two_blocks = [(own, 4, 4)], [(own, 4, 4), (beside, 1, 7)]

    def last(g):
        if g < 12:
            rows = pl.ds(pl.multiple_of(24 * (1 - core), 8), 24)
            return [send(fa.at[g, rows], fa_in.at[g], sibling, g, 10)]
        if g == 15:
            return [send(fo.at[pl.ds(2 * (1 - core), 2)], fo_in, sibling, g, 10)]
        return []

    def add0(g):
        r0[g] += block(g, mine)[...]

    def add1(g):
        quarter(r0, g, own)[...] += r1[g, 0]
        quarter(r0, g, beside)[...] += r1[g, 1]

    def finish(g, value):
        if g < 12:
            fa[g] = value
        else:
            fo[g - 12] = value

    def add2(g):
        quarter(r0, g, own)[...] += r23[g, 0:4]

    def add3z(g):
        finish(g, r0[g, z, own].astype(WIDE) + r23[g, 0].astype(WIDE))

    def write(g):
        rows = pl.ds(pl.multiple_of(24 * core, 8), 24)
        if g < 8:
            pieces_out[g][:, mine] = fa[g, rows]
            pieces_out[g][:, other] = fa_in[g]
        elif g < 12:
            at = WIDTH * (g - 8)
            in_piece_out[:, pl.ds(pl.multiple_of(at + core * 384, 128), 384)] = fa[g, rows]
            in_piece_out[:, pl.ds(pl.multiple_of(at + 384 - core * 384, 128), 384)] = fa_in[g]
        elif g == 15:
            out_piece_out[:, mine] = fo[pl.ds(2 * core, 2)].reshape(96, 384)
            out_piece_out[:, other] = fo_in[...].reshape(96, 384)

    def start(copies):
        for copy in copies:
            copy.start()

    def wait(copies):
        for copy in copies:
            copy.wait()

    def along_z_after(g):
        return [g] if g < 12 else [12, 13, 14, 15] if g == 15 else []

    def event(g, s):
        z_second = g in FIRST_Z
        blocks = two_blocks if z_second else one_block
        if s == 0:
            start(swap(g))
        elif s == 1:
            wait(swap(g))
            add0(g)
            start(over_second(g))
        elif s == 2:
            wait(over_second(g))
            add1(g)
            z_start(g, blocks) if z_second else start(over_first(g))
        elif s == 3:
            if z_second:
                z_relay(g, blocks)
            else:
                wait(over_first(g))
                add2(g)
                for one in along_z_after(g):
                    z_start(one, blocks)
        elif s == 4:
            if z_second:
                z_wait(g, blocks)
                r0[g, z, own] = zsum[0].astype(LOW)
                r0[g, z, beside] = zsum[1].astype(LOW)
                start(over_first1(g))
            else:
                for one in along_z_after(g):
                    z_relay(one, blocks)
        elif s == 5:
            if z_second:
                wait(over_first1(g))
                add3z(g)
            else:
                for one in along_z_after(g):
                    z_wait(one, blocks)
                    finish(one, zsum[0])
            start(last(g))
        else:
            wait(last(g))
            write(g)

    def acc_copies(s):
        to = ([sibling], along_z, [first], [second])[s]
        at = (0, 1, 4, 5)[s]
        return [
            pltpu.make_async_remote_copy(
                src_ref=acc, dst_ref=acc_in.at[at + n], send_sem=ss0.at[at + n], recv_sem=rs0.at[at + n],
                device_id=d, device_id_type=MESH)
            for n, d in enumerate(to)
        ]

    lane = lax.broadcasted_iota(jnp.int32, (1, 128), 1)
    sides = [lane < 64, lane >= 64]

    def keep(g, value):
        grad[LINE.index(g) % 4] = value.astype(LOW).reshape(4, 4, 48, WIDTH)

    def begin():
        fetched("og")
        for s in range(2):
            rows = slice(s * LENGTH, (s + 1) * LENGTH)
            t = lax.broadcasted_iota(jnp.int32, (LENGTH, 1), 0)
            gl[rows, :] = jnp.where(t < lens_ref[s], gl[rows, :].astype(WIDE), 0.0).astype(LOW)
        fetched("act")

    def out_grad_part(j):
        grad[j] = dot_tn(act[:, j * WIDTH : (j + 1) * WIDTH], gl[...]).astype(LOW).reshape(4, 4, 48, WIDTH)

    def hidden_part(j):
        if j == 0:
            fetched("slope", "nff")
        cols = slice(j * WIDTH, (j + 1) * WIDTH)
        ghj[...] = (dot_nt(gl[...], weight(12 + j)) * slope[:, cols].astype(WIDE)).astype(LOW)
        keep(8 + j, dot_tn(nff[...], ghj[...]))

    def hidden_back(j):
        part = dot_nt(ghj[...], weight(8 + j))
        if j:
            up[...] += part
        else:
            up[...] = part

    def norm_back(value_ref, base_ref, n):
        g = gains[n : n + 1, :].astype(WIDE)

        def chunk(i, carried):
            rows = pl.ds(pl.multiple_of(i * 128, 128), 128)
            value = value_ref[rows, :].astype(WIDE)
            r = root_scale(value)
            unit_rows = value * r
            upstream = up[rows, :]
            weighted = upstream * g
            inner = jnp.mean(weighted * unit_rows, axis=-1, keepdims=True)
            new = base_ref[rows, :].astype(WIDE) + r * (weighted - unit_rows * inner)
            total[rows, :] = new
            low[rows, :] = new.astype(LOW)
            return carried + jnp.sum(upstream * unit_rows, axis=0, keepdims=True)

        acc[n : n + 1, 0:WIDTH] = lax.fori_loop(0, ROWS // 128, chunk, jnp.zeros((1, WIDTH), WIDE))

    def ff_norm_part():
        fetched("after_cross")
        norm_back(aft, gl, 2)
        fetch("p", p_hbm, act)
        fetch("normed", normed_hbm, slope.at[:, 0:768])
        fetch("q", q_hbm, slope.at[:, 768:1536])
        fetch("k", k_hbm, slope.at[:, 1536:2304])
        fetch("v", v_hbm, slope.at[:, 2304:3072])
        fetch("ctx", ctx_hbm, nff)
        fetch("after_self", after_self_hbm, aft)

    def cross_out_part():
        fetched("cctx")
        keep(7, dot_tn(cctx[...], low[...]))
        gctx[...] = dot_nt(low[...], weight(7)).astype(LOW)
        fetched("cq", "mk", "mv", "pc")

    def head_back(weights, gp, qp, kp, vp, side):
        p32 = weights.astype(WIDE)
        pull = dot_nt(jnp.where(sides[side], gp, jnp.zeros_like(gp)), vp)
        slant = p32 * (pull - jnp.sum(pull * p32, axis=-1, keepdims=True))
        rounded = slant.astype(LOW)
        return dot(rounded, kp), dot_tn(rounded, qp), dot_tn(weights, gp), slant

    def joined(low_part, high_part):
        return jnp.where(sides[0], low_part, high_part).astype(LOW)

    def cross_part(lo, hi):
        def it(i, c):
            s, pair = i // PAIRS, i % PAIRS
            rows = pl.ds(pl.multiple_of(s * LENGTH, LENGTH), LENGTH)
            deep = pl.ds(pl.multiple_of(s * MEMORY, MEMORY), MEMORY)
            cols = pl.ds(pl.multiple_of(pair * 128, 128), 128)
            gp, qp, kp, vp = gctx[rows, cols], cq[rows, cols], mk[deep, cols], mv[deep, cols]
            one, two = [
                head_back(pc[rows, pl.ds(pl.multiple_of((2 * pair + side) * MEMORY, 128), MEMORY)], gp, qp, kp, vp, side)
                for side in range(2)
            ]
            dq[rows, cols] = joined(one[0], two[0])
            dk[deep, cols] = joined(one[1], two[1])
            dv[deep, cols] = joined(one[2], two[2])
            return c

        lax.fori_loop(lo, hi, it, 0, unroll=UNROLL)

    def cross_query_part():
        fetched("ncross")
        keep(4, dot_tn(ncross[...], dq[...]))

    def cross_key_part():
        fetched("mem")
        keep(5, dot_tn(mem[...], dk[0:256, :]))

    def cross_value_part():
        keep(6, dot_tn(mem[...], dv[0:256, :]))

    def cross_norm_part():
        up[0:256, :] = dot_nt(dk[0:256, :], weight(5)) + dot_nt(dv[0:256, :], weight(6))
        copy = pltpu.make_async_copy(up.at[pl.ds(0, 256)], memory_out, out_sem.at[0])
        copy.start()
        copy.wait()
        up[...] = dot_nt(dq[...], weight(4))
        fetched("after_self")
        norm_back(aft, total, 1)

    def self_out_part():
        fetched("ctx")
        keep(3, dot_tn(nff[...], low[...]))
        gctx[...] = dot_nt(low[...], weight(3)).astype(LOW)
        fetched("p", "q", "k", "v")

    def self_part(lo, hi):
        def it(pair, c):
            cols = pl.ds(pl.multiple_of(pair * 128, 128), 128)
            q_cols = pl.ds(pl.multiple_of(768 + pair * 128, 128), 128)
            k_cols = pl.ds(pl.multiple_of(1536 + pair * 128, 128), 128)
            v_cols = pl.ds(pl.multiple_of(2304 + pair * 128, 128), 128)
            slants = []
            for s in range(2):
                rows = slice(s * LENGTH, (s + 1) * LENGTH)
                gp, qp, kp, vp = gctx[rows, cols], slope[rows, q_cols], slope[rows, k_cols], slope[rows, v_cols]
                one, two = [
                    head_back(act[rows, pl.ds(pl.multiple_of((2 * pair + side) * LENGTH, 256), LENGTH)], gp, qp, kp, vp, side)
                    for side in range(2)
                ]
                dq[rows, cols] = joined(one[0], two[0])
                dk[rows, cols] = joined(one[1], two[1])
                dv[rows, cols] = joined(one[2], two[2])
                slants.append((one[3], two[3]))
            t = lax.broadcasted_iota(jnp.int32, (LENGTH, LENGTH), 0)
            u = lax.broadcasted_iota(jnp.int32, (LENGTH, LENGTH), 1)
            upside = (t + u == LENGTH - 1).astype(LOW)
            for side in range(2):
                both = slants[0][side] + slants[1][side]
                coarse = both.astype(LOW)
                fine = (both - coarse.astype(WIDE)).astype(LOW)
                turned = dot(upside, coarse) + dot(upside, fine)
                rolled = pltpu.roll(turned, 1, 1, stride=1, stride_axis=0)
                dist[pl.ds(2 * pair + side, 1), :] = jnp.sum(rolled, axis=0, keepdims=True)
            return c

        lax.fori_loop(lo, hi, it, 0, unroll=UNROLL)

    def self_grads(n):
        fetched(*(["normed"] if n == 0 else []))
        keep(n, dot_tn(slope[:, 0:768], (dq, dk, dv)[n][...]))

    def input_part():
        up[...] = dot_nt(dq[...], weight(0)) + dot_nt(dk[...], weight(1)) + dot_nt(dv[...], weight(2))
        fetched("x")
        norm_back(x, total, 0)
        pltpu.make_async_copy(total, input_out, out_sem.at[1]).start()
        buckets = lax.dot_general(
            dist[...], bucket_columns(True), (((1,), (1,)), ((), ())),
            precision=lax.Precision.HIGHEST, preferred_element_type=WIDE)
        acc[:, WIDTH : WIDTH + BUCKETS] = buckets
        for copy in acc_copies(0):
            copy.start()

    pieces = [(0.5, begin, None, 6)]
    pieces += [(1.0, functools.partial(out_grad_part, j), 12 + j, 6) for j in range(4)]
    for j in range(4):
        pieces += [(2.0, functools.partial(hidden_part, j), 8 + j, 0), (1.0, functools.partial(hidden_back, j), None, 8 + 2 * j)]
    pieces += [
        (1.5, ff_norm_part, None, 0), (1.9, cross_out_part, 7, 15),
        (2.5, lambda: cross_part(0, 4), None, 0), (2.5, lambda: cross_part(4, 8), None, 0), (2.5, lambda: cross_part(8, 12), None, 0),
        (1.0, cross_query_part, 4, 0), (0.5, cross_key_part, 5, 0), (0.5, cross_value_part, 6, 0),
        (4.0, cross_norm_part, None, 16), (2.0, self_out_part, 3, 0),
        (4.0, lambda: self_part(0, 2), None, 0), (4.0, lambda: self_part(2, 4), None, 0), (4.0, lambda: self_part(4, 6), None, 0),
        (1.0, lambda: self_grads(0), 0, 0), (1.0, lambda: self_grads(1), 1, 0), (1.0, lambda: self_grads(2), 2, 0),
        (4.5, input_part, None, 0),
    ]

    acc[...] = jnp.zeros_like(acc)
    dist[...] = jnp.zeros_like(dist)
    fetch("og", og_hbm, gl)
    fetch("act", act_hbm, act)
    ask(2)
    fetch("slope", slope_hbm, slope)
    fetch("nff", nff_hbm, nff)
    fetch("after_cross", after_cross_hbm, aft)
    fetch("cctx", cctx_hbm, cctx)
    fetch("cq", cq_hbm, cq)
    fetch("mk", mk_hbm, mk)
    fetch("mv", mv_hbm, mv)
    fetch("pc", pc_hbm, pc)
    fetch("ncross", ncross_hbm, ncross)
    fetch("mem", mem_hbm, mem)
    fetch("x", x_hbm, x)
    clock, done, made, freed = 0.0, 0, set(), set()

    def run_piece():
        nonlocal clock, done
        cost, what, makes, asks = pieces[done]
        what()
        ask(asks)
        clock += cost
        made.add(makes)
        done += 1

    def may_run():
        makes = pieces[done][2]
        i = 0 if makes is None else LINE.index(makes)
        return i < 4 or LINE[i - 4] in freed

    def out_grads():
        while LINE[0] not in made:
            run_piece()

    greet([sibling, first, second] + along_z, out_grads)

    stage = None
    for r in range(GROUPS + LAGS[-1]):
        for s in range(1, 7):
            i = r - LAGS[s]
            if 0 <= i < GROUPS:
                event(LINE[i], s)
                if s == 1:
                    freed.add(LINE[i])
        if r < GROUPS:
            while LINE[r] not in made:
                assert may_run()
                run_piece()
            event(LINE[r], 0)
        while done < len(pieces) and clock < PACE * (r + 1) and may_run():
            run_piece()
        if done == len(pieces):
            if stage is None:
                stage = 0
            elif stage < 4:
                for copy in acc_copies(stage):
                    copy.wait()
                for n in ((0,), (1, 2, 3), (4,), (5,))[stage]:
                    acc[...] += acc_in[n]
                stage += 1
                if stage < 4:
                    for copy in acc_copies(stage):
                        copy.start()
    assert done == len(pieces) and stage == 4 and got[0] == GROUPS
    offset = (lax.axis_index("dp") * 4 + lax.axis_index("fsdp")) * 24
    sum_out[:, 0:WIDTH] = pltpu.roll(acc[:, 0:WIDTH], WIDTH - offset, 1)
    sum_out[:, WIDTH:] = acc[:, WIDTH:]
    pltpu.make_async_copy(total, input_out, out_sem.at[1]).wait()


BACKWARD_OUT = (
    (((512, 768), WIDE), ((256, 768), WIDE)),
    (((24, 768), WIDE),) * 8 + (((24, 3072), WIDE), ((96, 768), WIDE), ((16, 896), WIDE)),
)


def backward_call(gains, lens, *arrays):
    shape = lambda s: jax.ShapeDtypeStruct(*s)
    vmem = lambda *s: pltpu.VMEM(s, LOW)
    return pl.pallas_call(
        backward_kernel,
        out_shape=tuple(shape(s) for s in BACKWARD_OUT[0] + BACKWARD_OUT[1]),
        in_specs=[pl.BlockSpec(memory_space=pltpu.VMEM), pl.BlockSpec(memory_space=pltpu.SMEM)]
        + [pl.BlockSpec(memory_space=pl.ANY)] * len(arrays),
        out_specs=[pl.BlockSpec(memory_space=pl.ANY)] * 2 + [pl.BlockSpec(memory_space=pltpu.VMEM)] * 11,
        scratch_shapes=[
            vmem(SLOTS, 4, 4, 48, 768),
            vmem(512, 3072), vmem(512, 3072), vmem(512, 768),
            pltpu.VMEM((512, 768), WIDE),
            vmem(512, 768), vmem(512, 768), vmem(512, 768), vmem(256, 768), vmem(256, 768), vmem(256, 768),
            vmem(512, 1536),
            vmem(512, 768), vmem(512, 768),
            pltpu.VMEM((512, 768), WIDE), pltpu.VMEM((512, 768), WIDE),
            vmem(512, 768), vmem(512, 768), vmem(512, 768),
            vmem(512, 768), vmem(512, 768), vmem(512, 768),
            pltpu.VMEM((16, LENGTH), WIDE),
            vmem(4, 4, 4, 48, 768),
            vmem(GROUPS, 4, 4, 48, 384), vmem(GROUPS, 2, 4, 48, 384), vmem(GROUPS, 9, 48, 384),
            pltpu.VMEM((2, 48, 384), WIDE),
            pltpu.VMEM((12, 48, 384), WIDE), pltpu.VMEM((4, 48, 384), WIDE),
            pltpu.VMEM((12, 24, 384), WIDE), pltpu.VMEM((2, 48, 384), WIDE),
            pltpu.VMEM((16, 896), WIDE), pltpu.VMEM((6, 16, 896), WIDE),
            pltpu.SemaphoreType.DMA((GROUPS, 13)), pltpu.SemaphoreType.DMA((GROUPS, 13)),
            pltpu.SemaphoreType.DMA((6,)), pltpu.SemaphoreType.DMA((6,)),
            pltpu.SemaphoreType.DMA((24,)), pltpu.SemaphoreType.DMA((GROUPS,)), pltpu.SemaphoreType.DMA((2,)),
        ],
        compiler_params=pltpu.CompilerParams(collective_id=1, has_side_effects=True, vmem_limit_bytes=62 * 2**20),
    )(gains, lens, *arrays)


def place_kernel(*refs):
    small_ref, arrays = refs[0], refs[1:14]
    outs, held, sems = refs[14:31], refs[31:44], refs[44]
    copies = [pltpu.make_async_copy(src, dst, sems.at[0, n]) for n, (src, dst) in enumerate(zip(arrays, held))]
    for copy in copies:
        copy.start()
    onward = [pltpu.make_async_copy(src, dst, sems.at[1, n]) for n, (src, dst) in enumerate(zip(held, outs))]
    for n in range(3):
        outs[13 + n][...] = small_ref[n : n + 1, 0:24]
    outs[16][...] = small_ref[0:HEADS, WIDTH : WIDTH + BUCKETS]
    for copy, next_copy in zip(copies, onward):
        copy.wait()
        next_copy.start()
    for copy in onward:
        copy.wait()


def place_call(small, *arrays):
    shapes = [jax.ShapeDtypeStruct(a.shape, a.dtype) for a in arrays]
    shapes += [jax.ShapeDtypeStruct((1, 24), WIDE)] * 3 + [jax.ShapeDtypeStruct((HEADS, BUCKETS), WIDE)]
    return pl.pallas_call(
        place_kernel,
        out_shape=tuple(shapes),
        in_specs=[pl.BlockSpec(memory_space=pltpu.VMEM)] + [pl.BlockSpec(memory_space=pl.ANY)] * 13,
        out_specs=[pl.BlockSpec(memory_space=pl.ANY)] * 13 + [pl.BlockSpec(memory_space=pltpu.VMEM)] * 4,
        scratch_shapes=[pltpu.VMEM(a.shape, a.dtype) for a in arrays] + [pltpu.SemaphoreType.DMA((2, 13))],
    )(small, *arrays)


def layer_kernels(decoder_in, memory, out_grad, lengths, *params):
    shards, table = params[:13], params[13]
    (
        w, gains, normed, q, k, v, ctx, p, after_self, ncross, cq, mk, mv, cctx, pc, after_cross, nff, act, slope, layer,
    ) = forward(shards, decoder_in, memory, table, lengths)
    rows = decoder_in.reshape(ROWS, WIDTH)
    input_grad, memory_grad, *pieces, in_piece, out_piece, small = backward_call(
        gains, lengths.reshape(2), w, act, slope, nff, after_cross, cctx, ncross, cq, mk, mv,
        memory.reshape(2 * MEMORY, WIDTH), pc, after_self, p, normed, q, k, v, ctx, rows, out_grad.reshape(ROWS, WIDTH),
    )
    layer, input_grad, memory_grad, *rest = place_call(small, layer, input_grad, memory_grad, *pieces, in_piece, out_piece)
    return (
        layer.reshape(decoder_in.shape),
        input_grad.reshape(decoder_in.shape),
        memory_grad.reshape(memory.shape),
        *rest[:10],
        *[part.reshape(24) for part in rest[10:13]],
        rest[13].T,
    )


def body(decoder_in, memory, out_grad, lengths, *params):
    sizes = (lax.axis_size("dp"), lax.axis_size("fsdp"))
    if sizes == (8, 4) and decoder_in.shape == (2, 1, LENGTH, WIDTH) and params[0].shape == (24, WIDTH):
        return layer_kernels(decoder_in, memory, out_grad, lengths, *params)
    return plain_body(decoder_in, memory, out_grad, lengths, *params)


def solution(mesh):
    return jax.shard_map(
        body,
        mesh=mesh,
        in_specs=(
            P(None, ("dp", "fsdp"), None, None),
            P(None, ("dp", "fsdp"), None, None),
            P(None, ("dp", "fsdp"), None, None),
            P(None, ("dp", "fsdp")),
            P(("dp", "fsdp"), None),
            P(("dp", "fsdp"), None),
            P(("dp", "fsdp"), None),
            P(("dp", "fsdp"), None),
            P(("dp", "fsdp"), None),
            P(("dp", "fsdp"), None),
            P(("dp", "fsdp"), None),
            P(("dp", "fsdp"), None),
            P(("dp", "fsdp"), None),
            P(("dp", "fsdp"), None),
            P(("dp", "fsdp")),
            P(("dp", "fsdp")),
            P(("dp", "fsdp")),
            P(),
        ),
        out_specs=(
            P(None, ("dp", "fsdp"), None, None),
            P(None, ("dp", "fsdp"), None, None),
            P(None, ("dp", "fsdp"), None, None),
            P(("dp", "fsdp"), None),
            P(("dp", "fsdp"), None),
            P(("dp", "fsdp"), None),
            P(("dp", "fsdp"), None),
            P(("dp", "fsdp"), None),
            P(("dp", "fsdp"), None),
            P(("dp", "fsdp"), None),
            P(("dp", "fsdp"), None),
            P(("dp", "fsdp"), None),
            P(("dp", "fsdp"), None),
            P(("dp", "fsdp")),
            P(("dp", "fsdp")),
            P(("dp", "fsdp")),
            P(),
        ),
        check_vma=False,
    )
```

```python
import functools
import math

import jax
import jax.numpy as jnp
from jax import lax
from jax.experimental import pallas as pl
from jax.experimental.pallas import tpu as pltpu
from jax.sharding import PartitionSpec as P

HEADS = 12
BUCKETS = 32
MAX_DIST = 128


EPS = 1e-06
MASKED = -1e30
TOP_PRECISION = lax.Precision.HIGHEST


def bucket_onehot(length):
    half_count = BUCKETS // 2
    positions = jnp.arange(length, dtype=jnp.int32)
    distance = jnp.maximum(positions[:, None] - positions[None, :], 0)
    farther = jnp.zeros_like(distance)
    for level in range(1, half_count):
        border = int(math.ceil(half_count * (MAX_DIST / half_count) ** (level / half_count)))
        farther = farther + (distance >= border).astype(jnp.int32)
    bucket = jnp.where(distance < half_count, distance, half_count + farther)
    return (bucket[None] == jnp.arange(BUCKETS, dtype=jnp.int32)[:, None, None]).astype(jnp.float32)


def normalize(vector, gain_row):
    return vector * lax.rsqrt(jnp.mean(vector * vector, axis=-1, keepdims=True) + EPS) * gain_row


def project(operand, weight):
    return jnp.dot(operand, weight, preferred_element_type=jnp.float32)


def project_back(operand, weight):
    return lax.dot_general(
        operand, weight, (((1,), (1,)), ((), ())), preferred_element_type=jnp.float32
    )


def weight_grad(inputs_rows, grad_rows):
    return lax.dot_general(
        inputs_rows, grad_rows, (((0,), (0,)), ((), ())), preferred_element_type=jnp.float32
    )


def split_heads(matrix):
    return matrix.reshape(matrix.shape[:-1] + (HEADS, matrix.shape[-1] // HEADS))


def head_scores(queries, key_rows):
    return jnp.einsum(
        "gqhe,gkhe->ghqk",
        split_heads(queries),
        split_heads(key_rows),
        preferred_element_type=jnp.float32,
    )


def attend_forward(queries, key_rows, values, relative_position_bias, allowed):
    scores = jnp.where(allowed, head_scores(queries, key_rows) + relative_position_bias, MASKED)
    largest = jnp.max(scores, axis=-1, keepdims=True)
    exponent = jnp.exp(scores - largest)
    row_totals = jnp.sum(exponent, axis=-1, keepdims=True)
    attention_weights = exponent / row_totals
    context = jnp.einsum(
        "ghqk,gkhe->gqhe",
        attention_weights.astype(jnp.bfloat16),
        split_heads(values),
        preferred_element_type=jnp.float32,
    )
    return (context.reshape(queries.shape).astype(jnp.bfloat16), attention_weights)


def attend_backward(queries, key_rows, values, attention_weights, grad_context):
    grad_heads = split_heads(grad_context)
    grad_values = jnp.einsum(
        "ghqk,gqhe->gkhe",
        attention_weights.astype(jnp.bfloat16),
        grad_heads,
        preferred_element_type=jnp.float32,
    )
    grad_weights = jnp.einsum(
        "gqhe,gkhe->ghqk", grad_heads, split_heads(values), preferred_element_type=jnp.float32
    )
    score_gradient = attention_weights * (
        grad_weights - jnp.sum(grad_weights * attention_weights, axis=-1, keepdims=True)
    )
    rounded = score_gradient.astype(jnp.bfloat16)
    grad_queries = jnp.einsum(
        "ghqk,gkhe->gqhe", rounded, split_heads(key_rows), preferred_element_type=jnp.float32
    )
    grad_keys = jnp.einsum(
        "ghqk,gqhe->gkhe", rounded, split_heads(queries), preferred_element_type=jnp.float32
    )
    return (
        grad_queries.reshape(queries.shape).astype(jnp.bfloat16),
        grad_keys.reshape(key_rows.shape).astype(jnp.bfloat16),
        grad_values.reshape(values.shape).astype(jnp.bfloat16),
        score_gradient,
    )


AXES = ("dp", "fsdp")


def rows_of(matrix):
    return matrix.reshape(-1, matrix.shape[-1])


def gather_all(shards):
    width = shards[0].shape[1]
    blocks = []
    for shard in shards:
        if shard.ndim == 1:
            continue
        blocks.append(shard.reshape(-1, width) if shard.shape[1] != width else shard)
    packed = lax.all_gather(jnp.concatenate(blocks, axis=0), AXES, axis=0)
    whole, at = [], 0
    devices = packed.shape[0]
    for shard, block in zip(shards, blocks):
        part = packed[:, at : at + block.shape[0]]
        at += block.shape[0]
        whole.append(part.reshape(devices * shard.shape[0], shard.shape[1]))
    gains = jnp.stack(shards[len(blocks) :])
    gains = lax.all_gather(gains, AXES, axis=1, tiled=True)
    return whole, [gains[k] for k in range(gains.shape[0])]


def scatter_all(grads, shards):
    width = shards[0].shape[1]
    devices = lax.axis_size(AXES)
    blocks = [grad.astype(jnp.bfloat16).reshape(devices, -1, width) for grad in grads]
    summed = lax.psum_scatter(
        jnp.concatenate(blocks, axis=1), AXES, scatter_dimension=0, tiled=False
    ).astype(jnp.float32)
    pieces, at = [], 0
    for block, shard in zip(blocks, shards):
        pieces.append(summed[at : at + block.shape[1]].reshape(shard.shape))
        at += block.shape[1]
    return pieces


def plain_body(decoder_in, memory, out_grad, lengths, *params):
    shards, bucket_bias_table = params[:13], params[13]
    matrices, gains = gather_all(shards)
    (
        self_query,
        self_key,
        self_value,
        self_out,
        cross_query,
        cross_key,
        cross_value,
        cross_out,
        ff_in,
        ff_out,
    ) = matrices
    norm_self, norm_cross, norm_ff = [gain.astype(jnp.float32) for gain in gains]
    micro, seqs, seq_length, width = decoder_in.shape
    groups = micro * seqs
    memory_bf = memory.reshape(groups, memory.shape[2], width)
    grad_bf = out_grad.reshape(groups, seq_length, width)
    group_lengths = lengths.reshape(groups)
    bucket_indicator = bucket_onehot(seq_length)
    relative_position_bias = jnp.einsum(
        "fsn,fe->esn",
        bucket_indicator,
        bucket_bias_table.astype(jnp.float32),
        precision=TOP_PRECISION,
    )
    positions = jnp.arange(seq_length, dtype=jnp.int32)
    causal = positions[:, None] >= positions[None, :]
    present = positions[None, :] < group_lengths[:, None]
    valid_rows = present[:, :, None].astype(jnp.float32)
    allowed = causal[None, None] & present[:, None, None, :]

    def grad_of(inputs, upstream):
        return weight_grad(rows_of(inputs), rows_of(upstream))

    decoded = decoder_in.reshape(groups, seq_length, width).astype(jnp.float32)
    normed = normalize(decoded, norm_self).astype(jnp.bfloat16)
    queries = project(normed, self_query).astype(jnp.bfloat16)
    key_rows = project(normed, self_key).astype(jnp.bfloat16)
    values = project(normed, self_value).astype(jnp.bfloat16)
    context, self_weights = attend_forward(
        queries, key_rows, values, relative_position_bias, allowed
    )
    after_self = decoded + project(context, self_out)
    normed_cross = normalize(after_self, norm_cross).astype(jnp.bfloat16)
    cross_queries = project(normed_cross, cross_query).astype(jnp.bfloat16)
    memory_keys = project(memory_bf, cross_key).astype(jnp.bfloat16)
    memory_values = project(memory_bf, cross_value).astype(jnp.bfloat16)
    cross_context, cross_weights = attend_forward(
        cross_queries, memory_keys, memory_values, 0.0, True
    )
    after_cross = after_self + project(cross_context, cross_out)
    normed_ff = normalize(after_cross, norm_ff).astype(jnp.bfloat16)
    hidden = project(normed_ff, ff_in)
    activated = jax.nn.gelu(hidden, approximate=True).astype(jnp.bfloat16)
    after_ff = after_cross + project(activated, ff_out)
    layer_out = (after_ff * valid_rows).astype(jnp.bfloat16)

    def back(operand, weight):
        return lax.dot_general(
            operand, weight, (((2,), (1,)), ((), ())), preferred_element_type=jnp.float32
        )

    grad_after = grad_bf.astype(jnp.float32) * valid_rows
    grad_branch = grad_after.astype(jnp.bfloat16)
    grad_ff_out = grad_of(activated, grad_branch)
    gelu_pull = jax.vjp(lambda pre_act: jax.nn.gelu(pre_act, approximate=True), hidden)[1]
    grad_hidden = gelu_pull(back(grad_branch, ff_out))[0].astype(jnp.bfloat16)
    grad_ff_in = grad_of(normed_ff, grad_hidden)
    norm_pull = jax.vjp(normalize, after_cross, norm_ff)[1]
    grad_rows, grad_norm_ff = norm_pull(back(grad_hidden, ff_in))
    grad_after = grad_after + grad_rows
    grad_branch = grad_after.astype(jnp.bfloat16)
    grad_cross_out = grad_of(cross_context, grad_branch)
    grad_context = back(grad_branch, cross_out).astype(jnp.bfloat16)
    grad_cross_rows, grad_memory_keys, grad_memory_values, unused = attend_backward(
        cross_queries, memory_keys, memory_values, cross_weights, grad_context
    )
    grad_cross_query = grad_of(normed_cross, grad_cross_rows)
    grad_cross_key = grad_of(memory_bf, grad_memory_keys)
    grad_cross_value = grad_of(memory_bf, grad_memory_values)
    grad_memory = back(grad_memory_keys, cross_key) + back(grad_memory_values, cross_value)
    norm_pull = jax.vjp(normalize, after_self, norm_cross)[1]
    grad_rows, grad_norm_cross = norm_pull(back(grad_cross_rows, cross_query))
    grad_after = grad_after + grad_rows
    grad_branch = grad_after.astype(jnp.bfloat16)
    grad_self_out = grad_of(context, grad_branch)
    grad_context = back(grad_branch, self_out).astype(jnp.bfloat16)
    grad_queries, grad_key_rows, grad_values, score_gradient = attend_backward(
        queries, key_rows, values, self_weights, grad_context
    )
    grad_self_query = grad_of(normed, grad_queries)
    grad_self_key = grad_of(normed, grad_key_rows)
    grad_self_value = grad_of(normed, grad_values)
    grad_normed = (
        back(grad_queries, self_query) + back(grad_key_rows, self_key) + back(grad_values, self_value)
    )
    norm_pull = jax.vjp(normalize, decoded, norm_self)[1]
    grad_rows, grad_norm_self = norm_pull(grad_normed)
    grad_input = grad_after + grad_rows
    bias_grad = jnp.einsum(
        "fgd,ogd->fo", bucket_indicator, jnp.sum(score_gradient, axis=0), precision=TOP_PRECISION
    )
    pieces = scatter_all(
        (
            grad_self_query,
            grad_self_key,
            grad_self_value,
            grad_self_out,
            grad_cross_query,
            grad_cross_key,
            grad_cross_value,
            grad_cross_out,
            grad_ff_in,
            grad_ff_out,
        ),
        shards[:10],
    )
    small = lax.psum(
        jnp.concatenate([grad_norm_self, grad_norm_cross, grad_norm_ff, bias_grad.reshape(-1)]),
        AXES,
    )
    mine = shards[10].shape[0]
    at = lax.axis_index(AXES) * mine
    gains_out = [
        lax.dynamic_slice_in_dim(small[k * width : (k + 1) * width], at, mine) for k in range(3)
    ]
    return (
        layer_out.reshape(decoder_in.shape),
        grad_input.reshape(decoder_in.shape),
        grad_memory.reshape(memory.shape),
        *pieces,
        *gains_out,
        small[3 * width :].reshape(bucket_bias_table.shape),
    )


MESH = pl.DeviceIdType.MESH
LOW = jnp.bfloat16
WIDE = jnp.float32
GROUPS = 16
WIDTH = 768
ROWS = 512
LENGTH = 256
MEMORY = 128
PAIRS = 6
CURVE = math.sqrt(2.0 / math.pi)


def place():
    dp, fsdp = lax.axis_index("dp"), lax.axis_index("fsdp")
    z, y, x, core = dp // 2, dp % 2, fsdp // 2, fsdp % 2
    sibling = (dp, x * 2 + 1 - core)
    over_x = (dp, (1 - x) * 2 + core)
    over_y = (z * 2 + 1 - y, fsdp)
    first = (jnp.where(core == 0, over_x[0], over_y[0]), jnp.where(core == 0, over_x[1], over_y[1]))
    second = (jnp.where(core == 0, over_y[0], over_x[0]), jnp.where(core == 0, over_y[1], over_x[1]))
    along_z = [(((z + k) % 4) * 2 + y, fsdp) for k in (1, 2, 3)]
    own = y * 2 + x
    beside = jnp.where(core == 0, y * 2 + 1 - x, (1 - y) * 2 + x)
    return z, own, beside, core, sibling, first, second, along_z


def greet(partners, meanwhile):
    barrier = pltpu.get_barrier_semaphore()
    for partner in partners:
        pl.semaphore_signal(barrier, inc=1, device_id=partner, device_id_type=MESH)
    meanwhile()
    pl.semaphore_wait(barrier, len(partners))


def half(core):
    return pl.ds(pl.multiple_of(core * 384, 128), 384)


def skew(ahead, groups=GROUPS):
    order = []
    for t in range(-max(ahead), groups + 8):
        for s in range(len(ahead)):
            g = t + ahead[s]
            if 0 <= g < groups:
                order.append((g, s))
    return order


def dot(a, b):
    return jnp.dot(a, b, preferred_element_type=WIDE)


def dot_nt(a, b):
    return lax.dot_general(a, b, (((1,), (1,)), ((), ())), preferred_element_type=WIDE)


def dot_tn(a, b):
    return lax.dot_general(a, b, (((0,), (0,)), ((), ())), preferred_element_type=WIDE)


def unit(w, u):
    return w[u].reshape(WIDTH, WIDTH)


def root_scale(value):
    return lax.rsqrt(jnp.mean(value * value, axis=-1, keepdims=True) + EPS)


def bucket_columns(flipped):
    j = lax.broadcasted_iota(jnp.int32, (BUCKETS, LENGTH), 1)
    row = lax.broadcasted_iota(jnp.int32, (BUCKETS, LENGTH), 0)
    n = jnp.where(j == 0, 0, LENGTH - j) if flipped else j
    half_count = BUCKETS // 2
    farther = jnp.zeros_like(n)
    for level in range(1, half_count):
        border = int(math.ceil(half_count * (MAX_DIST / half_count) ** (level / half_count)))
        farther = farther + (n >= border).astype(jnp.int32)
    bucket = jnp.where(n < half_count, n, half_count + farther)
    return (bucket == row).astype(WIDE)


QUEUE = (0, 1, 2, 3, 4, 5, 6, 7, 12, 13, 14, 15, 8, 9, 10, 11)
ZS = (1, 3, 5, 7, 8, 9, 11, 13, 14, 15)
AHEAD = (9, 8, 6, 3, 1, 0)
GAIN_AT = (8, 11, 14)
BUDGET = 3.0
UNROLL = 2


def forward_kernel(*refs):
    shard_refs, gain_refs = refs[:9], refs[9:12]
    forward_steps(shard_refs, gain_refs, *refs[12:])


def forward_steps(
    shard_refs, gain_refs, tall_ref, x_hbm, mem_hbm, table_ref, lens_ref,
    w_out, gains_out, normed_out, q_out, k_out, v_out, ctx_out, p_out, after_self_out, ncross_out,
    cq_out, mk_out, mv_out, cctx_out, pc_out, after_cross_out, nff_out, act_out, slope_out, layer_out,
    w, gains, normed, q, k, v, ctx, p, after_self, ncross, cq, mk, mv, cctx, pc, after_cross, nff, act, slope, layer,
    x_ref, mem_ref, total, bias, small, sib, gain_in, ss, rs, ss0, rs0, out_sem, in_sem,
):
    z, own, beside, core, sibling, first, second, along_z = place()
    mine, other = half(core), half(1 - core)

    def along_at(zi):
        return (zi * 2 + lax.axis_index("dp") % 2, lax.axis_index("fsdp"))

    def view(g, zi, yx, cols):
        if g < 12:
            return w.at[g, slice(None) if zi is None else zi, yx, :, cols]
        return w.at[pl.ds(12, 4) if zi is None else 12 + zi, yx, g - 12, :, cols]

    def whole(g, cols):
        return w.at[g, :, :, :, cols] if g < 12 else w.at[pl.ds(12, 4), :, g - 12, :, cols]

    def send(ref, to, g, n):
        return pltpu.make_async_remote_copy(
            src_ref=ref, dst_ref=ref, send_sem=ss.at[g, n], recv_sem=rs.at[g, n], device_id=to, device_id_type=MESH)

    inner = (z == 1) | (z == 2)
    far = (z + 2) % 4
    end = along_at(jnp.where(z == 1, 0, 3))

    def z_send(g, block, n):
        yx, at = block
        return send(view(g, z, yx, mine), along_z[n], g, at + n)

    def z_hand_on(g, block):
        yx, at = block
        return send(view(g, far, yx, mine), end, g, 10 + (at > 0))

    def z_start(g, blocks):
        for block in blocks:
            z_send(g, block, 1).start()
            pl.when(z < 3)(lambda: z_send(g, block, 0).start())
            pl.when(z > 0)(lambda: z_send(g, block, 2).start())

    def z_relay(g, blocks):
        @pl.when(inner)
        def _():
            for block in blocks:
                z_send(g, block, 1).wait_recv()
                z_hand_on(g, block).start()

    def z_wait(g, blocks):
        for block in blocks:
            z_send(g, block, 1).wait_send()

            @pl.when(z < 3)
            def _():
                z_send(g, block, 0).wait_send()
                z_send(g, block, 2).wait_recv()

            @pl.when(z > 0)
            def _():
                z_send(g, block, 2).wait_send()
                z_send(g, block, 0).wait_recv()

            @pl.when(inner)
            def _():
                z_hand_on(g, block).wait_send()

            @pl.when(jnp.logical_not(inner))
            def _():
                z_send(g, block, 1).wait_recv()
                z_hand_on(g, block).wait_recv()

    one_block, two_blocks = [(own, 0)], [(own, 0), (beside, 7)]

    def step_b(g):
        return [send(view(g, None, own, mine), first, g, 3)]

    def step_c(g):
        return [send(view(g, None, own, mine), second, g, 4), send(view(g, None, beside, mine), second, g, 5)]

    def step_d(g):
        return [send(whole(g, mine), sibling, g, 6)]

    def step_b1(g):
        return [send(view(g, z, own, mine), first, g, 3)]

    def wait(copies):
        for copy in copies:
            copy.wait()

    def event(g, s, z_second):
        blocks = two_blocks if z_second else one_block
        if s == 0:
            start(step_b1(g)) if z_second else z_start(g, blocks)
        elif s == 1:
            if z_second:
                wait(step_b1(g))
                z_start(g, blocks)
            else:
                z_relay(g, blocks)
        elif s == 2:
            if z_second:
                z_relay(g, blocks)
            else:
                z_wait(g, blocks)
                start(step_b(g))
        elif s == 3:
            z_wait(g, blocks) if z_second else wait(step_b(g))
            start(step_c(g))
        elif s == 4:
            wait(step_c(g))
            start(step_d(g))
        else:
            wait(step_d(g))

    def gain_copies(s):
        to = ([sibling], along_z, [first], [second])[s]
        at = (0, 1, 4, 5)[s]
        return [
            pltpu.make_async_remote_copy(
                src_ref=gains, dst_ref=gain_in.at[at + n], send_sem=ss0.at[2 + at + n], recv_sem=rs0.at[2 + at + n],
                device_id=d, device_id_type=MESH)
            for n, d in enumerate(to)
        ]

    def start(copies):
        for copy in copies:
            copy.start()

    def gain_finish(s):
        for copy in gain_copies(s):
            copy.wait()
        for n in ((0,), (1, 2, 3), (4,), (5,))[s]:
            gains[...] += gain_in[n]

    stores = []

    def store(src, dst):
        copy = pltpu.make_async_copy(src, dst, out_sem.at[len(stores)])
        stores.append(copy)
        copy.start()

    def store_unit(g):
        if g < 12:
            store(w.at[g], w_out.at[g])
        elif g == 15:
            store(w.at[pl.ds(12, 4)], w_out.at[pl.ds(12, 4)])

    def gain(n):
        return gains[n : n + 1, :].astype(WIDE)

    def scale_rows(src, n, dst):
        g = gain(n)

        def chunk(i, c):
            rows = pl.ds(pl.multiple_of(i * 128, 128), 128)
            value = src[rows, :].astype(WIDE)
            dst[rows, :] = (value * root_scale(value) * g).astype(LOW)
            return c

        lax.fori_loop(0, ROWS // 128, chunk, 0)

    def make_bias():
        by_distance = dot(table_ref[...], bucket_columns(True).astype(LOW))
        for h in range(HEADS):
            row = jnp.broadcast_to(by_distance[h : h + 1, :], (LENGTH, LENGTH))
            bias[h] = pltpu.roll(row, 0, 1, stride=1, stride_axis=0)

    def project_into(src, u, dst):
        dst[...] = dot(src[...], unit(w, u)).astype(LOW)

    lane = lax.broadcasted_iota(jnp.int32, (1, 128), 1)
    sides = [lane < 64, lane >= 64]

    def attend(i, queries, keys, vals, keep_p, into, depth, masked):
        s, pair = i // PAIRS, i % PAIRS
        rows = pl.ds(pl.multiple_of(s * LENGTH, LENGTH), LENGTH)
        deep = pl.ds(pl.multiple_of(s * depth, depth), depth)
        cols = pl.ds(pl.multiple_of(pair * 128, 128), 128)
        qp, kp, vp = queries[rows, cols], keys[deep, cols], vals[deep, cols]
        parts = []
        for side in range(2):
            scores = dot_nt(jnp.where(sides[side], qp, jnp.zeros_like(qp)), kp)
            if masked:
                t = lax.broadcasted_iota(jnp.int32, (LENGTH, LENGTH), 0)
                u = lax.broadcasted_iota(jnp.int32, (LENGTH, LENGTH), 1)
                allowed = (u <= t) & (u < lens_ref[s])
                scores = jnp.where(allowed, scores + bias[2 * pair + side], MASKED)
            e = jnp.exp(scores - jnp.max(scores, axis=-1, keepdims=True))
            weights = (e * (1.0 / jnp.sum(e, axis=-1, keepdims=True))).astype(LOW)
            keep_p[rows, pl.ds(pl.multiple_of((2 * pair + side) * depth, 128), depth)] = weights
            parts.append(dot(weights, vp))
        into[rows, cols] = jnp.where(sides[0], parts[0], parts[1]).astype(LOW)

    def self_part(lo, hi):
        def it(i, c):
            attend(i, q, k, v, p, ctx, LENGTH, True)
            return c

        lax.fori_loop(lo, hi, it, 0, unroll=UNROLL)

    def cross_part(lo, hi):
        def it(i, c):
            attend(i, cq, mk, mv, pc, cctx, MEMORY, False)
            return c

        lax.fori_loop(lo, hi, it, 0, unroll=UNROLL)

    def after_self_part():
        after_self[...] = x_ref[...].astype(WIDE) + dot(ctx[...], unit(w, 3))
        scale_rows(after_self, 1, ncross)

    def after_cross_part():
        after_cross[...] = after_self[...] + dot(cctx[...], unit(w, 7))
        scale_rows(after_cross, 2, nff)

    def hidden_part(j):
        cols = slice(j * WIDTH, (j + 1) * WIDTH)
        for m in range(2):
            rows = slice(m * 256, m * 256 + 256)
            a = dot(nff[rows, :], unit(w, 8 + j))
            sq = a * a
            th = jnp.tanh(a * (CURVE + (CURVE * 0.044715) * sq))
            act[rows, cols] = (0.5 * a * (1.0 + th)).astype(LOW)
            slope[rows, cols] = (
                0.5 * (1.0 + th) + 0.5 * a * (1.0 - th * th) * (CURVE + (3.0 * CURVE * 0.044715) * sq)
            ).astype(LOW)
        store(act.at[:, pl.ds(j * WIDTH, WIDTH)], act_out.at[:, pl.ds(j * WIDTH, WIDTH)])
        store(slope.at[:, pl.ds(j * WIDTH, WIDTH)], slope_out.at[:, pl.ds(j * WIDTH, WIDTH)])
        part = dot(act[:, cols], unit(w, 12 + j))
        if j == 0:
            total[...] = after_cross[...] + part
        elif j < 3:
            total[...] += part
        else:
            part = total[...] + part
            for s in range(2):
                rows = slice(s * LENGTH, (s + 1) * LENGTH)
                t = lax.broadcasted_iota(jnp.int32, (LENGTH, 1), 0)
                layer[rows, :] = (part[rows] * (t < lens_ref[s]).astype(WIDE)).astype(LOW)

    pieces = [
        (0, 1.0, lambda: project_into(normed, 0, q)), (0, 0.1, lambda: store(q, q_out)),
        (1, 1.0, lambda: project_into(normed, 1, k)), (1, 0.1, lambda: store(k, k_out)),
        (2, 1.0, lambda: project_into(normed, 2, v)), (2, 0.1, lambda: store(v, v_out)),
        *[(2, 1.8, functools.partial(self_part, 2 * n, 2 * n + 2)) for n in range(6)],
        (2, 0.1, lambda: store(ctx, ctx_out)), (2, 0.1, lambda: store(p, p_out)),
        (3, 2.0, after_self_part), (3, 0.1, lambda: store(after_self, after_self_out)), (3, 0.1, lambda: store(ncross, ncross_out)),
        (4, 1.0, lambda: project_into(ncross, 4, cq)), (4, 0.1, lambda: store(cq, cq_out)),
        (5, 0.6, lambda: project_into(mem_ref, 5, mk)), (5, 0.1, lambda: store(mk, mk_out)),
        (6, 0.6, lambda: project_into(mem_ref, 6, mv)), (6, 0.1, lambda: store(mv, mv_out)),
        *[(6, 1.5, functools.partial(cross_part, 2 * n, 2 * n + 2)) for n in range(6)],
        (6, 0.1, lambda: store(cctx, cctx_out)), (6, 0.1, lambda: store(pc, pc_out)),
        (7, 2.0, after_cross_part), (7, 0.1, lambda: store(after_cross, after_cross_out)), (7, 0.1, lambda: store(nff, nff_out)),
        (8, 3.0, lambda: hidden_part(0)), (9, 3.0, lambda: hidden_part(1)), (10, 3.0, lambda: hidden_part(2)),
        (11, 3.0, lambda: hidden_part(3)), (11, 0.1, lambda: store(layer, layer_out)),
    ]

    load_x = pltpu.make_async_copy(x_hbm, x_ref, in_sem.at[0])
    load_mem = pltpu.make_async_copy(mem_hbm, mem_ref, in_sem.at[1])

    def prepare():
        load_x.start()
        load_mem.start()
        for u in range(12):
            rows = shard_refs[u][...] if u < 8 else shard_refs[8][:, WIDTH * (u - 8) : WIDTH * (u - 7)]
            rows = rows.astype(WIDE)
            none = jnp.zeros_like(rows)
            small[u] = jnp.concatenate(
                [jnp.where(core == 0, rows, none), jnp.where(core == 0, none, rows)], axis=0).astype(LOW)
        offset = (lax.axis_index("dp") * 4 + lax.axis_index("fsdp")) * 24
        spot = (lax.broadcasted_iota(jnp.int32, (24, WIDTH), 1) == lax.broadcasted_iota(jnp.int32, (24, WIDTH), 0) + offset)
        placed = [dot(ref[...], spot.astype(LOW)) for ref in gain_refs]
        gains[...] = jnp.concatenate(placed + [jnp.zeros((13, WIDTH), WIDE)], axis=0).astype(LOW)

    greet([sibling, first, second] + along_z, prepare)
    swap_small = pltpu.make_async_remote_copy(
        src_ref=small.at[:, :, other], dst_ref=sib, send_sem=ss0.at[0], recv_sem=rs0.at[0],
        device_id=sibling, device_id_type=MESH)

    def tall_view(cols):
        return w.at[12 + z, own, pl.ds(2 * core, 2), :, cols]

    swap_tall = pltpu.make_async_remote_copy(
        src_ref=tall_ref.at[:, :, other], dst_ref=tall_view(other), send_sem=ss0.at[1], recv_sem=rs0.at[1],
        device_id=sibling, device_id_type=MESH)
    swap_small.start()
    swap_tall.start()
    start(gain_copies(0))
    w[12 + z, own, pl.ds(2 * core, 2), :, mine] = tall_ref[:, :, mine]
    swap_small.wait()

    def assemble(u):
        w[u, z, own, :, mine] = small[u, :, mine] + sib[u]

    early = skew(AHEAD)[:2]
    assert all(s == 0 and QUEUE[at] < 12 for at, s in early)
    for at, s in early:
        assemble(QUEUE[at])
        event(QUEUE[at], 0, at in ZS)
    for u in range(12):
        if u not in [QUEUE[at] for at, s in early]:
            assemble(u)
    gain_finish(0)
    start(gain_copies(1))
    swap_tall.wait()
    make_bias()
    load_x.wait()
    load_mem.wait()

    stage, done = 1, 0
    for n, (at, s) in enumerate(skew(AHEAD)):
        g = QUEUE[at]
        if n >= 2:
            event(g, s, at in ZS)
        if n in GAIN_AT:
            gain_finish(stage)
            stage += 1
            if stage < 4:
                start(gain_copies(stage))
            else:
                scale_rows(x_ref, 0, normed)
                store(normed, normed_out)
                store(gains, gains_out)
        if s == 5:
            store_unit(g)
            spent = 0.0
            while done < len(pieces) and QUEUE.index(pieces[done][0]) <= at and (spent < BUDGET or at == GROUPS - 1):
                spent += pieces[done][1]
                pieces[done][2]()
                done += 1
    assert done == len(pieces) and stage == 4
    for copy in stores:
        copy.wait()


FORWARD_OUT = (
    ((16, 4, 4, 48, 768), LOW),
    ((16, 768), LOW),
    ((512, 768), LOW), ((512, 768), LOW), ((512, 768), LOW), ((512, 768), LOW),
    ((512, 768), LOW),
    ((512, 3072), LOW),
    ((512, 768), WIDE),
    ((512, 768), LOW),
    ((512, 768), LOW), ((256, 768), LOW), ((256, 768), LOW), ((512, 768), LOW),
    ((512, 1536), LOW),
    ((512, 768), WIDE),
    ((512, 768), LOW),
    ((512, 3072), LOW), ((512, 3072), LOW),
    ((512, 768), LOW),
)


def forward_call(*operands):
    return pl.pallas_call(
        forward_kernel,
        out_shape=tuple(jax.ShapeDtypeStruct(s, t) for s, t in FORWARD_OUT),
        in_specs=[pl.BlockSpec(memory_space=pltpu.VMEM)] * 13
        + [pl.BlockSpec(memory_space=pl.ANY)] * 2
        + [pl.BlockSpec(memory_space=pltpu.VMEM), pl.BlockSpec(memory_space=pltpu.SMEM)],
        out_specs=[pl.BlockSpec(memory_space=pl.ANY)] * len(FORWARD_OUT),
        scratch_shapes=[pltpu.VMEM(s, t) for s, t in FORWARD_OUT]
        + [
            pltpu.VMEM((ROWS, WIDTH), LOW),
            pltpu.VMEM((2 * MEMORY, WIDTH), LOW),
            pltpu.VMEM((ROWS, WIDTH), WIDE),
            pltpu.VMEM((HEADS, LENGTH, LENGTH), WIDE),
            pltpu.VMEM((12, 48, 768), LOW),
            pltpu.VMEM((12, 48, 384), LOW),
            pltpu.VMEM((6, 16, 768), LOW),
            pltpu.SemaphoreType.DMA((GROUPS, 12)),
            pltpu.SemaphoreType.DMA((GROUPS, 12)),
            pltpu.SemaphoreType.DMA((8,)),
            pltpu.SemaphoreType.DMA((8,)),
            pltpu.SemaphoreType.DMA((40,)),
            pltpu.SemaphoreType.DMA((2,)),
        ],
        compiler_params=pltpu.CompilerParams(collective_id=0, has_side_effects=True, vmem_limit_bytes=60 * 2**20),
    )(*operands)


def forward(shards, decoder_in, memory, table, lengths):
    return forward_call(
        *shards[:9],
        *[shard.reshape(1, 24) for shard in shards[10:13]],
        shards[9].reshape(2, 48, WIDTH),
        decoder_in.reshape(ROWS, WIDTH),
        memory.reshape(2 * MEMORY, WIDTH),
        table.T,
        lengths.reshape(2),
    )


LINE = (12, 13, 14, 15, 8, 9, 10, 11, 7, 4, 5, 6, 3, 0, 1, 2)
USED = (12, 8, 13, 9, 14, 10, 15, 11, 7, 5, 6, 4, 3, 0, 1, 2)
SLOTS = 6
LAGS = (0, 1, 3, 5, 7, 9, 10)
PACE = 3.5
FIRST_Z = (8, 10, 7, 5, 3)


def backward_kernel(
    gains, lens_ref, w_hbm, act_hbm, slope_hbm, nff_hbm, after_cross_hbm, cctx_hbm, ncross_hbm, cq_hbm, mk_hbm, mv_hbm,
    mem_hbm, pc_hbm, after_self_hbm, p_hbm, normed_hbm, q_hbm, k_hbm, v_hbm, ctx_hbm, x_hbm, og_hbm,
    input_out, memory_out, *rest,
):
    pieces_out, rest = rest[:8], rest[8:]
    (
        in_piece_out, out_piece_out, sum_out,
        ring, act, slope, mem_grad, nff, aft, cctx, ncross, cq, mk, mv, mem, pc, x, gl, total, up, ghj, low, gctx, dq, dk, dv,
        dist, grad, r0, r1, r23, zsum, fa, fo, fa_in, fo_in, acc, acc_in, ss, rs, ss0, rs0, in_sem, ring_sem, out_sem,
    ) = rest
    z, own, beside, core, sibling, first, second, along_z = place()
    mine, other = half(core), half(1 - core)
    diag, across = 3 - own, 3 - beside

    fetches = {}

    def fetch(name, src, dst):
        copy = pltpu.make_async_copy(src, dst, in_sem.at[len(fetches)])
        fetches[name] = copy
        copy.start()

    def fetched(*names):
        for name in names:
            fetches[name].wait()

    def weight_copy(n):
        return pltpu.make_async_copy(w_hbm.at[USED[n]], ring.at[n % SLOTS], ring_sem.at[n])

    asked, got = [0], [0]

    def ask(n):
        while asked[0] < min(n, GROUPS):
            weight_copy(asked[0]).start()
            asked[0] += 1

    def weight(u):
        n = USED.index(u)
        while got[0] <= n:
            weight_copy(got[0]).wait()
            got[0] += 1
        return ring[n % SLOTS].reshape(WIDTH, WIDTH)

    def send(src, dst, to, g, n):
        return pltpu.make_async_remote_copy(
            src_ref=src, dst_ref=dst, send_sem=ss.at[g, n], recv_sem=rs.at[g, n], device_id=to, device_id_type=MESH)

    def block(g, cols):
        return grad.at[LINE.index(g) % 4, :, :, :, cols]

    def swap(g):
        return [send(block(g, other), r0.at[g], sibling, g, 0)]

    def quarter(ref, g, yx):
        return ref.at[g, :, yx] if g < 12 else ref.at[g, yx]

    def share(g, zi, yx):
        return r0.at[g, zi, yx] if g < 12 else r0.at[12 + zi, yx, g - 12]

    def over_second(g):
        return [
            send(quarter(r0, g, across), r1.at[g, 0], second, g, 1),
            send(quarter(r0, g, diag), r1.at[g, 1], second, g, 2),
        ]

    def over_first(g):
        return [send(quarter(r0, g, beside), r23.at[g, pl.ds(0, 4)], first, g, 3)]

    def over_first1(g):
        return [send(r0.at[g, z, beside], r23.at[g, 0], first, g, 3)]

    inner = (z == 1) | (z == 2)
    far = (z + 2) % 4
    next_in = (jnp.where(z == 0, 1, 2) * 2 + lax.axis_index("dp") % 2, lax.axis_index("fsdp"))

    def z_send(g, block, n):
        yx, at, sem = block
        return send(share(g, (z + n + 1) % 4, yx), r23.at[g, at + n], along_z[n], g, sem + n)

    def z_hand_over(g, block, slot):
        return send(share(g, 3 - z, block[0]), r23.at[g, 7 + slot], next_in, g, 11 + slot)

    def z_start(g, blocks):
        for slot, block in enumerate(blocks):

            @pl.when(jnp.logical_not(inner))
            def _():
                z_hand_over(g, block, slot).start()
                z_send(g, block, 1).start()

            pl.when(z < 3)(lambda: z_send(g, block, 0).start())
            pl.when(z > 0)(lambda: z_send(g, block, 2).start())

    def z_relay(g, blocks):
        @pl.when(inner)
        def _():
            for slot, block in enumerate(blocks):
                z_hand_over(g, block, slot).wait_recv()
                both = share(g, far, block[0])[...].astype(WIDE) + r23[g, 7 + slot].astype(WIDE)
                share(g, far, block[0])[...] = both.astype(LOW)
                z_send(g, block, 1).start()

    def z_wait(g, blocks):
        for slot, block in enumerate(blocks):
            yx, at, sem = block
            z_send(g, block, 1).wait()
            pl.when(jnp.logical_not(inner))(lambda: z_hand_over(g, block, slot).wait_send())
            zsum[slot] = share(g, z, yx)[...].astype(WIDE) + r23[g, at + 1].astype(WIDE)

            @pl.when(z > 0)
            def _():
                z_send(g, block, 2).wait_send()
                z_send(g, block, 0).wait_recv()
                zsum[slot] += r23[g, at].astype(WIDE)

            @pl.when(z < 3)
            def _():
                z_send(g, block, 0).wait_send()
                z_send(g, block, 2).wait_recv()
                zsum[slot] += r23[g, at + 2].astype(WIDE)

    one_block, two_blocks = [(own, 4, 4)], [(own, 4, 4), (beside, 1, 7)]

    def last(g):
        if g < 12:
            rows = pl.ds(pl.multiple_of(24 * (1 - core), 8), 24)
            return [send(fa.at[g, rows], fa_in.at[g], sibling, g, 10)]
        if g == 15:
            return [send(fo.at[pl.ds(2 * (1 - core), 2)], fo_in, sibling, g, 10)]
        return []

    def add0(g):
        r0[g] += block(g, mine)[...]

    def add1(g):
        quarter(r0, g, own)[...] += r1[g, 0]
        quarter(r0, g, beside)[...] += r1[g, 1]

    def finish(g, value):
        if g < 12:
            fa[g] = value
        else:
            fo[g - 12] = value

    def add2(g):
        quarter(r0, g, own)[...] += r23[g, 0:4]

    def add3z(g):
        finish(g, r0[g, z, own].astype(WIDE) + r23[g, 0].astype(WIDE))

    def write(g):
        rows = pl.ds(pl.multiple_of(24 * core, 8), 24)
        if g < 8:
            pieces_out[g][:, mine] = fa[g, rows]
            pieces_out[g][:, other] = fa_in[g]
        elif g < 12:
            at = WIDTH * (g - 8)
            in_piece_out[:, pl.ds(pl.multiple_of(at + core * 384, 128), 384)] = fa[g, rows]
            in_piece_out[:, pl.ds(pl.multiple_of(at + 384 - core * 384, 128), 384)] = fa_in[g]
        elif g == 15:
            out_piece_out[:, mine] = fo[pl.ds(2 * core, 2)].reshape(96, 384)
            out_piece_out[:, other] = fo_in[...].reshape(96, 384)

    def start(copies):
        for copy in copies:
            copy.start()

    def wait(copies):
        for copy in copies:
            copy.wait()

    def along_z_after(g):
        return [g] if g < 12 else [12, 13, 14, 15] if g == 15 else []

    def event(g, s):
        z_second = g in FIRST_Z
        blocks = two_blocks if z_second else one_block
        if s == 0:
            start(swap(g))
        elif s == 1:
            wait(swap(g))
            add0(g)
            start(over_second(g))
        elif s == 2:
            wait(over_second(g))
            add1(g)
            z_start(g, blocks) if z_second else start(over_first(g))
        elif s == 3:
            if z_second:
                z_relay(g, blocks)
            else:
                wait(over_first(g))
                add2(g)
                for one in along_z_after(g):
                    z_start(one, blocks)
        elif s == 4:
            if z_second:
                z_wait(g, blocks)
                r0[g, z, own] = zsum[0].astype(LOW)
                r0[g, z, beside] = zsum[1].astype(LOW)
                start(over_first1(g))
            else:
                for one in along_z_after(g):
                    z_relay(one, blocks)
        elif s == 5:
            if z_second:
                wait(over_first1(g))
                add3z(g)
            else:
                for one in along_z_after(g):
                    z_wait(one, blocks)
                    finish(one, zsum[0])
            start(last(g))
        else:
            wait(last(g))
            write(g)

    def acc_copies(s):
        to = ([sibling], along_z, [first], [second])[s]
        at = (0, 1, 4, 5)[s]
        return [
            pltpu.make_async_remote_copy(
                src_ref=acc, dst_ref=acc_in.at[at + n], send_sem=ss0.at[at + n], recv_sem=rs0.at[at + n],
                device_id=d, device_id_type=MESH)
            for n, d in enumerate(to)
        ]

    lane = lax.broadcasted_iota(jnp.int32, (1, 128), 1)
    sides = [lane < 64, lane >= 64]

    def keep(g, value):
        grad[LINE.index(g) % 4] = value.astype(LOW).reshape(4, 4, 48, WIDTH)

    def begin():
        fetched("og")
        for s in range(2):
            rows = slice(s * LENGTH, (s + 1) * LENGTH)
            t = lax.broadcasted_iota(jnp.int32, (LENGTH, 1), 0)
            gl[rows, :] = jnp.where(t < lens_ref[s], gl[rows, :].astype(WIDE), 0.0).astype(LOW)

    def out_grad_part(j):
        fetched(f"act{j}")
        grad[j] = dot_tn(act[:, j * WIDTH : (j + 1) * WIDTH], gl[...]).astype(LOW).reshape(4, 4, 48, WIDTH)

    def hidden_part(j):
        if j == 0:
            fetched("slope", "nff")
        cols = slice(j * WIDTH, (j + 1) * WIDTH)
        ghj[...] = (dot_nt(gl[...], weight(12 + j)) * slope[:, cols].astype(WIDE)).astype(LOW)
        keep(8 + j, dot_tn(nff[...], ghj[...]))

    def hidden_back(j):
        part = dot_nt(ghj[...], weight(8 + j))
        if j:
            up[...] += part
        else:
            up[...] = part

    def norm_back(value_ref, base_ref, n):
        g = gains[n : n + 1, :].astype(WIDE)

        def chunk(i, carried):
            rows = pl.ds(pl.multiple_of(i * 128, 128), 128)
            value = value_ref[rows, :].astype(WIDE)
            r = root_scale(value)
            unit_rows = value * r
            upstream = up[rows, :]
            weighted = upstream * g
            inner = jnp.mean(weighted * unit_rows, axis=-1, keepdims=True)
            new = base_ref[rows, :].astype(WIDE) + r * (weighted - unit_rows * inner)
            total[rows, :] = new
            low[rows, :] = new.astype(LOW)
            return carried + jnp.sum(upstream * unit_rows, axis=0, keepdims=True)

        acc[n : n + 1, 0:WIDTH] = lax.fori_loop(0, ROWS // 128, chunk, jnp.zeros((1, WIDTH), WIDE))

    def ff_norm_part():
        fetched("after_cross")
        norm_back(aft, gl, 2)
        fetch("p", p_hbm, act)
        fetch("normed", normed_hbm, slope.at[:, 0:768])
        fetch("q", q_hbm, slope.at[:, 768:1536])
        fetch("k", k_hbm, slope.at[:, 1536:2304])
        fetch("v", v_hbm, slope.at[:, 2304:3072])
        fetch("ctx", ctx_hbm, nff)
        fetch("after_self", after_self_hbm, aft)

    def cross_out_part():
        fetched("cctx")
        keep(7, dot_tn(cctx[...], low[...]))
        gctx[...] = dot_nt(low[...], weight(7)).astype(LOW)
        fetched("cq", "mk", "mv", "pc")

    def head_back(weights, gp, qp, kp, vp, side):
        p32 = weights.astype(WIDE)
        pull = dot_nt(jnp.where(sides[side], gp, jnp.zeros_like(gp)), vp)
        slant = p32 * (pull - jnp.sum(pull * p32, axis=-1, keepdims=True))
        rounded = slant.astype(LOW)
        return dot(rounded, kp), dot_tn(rounded, qp), dot_tn(weights, gp), slant

    def joined(low_part, high_part):
        return jnp.where(sides[0], low_part, high_part).astype(LOW)

    def cross_part(lo, hi):
        def it(i, c):
            s, pair = i // PAIRS, i % PAIRS
            rows = pl.ds(pl.multiple_of(s * LENGTH, LENGTH), LENGTH)
            deep = pl.ds(pl.multiple_of(s * MEMORY, MEMORY), MEMORY)
            cols = pl.ds(pl.multiple_of(pair * 128, 128), 128)
            gp, qp, kp, vp = gctx[rows, cols], cq[rows, cols], mk[deep, cols], mv[deep, cols]
            one, two = [
                head_back(pc[rows, pl.ds(pl.multiple_of((2 * pair + side) * MEMORY, 128), MEMORY)], gp, qp, kp, vp, side)
                for side in range(2)
            ]
            dq[rows, cols] = joined(one[0], two[0])
            dk[deep, cols] = joined(one[1], two[1])
            dv[deep, cols] = joined(one[2], two[2])
            return c

        lax.fori_loop(lo, hi, it, 0)

    def cross_query_part():
        fetched("ncross")
        keep(4, dot_tn(ncross[...], dq[...]))

    def cross_key_part():
        fetched("mem")
        keep(5, dot_tn(mem[...], dk[0:256, :]))

    def cross_value_part():
        keep(6, dot_tn(mem[...], dv[0:256, :]))

    def memory_part():
        mem_grad[...] = dot_nt(dk[0:256, :], weight(5)) + dot_nt(dv[0:256, :], weight(6))
        pltpu.make_async_copy(mem_grad, memory_out, out_sem.at[0]).start()

    def cross_query_back():
        up[...] = dot_nt(dq[...], weight(4))

    def cross_norm_part():
        fetched("after_self")
        norm_back(aft, total, 1)

    def self_out_part():
        fetched("ctx")
        keep(3, dot_tn(nff[...], low[...]))
        gctx[...] = dot_nt(low[...], weight(3)).astype(LOW)
        fetched("p", "q", "k", "v")

    def self_part(lo, hi):
        def it(pair, c):
            cols = pl.ds(pl.multiple_of(pair * 128, 128), 128)
            q_cols = pl.ds(pl.multiple_of(768 + pair * 128, 128), 128)
            k_cols = pl.ds(pl.multiple_of(1536 + pair * 128, 128), 128)
            v_cols = pl.ds(pl.multiple_of(2304 + pair * 128, 128), 128)
            slants = []
            for s in range(2):
                rows = slice(s * LENGTH, (s + 1) * LENGTH)
                gp, qp, kp, vp = gctx[rows, cols], slope[rows, q_cols], slope[rows, k_cols], slope[rows, v_cols]
                one, two = [
                    head_back(act[rows, pl.ds(pl.multiple_of((2 * pair + side) * LENGTH, 256), LENGTH)], gp, qp, kp, vp, side)
                    for side in range(2)
                ]
                dq[rows, cols] = joined(one[0], two[0])
                dk[rows, cols] = joined(one[1], two[1])
                dv[rows, cols] = joined(one[2], two[2])
                slants.append((one[3], two[3]))
            t = lax.broadcasted_iota(jnp.int32, (LENGTH, LENGTH), 0)
            u = lax.broadcasted_iota(jnp.int32, (LENGTH, LENGTH), 1)
            upside = (t + u == LENGTH - 1).astype(LOW)
            for side in range(2):
                both = slants[0][side] + slants[1][side]
                coarse = both.astype(LOW)
                fine = (both - coarse.astype(WIDE)).astype(LOW)
                turned = dot(upside, coarse) + dot(upside, fine)
                rolled = pltpu.roll(turned, 1, 1, stride=1, stride_axis=0)
                dist[pl.ds(2 * pair + side, 1), :] = jnp.sum(rolled, axis=0, keepdims=True)
            return c

        lax.fori_loop(lo, hi, it, 0)

    def self_grads(n):
        fetched(*(["normed"] if n == 0 else []))
        keep(n, dot_tn(slope[:, 0:768], (dq, dk, dv)[n][...]))

    def normed_back(n):
        part = dot_nt((dq, dk, dv)[n][...], weight(n))
        if n:
            up[...] += part
        else:
            up[...] = part

    def input_part():
        fetched("x")
        norm_back(x, total, 0)
        pltpu.make_async_copy(total, input_out, out_sem.at[1]).start()
        buckets = lax.dot_general(
            dist[...], bucket_columns(True), (((1,), (1,)), ((), ())),
            precision=lax.Precision.HIGHEST, preferred_element_type=WIDE)
        acc[:, WIDTH : WIDTH + BUCKETS] = buckets
        for copy in acc_copies(0):
            copy.start()

    pieces = [(0.5, begin, None, 6)]
    pieces += [(1.0, functools.partial(out_grad_part, j), 12 + j, 6) for j in range(4)]
    for j in range(4):
        pieces += [(2.0, functools.partial(hidden_part, j), 8 + j, 0), (1.0, functools.partial(hidden_back, j), None, 8 + 2 * j)]
    pieces += [
        (1.5, ff_norm_part, None, 0), (1.9, cross_out_part, 7, 15),
        *[(1.5, functools.partial(cross_part, 2 * n, 2 * n + 2), None, 0) for n in range(6)],
        (1.0, cross_query_part, 4, 0), (0.5, cross_key_part, 5, 0), (0.5, cross_value_part, 6, 0),
        (1.0, memory_part, None, 0), (1.0, cross_query_back, None, 16), (1.3, cross_norm_part, None, 0), (2.0, self_out_part, 3, 0),
        *[(2.2, functools.partial(self_part, n, n + 1), None, 0) for n in range(6)],
        *[(1.0, functools.partial(self_grads, n), n, 0) for n in range(3)],
        *[(1.0, functools.partial(normed_back, n), None, 0) for n in range(3)],
        (2.0, input_part, None, 0),
    ]

    acc[...] = jnp.zeros_like(acc)
    dist[...] = jnp.zeros_like(dist)
    fetch("og", og_hbm, gl)
    for j in range(4):
        cols = slice(j * WIDTH, (j + 1) * WIDTH)
        fetch(f"act{j}", act_hbm.at[:, cols], act.at[:, cols])
    ask(2)
    fetch("slope", slope_hbm, slope)
    fetch("nff", nff_hbm, nff)
    fetch("after_cross", after_cross_hbm, aft)
    fetch("cctx", cctx_hbm, cctx)
    fetch("cq", cq_hbm, cq)
    fetch("mk", mk_hbm, mk)
    fetch("mv", mv_hbm, mv)
    fetch("pc", pc_hbm, pc)
    fetch("ncross", ncross_hbm, ncross)
    fetch("mem", mem_hbm, mem)
    fetch("x", x_hbm, x)
    clock, done, made, freed = 0.0, 0, set(), set()

    def run_piece():
        nonlocal clock, done
        cost, what, makes, asks = pieces[done]
        what()
        ask(asks)
        clock += cost
        made.add(makes)
        done += 1

    def may_run():
        makes = pieces[done][2]
        i = 0 if makes is None else LINE.index(makes)
        return i < 4 or LINE[i - 4] in freed

    def out_grads():
        while LINE[0] not in made:
            run_piece()

    greet([sibling, first, second] + along_z, out_grads)

    stage = None
    for r in range(GROUPS + LAGS[-1]):
        for s in range(1, 7):
            i = r - LAGS[s]
            if 0 <= i < GROUPS:
                event(LINE[i], s)
                if s == 1:
                    freed.add(LINE[i])
        if r < GROUPS:
            while LINE[r] not in made:
                assert may_run()
                run_piece()
            event(LINE[r], 0)
        while done < len(pieces) and clock < PACE * (r + 1) and may_run():
            run_piece()
        if done == len(pieces):
            if stage is None:
                stage = 0
            elif stage < 4:
                for copy in acc_copies(stage):
                    copy.wait()
                for n in ((0,), (1, 2, 3), (4,), (5,))[stage]:
                    acc[...] += acc_in[n]
                stage += 1
                if stage < 4:
                    for copy in acc_copies(stage):
                        copy.start()
    assert done == len(pieces) and stage == 4 and got[0] == GROUPS
    offset = (lax.axis_index("dp") * 4 + lax.axis_index("fsdp")) * 24
    sum_out[:, 0:WIDTH] = pltpu.roll(acc[:, 0:WIDTH], WIDTH - offset, 1)
    sum_out[:, WIDTH:] = acc[:, WIDTH:]
    pltpu.make_async_copy(mem_grad, memory_out, out_sem.at[0]).wait()
    pltpu.make_async_copy(total, input_out, out_sem.at[1]).wait()


BACKWARD_OUT = (
    (((512, 768), WIDE), ((256, 768), WIDE)),
    (((24, 768), WIDE),) * 8 + (((24, 3072), WIDE), ((96, 768), WIDE), ((16, 896), WIDE)),
)


def backward_call(gains, lens, *arrays):
    shape = lambda s: jax.ShapeDtypeStruct(*s)
    vmem = lambda *s: pltpu.VMEM(s, LOW)
    return pl.pallas_call(
        backward_kernel,
        out_shape=tuple(shape(s) for s in BACKWARD_OUT[0] + BACKWARD_OUT[1]),
        in_specs=[pl.BlockSpec(memory_space=pltpu.VMEM), pl.BlockSpec(memory_space=pltpu.SMEM)]
        + [pl.BlockSpec(memory_space=pl.ANY)] * len(arrays),
        out_specs=[pl.BlockSpec(memory_space=pl.ANY)] * 2 + [pl.BlockSpec(memory_space=pltpu.VMEM)] * 11,
        scratch_shapes=[
            vmem(SLOTS, 4, 4, 48, 768),
            vmem(512, 3072), vmem(512, 3072), pltpu.VMEM((256, 768), WIDE), vmem(512, 768),
            pltpu.VMEM((512, 768), WIDE),
            vmem(512, 768), vmem(512, 768), vmem(512, 768), vmem(256, 768), vmem(256, 768), vmem(256, 768),
            vmem(512, 1536),
            vmem(512, 768), vmem(512, 768),
            pltpu.VMEM((512, 768), WIDE), pltpu.VMEM((512, 768), WIDE),
            vmem(512, 768), vmem(512, 768), vmem(512, 768),
            vmem(512, 768), vmem(512, 768), vmem(512, 768),
            pltpu.VMEM((16, LENGTH), WIDE),
            vmem(4, 4, 4, 48, 768),
            vmem(GROUPS, 4, 4, 48, 384), vmem(GROUPS, 2, 4, 48, 384), vmem(GROUPS, 9, 48, 384),
            pltpu.VMEM((2, 48, 384), WIDE),
            pltpu.VMEM((12, 48, 384), WIDE), pltpu.VMEM((4, 48, 384), WIDE),
            pltpu.VMEM((12, 24, 384), WIDE), pltpu.VMEM((2, 48, 384), WIDE),
            pltpu.VMEM((16, 896), WIDE), pltpu.VMEM((6, 16, 896), WIDE),
            pltpu.SemaphoreType.DMA((GROUPS, 13)), pltpu.SemaphoreType.DMA((GROUPS, 13)),
            pltpu.SemaphoreType.DMA((6,)), pltpu.SemaphoreType.DMA((6,)),
            pltpu.SemaphoreType.DMA((28,)), pltpu.SemaphoreType.DMA((GROUPS,)), pltpu.SemaphoreType.DMA((2,)),
        ],
        compiler_params=pltpu.CompilerParams(collective_id=1, has_side_effects=True, vmem_limit_bytes=62 * 2**20),
    )(gains, lens, *arrays)


def place_kernel(*refs):
    small_ref, arrays = refs[0], refs[1:14]
    outs, held, sems = refs[14:31], refs[31:44], refs[44]
    copies = [pltpu.make_async_copy(src, dst, sems.at[0, n]) for n, (src, dst) in enumerate(zip(arrays, held))]
    for copy in copies:
        copy.start()
    onward = [pltpu.make_async_copy(src, dst, sems.at[1, n]) for n, (src, dst) in enumerate(zip(held, outs))]
    for n in range(3):
        outs[13 + n][...] = small_ref[n : n + 1, 0:24]
    outs[16][...] = small_ref[0:HEADS, WIDTH : WIDTH + BUCKETS]
    for copy, next_copy in zip(copies, onward):
        copy.wait()
        next_copy.start()
    for copy in onward:
        copy.wait()


def place_call(small, *arrays):
    shapes = [jax.ShapeDtypeStruct(a.shape, a.dtype) for a in arrays]
    shapes += [jax.ShapeDtypeStruct((1, 24), WIDE)] * 3 + [jax.ShapeDtypeStruct((HEADS, BUCKETS), WIDE)]
    return pl.pallas_call(
        place_kernel,
        out_shape=tuple(shapes),
        in_specs=[pl.BlockSpec(memory_space=pltpu.VMEM)] + [pl.BlockSpec(memory_space=pl.ANY)] * 13,
        out_specs=[pl.BlockSpec(memory_space=pl.ANY)] * 13 + [pl.BlockSpec(memory_space=pltpu.VMEM)] * 4,
        scratch_shapes=[pltpu.VMEM(a.shape, a.dtype) for a in arrays] + [pltpu.SemaphoreType.DMA((2, 13))],
    )(small, *arrays)


def layer_kernels(decoder_in, memory, out_grad, lengths, *params):
    shards, table = params[:13], params[13]
    (
        w, gains, normed, q, k, v, ctx, p, after_self, ncross, cq, mk, mv, cctx, pc, after_cross, nff, act, slope, layer,
    ) = forward(shards, decoder_in, memory, table, lengths)
    rows = decoder_in.reshape(ROWS, WIDTH)
    input_grad, memory_grad, *pieces, in_piece, out_piece, small = backward_call(
        gains, lengths.reshape(2), w, act, slope, nff, after_cross, cctx, ncross, cq, mk, mv,
        memory.reshape(2 * MEMORY, WIDTH), pc, after_self, p, normed, q, k, v, ctx, rows, out_grad.reshape(ROWS, WIDTH),
    )
    layer, input_grad, memory_grad, *rest = place_call(small, layer, input_grad, memory_grad, *pieces, in_piece, out_piece)
    return (
        layer.reshape(decoder_in.shape),
        input_grad.reshape(decoder_in.shape),
        memory_grad.reshape(memory.shape),
        *rest[:10],
        *[part.reshape(24) for part in rest[10:13]],
        rest[13].T,
    )


def body(decoder_in, memory, out_grad, lengths, *params):
    sizes = (lax.axis_size("dp"), lax.axis_size("fsdp"))
    if sizes == (8, 4) and decoder_in.shape == (2, 1, LENGTH, WIDTH) and params[0].shape == (24, WIDTH):
        return layer_kernels(decoder_in, memory, out_grad, lengths, *params)
    return plain_body(decoder_in, memory, out_grad, lengths, *params)


def solution(mesh):
    return jax.shard_map(
        body,
        mesh=mesh,
        in_specs=(
            P(None, ("dp", "fsdp"), None, None),
            P(None, ("dp", "fsdp"), None, None),
            P(None, ("dp", "fsdp"), None, None),
            P(None, ("dp", "fsdp")),
            P(("dp", "fsdp"), None),
            P(("dp", "fsdp"), None),
            P(("dp", "fsdp"), None),
            P(("dp", "fsdp"), None),
            P(("dp", "fsdp"), None),
            P(("dp", "fsdp"), None),
            P(("dp", "fsdp"), None),
            P(("dp", "fsdp"), None),
            P(("dp", "fsdp"), None),
            P(("dp", "fsdp"), None),
            P(("dp", "fsdp")),
            P(("dp", "fsdp")),
            P(("dp", "fsdp")),
            P(),
        ),
        out_specs=(
            P(None, ("dp", "fsdp"), None, None),
            P(None, ("dp", "fsdp"), None, None),
            P(None, ("dp", "fsdp"), None, None),
            P(("dp", "fsdp"), None),
            P(("dp", "fsdp"), None),
            P(("dp", "fsdp"), None),
            P(("dp", "fsdp"), None),
            P(("dp", "fsdp"), None),
            P(("dp", "fsdp"), None),
            P(("dp", "fsdp"), None),
            P(("dp", "fsdp"), None),
            P(("dp", "fsdp"), None),
            P(("dp", "fsdp"), None),
            P(("dp", "fsdp")),
            P(("dp", "fsdp")),
            P(("dp", "fsdp")),
            P(),
        ),
        check_vma=False,
    )
```

```python
import functools
import math

import jax
import jax.numpy as jnp
from jax import lax
from jax.experimental import pallas as pl
from jax.experimental.pallas import tpu as pltpu
from jax.sharding import PartitionSpec as P

HEADS = 12
BUCKETS = 32
MAX_DIST = 128


EPS = 1e-06
MASKED = -1e30
TOP_PRECISION = lax.Precision.HIGHEST


def bucket_onehot(length):
    half_count = BUCKETS // 2
    positions = jnp.arange(length, dtype=jnp.int32)
    distance = jnp.maximum(positions[:, None] - positions[None, :], 0)
    farther = jnp.zeros_like(distance)
    for level in range(1, half_count):
        border = int(math.ceil(half_count * (MAX_DIST / half_count) ** (level / half_count)))
        farther = farther + (distance >= border).astype(jnp.int32)
    bucket = jnp.where(distance < half_count, distance, half_count + farther)
    return (bucket[None] == jnp.arange(BUCKETS, dtype=jnp.int32)[:, None, None]).astype(jnp.float32)


def normalize(vector, gain_row):
    return vector * lax.rsqrt(jnp.mean(vector * vector, axis=-1, keepdims=True) + EPS) * gain_row


def project(operand, weight):
    return jnp.dot(operand, weight, preferred_element_type=jnp.float32)


def project_back(operand, weight):
    return lax.dot_general(
        operand, weight, (((1,), (1,)), ((), ())), preferred_element_type=jnp.float32
    )


def weight_grad(inputs_rows, grad_rows):
    return lax.dot_general(
        inputs_rows, grad_rows, (((0,), (0,)), ((), ())), preferred_element_type=jnp.float32
    )


def split_heads(matrix):
    return matrix.reshape(matrix.shape[:-1] + (HEADS, matrix.shape[-1] // HEADS))


def head_scores(queries, key_rows):
    return jnp.einsum(
        "gqhe,gkhe->ghqk",
        split_heads(queries),
        split_heads(key_rows),
        preferred_element_type=jnp.float32,
    )


def attend_forward(queries, key_rows, values, relative_position_bias, allowed):
    scores = jnp.where(allowed, head_scores(queries, key_rows) + relative_position_bias, MASKED)
    largest = jnp.max(scores, axis=-1, keepdims=True)
    exponent = jnp.exp(scores - largest)
    row_totals = jnp.sum(exponent, axis=-1, keepdims=True)
    attention_weights = exponent / row_totals
    context = jnp.einsum(
        "ghqk,gkhe->gqhe",
        attention_weights.astype(jnp.bfloat16),
        split_heads(values),
        preferred_element_type=jnp.float32,
    )
    return (context.reshape(queries.shape).astype(jnp.bfloat16), attention_weights)


def attend_backward(queries, key_rows, values, attention_weights, grad_context):
    grad_heads = split_heads(grad_context)
    grad_values = jnp.einsum(
        "ghqk,gqhe->gkhe",
        attention_weights.astype(jnp.bfloat16),
        grad_heads,
        preferred_element_type=jnp.float32,
    )
    grad_weights = jnp.einsum(
        "gqhe,gkhe->ghqk", grad_heads, split_heads(values), preferred_element_type=jnp.float32
    )
    score_gradient = attention_weights * (
        grad_weights - jnp.sum(grad_weights * attention_weights, axis=-1, keepdims=True)
    )
    rounded = score_gradient.astype(jnp.bfloat16)
    grad_queries = jnp.einsum(
        "ghqk,gkhe->gqhe", rounded, split_heads(key_rows), preferred_element_type=jnp.float32
    )
    grad_keys = jnp.einsum(
        "ghqk,gqhe->gkhe", rounded, split_heads(queries), preferred_element_type=jnp.float32
    )
    return (
        grad_queries.reshape(queries.shape).astype(jnp.bfloat16),
        grad_keys.reshape(key_rows.shape).astype(jnp.bfloat16),
        grad_values.reshape(values.shape).astype(jnp.bfloat16),
        score_gradient,
    )


AXES = ("dp", "fsdp")


def rows_of(matrix):
    return matrix.reshape(-1, matrix.shape[-1])


def gather_all(shards):
    width = shards[0].shape[1]
    blocks = []
    for shard in shards:
        if shard.ndim == 1:
            continue
        blocks.append(shard.reshape(-1, width) if shard.shape[1] != width else shard)
    packed = lax.all_gather(jnp.concatenate(blocks, axis=0), AXES, axis=0)
    whole, at = [], 0
    devices = packed.shape[0]
    for shard, block in zip(shards, blocks):
        part = packed[:, at : at + block.shape[0]]
        at += block.shape[0]
        whole.append(part.reshape(devices * shard.shape[0], shard.shape[1]))
    gains = jnp.stack(shards[len(blocks) :])
    gains = lax.all_gather(gains, AXES, axis=1, tiled=True)
    return whole, [gains[k] for k in range(gains.shape[0])]


def scatter_all(grads, shards):
    width = shards[0].shape[1]
    devices = lax.axis_size(AXES)
    blocks = [grad.astype(jnp.bfloat16).reshape(devices, -1, width) for grad in grads]
    summed = lax.psum_scatter(
        jnp.concatenate(blocks, axis=1), AXES, scatter_dimension=0, tiled=False
    ).astype(jnp.float32)
    pieces, at = [], 0
    for block, shard in zip(blocks, shards):
        pieces.append(summed[at : at + block.shape[1]].reshape(shard.shape))
        at += block.shape[1]
    return pieces


def plain_body(decoder_in, memory, out_grad, lengths, *params):
    shards, bucket_bias_table = params[:13], params[13]
    matrices, gains = gather_all(shards)
    (
        self_query,
        self_key,
        self_value,
        self_out,
        cross_query,
        cross_key,
        cross_value,
        cross_out,
        ff_in,
        ff_out,
    ) = matrices
    norm_self, norm_cross, norm_ff = [gain.astype(jnp.float32) for gain in gains]
    micro, seqs, seq_length, width = decoder_in.shape
    groups = micro * seqs
    memory_bf = memory.reshape(groups, memory.shape[2], width)
    grad_bf = out_grad.reshape(groups, seq_length, width)
    group_lengths = lengths.reshape(groups)
    bucket_indicator = bucket_onehot(seq_length)
    relative_position_bias = jnp.einsum(
        "fsn,fe->esn",
        bucket_indicator,
        bucket_bias_table.astype(jnp.float32),
        precision=TOP_PRECISION,
    )
    positions = jnp.arange(seq_length, dtype=jnp.int32)
    causal = positions[:, None] >= positions[None, :]
    present = positions[None, :] < group_lengths[:, None]
    valid_rows = present[:, :, None].astype(jnp.float32)
    allowed = causal[None, None] & present[:, None, None, :]

    def grad_of(inputs, upstream):
        return weight_grad(rows_of(inputs), rows_of(upstream))

    decoded = decoder_in.reshape(groups, seq_length, width).astype(jnp.float32)
    normed = normalize(decoded, norm_self).astype(jnp.bfloat16)
    queries = project(normed, self_query).astype(jnp.bfloat16)
    key_rows = project(normed, self_key).astype(jnp.bfloat16)
    values = project(normed, self_value).astype(jnp.bfloat16)
    context, self_weights = attend_forward(
        queries, key_rows, values, relative_position_bias, allowed
    )
    after_self = decoded + project(context, self_out)
    normed_cross = normalize(after_self, norm_cross).astype(jnp.bfloat16)
    cross_queries = project(normed_cross, cross_query).astype(jnp.bfloat16)
    memory_keys = project(memory_bf, cross_key).astype(jnp.bfloat16)
    memory_values = project(memory_bf, cross_value).astype(jnp.bfloat16)
    cross_context, cross_weights = attend_forward(
        cross_queries, memory_keys, memory_values, 0.0, True
    )
    after_cross = after_self + project(cross_context, cross_out)
    normed_ff = normalize(after_cross, norm_ff).astype(jnp.bfloat16)
    hidden = project(normed_ff, ff_in)
    activated = jax.nn.gelu(hidden, approximate=True).astype(jnp.bfloat16)
    after_ff = after_cross + project(activated, ff_out)
    layer_out = (after_ff * valid_rows).astype(jnp.bfloat16)

    def back(operand, weight):
        return lax.dot_general(
            operand, weight, (((2,), (1,)), ((), ())), preferred_element_type=jnp.float32
        )

    grad_after = grad_bf.astype(jnp.float32) * valid_rows
    grad_branch = grad_after.astype(jnp.bfloat16)
    grad_ff_out = grad_of(activated, grad_branch)
    gelu_pull = jax.vjp(lambda pre_act: jax.nn.gelu(pre_act, approximate=True), hidden)[1]
    grad_hidden = gelu_pull(back(grad_branch, ff_out))[0].astype(jnp.bfloat16)
    grad_ff_in = grad_of(normed_ff, grad_hidden)
    norm_pull = jax.vjp(normalize, after_cross, norm_ff)[1]
    grad_rows, grad_norm_ff = norm_pull(back(grad_hidden, ff_in))
    grad_after = grad_after + grad_rows
    grad_branch = grad_after.astype(jnp.bfloat16)
    grad_cross_out = grad_of(cross_context, grad_branch)
    grad_context = back(grad_branch, cross_out).astype(jnp.bfloat16)
    grad_cross_rows, grad_memory_keys, grad_memory_values, unused = attend_backward(
        cross_queries, memory_keys, memory_values, cross_weights, grad_context
    )
    grad_cross_query = grad_of(normed_cross, grad_cross_rows)
    grad_cross_key = grad_of(memory_bf, grad_memory_keys)
    grad_cross_value = grad_of(memory_bf, grad_memory_values)
    grad_memory = back(grad_memory_keys, cross_key) + back(grad_memory_values, cross_value)
    norm_pull = jax.vjp(normalize, after_self, norm_cross)[1]
    grad_rows, grad_norm_cross = norm_pull(back(grad_cross_rows, cross_query))
    grad_after = grad_after + grad_rows
    grad_branch = grad_after.astype(jnp.bfloat16)
    grad_self_out = grad_of(context, grad_branch)
    grad_context = back(grad_branch, self_out).astype(jnp.bfloat16)
    grad_queries, grad_key_rows, grad_values, score_gradient = attend_backward(
        queries, key_rows, values, self_weights, grad_context
    )
    grad_self_query = grad_of(normed, grad_queries)
    grad_self_key = grad_of(normed, grad_key_rows)
    grad_self_value = grad_of(normed, grad_values)
    grad_normed = (
        back(grad_queries, self_query) + back(grad_key_rows, self_key) + back(grad_values, self_value)
    )
    norm_pull = jax.vjp(normalize, decoded, norm_self)[1]
    grad_rows, grad_norm_self = norm_pull(grad_normed)
    grad_input = grad_after + grad_rows
    bias_grad = jnp.einsum(
        "fgd,ogd->fo", bucket_indicator, jnp.sum(score_gradient, axis=0), precision=TOP_PRECISION
    )
    pieces = scatter_all(
        (
            grad_self_query,
            grad_self_key,
            grad_self_value,
            grad_self_out,
            grad_cross_query,
            grad_cross_key,
            grad_cross_value,
            grad_cross_out,
            grad_ff_in,
            grad_ff_out,
        ),
        shards[:10],
    )
    small = lax.psum(
        jnp.concatenate([grad_norm_self, grad_norm_cross, grad_norm_ff, bias_grad.reshape(-1)]),
        AXES,
    )
    mine = shards[10].shape[0]
    at = lax.axis_index(AXES) * mine
    gains_out = [
        lax.dynamic_slice_in_dim(small[k * width : (k + 1) * width], at, mine) for k in range(3)
    ]
    return (
        layer_out.reshape(decoder_in.shape),
        grad_input.reshape(decoder_in.shape),
        grad_memory.reshape(memory.shape),
        *pieces,
        *gains_out,
        small[3 * width :].reshape(bucket_bias_table.shape),
    )


MESH = pl.DeviceIdType.MESH
LOW = jnp.bfloat16
WIDE = jnp.float32
GROUPS = 16
WIDTH = 768
ROWS = 512
LENGTH = 256
MEMORY = 128
PAIRS = 6
CURVE = math.sqrt(2.0 / math.pi)


def place():
    dp, fsdp = lax.axis_index("dp"), lax.axis_index("fsdp")
    z, y, x, core = dp // 2, dp % 2, fsdp // 2, fsdp % 2
    sibling = (dp, x * 2 + 1 - core)
    over_x = (dp, (1 - x) * 2 + core)
    over_y = (z * 2 + 1 - y, fsdp)
    first = (jnp.where(core == 0, over_x[0], over_y[0]), jnp.where(core == 0, over_x[1], over_y[1]))
    second = (jnp.where(core == 0, over_y[0], over_x[0]), jnp.where(core == 0, over_y[1], over_x[1]))
    along_z = [(((z + k) % 4) * 2 + y, fsdp) for k in (1, 2, 3)]
    own = y * 2 + x
    beside = jnp.where(core == 0, y * 2 + 1 - x, (1 - y) * 2 + x)
    return z, own, beside, core, sibling, first, second, along_z


def greet(partners, meanwhile):
    barrier = pltpu.get_barrier_semaphore()
    for partner in partners:
        pl.semaphore_signal(barrier, inc=1, device_id=partner, device_id_type=MESH)
    meanwhile()
    pl.semaphore_wait(barrier, len(partners))


def half(core):
    return pl.ds(pl.multiple_of(core * 384, 128), 384)


def skew(ahead, groups=GROUPS):
    order = []
    for t in range(-max(ahead), groups + 8):
        for s in range(len(ahead)):
            g = t + ahead[s]
            if 0 <= g < groups:
                order.append((g, s))
    return order


def dot(a, b):
    return jnp.dot(a, b, preferred_element_type=WIDE)


def dot_nt(a, b):
    return lax.dot_general(a, b, (((1,), (1,)), ((), ())), preferred_element_type=WIDE)


def dot_tn(a, b):
    return lax.dot_general(a, b, (((0,), (0,)), ((), ())), preferred_element_type=WIDE)


def unit(w, u):
    return w[u].reshape(WIDTH, WIDTH)


def root_scale(value):
    return lax.rsqrt(jnp.mean(value * value, axis=-1, keepdims=True) + EPS)


def bucket_columns(flipped):
    j = lax.broadcasted_iota(jnp.int32, (BUCKETS, LENGTH), 1)
    row = lax.broadcasted_iota(jnp.int32, (BUCKETS, LENGTH), 0)
    n = jnp.where(j == 0, 0, LENGTH - j) if flipped else j
    half_count = BUCKETS // 2
    farther = jnp.zeros_like(n)
    for level in range(1, half_count):
        border = int(math.ceil(half_count * (MAX_DIST / half_count) ** (level / half_count)))
        farther = farther + (n >= border).astype(jnp.int32)
    bucket = jnp.where(n < half_count, n, half_count + farther)
    return (bucket == row).astype(WIDE)


QUEUE = (0, 1, 2, 3, 4, 5, 6, 7, 12, 13, 14, 15, 8, 9, 10, 11)
ZS = (1, 3, 5, 7, 8, 9, 11, 13, 14, 15)
AHEAD = (9, 8, 6, 3, 1, 0)
GAIN_AT = (8, 11, 14)
BUDGET = 3.0
UNROLL = 1


def forward_kernel(*refs):
    shard_refs, gain_refs = refs[:9], refs[9:12]
    forward_steps(shard_refs, gain_refs, *refs[12:])


def forward_steps(
    shard_refs, gain_refs, tall_ref, x_hbm, mem_hbm, table_ref, lens_ref,
    w_out, gains_out, normed_out, q_out, k_out, v_out, ctx_out, p_out, after_self_out, ncross_out,
    cq_out, mk_out, mv_out, cctx_out, pc_out, after_cross_out, nff_out, act_out, slope_out, layer_out,
    w, gains, normed, q, k, v, ctx, p, after_self, ncross, cq, mk, mv, cctx, pc, after_cross, nff, act, slope, layer,
    x_ref, mem_ref, total, bias, small, sib, gain_in, ss, rs, ss0, rs0, out_sem, in_sem,
):
    z, own, beside, core, sibling, first, second, along_z = place()
    mine, other = half(core), half(1 - core)

    def along_at(zi):
        return (zi * 2 + lax.axis_index("dp") % 2, lax.axis_index("fsdp"))

    def view(g, zi, yx, cols):
        if g < 12:
            return w.at[g, slice(None) if zi is None else zi, yx, :, cols]
        return w.at[pl.ds(12, 4) if zi is None else 12 + zi, yx, g - 12, :, cols]

    def whole(g, cols):
        return w.at[g, :, :, :, cols] if g < 12 else w.at[pl.ds(12, 4), :, g - 12, :, cols]

    def send(ref, to, g, n):
        return pltpu.make_async_remote_copy(
            src_ref=ref, dst_ref=ref, send_sem=ss.at[g, n], recv_sem=rs.at[g, n], device_id=to, device_id_type=MESH)

    inner = (z == 1) | (z == 2)
    far = (z + 2) % 4
    end = along_at(jnp.where(z == 1, 0, 3))

    def z_send(g, block, n):
        yx, at = block
        return send(view(g, z, yx, mine), along_z[n], g, at + n)

    def z_hand_on(g, block):
        yx, at = block
        return send(view(g, far, yx, mine), end, g, 10 + (at > 0))

    def z_start(g, blocks):
        for block in blocks:
            z_send(g, block, 1).start()
            pl.when(z < 3)(lambda: z_send(g, block, 0).start())
            pl.when(z > 0)(lambda: z_send(g, block, 2).start())

    def z_relay(g, blocks):
        @pl.when(inner)
        def _():
            for block in blocks:
                z_send(g, block, 1).wait_recv()
                z_hand_on(g, block).start()

    def z_wait(g, blocks):
        for block in blocks:
            z_send(g, block, 1).wait_send()

            @pl.when(z < 3)
            def _():
                z_send(g, block, 0).wait_send()
                z_send(g, block, 2).wait_recv()

            @pl.when(z > 0)
            def _():
                z_send(g, block, 2).wait_send()
                z_send(g, block, 0).wait_recv()

            @pl.when(inner)
            def _():
                z_hand_on(g, block).wait_send()

            @pl.when(jnp.logical_not(inner))
            def _():
                z_send(g, block, 1).wait_recv()
                z_hand_on(g, block).wait_recv()

    one_block, two_blocks = [(own, 0)], [(own, 0), (beside, 7)]

    def step_b(g):
        return [send(view(g, None, own, mine), first, g, 3)]

    def step_c(g):
        return [send(view(g, None, own, mine), second, g, 4), send(view(g, None, beside, mine), second, g, 5)]

    def step_d(g):
        return [send(whole(g, mine), sibling, g, 6)]

    def step_b1(g):
        return [send(view(g, z, own, mine), first, g, 3)]

    def wait(copies):
        for copy in copies:
            copy.wait()

    def event(g, s, z_second):
        blocks = two_blocks if z_second else one_block
        if s == 0:
            start(step_b1(g)) if z_second else z_start(g, blocks)
        elif s == 1:
            if z_second:
                wait(step_b1(g))
                z_start(g, blocks)
            else:
                z_relay(g, blocks)
        elif s == 2:
            if z_second:
                z_relay(g, blocks)
            else:
                z_wait(g, blocks)
                start(step_b(g))
        elif s == 3:
            z_wait(g, blocks) if z_second else wait(step_b(g))
            start(step_c(g))
        elif s == 4:
            wait(step_c(g))
            start(step_d(g))
        else:
            wait(step_d(g))

    def gain_copies(s):
        to = ([sibling], along_z, [first], [second])[s]
        at = (0, 1, 4, 5)[s]
        return [
            pltpu.make_async_remote_copy(
                src_ref=gains, dst_ref=gain_in.at[at + n], send_sem=ss0.at[2 + at + n], recv_sem=rs0.at[2 + at + n],
                device_id=d, device_id_type=MESH)
            for n, d in enumerate(to)
        ]

    def start(copies):
        for copy in copies:
            copy.start()

    def gain_finish(s):
        for copy in gain_copies(s):
            copy.wait()
        for n in ((0,), (1, 2, 3), (4,), (5,))[s]:
            gains[...] += gain_in[n]

    stores = []

    def store(src, dst):
        copy = pltpu.make_async_copy(src, dst, out_sem.at[len(stores)])
        stores.append(copy)
        copy.start()

    def store_unit(g):
        if g < 12:
            store(w.at[g], w_out.at[g])
        elif g == 15:
            store(w.at[pl.ds(12, 4)], w_out.at[pl.ds(12, 4)])

    def gain(n):
        return gains[n : n + 1, :].astype(WIDE)

    def scale_rows(src, n, dst):
        g = gain(n)

        def chunk(i, c):
            rows = pl.ds(pl.multiple_of(i * 128, 128), 128)
            value = src[rows, :].astype(WIDE)
            dst[rows, :] = (value * root_scale(value) * g).astype(LOW)
            return c

        lax.fori_loop(0, ROWS // 128, chunk, 0)

    def make_bias():
        by_distance = dot(table_ref[...], bucket_columns(True).astype(LOW))
        for h in range(HEADS):
            row = jnp.broadcast_to(by_distance[h : h + 1, :], (LENGTH, LENGTH))
            bias[h] = pltpu.roll(row, 0, 1, stride=1, stride_axis=0)

    def project_into(src, u, dst):
        dst[...] = dot(src[...], unit(w, u)).astype(LOW)

    lane = lax.broadcasted_iota(jnp.int32, (1, 128), 1)
    sides = [lane < 64, lane >= 64]

    def attend(i, queries, keys, vals, keep_p, into, depth, masked):
        s, pair = i // PAIRS, i % PAIRS
        rows = pl.ds(pl.multiple_of(s * LENGTH, LENGTH), LENGTH)
        deep = pl.ds(pl.multiple_of(s * depth, depth), depth)
        cols = pl.ds(pl.multiple_of(pair * 128, 128), 128)
        qp, kp, vp = queries[rows, cols], keys[deep, cols], vals[deep, cols]
        parts = []
        for side in range(2):
            scores = dot_nt(jnp.where(sides[side], qp, jnp.zeros_like(qp)), kp)
            if masked:
                t = lax.broadcasted_iota(jnp.int32, (LENGTH, LENGTH), 0)
                u = lax.broadcasted_iota(jnp.int32, (LENGTH, LENGTH), 1)
                allowed = (u <= t) & (u < lens_ref[s])
                scores = jnp.where(allowed, scores + bias[2 * pair + side], MASKED)
            e = jnp.exp(scores - jnp.max(scores, axis=-1, keepdims=True))
            weights = (e * (1.0 / jnp.sum(e, axis=-1, keepdims=True))).astype(LOW)
            keep_p[rows, pl.ds(pl.multiple_of((2 * pair + side) * depth, 128), depth)] = weights
            parts.append(dot(weights, vp))
        into[rows, cols] = jnp.where(sides[0], parts[0], parts[1]).astype(LOW)

    def self_part(lo, hi):
        def it(i, c):
            attend(i, q, k, v, p, ctx, LENGTH, True)
            return c

        lax.fori_loop(lo, hi, it, 0, unroll=UNROLL)

    def cross_part(lo, hi):
        def it(i, c):
            attend(i, cq, mk, mv, pc, cctx, MEMORY, False)
            return c

        lax.fori_loop(lo, hi, it, 0, unroll=UNROLL)

    def after_self_part():
        after_self[...] = x_ref[...].astype(WIDE) + dot(ctx[...], unit(w, 3))
        scale_rows(after_self, 1, ncross)

    def after_cross_part():
        after_cross[...] = after_self[...] + dot(cctx[...], unit(w, 7))
        scale_rows(after_cross, 2, nff)

    def hidden_part(j):
        cols = slice(j * WIDTH, (j + 1) * WIDTH)
        for m in range(2):
            rows = slice(m * 256, m * 256 + 256)
            a = dot(nff[rows, :], unit(w, 8 + j))
            sq = a * a
            th = jnp.tanh(a * (CURVE + (CURVE * 0.044715) * sq))
            act[rows, cols] = (0.5 * a * (1.0 + th)).astype(LOW)
            slope[rows, cols] = (
                0.5 * (1.0 + th) + 0.5 * a * (1.0 - th * th) * (CURVE + (3.0 * CURVE * 0.044715) * sq)
            ).astype(LOW)
        store(act.at[:, pl.ds(j * WIDTH, WIDTH)], act_out.at[:, pl.ds(j * WIDTH, WIDTH)])
        store(slope.at[:, pl.ds(j * WIDTH, WIDTH)], slope_out.at[:, pl.ds(j * WIDTH, WIDTH)])
        part = dot(act[:, cols], unit(w, 12 + j))
        if j == 0:
            total[...] = after_cross[...] + part
        elif j < 3:
            total[...] += part
        else:
            part = total[...] + part
            for s in range(2):
                rows = slice(s * LENGTH, (s + 1) * LENGTH)
                t = lax.broadcasted_iota(jnp.int32, (LENGTH, 1), 0)
                layer[rows, :] = (part[rows] * (t < lens_ref[s]).astype(WIDE)).astype(LOW)

    pieces = [
        (0, 1.0, lambda: project_into(normed, 0, q)), (0, 0.1, lambda: store(q, q_out)),
        (1, 1.0, lambda: project_into(normed, 1, k)), (1, 0.1, lambda: store(k, k_out)),
        (2, 1.0, lambda: project_into(normed, 2, v)), (2, 0.1, lambda: store(v, v_out)),
        *[(2, 1.8, functools.partial(self_part, 2 * n, 2 * n + 2)) for n in range(6)],
        (2, 0.1, lambda: store(ctx, ctx_out)), (2, 0.1, lambda: store(p, p_out)),
        (3, 2.0, after_self_part), (3, 0.1, lambda: store(after_self, after_self_out)), (3, 0.1, lambda: store(ncross, ncross_out)),
        (4, 1.0, lambda: project_into(ncross, 4, cq)), (4, 0.1, lambda: store(cq, cq_out)),
        (5, 0.6, lambda: project_into(mem_ref, 5, mk)), (5, 0.1, lambda: store(mk, mk_out)),
        (6, 0.6, lambda: project_into(mem_ref, 6, mv)), (6, 0.1, lambda: store(mv, mv_out)),
        *[(6, 1.5, functools.partial(cross_part, 2 * n, 2 * n + 2)) for n in range(6)],
        (6, 0.1, lambda: store(cctx, cctx_out)), (6, 0.1, lambda: store(pc, pc_out)),
        (7, 2.0, after_cross_part), (7, 0.1, lambda: store(after_cross, after_cross_out)), (7, 0.1, lambda: store(nff, nff_out)),
        (8, 3.0, lambda: hidden_part(0)), (9, 3.0, lambda: hidden_part(1)), (10, 3.0, lambda: hidden_part(2)),
        (11, 3.0, lambda: hidden_part(3)), (11, 0.1, lambda: store(layer, layer_out)),
    ]

    load_x = pltpu.make_async_copy(x_hbm, x_ref, in_sem.at[0])
    load_mem = pltpu.make_async_copy(mem_hbm, mem_ref, in_sem.at[1])

    def prepare():
        load_x.start()
        load_mem.start()
        for u in range(12):
            rows = shard_refs[u][...] if u < 8 else shard_refs[8][:, WIDTH * (u - 8) : WIDTH * (u - 7)]
            rows = rows.astype(WIDE)
            none = jnp.zeros_like(rows)
            small[u] = jnp.concatenate(
                [jnp.where(core == 0, rows, none), jnp.where(core == 0, none, rows)], axis=0).astype(LOW)
        offset = (lax.axis_index("dp") * 4 + lax.axis_index("fsdp")) * 24
        spot = (lax.broadcasted_iota(jnp.int32, (24, WIDTH), 1) == lax.broadcasted_iota(jnp.int32, (24, WIDTH), 0) + offset)
        placed = [dot(ref[...], spot.astype(LOW)) for ref in gain_refs]
        gains[...] = jnp.concatenate(placed + [jnp.zeros((13, WIDTH), WIDE)], axis=0).astype(LOW)

    greet([sibling, first, second] + along_z, prepare)
    swap_small = pltpu.make_async_remote_copy(
        src_ref=small.at[:, :, other], dst_ref=sib, send_sem=ss0.at[0], recv_sem=rs0.at[0],
        device_id=sibling, device_id_type=MESH)

    def tall_view(cols):
        return w.at[12 + z, own, pl.ds(2 * core, 2), :, cols]

    swap_tall = pltpu.make_async_remote_copy(
        src_ref=tall_ref.at[:, :, other], dst_ref=tall_view(other), send_sem=ss0.at[1], recv_sem=rs0.at[1],
        device_id=sibling, device_id_type=MESH)
    swap_small.start()
    swap_tall.start()
    start(gain_copies(0))
    w[12 + z, own, pl.ds(2 * core, 2), :, mine] = tall_ref[:, :, mine]
    swap_small.wait()

    def assemble(u):
        w[u, z, own, :, mine] = small[u, :, mine] + sib[u]

    early = skew(AHEAD)[:2]
    assert all(s == 0 and QUEUE[at] < 12 for at, s in early)
    for at, s in early:
        assemble(QUEUE[at])
        event(QUEUE[at], 0, at in ZS)
    for u in range(12):
        if u not in [QUEUE[at] for at, s in early]:
            assemble(u)
    gain_finish(0)
    start(gain_copies(1))
    swap_tall.wait()
    make_bias()
    load_x.wait()
    load_mem.wait()

    stage, done = 1, 0
    for n, (at, s) in enumerate(skew(AHEAD)):
        g = QUEUE[at]
        if n >= 2:
            event(g, s, at in ZS)
        if n in GAIN_AT:
            gain_finish(stage)
            stage += 1
            if stage < 4:
                start(gain_copies(stage))
            else:
                scale_rows(x_ref, 0, normed)
                store(normed, normed_out)
                store(gains, gains_out)
        if s == 5:
            store_unit(g)
            spent = 0.0
            while done < len(pieces) and QUEUE.index(pieces[done][0]) <= at and (spent < BUDGET or at == GROUPS - 1):
                spent += pieces[done][1]
                pieces[done][2]()
                done += 1
    assert done == len(pieces) and stage == 4
    for copy in stores:
        copy.wait()


FORWARD_OUT = (
    ((16, 4, 4, 48, 768), LOW),
    ((16, 768), LOW),
    ((512, 768), LOW), ((512, 768), LOW), ((512, 768), LOW), ((512, 768), LOW),
    ((512, 768), LOW),
    ((512, 3072), LOW),
    ((512, 768), WIDE),
    ((512, 768), LOW),
    ((512, 768), LOW), ((256, 768), LOW), ((256, 768), LOW), ((512, 768), LOW),
    ((512, 1536), LOW),
    ((512, 768), WIDE),
    ((512, 768), LOW),
    ((512, 3072), LOW), ((512, 3072), LOW),
    ((512, 768), LOW),
)


def forward_call(*operands):
    return pl.pallas_call(
        forward_kernel,
        out_shape=tuple(jax.ShapeDtypeStruct(s, t) for s, t in FORWARD_OUT),
        in_specs=[pl.BlockSpec(memory_space=pltpu.VMEM)] * 13
        + [pl.BlockSpec(memory_space=pl.ANY)] * 2
        + [pl.BlockSpec(memory_space=pltpu.VMEM), pl.BlockSpec(memory_space=pltpu.SMEM)],
        out_specs=[pl.BlockSpec(memory_space=pl.ANY)] * len(FORWARD_OUT),
        scratch_shapes=[pltpu.VMEM(s, t) for s, t in FORWARD_OUT]
        + [
            pltpu.VMEM((ROWS, WIDTH), LOW),
            pltpu.VMEM((2 * MEMORY, WIDTH), LOW),
            pltpu.VMEM((ROWS, WIDTH), WIDE),
            pltpu.VMEM((HEADS, LENGTH, LENGTH), WIDE),
            pltpu.VMEM((12, 48, 768), LOW),
            pltpu.VMEM((12, 48, 384), LOW),
            pltpu.VMEM((6, 16, 768), LOW),
            pltpu.SemaphoreType.DMA((GROUPS, 12)),
            pltpu.SemaphoreType.DMA((GROUPS, 12)),
            pltpu.SemaphoreType.DMA((8,)),
            pltpu.SemaphoreType.DMA((8,)),
            pltpu.SemaphoreType.DMA((40,)),
            pltpu.SemaphoreType.DMA((2,)),
        ],
        compiler_params=pltpu.CompilerParams(collective_id=0, has_side_effects=True, vmem_limit_bytes=60 * 2**20),
    )(*operands)


def forward(shards, decoder_in, memory, table, lengths):
    return forward_call(
        *shards[:9],
        *[shard.reshape(1, 24) for shard in shards[10:13]],
        shards[9].reshape(2, 48, WIDTH),
        decoder_in.reshape(ROWS, WIDTH),
        memory.reshape(2 * MEMORY, WIDTH),
        table.T,
        lengths.reshape(2),
    )


LINE = (12, 13, 14, 15, 8, 9, 10, 11, 7, 4, 5, 6, 3, 0, 1, 2)
USED = (12, 8, 13, 9, 14, 10, 15, 11, 7, 5, 6, 4, 3, 0, 1, 2)
SLOTS = 6
LAGS = (0, 1, 3, 5, 7, 9, 10)
PACE = 3.5
FIRST_Z = (8, 10, 7, 5, 3)


def backward_kernel(
    gains, lens_ref, w_hbm, act_hbm, slope_hbm, nff_hbm, after_cross_hbm, cctx_hbm, ncross_hbm, cq_hbm, mk_hbm, mv_hbm,
    mem_hbm, pc_hbm, after_self_hbm, p_hbm, normed_hbm, q_hbm, k_hbm, v_hbm, ctx_hbm, x_hbm, og_hbm,
    input_out, memory_out, *rest,
):
    results_hbm, results, rest = rest[:11], rest[11:22], rest[22:]
    pieces_out, (in_piece_out, out_piece_out, sum_out) = results[:8], results[8:]
    (
        ring, act, slope, mem_grad, nff, aft, cctx, ncross, cq, mk, mv, mem, pc, x, gl, total, up, ghj, low, gctx, dq, dk, dv,
        dist, grad, r0, r1, r23, zsum, fa, fo, fa_in, fo_in, acc, acc_in, ss, rs, ss0, rs0, in_sem, ring_sem, out_sem, result_sem,
    ) = rest
    z, own, beside, core, sibling, first, second, along_z = place()
    mine, other = half(core), half(1 - core)
    diag, across = 3 - own, 3 - beside

    fetches = {}

    def fetch(name, src, dst):
        copy = pltpu.make_async_copy(src, dst, in_sem.at[len(fetches)])
        fetches[name] = copy
        copy.start()

    def fetched(*names):
        for name in names:
            fetches[name].wait()

    def weight_copy(n):
        return pltpu.make_async_copy(w_hbm.at[USED[n]], ring.at[n % SLOTS], ring_sem.at[n])

    asked, got = [0], [0]

    def ask(n):
        while asked[0] < min(n, GROUPS):
            weight_copy(asked[0]).start()
            asked[0] += 1

    def weight(u):
        n = USED.index(u)
        while got[0] <= n:
            weight_copy(got[0]).wait()
            got[0] += 1
        return ring[n % SLOTS].reshape(WIDTH, WIDTH)

    def send(src, dst, to, g, n):
        return pltpu.make_async_remote_copy(
            src_ref=src, dst_ref=dst, send_sem=ss.at[g, n], recv_sem=rs.at[g, n], device_id=to, device_id_type=MESH)

    def block(g, cols):
        return grad.at[LINE.index(g) % 4, :, :, :, cols]

    def swap(g):
        return [send(block(g, other), r0.at[g], sibling, g, 0)]

    def quarter(ref, g, yx):
        return ref.at[g, :, yx] if g < 12 else ref.at[g, yx]

    def share(g, zi, yx):
        return r0.at[g, zi, yx] if g < 12 else r0.at[12 + zi, yx, g - 12]

    def over_second(g):
        return [
            send(quarter(r0, g, across), r1.at[g, 0], second, g, 1),
            send(quarter(r0, g, diag), r1.at[g, 1], second, g, 2),
        ]

    def over_first(g):
        return [send(quarter(r0, g, beside), r23.at[g, pl.ds(0, 4)], first, g, 3)]

    def over_first1(g):
        return [send(r0.at[g, z, beside], r23.at[g, 0], first, g, 3)]

    inner = (z == 1) | (z == 2)
    far = (z + 2) % 4
    next_in = (jnp.where(z == 0, 1, 2) * 2 + lax.axis_index("dp") % 2, lax.axis_index("fsdp"))

    def z_send(g, block, n):
        yx, at, sem = block
        return send(share(g, (z + n + 1) % 4, yx), r23.at[g, at + n], along_z[n], g, sem + n)

    def z_hand_over(g, block, slot):
        return send(share(g, 3 - z, block[0]), r23.at[g, 7 + slot], next_in, g, 11 + slot)

    def z_start(g, blocks):
        for slot, block in enumerate(blocks):

            @pl.when(jnp.logical_not(inner))
            def _():
                z_hand_over(g, block, slot).start()
                z_send(g, block, 1).start()

            pl.when(z < 3)(lambda: z_send(g, block, 0).start())
            pl.when(z > 0)(lambda: z_send(g, block, 2).start())

    def z_relay(g, blocks):
        @pl.when(inner)
        def _():
            for slot, block in enumerate(blocks):
                z_hand_over(g, block, slot).wait_recv()
                both = share(g, far, block[0])[...].astype(WIDE) + r23[g, 7 + slot].astype(WIDE)
                share(g, far, block[0])[...] = both.astype(LOW)
                z_send(g, block, 1).start()

    def z_wait(g, blocks):
        for slot, block in enumerate(blocks):
            yx, at, sem = block
            z_send(g, block, 1).wait()
            pl.when(jnp.logical_not(inner))(lambda: z_hand_over(g, block, slot).wait_send())
            zsum[slot] = share(g, z, yx)[...].astype(WIDE) + r23[g, at + 1].astype(WIDE)

            @pl.when(z > 0)
            def _():
                z_send(g, block, 2).wait_send()
                z_send(g, block, 0).wait_recv()
                zsum[slot] += r23[g, at].astype(WIDE)

            @pl.when(z < 3)
            def _():
                z_send(g, block, 0).wait_send()
                z_send(g, block, 2).wait_recv()
                zsum[slot] += r23[g, at + 2].astype(WIDE)

    one_block, two_blocks = [(own, 4, 4)], [(own, 4, 4), (beside, 1, 7)]

    def last(g):
        if g < 12:
            rows = pl.ds(pl.multiple_of(24 * (1 - core), 8), 24)
            return [send(fa.at[g, rows], fa_in.at[g], sibling, g, 10)]
        if g == 15:
            return [send(fo.at[pl.ds(2 * (1 - core), 2)], fo_in, sibling, g, 10)]
        return []

    def add0(g):
        r0[g] += block(g, mine)[...]

    def add1(g):
        quarter(r0, g, own)[...] += r1[g, 0]
        quarter(r0, g, beside)[...] += r1[g, 1]

    def finish(g, value):
        if g < 12:
            fa[g] = value
        else:
            fo[g - 12] = value

    def add2(g):
        quarter(r0, g, own)[...] += r23[g, 0:4]

    def add3z(g):
        finish(g, r0[g, z, own].astype(WIDE) + r23[g, 0].astype(WIDE))

    def put(n):
        return pltpu.make_async_copy(results[n], results_hbm[n], result_sem.at[n])

    def write(g):
        rows = pl.ds(pl.multiple_of(24 * core, 8), 24)
        if g < 8:
            pieces_out[g][:, mine] = fa[g, rows]
            pieces_out[g][:, other] = fa_in[g]
            put(g).start()
        elif g < 12:
            at = WIDTH * (g - 8)
            in_piece_out[:, pl.ds(pl.multiple_of(at + core * 384, 128), 384)] = fa[g, rows]
            in_piece_out[:, pl.ds(pl.multiple_of(at + 384 - core * 384, 128), 384)] = fa_in[g]
            if g == 11:
                put(8).start()
        elif g == 15:
            out_piece_out[:, mine] = fo[pl.ds(2 * core, 2)].reshape(96, 384)
            out_piece_out[:, other] = fo_in[...].reshape(96, 384)
            put(9).start()

    def start(copies):
        for copy in copies:
            copy.start()

    def wait(copies):
        for copy in copies:
            copy.wait()

    def along_z_after(g):
        return [g] if g < 12 else [12, 13, 14, 15] if g == 15 else []

    def event(g, s):
        z_second = g in FIRST_Z
        blocks = two_blocks if z_second else one_block
        if s == 0:
            start(swap(g))
        elif s == 1:
            wait(swap(g))
            add0(g)
            start(over_second(g))
        elif s == 2:
            wait(over_second(g))
            add1(g)
            z_start(g, blocks) if z_second else start(over_first(g))
        elif s == 3:
            if z_second:
                z_relay(g, blocks)
            else:
                wait(over_first(g))
                add2(g)
                for one in along_z_after(g):
                    z_start(one, blocks)
        elif s == 4:
            if z_second:
                z_wait(g, blocks)
                r0[g, z, own] = zsum[0].astype(LOW)
                r0[g, z, beside] = zsum[1].astype(LOW)
                start(over_first1(g))
            else:
                for one in along_z_after(g):
                    z_relay(one, blocks)
        elif s == 5:
            if z_second:
                wait(over_first1(g))
                add3z(g)
            else:
                for one in along_z_after(g):
                    z_wait(one, blocks)
                    finish(one, zsum[0])
            start(last(g))
        else:
            wait(last(g))
            write(g)

    def acc_copies(s):
        to = ([sibling], along_z, [first], [second])[s]
        at = (0, 1, 4, 5)[s]
        return [
            pltpu.make_async_remote_copy(
                src_ref=acc, dst_ref=acc_in.at[at + n], send_sem=ss0.at[at + n], recv_sem=rs0.at[at + n],
                device_id=d, device_id_type=MESH)
            for n, d in enumerate(to)
        ]

    lane = lax.broadcasted_iota(jnp.int32, (1, 128), 1)
    sides = [lane < 64, lane >= 64]

    def keep(g, value):
        grad[LINE.index(g) % 4] = value.astype(LOW).reshape(4, 4, 48, WIDTH)

    def begin():
        fetched("og")
        for s in range(2):
            rows = slice(s * LENGTH, (s + 1) * LENGTH)
            t = lax.broadcasted_iota(jnp.int32, (LENGTH, 1), 0)
            gl[rows, :] = jnp.where(t < lens_ref[s], gl[rows, :].astype(WIDE), 0.0).astype(LOW)

    def out_grad_part(j):
        fetched(f"act{j}")
        grad[j] = dot_tn(act[:, j * WIDTH : (j + 1) * WIDTH], gl[...]).astype(LOW).reshape(4, 4, 48, WIDTH)

    def hidden_part(j):
        if j == 0:
            fetched("slope", "nff")
        cols = slice(j * WIDTH, (j + 1) * WIDTH)
        ghj[...] = (dot_nt(gl[...], weight(12 + j)) * slope[:, cols].astype(WIDE)).astype(LOW)
        keep(8 + j, dot_tn(nff[...], ghj[...]))

    def hidden_back(j):
        part = dot_nt(ghj[...], weight(8 + j))
        if j:
            up[...] += part
        else:
            up[...] = part

    def norm_back(value_ref, base_ref, n):
        g = gains[n : n + 1, :].astype(WIDE)

        def chunk(i, carried):
            rows = pl.ds(pl.multiple_of(i * 128, 128), 128)
            value = value_ref[rows, :].astype(WIDE)
            r = root_scale(value)
            unit_rows = value * r
            upstream = up[rows, :]
            weighted = upstream * g
            inner = jnp.mean(weighted * unit_rows, axis=-1, keepdims=True)
            new = base_ref[rows, :].astype(WIDE) + r * (weighted - unit_rows * inner)
            total[rows, :] = new
            low[rows, :] = new.astype(LOW)
            return carried + jnp.sum(upstream * unit_rows, axis=0, keepdims=True)

        acc[n : n + 1, 0:WIDTH] = lax.fori_loop(0, ROWS // 128, chunk, jnp.zeros((1, WIDTH), WIDE))

    def ff_norm_part():
        fetched("after_cross")
        norm_back(aft, gl, 2)
        fetch("p", p_hbm, act)
        fetch("normed", normed_hbm, slope.at[:, 0:768])
        fetch("q", q_hbm, slope.at[:, 768:1536])
        fetch("k", k_hbm, slope.at[:, 1536:2304])
        fetch("v", v_hbm, slope.at[:, 2304:3072])
        fetch("ctx", ctx_hbm, nff)
        fetch("after_self", after_self_hbm, aft)

    def cross_out_part():
        fetched("cctx")
        keep(7, dot_tn(cctx[...], low[...]))
        gctx[...] = dot_nt(low[...], weight(7)).astype(LOW)
        fetched("cq", "mk", "mv", "pc")

    def head_back(weights, gp, qp, kp, vp, side):
        p32 = weights.astype(WIDE)
        pull = dot_nt(jnp.where(sides[side], gp, jnp.zeros_like(gp)), vp)
        slant = p32 * (pull - jnp.sum(pull * p32, axis=-1, keepdims=True))
        rounded = slant.astype(LOW)
        return dot(rounded, kp), dot_tn(rounded, qp), dot_tn(weights, gp), slant

    def joined(low_part, high_part):
        return jnp.where(sides[0], low_part, high_part).astype(LOW)

    def cross_part(lo, hi):
        def it(i, c):
            s, pair = i // PAIRS, i % PAIRS
            rows = pl.ds(pl.multiple_of(s * LENGTH, LENGTH), LENGTH)
            deep = pl.ds(pl.multiple_of(s * MEMORY, MEMORY), MEMORY)
            cols = pl.ds(pl.multiple_of(pair * 128, 128), 128)
            gp, qp, kp, vp = gctx[rows, cols], cq[rows, cols], mk[deep, cols], mv[deep, cols]
            one, two = [
                head_back(pc[rows, pl.ds(pl.multiple_of((2 * pair + side) * MEMORY, 128), MEMORY)], gp, qp, kp, vp, side)
                for side in range(2)
            ]
            dq[rows, cols] = joined(one[0], two[0])
            dk[deep, cols] = joined(one[1], two[1])
            dv[deep, cols] = joined(one[2], two[2])
            return c

        lax.fori_loop(lo, hi, it, 0)

    def cross_query_part():
        fetched("ncross")
        keep(4, dot_tn(ncross[...], dq[...]))

    def cross_key_part():
        fetched("mem")
        keep(5, dot_tn(mem[...], dk[0:256, :]))

    def cross_value_part():
        keep(6, dot_tn(mem[...], dv[0:256, :]))

    def memory_part():
        mem_grad[...] = dot_nt(dk[0:256, :], weight(5)) + dot_nt(dv[0:256, :], weight(6))
        pltpu.make_async_copy(mem_grad, memory_out, out_sem.at[0]).start()

    def cross_query_back():
        up[...] = dot_nt(dq[...], weight(4))

    def cross_norm_part():
        fetched("after_self")
        norm_back(aft, total, 1)

    def self_out_part():
        fetched("ctx")
        keep(3, dot_tn(nff[...], low[...]))
        gctx[...] = dot_nt(low[...], weight(3)).astype(LOW)
        fetched("p", "q", "k", "v")

    def self_part(lo, hi):
        def it(pair, c):
            cols = pl.ds(pl.multiple_of(pair * 128, 128), 128)
            q_cols = pl.ds(pl.multiple_of(768 + pair * 128, 128), 128)
            k_cols = pl.ds(pl.multiple_of(1536 + pair * 128, 128), 128)
            v_cols = pl.ds(pl.multiple_of(2304 + pair * 128, 128), 128)
            slants = []
            for s in range(2):
                rows = slice(s * LENGTH, (s + 1) * LENGTH)
                gp, qp, kp, vp = gctx[rows, cols], slope[rows, q_cols], slope[rows, k_cols], slope[rows, v_cols]
                one, two = [
                    head_back(act[rows, pl.ds(pl.multiple_of((2 * pair + side) * LENGTH, 256), LENGTH)], gp, qp, kp, vp, side)
                    for side in range(2)
                ]
                dq[rows, cols] = joined(one[0], two[0])
                dk[rows, cols] = joined(one[1], two[1])
                dv[rows, cols] = joined(one[2], two[2])
                slants.append((one[3], two[3]))
            t = lax.broadcasted_iota(jnp.int32, (LENGTH, LENGTH), 0)
            u = lax.broadcasted_iota(jnp.int32, (LENGTH, LENGTH), 1)
            upside = (t + u == LENGTH - 1).astype(LOW)
            for side in range(2):
                both = slants[0][side] + slants[1][side]
                coarse = both.astype(LOW)
                fine = (both - coarse.astype(WIDE)).astype(LOW)
                turned = dot(upside, coarse) + dot(upside, fine)
                rolled = pltpu.roll(turned, 1, 1, stride=1, stride_axis=0)
                dist[pl.ds(2 * pair + side, 1), :] = jnp.sum(rolled, axis=0, keepdims=True)
            return c

        lax.fori_loop(lo, hi, it, 0)

    def self_grads(n):
        fetched(*(["normed"] if n == 0 else []))
        keep(n, dot_tn(slope[:, 0:768], (dq, dk, dv)[n][...]))

    def normed_back(n):
        part = dot_nt((dq, dk, dv)[n][...], weight(n))
        if n:
            up[...] += part
        else:
            up[...] = part

    def input_part():
        fetched("x")
        norm_back(x, total, 0)
        pltpu.make_async_copy(total, input_out, out_sem.at[1]).start()
        buckets = lax.dot_general(
            dist[...], bucket_columns(True), (((1,), (1,)), ((), ())),
            precision=lax.Precision.HIGHEST, preferred_element_type=WIDE)
        acc[:, WIDTH : WIDTH + BUCKETS] = buckets
        for copy in acc_copies(0):
            copy.start()

    pieces = [(0.5, begin, None, 6)]
    pieces += [(1.0, functools.partial(out_grad_part, j), 12 + j, 6) for j in range(4)]
    for j in range(4):
        pieces += [(2.0, functools.partial(hidden_part, j), 8 + j, 0), (1.0, functools.partial(hidden_back, j), None, 8 + 2 * j)]
    pieces += [
        (1.5, ff_norm_part, None, 0), (1.9, cross_out_part, 7, 15),
        *[(1.5, functools.partial(cross_part, 2 * n, 2 * n + 2), None, 0) for n in range(6)],
        (1.0, cross_query_part, 4, 0), (0.5, cross_key_part, 5, 0), (0.5, cross_value_part, 6, 0),
        (1.0, memory_part, None, 0), (1.0, cross_query_back, None, 16), (1.3, cross_norm_part, None, 0), (2.0, self_out_part, 3, 0),
        *[(2.2, functools.partial(self_part, n, n + 1), None, 0) for n in range(6)],
        *[(1.0, functools.partial(self_grads, n), n, 0) for n in range(3)],
        *[(1.0, functools.partial(normed_back, n), None, 0) for n in range(3)],
        (2.0, input_part, None, 0),
    ]

    acc[...] = jnp.zeros_like(acc)
    dist[...] = jnp.zeros_like(dist)
    fetch("og", og_hbm, gl)
    for j in range(4):
        cols = slice(j * WIDTH, (j + 1) * WIDTH)
        fetch(f"act{j}", act_hbm.at[:, cols], act.at[:, cols])
    ask(2)
    fetch("slope", slope_hbm, slope)
    fetch("nff", nff_hbm, nff)
    fetch("after_cross", after_cross_hbm, aft)
    fetch("cctx", cctx_hbm, cctx)
    fetch("cq", cq_hbm, cq)
    fetch("mk", mk_hbm, mk)
    fetch("mv", mv_hbm, mv)
    fetch("pc", pc_hbm, pc)
    fetch("ncross", ncross_hbm, ncross)
    fetch("mem", mem_hbm, mem)
    fetch("x", x_hbm, x)
    clock, done, made, freed = 0.0, 0, set(), set()

    def run_piece():
        nonlocal clock, done
        cost, what, makes, asks = pieces[done]
        what()
        ask(asks)
        clock += cost
        made.add(makes)
        done += 1

    def may_run():
        makes = pieces[done][2]
        i = 0 if makes is None else LINE.index(makes)
        return i < 4 or LINE[i - 4] in freed

    def out_grads():
        while LINE[0] not in made:
            run_piece()

    greet([sibling, first, second] + along_z, out_grads)

    stage = None
    for r in range(GROUPS + LAGS[-1]):
        for s in range(1, 7):
            i = r - LAGS[s]
            if 0 <= i < GROUPS:
                event(LINE[i], s)
                if s == 1:
                    freed.add(LINE[i])
        if r < GROUPS:
            while LINE[r] not in made:
                assert may_run()
                run_piece()
            event(LINE[r], 0)
        while done < len(pieces) and clock < PACE * (r + 1) and may_run():
            run_piece()
        if done == len(pieces):
            if stage is None:
                stage = 0
            elif stage < 4:
                for copy in acc_copies(stage):
                    copy.wait()
                for n in ((0,), (1, 2, 3), (4,), (5,))[stage]:
                    acc[...] += acc_in[n]
                stage += 1
                if stage < 4:
                    for copy in acc_copies(stage):
                        copy.start()
    assert done == len(pieces) and stage == 4 and got[0] == GROUPS
    offset = (lax.axis_index("dp") * 4 + lax.axis_index("fsdp")) * 24
    sum_out[:, 0:WIDTH] = pltpu.roll(acc[:, 0:WIDTH], WIDTH - offset, 1)
    sum_out[:, WIDTH:] = acc[:, WIDTH:]
    put(10).start()
    for n in range(11):
        put(n).wait()
    pltpu.make_async_copy(mem_grad, memory_out, out_sem.at[0]).wait()
    pltpu.make_async_copy(total, input_out, out_sem.at[1]).wait()


BACKWARD_OUT = (
    (((512, 768), WIDE), ((256, 768), WIDE)),
    (((24, 768), WIDE),) * 8 + (((24, 3072), WIDE), ((96, 768), WIDE), ((16, 896), WIDE)),
)


def backward_call(gains, lens, *arrays):
    shape = lambda s: jax.ShapeDtypeStruct(*s)
    vmem = lambda *s: pltpu.VMEM(s, LOW)
    return pl.pallas_call(
        backward_kernel,
        out_shape=tuple(shape(s) for s in BACKWARD_OUT[0] + BACKWARD_OUT[1]),
        in_specs=[pl.BlockSpec(memory_space=pltpu.VMEM), pl.BlockSpec(memory_space=pltpu.SMEM)]
        + [pl.BlockSpec(memory_space=pl.ANY)] * len(arrays),
        out_specs=[pl.BlockSpec(memory_space=pl.ANY)] * 13,
        scratch_shapes=[
            *[pltpu.VMEM(*s) for s in BACKWARD_OUT[1]],
            vmem(SLOTS, 4, 4, 48, 768),
            vmem(512, 3072), vmem(512, 3072), pltpu.VMEM((256, 768), WIDE), vmem(512, 768),
            pltpu.VMEM((512, 768), WIDE),
            vmem(512, 768), vmem(512, 768), vmem(512, 768), vmem(256, 768), vmem(256, 768), vmem(256, 768),
            vmem(512, 1536),
            vmem(512, 768), vmem(512, 768),
            pltpu.VMEM((512, 768), WIDE), pltpu.VMEM((512, 768), WIDE),
            vmem(512, 768), vmem(512, 768), vmem(512, 768),
            vmem(512, 768), vmem(512, 768), vmem(512, 768),
            pltpu.VMEM((16, LENGTH), WIDE),
            vmem(4, 4, 4, 48, 768),
            vmem(GROUPS, 4, 4, 48, 384), vmem(GROUPS, 2, 4, 48, 384), vmem(GROUPS, 9, 48, 384),
            pltpu.VMEM((2, 48, 384), WIDE),
            pltpu.VMEM((12, 48, 384), WIDE), pltpu.VMEM((4, 48, 384), WIDE),
            pltpu.VMEM((12, 24, 384), WIDE), pltpu.VMEM((2, 48, 384), WIDE),
            pltpu.VMEM((16, 896), WIDE), pltpu.VMEM((6, 16, 896), WIDE),
            pltpu.SemaphoreType.DMA((GROUPS, 13)), pltpu.SemaphoreType.DMA((GROUPS, 13)),
            pltpu.SemaphoreType.DMA((6,)), pltpu.SemaphoreType.DMA((6,)),
            pltpu.SemaphoreType.DMA((28,)), pltpu.SemaphoreType.DMA((GROUPS,)), pltpu.SemaphoreType.DMA((2,)),
            pltpu.SemaphoreType.DMA((11,)),
        ],
        compiler_params=pltpu.CompilerParams(collective_id=1, has_side_effects=True, vmem_limit_bytes=62 * 2**20),
    )(gains, lens, *arrays)


def place_kernel(*refs):
    arrays, outs, held, own, sems = refs[:14], refs[14:31], refs[31:45], refs[45:49], refs[49]
    copies = [pltpu.make_async_copy(src, dst, sems.at[0, n]) for n, (src, dst) in enumerate(zip(arrays, held))]
    for copy in copies:
        copy.start()
    copies[13].wait()
    small = held[13]
    for n in range(3):
        own[n][...] = small[n : n + 1, 0:24]
    own[3][...] = small[0:HEADS, WIDTH : WIDTH + BUCKETS]
    sources = list(held[:13]) + list(own)
    onward = [pltpu.make_async_copy(src, dst, sems.at[1, n]) for n, (src, dst) in enumerate(zip(sources, outs))]
    for copy in onward[13:]:
        copy.start()
    for n in range(13):
        copies[n].wait()
        onward[n].start()
    for copy in onward:
        copy.wait()


def place_call(small, *arrays):
    last = [((1, 24), WIDE)] * 3 + [((HEADS, BUCKETS), WIDE)]
    shapes = [(a.shape, a.dtype) for a in arrays] + last
    return pl.pallas_call(
        place_kernel,
        out_shape=tuple(jax.ShapeDtypeStruct(*s) for s in shapes),
        in_specs=[pl.BlockSpec(memory_space=pl.ANY)] * 14,
        out_specs=[pl.BlockSpec(memory_space=pl.ANY)] * 17,
        scratch_shapes=[pltpu.VMEM(a.shape, a.dtype) for a in arrays]
        + [pltpu.VMEM(small.shape, small.dtype)]
        + [pltpu.VMEM(*s) for s in last]
        + [pltpu.SemaphoreType.DMA((2, 17))],
    )(*arrays, small)


def layer_kernels(decoder_in, memory, out_grad, lengths, *params):
    shards, table = params[:13], params[13]
    (
        w, gains, normed, q, k, v, ctx, p, after_self, ncross, cq, mk, mv, cctx, pc, after_cross, nff, act, slope, layer,
    ) = forward(shards, decoder_in, memory, table, lengths)
    rows = decoder_in.reshape(ROWS, WIDTH)
    input_grad, memory_grad, *pieces, in_piece, out_piece, small = backward_call(
        gains, lengths.reshape(2), w, act, slope, nff, after_cross, cctx, ncross, cq, mk, mv,
        memory.reshape(2 * MEMORY, WIDTH), pc, after_self, p, normed, q, k, v, ctx, rows, out_grad.reshape(ROWS, WIDTH),
    )
    layer, input_grad, memory_grad, *rest = place_call(small, layer, input_grad, memory_grad, *pieces, in_piece, out_piece)
    return (
        layer.reshape(decoder_in.shape),
        input_grad.reshape(decoder_in.shape),
        memory_grad.reshape(memory.shape),
        *rest[:10],
        *[part.reshape(24) for part in rest[10:13]],
        rest[13].T,
    )


def body(decoder_in, memory, out_grad, lengths, *params):
    sizes = (lax.axis_size("dp"), lax.axis_size("fsdp"))
    if sizes == (8, 4) and decoder_in.shape == (2, 1, LENGTH, WIDTH) and params[0].shape == (24, WIDTH):
        return layer_kernels(decoder_in, memory, out_grad, lengths, *params)
    return plain_body(decoder_in, memory, out_grad, lengths, *params)


def solution(mesh):
    return jax.shard_map(
        body,
        mesh=mesh,
        in_specs=(
            P(None, ("dp", "fsdp"), None, None),
            P(None, ("dp", "fsdp"), None, None),
            P(None, ("dp", "fsdp"), None, None),
            P(None, ("dp", "fsdp")),
            P(("dp", "fsdp"), None),
            P(("dp", "fsdp"), None),
            P(("dp", "fsdp"), None),
            P(("dp", "fsdp"), None),
            P(("dp", "fsdp"), None),
            P(("dp", "fsdp"), None),
            P(("dp", "fsdp"), None),
            P(("dp", "fsdp"), None),
            P(("dp", "fsdp"), None),
            P(("dp", "fsdp"), None),
            P(("dp", "fsdp")),
            P(("dp", "fsdp")),
            P(("dp", "fsdp")),
            P(),
        ),
        out_specs=(
            P(None, ("dp", "fsdp"), None, None),
            P(None, ("dp", "fsdp"), None, None),
            P(None, ("dp", "fsdp"), None, None),
            P(("dp", "fsdp"), None),
            P(("dp", "fsdp"), None),
            P(("dp", "fsdp"), None),
            P(("dp", "fsdp"), None),
            P(("dp", "fsdp"), None),
            P(("dp", "fsdp"), None),
            P(("dp", "fsdp"), None),
            P(("dp", "fsdp"), None),
            P(("dp", "fsdp"), None),
            P(("dp", "fsdp"), None),
            P(("dp", "fsdp")),
            P(("dp", "fsdp")),
            P(("dp", "fsdp")),
            P(),
        ),
        check_vma=False,
    )
```

```python
import functools
import math

import jax
import jax.numpy as jnp
from jax import lax
from jax.experimental import pallas as pl
from jax.experimental.pallas import tpu as pltpu
from jax.sharding import PartitionSpec as P

HEADS = 12
BUCKETS = 32
MAX_DIST = 128


EPS = 1e-06
MASKED = -1e30
TOP_PRECISION = lax.Precision.HIGHEST


def bucket_onehot(length):
    half_count = BUCKETS // 2
    positions = jnp.arange(length, dtype=jnp.int32)
    distance = jnp.maximum(positions[:, None] - positions[None, :], 0)
    farther = jnp.zeros_like(distance)
    for level in range(1, half_count):
        border = int(math.ceil(half_count * (MAX_DIST / half_count) ** (level / half_count)))
        farther = farther + (distance >= border).astype(jnp.int32)
    bucket = jnp.where(distance < half_count, distance, half_count + farther)
    return (bucket[None] == jnp.arange(BUCKETS, dtype=jnp.int32)[:, None, None]).astype(jnp.float32)


def normalize(vector, gain_row):
    return vector * lax.rsqrt(jnp.mean(vector * vector, axis=-1, keepdims=True) + EPS) * gain_row


def project(operand, weight):
    return jnp.dot(operand, weight, preferred_element_type=jnp.float32)


def project_back(operand, weight):
    return lax.dot_general(
        operand, weight, (((1,), (1,)), ((), ())), preferred_element_type=jnp.float32
    )


def weight_grad(inputs_rows, grad_rows):
    return lax.dot_general(
        inputs_rows, grad_rows, (((0,), (0,)), ((), ())), preferred_element_type=jnp.float32
    )


def split_heads(matrix):
    return matrix.reshape(matrix.shape[:-1] + (HEADS, matrix.shape[-1] // HEADS))


def head_scores(queries, key_rows):
    return jnp.einsum(
        "gqhe,gkhe->ghqk",
        split_heads(queries),
        split_heads(key_rows),
        preferred_element_type=jnp.float32,
    )


def attend_forward(queries, key_rows, values, relative_position_bias, allowed):
    scores = jnp.where(allowed, head_scores(queries, key_rows) + relative_position_bias, MASKED)
    largest = jnp.max(scores, axis=-1, keepdims=True)
    exponent = jnp.exp(scores - largest)
    row_totals = jnp.sum(exponent, axis=-1, keepdims=True)
    attention_weights = exponent / row_totals
    context = jnp.einsum(
        "ghqk,gkhe->gqhe",
        attention_weights.astype(jnp.bfloat16),
        split_heads(values),
        preferred_element_type=jnp.float32,
    )
    return (context.reshape(queries.shape).astype(jnp.bfloat16), attention_weights)


def attend_backward(queries, key_rows, values, attention_weights, grad_context):
    grad_heads = split_heads(grad_context)
    grad_values = jnp.einsum(
        "ghqk,gqhe->gkhe",
        attention_weights.astype(jnp.bfloat16),
        grad_heads,
        preferred_element_type=jnp.float32,
    )
    grad_weights = jnp.einsum(
        "gqhe,gkhe->ghqk", grad_heads, split_heads(values), preferred_element_type=jnp.float32
    )
    score_gradient = attention_weights * (
        grad_weights - jnp.sum(grad_weights * attention_weights, axis=-1, keepdims=True)
    )
    rounded = score_gradient.astype(jnp.bfloat16)
    grad_queries = jnp.einsum(
        "ghqk,gkhe->gqhe", rounded, split_heads(key_rows), preferred_element_type=jnp.float32
    )
    grad_keys = jnp.einsum(
        "ghqk,gqhe->gkhe", rounded, split_heads(queries), preferred_element_type=jnp.float32
    )
    return (
        grad_queries.reshape(queries.shape).astype(jnp.bfloat16),
        grad_keys.reshape(key_rows.shape).astype(jnp.bfloat16),
        grad_values.reshape(values.shape).astype(jnp.bfloat16),
        score_gradient,
    )


AXES = ("dp", "fsdp")


def rows_of(matrix):
    return matrix.reshape(-1, matrix.shape[-1])


def gather_all(shards):
    width = shards[0].shape[1]
    blocks = []
    for shard in shards:
        if shard.ndim == 1:
            continue
        blocks.append(shard.reshape(-1, width) if shard.shape[1] != width else shard)
    packed = lax.all_gather(jnp.concatenate(blocks, axis=0), AXES, axis=0)
    whole, at = [], 0
    devices = packed.shape[0]
    for shard, block in zip(shards, blocks):
        part = packed[:, at : at + block.shape[0]]
        at += block.shape[0]
        whole.append(part.reshape(devices * shard.shape[0], shard.shape[1]))
    gains = jnp.stack(shards[len(blocks) :])
    gains = lax.all_gather(gains, AXES, axis=1, tiled=True)
    return whole, [gains[k] for k in range(gains.shape[0])]


def scatter_all(grads, shards):
    width = shards[0].shape[1]
    devices = lax.axis_size(AXES)
    blocks = [grad.astype(jnp.bfloat16).reshape(devices, -1, width) for grad in grads]
    summed = lax.psum_scatter(
        jnp.concatenate(blocks, axis=1), AXES, scatter_dimension=0, tiled=False
    ).astype(jnp.float32)
    pieces, at = [], 0
    for block, shard in zip(blocks, shards):
        pieces.append(summed[at : at + block.shape[1]].reshape(shard.shape))
        at += block.shape[1]
    return pieces


def plain_body(decoder_in, memory, out_grad, lengths, *params):
    shards, bucket_bias_table = params[:13], params[13]
    matrices, gains = gather_all(shards)
    (
        self_query,
        self_key,
        self_value,
        self_out,
        cross_query,
        cross_key,
        cross_value,
        cross_out,
        ff_in,
        ff_out,
    ) = matrices
    norm_self, norm_cross, norm_ff = [gain.astype(jnp.float32) for gain in gains]
    micro, seqs, seq_length, width = decoder_in.shape
    groups = micro * seqs
    memory_bf = memory.reshape(groups, memory.shape[2], width)
    grad_bf = out_grad.reshape(groups, seq_length, width)
    group_lengths = lengths.reshape(groups)
    bucket_indicator = bucket_onehot(seq_length)
    relative_position_bias = jnp.einsum(
        "fsn,fe->esn",
        bucket_indicator,
        bucket_bias_table.astype(jnp.float32),
        precision=TOP_PRECISION,
    )
    positions = jnp.arange(seq_length, dtype=jnp.int32)
    causal = positions[:, None] >= positions[None, :]
    present = positions[None, :] < group_lengths[:, None]
    valid_rows = present[:, :, None].astype(jnp.float32)
    allowed = causal[None, None] & present[:, None, None, :]

    def grad_of(inputs, upstream):
        return weight_grad(rows_of(inputs), rows_of(upstream))

    decoded = decoder_in.reshape(groups, seq_length, width).astype(jnp.float32)
    normed = normalize(decoded, norm_self).astype(jnp.bfloat16)
    queries = project(normed, self_query).astype(jnp.bfloat16)
    key_rows = project(normed, self_key).astype(jnp.bfloat16)
    values = project(normed, self_value).astype(jnp.bfloat16)
    context, self_weights = attend_forward(
        queries, key_rows, values, relative_position_bias, allowed
    )
    after_self = decoded + project(context, self_out)
    normed_cross = normalize(after_self, norm_cross).astype(jnp.bfloat16)
    cross_queries = project(normed_cross, cross_query).astype(jnp.bfloat16)
    memory_keys = project(memory_bf, cross_key).astype(jnp.bfloat16)
    memory_values = project(memory_bf, cross_value).astype(jnp.bfloat16)
    cross_context, cross_weights = attend_forward(
        cross_queries, memory_keys, memory_values, 0.0, True
    )
    after_cross = after_self + project(cross_context, cross_out)
    normed_ff = normalize(after_cross, norm_ff).astype(jnp.bfloat16)
    hidden = project(normed_ff, ff_in)
    activated = jax.nn.gelu(hidden, approximate=True).astype(jnp.bfloat16)
    after_ff = after_cross + project(activated, ff_out)
    layer_out = (after_ff * valid_rows).astype(jnp.bfloat16)

    def back(operand, weight):
        return lax.dot_general(
            operand, weight, (((2,), (1,)), ((), ())), preferred_element_type=jnp.float32
        )

    grad_after = grad_bf.astype(jnp.float32) * valid_rows
    grad_branch = grad_after.astype(jnp.bfloat16)
    grad_ff_out = grad_of(activated, grad_branch)
    gelu_pull = jax.vjp(lambda pre_act: jax.nn.gelu(pre_act, approximate=True), hidden)[1]
    grad_hidden = gelu_pull(back(grad_branch, ff_out))[0].astype(jnp.bfloat16)
    grad_ff_in = grad_of(normed_ff, grad_hidden)
    norm_pull = jax.vjp(normalize, after_cross, norm_ff)[1]
    grad_rows, grad_norm_ff = norm_pull(back(grad_hidden, ff_in))
    grad_after = grad_after + grad_rows
    grad_branch = grad_after.astype(jnp.bfloat16)
    grad_cross_out = grad_of(cross_context, grad_branch)
    grad_context = back(grad_branch, cross_out).astype(jnp.bfloat16)
    grad_cross_rows, grad_memory_keys, grad_memory_values, unused = attend_backward(
        cross_queries, memory_keys, memory_values, cross_weights, grad_context
    )
    grad_cross_query = grad_of(normed_cross, grad_cross_rows)
    grad_cross_key = grad_of(memory_bf, grad_memory_keys)
    grad_cross_value = grad_of(memory_bf, grad_memory_values)
    grad_memory = back(grad_memory_keys, cross_key) + back(grad_memory_values, cross_value)
    norm_pull = jax.vjp(normalize, after_self, norm_cross)[1]
    grad_rows, grad_norm_cross = norm_pull(back(grad_cross_rows, cross_query))
    grad_after = grad_after + grad_rows
    grad_branch = grad_after.astype(jnp.bfloat16)
    grad_self_out = grad_of(context, grad_branch)
    grad_context = back(grad_branch, self_out).astype(jnp.bfloat16)
    grad_queries, grad_key_rows, grad_values, score_gradient = attend_backward(
        queries, key_rows, values, self_weights, grad_context
    )
    grad_self_query = grad_of(normed, grad_queries)
    grad_self_key = grad_of(normed, grad_key_rows)
    grad_self_value = grad_of(normed, grad_values)
    grad_normed = (
        back(grad_queries, self_query) + back(grad_key_rows, self_key) + back(grad_values, self_value)
    )
    norm_pull = jax.vjp(normalize, decoded, norm_self)[1]
    grad_rows, grad_norm_self = norm_pull(grad_normed)
    grad_input = grad_after + grad_rows
    bias_grad = jnp.einsum(
        "fgd,ogd->fo", bucket_indicator, jnp.sum(score_gradient, axis=0), precision=TOP_PRECISION
    )
    pieces = scatter_all(
        (
            grad_self_query,
            grad_self_key,
            grad_self_value,
            grad_self_out,
            grad_cross_query,
            grad_cross_key,
            grad_cross_value,
            grad_cross_out,
            grad_ff_in,
            grad_ff_out,
        ),
        shards[:10],
    )
    small = lax.psum(
        jnp.concatenate([grad_norm_self, grad_norm_cross, grad_norm_ff, bias_grad.reshape(-1)]),
        AXES,
    )
    mine = shards[10].shape[0]
    at = lax.axis_index(AXES) * mine
    gains_out = [
        lax.dynamic_slice_in_dim(small[k * width : (k + 1) * width], at, mine) for k in range(3)
    ]
    return (
        layer_out.reshape(decoder_in.shape),
        grad_input.reshape(decoder_in.shape),
        grad_memory.reshape(memory.shape),
        *pieces,
        *gains_out,
        small[3 * width :].reshape(bucket_bias_table.shape),
    )


MESH = pl.DeviceIdType.MESH
LOW = jnp.bfloat16
WIDE = jnp.float32
GROUPS = 16
WIDTH = 768
ROWS = 512
LENGTH = 256
MEMORY = 128
PAIRS = 6
CURVE = math.sqrt(2.0 / math.pi)


def place():
    dp, fsdp = lax.axis_index("dp"), lax.axis_index("fsdp")
    z, y, x, core = dp // 2, dp % 2, fsdp // 2, fsdp % 2
    sibling = (dp, x * 2 + 1 - core)
    over_x = (dp, (1 - x) * 2 + core)
    over_y = (z * 2 + 1 - y, fsdp)
    first = (jnp.where(core == 0, over_x[0], over_y[0]), jnp.where(core == 0, over_x[1], over_y[1]))
    second = (jnp.where(core == 0, over_y[0], over_x[0]), jnp.where(core == 0, over_y[1], over_x[1]))
    along_z = [(((z + k) % 4) * 2 + y, fsdp) for k in (1, 2, 3)]
    own = y * 2 + x
    beside = jnp.where(core == 0, y * 2 + 1 - x, (1 - y) * 2 + x)
    return z, own, beside, core, sibling, first, second, along_z


def greet(partners, meanwhile):
    barrier = pltpu.get_barrier_semaphore()
    for partner in partners:
        pl.semaphore_signal(barrier, inc=1, device_id=partner, device_id_type=MESH)
    meanwhile()
    pl.semaphore_wait(barrier, len(partners))


def half(core):
    return pl.ds(pl.multiple_of(core * 384, 128), 384)


def skew(ahead, groups=GROUPS):
    order = []
    for t in range(-max(ahead), groups + 8):
        for s in range(len(ahead)):
            g = t + ahead[s]
            if 0 <= g < groups:
                order.append((g, s))
    return order


def dot(a, b):
    return jnp.dot(a, b, preferred_element_type=WIDE)


def dot_nt(a, b):
    return lax.dot_general(a, b, (((1,), (1,)), ((), ())), preferred_element_type=WIDE)


def dot_tn(a, b):
    return lax.dot_general(a, b, (((0,), (0,)), ((), ())), preferred_element_type=WIDE)


def unit(w, u):
    return w[u].reshape(WIDTH, WIDTH)


def root_scale(value):
    return lax.rsqrt(jnp.mean(value * value, axis=-1, keepdims=True) + EPS)


def bucket_columns(flipped):
    j = lax.broadcasted_iota(jnp.int32, (BUCKETS, LENGTH), 1)
    row = lax.broadcasted_iota(jnp.int32, (BUCKETS, LENGTH), 0)
    n = jnp.where(j == 0, 0, LENGTH - j) if flipped else j
    half_count = BUCKETS // 2
    farther = jnp.zeros_like(n)
    for level in range(1, half_count):
        border = int(math.ceil(half_count * (MAX_DIST / half_count) ** (level / half_count)))
        farther = farther + (n >= border).astype(jnp.int32)
    bucket = jnp.where(n < half_count, n, half_count + farther)
    return (bucket == row).astype(WIDE)


QUEUE = (0, 1, 2, 3, 4, 5, 6, 7, 12, 13, 14, 15, 8, 9, 10, 11)
ZS = (1, 2, 3, 5, 7, 8, 9, 11, 13, 14, 15)
AHEAD = (9, 8, 6, 3, 1, 0)
GAIN_AT = (8, 11, 14)
BUDGET = 3.0
UNROLL = 1


def forward_kernel(*refs):
    shard_refs, gain_refs = refs[:9], refs[9:12]
    forward_steps(shard_refs, gain_refs, *refs[12:])


def forward_steps(
    shard_refs, gain_refs, tall_ref, x_hbm, mem_hbm, table_ref, lens_ref,
    w_out, gains_out, normed_out, q_out, k_out, v_out, ctx_out, p_out, after_self_out, ncross_out,
    cq_out, mk_out, mv_out, cctx_out, pc_out, after_cross_out, nff_out, act_out, slope_out, layer_out,
    w, gains, normed, q, k, v, ctx, p, after_self, ncross, cq, mk, mv, cctx, pc, after_cross, nff, act, slope, layer,
    x_ref, mem_ref, total, bias, small, sib, gain_in, ss, rs, ss0, rs0, out_sem, in_sem,
):
    z, own, beside, core, sibling, first, second, along_z = place()
    mine, other = half(core), half(1 - core)

    def along_at(zi):
        return (zi * 2 + lax.axis_index("dp") % 2, lax.axis_index("fsdp"))

    def view(g, zi, yx, cols):
        if g < 12:
            return w.at[g, slice(None) if zi is None else zi, yx, :, cols]
        return w.at[pl.ds(12, 4) if zi is None else 12 + zi, yx, g - 12, :, cols]

    def whole(g, cols):
        return w.at[g, :, :, :, cols] if g < 12 else w.at[pl.ds(12, 4), :, g - 12, :, cols]

    def send(ref, to, g, n):
        return pltpu.make_async_remote_copy(
            src_ref=ref, dst_ref=ref, send_sem=ss.at[g, n], recv_sem=rs.at[g, n], device_id=to, device_id_type=MESH)

    inner = (z == 1) | (z == 2)
    far = (z + 2) % 4
    end = along_at(jnp.where(z == 1, 0, 3))

    def z_send(g, block, n):
        yx, at = block
        return send(view(g, z, yx, mine), along_z[n], g, at + n)

    def z_hand_on(g, block):
        yx, at = block
        return send(view(g, far, yx, mine), end, g, 10 + (at > 0))

    def z_start(g, blocks):
        for block in blocks:
            z_send(g, block, 1).start()
            pl.when(z < 3)(lambda: z_send(g, block, 0).start())
            pl.when(z > 0)(lambda: z_send(g, block, 2).start())

    def z_relay(g, blocks):
        @pl.when(inner)
        def _():
            for block in blocks:
                z_send(g, block, 1).wait_recv()
                z_hand_on(g, block).start()

    def z_wait(g, blocks):
        for block in blocks:
            z_send(g, block, 1).wait_send()

            @pl.when(z < 3)
            def _():
                z_send(g, block, 0).wait_send()
                z_send(g, block, 2).wait_recv()

            @pl.when(z > 0)
            def _():
                z_send(g, block, 2).wait_send()
                z_send(g, block, 0).wait_recv()

            @pl.when(inner)
            def _():
                z_hand_on(g, block).wait_send()

            @pl.when(jnp.logical_not(inner))
            def _():
                z_send(g, block, 1).wait_recv()
                z_hand_on(g, block).wait_recv()

    one_block, two_blocks = [(own, 0)], [(own, 0), (beside, 7)]

    def step_b(g):
        return [send(view(g, None, own, mine), first, g, 3)]

    def step_c(g):
        return [send(view(g, None, own, mine), second, g, 4), send(view(g, None, beside, mine), second, g, 5)]

    def step_d(g):
        return [send(whole(g, mine), sibling, g, 6)]

    def step_b1(g):
        return [send(view(g, z, own, mine), first, g, 3)]

    def wait(copies):
        for copy in copies:
            copy.wait()

    def event(g, s, z_second):
        blocks = two_blocks if z_second else one_block
        if s == 0:
            start(step_b1(g)) if z_second else z_start(g, blocks)
        elif s == 1:
            if z_second:
                wait(step_b1(g))
                z_start(g, blocks)
            else:
                z_relay(g, blocks)
        elif s == 2:
            if z_second:
                z_relay(g, blocks)
            else:
                z_wait(g, blocks)
                start(step_b(g))
        elif s == 3:
            z_wait(g, blocks) if z_second else wait(step_b(g))
            start(step_c(g))
        elif s == 4:
            wait(step_c(g))
            start(step_d(g))
        else:
            wait(step_d(g))

    def gain_copies(s):
        to = ([sibling], along_z, [first], [second])[s]
        at = (0, 1, 4, 5)[s]
        return [
            pltpu.make_async_remote_copy(
                src_ref=gains, dst_ref=gain_in.at[at + n], send_sem=ss0.at[2 + at + n], recv_sem=rs0.at[2 + at + n],
                device_id=d, device_id_type=MESH)
            for n, d in enumerate(to)
        ]

    def start(copies):
        for copy in copies:
            copy.start()

    def gain_finish(s):
        for copy in gain_copies(s):
            copy.wait()
        for n in ((0,), (1, 2, 3), (4,), (5,))[s]:
            gains[...] += gain_in[n]

    stores = []

    def store(src, dst):
        copy = pltpu.make_async_copy(src, dst, out_sem.at[len(stores)])
        stores.append(copy)
        copy.start()

    def store_unit(g):
        if g < 12:
            store(w.at[g], w_out.at[g])
        elif g == 15:
            store(w.at[pl.ds(12, 4)], w_out.at[pl.ds(12, 4)])

    def gain(n):
        return gains[n : n + 1, :].astype(WIDE)

    def scale_rows(src, n, dst):
        g = gain(n)

        def chunk(i, c):
            rows = pl.ds(pl.multiple_of(i * 128, 128), 128)
            value = src[rows, :].astype(WIDE)
            dst[rows, :] = (value * root_scale(value) * g).astype(LOW)
            return c

        lax.fori_loop(0, ROWS // 128, chunk, 0)

    def make_bias():
        by_distance = dot(table_ref[...], bucket_columns(True).astype(LOW))
        for h in range(HEADS):
            row = jnp.broadcast_to(by_distance[h : h + 1, :], (LENGTH, LENGTH))
            bias[h] = pltpu.roll(row, 0, 1, stride=1, stride_axis=0)

    def project_into(src, u, dst):
        dst[...] = dot(src[...], unit(w, u)).astype(LOW)

    lane = lax.broadcasted_iota(jnp.int32, (1, 128), 1)
    sides = [lane < 64, lane >= 64]

    def attend(i, queries, keys, vals, keep_p, into, depth, masked):
        s, pair = i // PAIRS, i % PAIRS
        rows = pl.ds(pl.multiple_of(s * LENGTH, LENGTH), LENGTH)
        deep = pl.ds(pl.multiple_of(s * depth, depth), depth)
        cols = pl.ds(pl.multiple_of(pair * 128, 128), 128)
        qp, kp, vp = queries[rows, cols], keys[deep, cols], vals[deep, cols]
        parts = []
        for side in range(2):
            scores = dot_nt(jnp.where(sides[side], qp, jnp.zeros_like(qp)), kp)
            if masked:
                t = lax.broadcasted_iota(jnp.int32, (LENGTH, LENGTH), 0)
                u = lax.broadcasted_iota(jnp.int32, (LENGTH, LENGTH), 1)
                allowed = (u <= t) & (u < lens_ref[s])
                scores = jnp.where(allowed, scores + bias[2 * pair + side], MASKED)
            e = jnp.exp(scores - jnp.max(scores, axis=-1, keepdims=True))
            weights = (e * (1.0 / jnp.sum(e, axis=-1, keepdims=True))).astype(LOW)
            keep_p[rows, pl.ds(pl.multiple_of((2 * pair + side) * depth, 128), depth)] = weights
            parts.append(dot(weights, vp))
        into[rows, cols] = jnp.where(sides[0], parts[0], parts[1]).astype(LOW)

    def self_part(lo, hi):
        def it(i, c):
            attend(i, q, k, v, p, ctx, LENGTH, True)
            return c

        lax.fori_loop(lo, hi, it, 0, unroll=UNROLL)

    def cross_part(lo, hi):
        def it(i, c):
            attend(i, cq, mk, mv, pc, cctx, MEMORY, False)
            return c

        lax.fori_loop(lo, hi, it, 0, unroll=UNROLL)

    def after_self_part():
        after_self[...] = x_ref[...].astype(WIDE) + dot(ctx[...], unit(w, 3))
        scale_rows(after_self, 1, ncross)

    def after_cross_part():
        after_cross[...] = after_self[...] + dot(cctx[...], unit(w, 7))
        scale_rows(after_cross, 2, nff)

    def hidden_part(j):
        cols = slice(j * WIDTH, (j + 1) * WIDTH)
        for m in range(2):
            rows = slice(m * 256, m * 256 + 256)
            a = dot(nff[rows, :], unit(w, 8 + j))
            sq = a * a
            th = jnp.tanh(a * (CURVE + (CURVE * 0.044715) * sq))
            act[rows, cols] = (0.5 * a * (1.0 + th)).astype(LOW)
            slope[rows, cols] = (
                0.5 * (1.0 + th) + 0.5 * a * (1.0 - th * th) * (CURVE + (3.0 * CURVE * 0.044715) * sq)
            ).astype(LOW)
        store(act.at[:, pl.ds(j * WIDTH, WIDTH)], act_out.at[:, pl.ds(j * WIDTH, WIDTH)])
        store(slope.at[:, pl.ds(j * WIDTH, WIDTH)], slope_out.at[:, pl.ds(j * WIDTH, WIDTH)])
        part = dot(act[:, cols], unit(w, 12 + j))
        if j == 0:
            total[...] = after_cross[...] + part
        elif j < 3:
            total[...] += part
        else:
            part = total[...] + part
            for s in range(2):
                rows = slice(s * LENGTH, (s + 1) * LENGTH)
                t = lax.broadcasted_iota(jnp.int32, (LENGTH, 1), 0)
                layer[rows, :] = (part[rows] * (t < lens_ref[s]).astype(WIDE)).astype(LOW)

    pieces = [
        (0, 1.0, lambda: project_into(normed, 0, q)), (0, 0.1, lambda: store(q, q_out)),
        (1, 1.0, lambda: project_into(normed, 1, k)), (1, 0.1, lambda: store(k, k_out)),
        (2, 1.0, lambda: project_into(normed, 2, v)), (2, 0.1, lambda: store(v, v_out)),
        *[(2, 1.8, functools.partial(self_part, 2 * n, 2 * n + 2)) for n in range(6)],
        (2, 0.1, lambda: store(ctx, ctx_out)), (2, 0.1, lambda: store(p, p_out)),
        (3, 2.0, after_self_part), (3, 0.1, lambda: store(after_self, after_self_out)), (3, 0.1, lambda: store(ncross, ncross_out)),
        (4, 1.0, lambda: project_into(ncross, 4, cq)), (4, 0.1, lambda: store(cq, cq_out)),
        (5, 0.6, lambda: project_into(mem_ref, 5, mk)), (5, 0.1, lambda: store(mk, mk_out)),
        (6, 0.6, lambda: project_into(mem_ref, 6, mv)), (6, 0.1, lambda: store(mv, mv_out)),
        *[(6, 1.5, functools.partial(cross_part, 2 * n, 2 * n + 2)) for n in range(6)],
        (6, 0.1, lambda: store(cctx, cctx_out)), (6, 0.1, lambda: store(pc, pc_out)),
        (7, 2.0, after_cross_part), (7, 0.1, lambda: store(after_cross, after_cross_out)), (7, 0.1, lambda: store(nff, nff_out)),
        (8, 3.0, lambda: hidden_part(0)), (9, 3.0, lambda: hidden_part(1)), (10, 3.0, lambda: hidden_part(2)),
        (11, 3.0, lambda: hidden_part(3)), (11, 0.1, lambda: store(layer, layer_out)),
    ]

    load_x = pltpu.make_async_copy(x_hbm, x_ref, in_sem.at[0])
    load_mem = pltpu.make_async_copy(mem_hbm, mem_ref, in_sem.at[1])

    def prepare():
        load_x.start()
        load_mem.start()
        for u in range(12):
            rows = shard_refs[u][...] if u < 8 else shard_refs[8][:, WIDTH * (u - 8) : WIDTH * (u - 7)]
            rows = rows.astype(WIDE)
            none = jnp.zeros_like(rows)
            small[u] = jnp.concatenate(
                [jnp.where(core == 0, rows, none), jnp.where(core == 0, none, rows)], axis=0).astype(LOW)
        offset = (lax.axis_index("dp") * 4 + lax.axis_index("fsdp")) * 24
        spot = (lax.broadcasted_iota(jnp.int32, (24, WIDTH), 1) == lax.broadcasted_iota(jnp.int32, (24, WIDTH), 0) + offset)
        placed = [dot(ref[...], spot.astype(LOW)) for ref in gain_refs]
        gains[...] = jnp.concatenate(placed + [jnp.zeros((13, WIDTH), WIDE)], axis=0).astype(LOW)

    greet([sibling, first, second] + along_z, prepare)
    swap_small = pltpu.make_async_remote_copy(
        src_ref=small.at[:, :, other], dst_ref=sib, send_sem=ss0.at[0], recv_sem=rs0.at[0],
        device_id=sibling, device_id_type=MESH)

    def tall_view(cols):
        return w.at[12 + z, own, pl.ds(2 * core, 2), :, cols]

    swap_tall = pltpu.make_async_remote_copy(
        src_ref=tall_ref.at[:, :, other], dst_ref=tall_view(other), send_sem=ss0.at[1], recv_sem=rs0.at[1],
        device_id=sibling, device_id_type=MESH)
    swap_small.start()
    swap_tall.start()
    start(gain_copies(0))
    w[12 + z, own, pl.ds(2 * core, 2), :, mine] = tall_ref[:, :, mine]
    swap_small.wait()

    def assemble(u):
        w[u, z, own, :, mine] = small[u, :, mine] + sib[u]

    early = skew(AHEAD)[:2]
    assert all(s == 0 and QUEUE[at] < 12 for at, s in early)
    for at, s in early:
        assemble(QUEUE[at])
        event(QUEUE[at], 0, at in ZS)
    for u in range(12):
        if u not in [QUEUE[at] for at, s in early]:
            assemble(u)
    gain_finish(0)
    start(gain_copies(1))
    swap_tall.wait()
    make_bias()
    load_x.wait()
    load_mem.wait()

    stage, done = 1, 0
    for n, (at, s) in enumerate(skew(AHEAD)):
        g = QUEUE[at]
        if n >= 2:
            event(g, s, at in ZS)
        if n in GAIN_AT:
            gain_finish(stage)
            stage += 1
            if stage < 4:
                start(gain_copies(stage))
            else:
                scale_rows(x_ref, 0, normed)
                store(normed, normed_out)
                store(gains, gains_out)
        if s == 5:
            store_unit(g)
            spent = 0.0
            while done < len(pieces) and QUEUE.index(pieces[done][0]) <= at and (spent < BUDGET or at == GROUPS - 1):
                spent += pieces[done][1]
                pieces[done][2]()
                done += 1
    assert done == len(pieces) and stage == 4
    for copy in stores:
        copy.wait()


FORWARD_OUT = (
    ((16, 4, 4, 48, 768), LOW),
    ((16, 768), LOW),
    ((512, 768), LOW), ((512, 768), LOW), ((512, 768), LOW), ((512, 768), LOW),
    ((512, 768), LOW),
    ((512, 3072), LOW),
    ((512, 768), WIDE),
    ((512, 768), LOW),
    ((512, 768), LOW), ((256, 768), LOW), ((256, 768), LOW), ((512, 768), LOW),
    ((512, 1536), LOW),
    ((512, 768), WIDE),
    ((512, 768), LOW),
    ((512, 3072), LOW), ((512, 3072), LOW),
    ((512, 768), LOW),
)


def forward_call(*operands):
    return pl.pallas_call(
        forward_kernel,
        out_shape=tuple(jax.ShapeDtypeStruct(s, t) for s, t in FORWARD_OUT),
        in_specs=[pl.BlockSpec(memory_space=pltpu.VMEM)] * 13
        + [pl.BlockSpec(memory_space=pl.ANY)] * 2
        + [pl.BlockSpec(memory_space=pltpu.VMEM), pl.BlockSpec(memory_space=pltpu.SMEM)],
        out_specs=[pl.BlockSpec(memory_space=pl.ANY)] * len(FORWARD_OUT),
        scratch_shapes=[pltpu.VMEM(s, t) for s, t in FORWARD_OUT]
        + [
            pltpu.VMEM((ROWS, WIDTH), LOW),
            pltpu.VMEM((2 * MEMORY, WIDTH), LOW),
            pltpu.VMEM((ROWS, WIDTH), WIDE),
            pltpu.VMEM((HEADS, LENGTH, LENGTH), WIDE),
            pltpu.VMEM((12, 48, 768), LOW),
            pltpu.VMEM((12, 48, 384), LOW),
            pltpu.VMEM((6, 16, 768), LOW),
            pltpu.SemaphoreType.DMA((GROUPS, 12)),
            pltpu.SemaphoreType.DMA((GROUPS, 12)),
            pltpu.SemaphoreType.DMA((8,)),
            pltpu.SemaphoreType.DMA((8,)),
            pltpu.SemaphoreType.DMA((40,)),
            pltpu.SemaphoreType.DMA((2,)),
        ],
        compiler_params=pltpu.CompilerParams(collective_id=0, has_side_effects=True, vmem_limit_bytes=60 * 2**20),
    )(*operands)


def forward(shards, decoder_in, memory, table, lengths):
    return forward_call(
        *shards[:9],
        *[shard.reshape(1, 24) for shard in shards[10:13]],
        shards[9].reshape(2, 48, WIDTH),
        decoder_in.reshape(ROWS, WIDTH),
        memory.reshape(2 * MEMORY, WIDTH),
        table.T,
        lengths.reshape(2),
    )


LINE = (12, 13, 14, 15, 8, 9, 10, 11, 7, 4, 5, 6, 3, 0, 1, 2)
USED = (12, 8, 13, 9, 14, 10, 15, 11, 7, 5, 6, 4, 3, 0, 1, 2)
SLOTS = 6
LAGS = (0, 1, 3, 5, 7, 9, 10)
PACE = 3.5
FIRST_Z = (8, 10, 7, 5, 3)


def backward_kernel(
    gains, lens_ref, w_hbm, act_hbm, slope_hbm, nff_hbm, after_cross_hbm, cctx_hbm, ncross_hbm, cq_hbm, mk_hbm, mv_hbm,
    mem_hbm, pc_hbm, after_self_hbm, p_hbm, normed_hbm, q_hbm, k_hbm, v_hbm, ctx_hbm, x_hbm, og_hbm,
    input_out, memory_out, *rest,
):
    results_hbm, results, rest = rest[:11], rest[11:22], rest[22:]
    pieces_out, (in_piece_out, out_piece_out, sum_out) = results[:8], results[8:]
    (
        ring, act, slope, mem_grad, nff, aft, cctx, ncross, cq, mk, mv, mem, pc, x, gl, total, up, ghj, low, gctx, dq, dk, dv,
        dist, grad, r0, r1, r23, zsum, fa, fo, fa_in, fo_in, acc, acc_in, ss, rs, ss0, rs0, in_sem, ring_sem, out_sem, result_sem,
    ) = rest
    z, own, beside, core, sibling, first, second, along_z = place()
    mine, other = half(core), half(1 - core)
    diag, across = 3 - own, 3 - beside

    fetches = {}

    def fetch(name, src, dst):
        copy = pltpu.make_async_copy(src, dst, in_sem.at[len(fetches)])
        fetches[name] = copy
        copy.start()

    def fetched(*names):
        for name in names:
            fetches[name].wait()

    def weight_copy(n):
        return pltpu.make_async_copy(w_hbm.at[USED[n]], ring.at[n % SLOTS], ring_sem.at[n])

    asked, got = [0], [0]

    def ask(n):
        while asked[0] < min(n, GROUPS):
            weight_copy(asked[0]).start()
            asked[0] += 1

    def weight(u):
        n = USED.index(u)
        while got[0] <= n:
            weight_copy(got[0]).wait()
            got[0] += 1
        return ring[n % SLOTS].reshape(WIDTH, WIDTH)

    def send(src, dst, to, g, n):
        return pltpu.make_async_remote_copy(
            src_ref=src, dst_ref=dst, send_sem=ss.at[g, n], recv_sem=rs.at[g, n], device_id=to, device_id_type=MESH)

    def block(g, cols):
        return grad.at[LINE.index(g) % 4, :, :, :, cols]

    def swap(g):
        return [send(block(g, other), r0.at[g], sibling, g, 0)]

    def quarter(ref, g, yx):
        return ref.at[g, :, yx] if g < 12 else ref.at[g, yx]

    def share(g, zi, yx):
        return r0.at[g, zi, yx] if g < 12 else r0.at[12 + zi, yx, g - 12]

    def over_second(g):
        return [
            send(quarter(r0, g, across), r1.at[g, 0], second, g, 1),
            send(quarter(r0, g, diag), r1.at[g, 1], second, g, 2),
        ]

    def over_first(g):
        return [send(quarter(r0, g, beside), r23.at[g, pl.ds(0, 4)], first, g, 3)]

    def over_first1(g):
        return [send(r0.at[g, z, beside], r23.at[g, 0], first, g, 3)]

    inner = (z == 1) | (z == 2)
    far = (z + 2) % 4
    next_in = (jnp.where(z == 0, 1, 2) * 2 + lax.axis_index("dp") % 2, lax.axis_index("fsdp"))

    def z_send(g, block, n):
        yx, at, sem = block
        return send(share(g, (z + n + 1) % 4, yx), r23.at[g, at + n], along_z[n], g, sem + n)

    def z_hand_over(g, block, slot):
        return send(share(g, 3 - z, block[0]), r23.at[g, 7 + slot], next_in, g, 11 + slot)

    def z_start(g, blocks):
        for slot, block in enumerate(blocks):

            @pl.when(jnp.logical_not(inner))
            def _():
                z_hand_over(g, block, slot).start()
                z_send(g, block, 1).start()

            pl.when(z < 3)(lambda: z_send(g, block, 0).start())
            pl.when(z > 0)(lambda: z_send(g, block, 2).start())

    def z_relay(g, blocks):
        @pl.when(inner)
        def _():
            for slot, block in enumerate(blocks):
                z_hand_over(g, block, slot).wait_recv()
                both = share(g, far, block[0])[...].astype(WIDE) + r23[g, 7 + slot].astype(WIDE)
                share(g, far, block[0])[...] = both.astype(LOW)
                z_send(g, block, 1).start()

    def z_wait(g, blocks):
        for slot, block in enumerate(blocks):
            yx, at, sem = block
            z_send(g, block, 1).wait()
            pl.when(jnp.logical_not(inner))(lambda: z_hand_over(g, block, slot).wait_send())
            zsum[slot] = share(g, z, yx)[...].astype(WIDE) + r23[g, at + 1].astype(WIDE)

            @pl.when(z > 0)
            def _():
                z_send(g, block, 2).wait_send()
                z_send(g, block, 0).wait_recv()
                zsum[slot] += r23[g, at].astype(WIDE)

            @pl.when(z < 3)
            def _():
                z_send(g, block, 0).wait_send()
                z_send(g, block, 2).wait_recv()
                zsum[slot] += r23[g, at + 2].astype(WIDE)

    one_block, two_blocks = [(own, 4, 4)], [(own, 4, 4), (beside, 1, 7)]

    def last(g):
        if g < 12:
            rows = pl.ds(pl.multiple_of(24 * (1 - core), 8), 24)
            return [send(fa.at[g, rows], fa_in.at[g], sibling, g, 10)]
        if g == 15:
            return [send(fo.at[pl.ds(2 * (1 - core), 2)], fo_in, sibling, g, 10)]
        return []

    def add0(g):
        r0[g] += block(g, mine)[...]

    def add1(g):
        quarter(r0, g, own)[...] += r1[g, 0]
        quarter(r0, g, beside)[...] += r1[g, 1]

    def finish(g, value):
        if g < 12:
            fa[g] = value
        else:
            fo[g - 12] = value

    def add2(g):
        quarter(r0, g, own)[...] += r23[g, 0:4]

    def add3z(g):
        finish(g, r0[g, z, own].astype(WIDE) + r23[g, 0].astype(WIDE))

    def put(n):
        return pltpu.make_async_copy(results[n], results_hbm[n], result_sem.at[n])

    def write(g):
        rows = pl.ds(pl.multiple_of(24 * core, 8), 24)
        if g < 8:
            pieces_out[g][:, mine] = fa[g, rows]
            pieces_out[g][:, other] = fa_in[g]
            put(g).start()
        elif g < 12:
            at = WIDTH * (g - 8)
            in_piece_out[:, pl.ds(pl.multiple_of(at + core * 384, 128), 384)] = fa[g, rows]
            in_piece_out[:, pl.ds(pl.multiple_of(at + 384 - core * 384, 128), 384)] = fa_in[g]
            if g == 11:
                put(8).start()
        elif g == 15:
            out_piece_out[:, mine] = fo[pl.ds(2 * core, 2)].reshape(96, 384)
            out_piece_out[:, other] = fo_in[...].reshape(96, 384)
            put(9).start()

    def start(copies):
        for copy in copies:
            copy.start()

    def wait(copies):
        for copy in copies:
            copy.wait()

    def along_z_after(g):
        return [g] if g < 12 else [12, 13, 14, 15] if g == 15 else []

    def event(g, s):
        z_second = g in FIRST_Z
        blocks = two_blocks if z_second else one_block
        if s == 0:
            start(swap(g))
        elif s == 1:
            wait(swap(g))
            add0(g)
            start(over_second(g))
        elif s == 2:
            wait(over_second(g))
            add1(g)
            z_start(g, blocks) if z_second else start(over_first(g))
        elif s == 3:
            if z_second:
                z_relay(g, blocks)
            else:
                wait(over_first(g))
                add2(g)
                for one in along_z_after(g):
                    z_start(one, blocks)
        elif s == 4:
            if z_second:
                z_wait(g, blocks)
                r0[g, z, own] = zsum[0].astype(LOW)
                r0[g, z, beside] = zsum[1].astype(LOW)
                start(over_first1(g))
            else:
                for one in along_z_after(g):
                    z_relay(one, blocks)
        elif s == 5:
            if z_second:
                wait(over_first1(g))
                add3z(g)
            else:
                for one in along_z_after(g):
                    z_wait(one, blocks)
                    finish(one, zsum[0])
            start(last(g))
        else:
            wait(last(g))
            write(g)

    def acc_copies(s):
        to = ([sibling], along_z, [first], [second])[s]
        at = (0, 1, 4, 5)[s]
        return [
            pltpu.make_async_remote_copy(
                src_ref=acc, dst_ref=acc_in.at[at + n], send_sem=ss0.at[at + n], recv_sem=rs0.at[at + n],
                device_id=d, device_id_type=MESH)
            for n, d in enumerate(to)
        ]

    lane = lax.broadcasted_iota(jnp.int32, (1, 128), 1)
    sides = [lane < 64, lane >= 64]

    def keep(g, value):
        grad[LINE.index(g) % 4] = value.astype(LOW).reshape(4, 4, 48, WIDTH)

    def begin():
        fetched("og")
        for s in range(2):
            rows = slice(s * LENGTH, (s + 1) * LENGTH)
            t = lax.broadcasted_iota(jnp.int32, (LENGTH, 1), 0)
            gl[rows, :] = jnp.where(t < lens_ref[s], gl[rows, :].astype(WIDE), 0.0).astype(LOW)

    def out_grad_part(j):
        fetched(f"act{j}")
        grad[j] = dot_tn(act[:, j * WIDTH : (j + 1) * WIDTH], gl[...]).astype(LOW).reshape(4, 4, 48, WIDTH)

    def hidden_part(j):
        if j == 0:
            fetched("slope", "nff")
        cols = slice(j * WIDTH, (j + 1) * WIDTH)
        ghj[...] = (dot_nt(gl[...], weight(12 + j)) * slope[:, cols].astype(WIDE)).astype(LOW)
        keep(8 + j, dot_tn(nff[...], ghj[...]))

    def hidden_back(j):
        part = dot_nt(ghj[...], weight(8 + j))
        if j:
            up[...] += part
        else:
            up[...] = part

    def norm_back(value_ref, base_ref, n):
        g = gains[n : n + 1, :].astype(WIDE)

        def chunk(i, carried):
            rows = pl.ds(pl.multiple_of(i * 128, 128), 128)
            value = value_ref[rows, :].astype(WIDE)
            r = root_scale(value)
            unit_rows = value * r
            upstream = up[rows, :]
            weighted = upstream * g
            inner = jnp.mean(weighted * unit_rows, axis=-1, keepdims=True)
            new = base_ref[rows, :].astype(WIDE) + r * (weighted - unit_rows * inner)
            total[rows, :] = new
            low[rows, :] = new.astype(LOW)
            return carried + jnp.sum(upstream * unit_rows, axis=0, keepdims=True)

        acc[n : n + 1, 0:WIDTH] = lax.fori_loop(0, ROWS // 128, chunk, jnp.zeros((1, WIDTH), WIDE))

    def ff_norm_part():
        fetched("after_cross")
        norm_back(aft, gl, 2)
        fetch("p", p_hbm, act)
        fetch("normed", normed_hbm, slope.at[:, 0:768])
        fetch("q", q_hbm, slope.at[:, 768:1536])
        fetch("k", k_hbm, slope.at[:, 1536:2304])
        fetch("v", v_hbm, slope.at[:, 2304:3072])
        fetch("ctx", ctx_hbm, nff)
        fetch("after_self", after_self_hbm, aft)

    def cross_out_part():
        fetched("cctx")
        keep(7, dot_tn(cctx[...], low[...]))
        gctx[...] = dot_nt(low[...], weight(7)).astype(LOW)
        fetched("cq", "mk", "mv", "pc")

    def head_back(weights, gp, qp, kp, vp, side):
        p32 = weights.astype(WIDE)
        pull = dot_nt(jnp.where(sides[side], gp, jnp.zeros_like(gp)), vp)
        slant = p32 * (pull - jnp.sum(pull * p32, axis=-1, keepdims=True))
        rounded = slant.astype(LOW)
        return dot(rounded, kp), dot_tn(rounded, qp), dot_tn(weights, gp), slant

    def joined(low_part, high_part):
        return jnp.where(sides[0], low_part, high_part).astype(LOW)

    def cross_part(lo, hi):
        def it(i, c):
            s, pair = i // PAIRS, i % PAIRS
            rows = pl.ds(pl.multiple_of(s * LENGTH, LENGTH), LENGTH)
            deep = pl.ds(pl.multiple_of(s * MEMORY, MEMORY), MEMORY)
            cols = pl.ds(pl.multiple_of(pair * 128, 128), 128)
            gp, qp, kp, vp = gctx[rows, cols], cq[rows, cols], mk[deep, cols], mv[deep, cols]
            one, two = [
                head_back(pc[rows, pl.ds(pl.multiple_of((2 * pair + side) * MEMORY, 128), MEMORY)], gp, qp, kp, vp, side)
                for side in range(2)
            ]
            dq[rows, cols] = joined(one[0], two[0])
            dk[deep, cols] = joined(one[1], two[1])
            dv[deep, cols] = joined(one[2], two[2])
            return c

        lax.fori_loop(lo, hi, it, 0)

    def cross_query_part():
        fetched("ncross")
        keep(4, dot_tn(ncross[...], dq[...]))

    def cross_key_part():
        fetched("mem")
        keep(5, dot_tn(mem[...], dk[0:256, :]))

    def cross_value_part():
        keep(6, dot_tn(mem[...], dv[0:256, :]))

    def memory_part():
        mem_grad[...] = dot_nt(dk[0:256, :], weight(5)) + dot_nt(dv[0:256, :], weight(6))
        pltpu.make_async_copy(mem_grad, memory_out, out_sem.at[0]).start()

    def cross_query_back():
        up[...] = dot_nt(dq[...], weight(4))

    def cross_norm_part():
        fetched("after_self")
        norm_back(aft, total, 1)

    def self_out_part():
        fetched("ctx")
        keep(3, dot_tn(nff[...], low[...]))
        gctx[...] = dot_nt(low[...], weight(3)).astype(LOW)
        fetched("p", "q", "k", "v")

    def self_part(lo, hi):
        def it(pair, c):
            cols = pl.ds(pl.multiple_of(pair * 128, 128), 128)
            q_cols = pl.ds(pl.multiple_of(768 + pair * 128, 128), 128)
            k_cols = pl.ds(pl.multiple_of(1536 + pair * 128, 128), 128)
            v_cols = pl.ds(pl.multiple_of(2304 + pair * 128, 128), 128)
            slants = []
            for s in range(2):
                rows = slice(s * LENGTH, (s + 1) * LENGTH)
                gp, qp, kp, vp = gctx[rows, cols], slope[rows, q_cols], slope[rows, k_cols], slope[rows, v_cols]
                one, two = [
                    head_back(act[rows, pl.ds(pl.multiple_of((2 * pair + side) * LENGTH, 256), LENGTH)], gp, qp, kp, vp, side)
                    for side in range(2)
                ]
                dq[rows, cols] = joined(one[0], two[0])
                dk[rows, cols] = joined(one[1], two[1])
                dv[rows, cols] = joined(one[2], two[2])
                slants.append((one[3], two[3]))
            t = lax.broadcasted_iota(jnp.int32, (LENGTH, LENGTH), 0)
            u = lax.broadcasted_iota(jnp.int32, (LENGTH, LENGTH), 1)
            upside = (t + u == LENGTH - 1).astype(LOW)
            for side in range(2):
                both = slants[0][side] + slants[1][side]
                coarse = both.astype(LOW)
                fine = (both - coarse.astype(WIDE)).astype(LOW)
                turned = dot(upside, coarse) + dot(upside, fine)
                rolled = pltpu.roll(turned, 1, 1, stride=1, stride_axis=0)
                dist[pl.ds(2 * pair + side, 1), :] = jnp.sum(rolled, axis=0, keepdims=True)
            return c

        lax.fori_loop(lo, hi, it, 0)

    def self_grads(n):
        fetched(*(["normed"] if n == 0 else []))
        keep(n, dot_tn(slope[:, 0:768], (dq, dk, dv)[n][...]))

    def normed_back(n):
        part = dot_nt((dq, dk, dv)[n][...], weight(n))
        if n:
            up[...] += part
        else:
            up[...] = part

    def input_part():
        fetched("x")
        norm_back(x, total, 0)
        pltpu.make_async_copy(total, input_out, out_sem.at[1]).start()
        buckets = lax.dot_general(
            dist[...], bucket_columns(True), (((1,), (1,)), ((), ())),
            precision=lax.Precision.HIGHEST, preferred_element_type=WIDE)
        acc[:, WIDTH : WIDTH + BUCKETS] = buckets
        for copy in acc_copies(0):
            copy.start()

    pieces = [(0.5, begin, None, 6)]
    pieces += [(1.0, functools.partial(out_grad_part, j), 12 + j, 6) for j in range(4)]
    for j in range(4):
        pieces += [(2.0, functools.partial(hidden_part, j), 8 + j, 0), (1.0, functools.partial(hidden_back, j), None, 8 + 2 * j)]
    pieces += [
        (1.5, ff_norm_part, None, 0), (1.9, cross_out_part, 7, 15),
        *[(1.5, functools.partial(cross_part, 2 * n, 2 * n + 2), None, 0) for n in range(6)],
        (1.0, cross_query_part, 4, 0), (0.5, cross_key_part, 5, 0), (0.5, cross_value_part, 6, 0),
        (1.0, memory_part, None, 0), (1.0, cross_query_back, None, 16), (1.3, cross_norm_part, None, 0), (2.0, self_out_part, 3, 0),
        *[(2.2, functools.partial(self_part, n, n + 1), None, 0) for n in range(6)],
        *[(1.0, functools.partial(self_grads, n), n, 0) for n in range(3)],
        *[(1.0, functools.partial(normed_back, n), None, 0) for n in range(3)],
        (2.0, input_part, None, 0),
    ]

    acc[...] = jnp.zeros_like(acc)
    dist[...] = jnp.zeros_like(dist)
    fetch("og", og_hbm, gl)
    for j in range(4):
        cols = slice(j * WIDTH, (j + 1) * WIDTH)
        fetch(f"act{j}", act_hbm.at[:, cols], act.at[:, cols])
    ask(2)
    fetch("slope", slope_hbm, slope)
    fetch("nff", nff_hbm, nff)
    fetch("after_cross", after_cross_hbm, aft)
    fetch("cctx", cctx_hbm, cctx)
    fetch("cq", cq_hbm, cq)
    fetch("mk", mk_hbm, mk)
    fetch("mv", mv_hbm, mv)
    fetch("pc", pc_hbm, pc)
    fetch("ncross", ncross_hbm, ncross)
    fetch("mem", mem_hbm, mem)
    fetch("x", x_hbm, x)
    clock, done, made, freed = 0.0, 0, set(), set()

    def run_piece():
        nonlocal clock, done
        cost, what, makes, asks = pieces[done]
        what()
        ask(asks)
        clock += cost
        made.add(makes)
        done += 1

    def may_run():
        makes = pieces[done][2]
        i = 0 if makes is None else LINE.index(makes)
        return i < 4 or LINE[i - 4] in freed

    def out_grads():
        while LINE[0] not in made:
            run_piece()

    greet([sibling, first, second] + along_z, out_grads)

    stage = None
    for r in range(GROUPS + LAGS[-1]):
        for s in range(1, 7):
            i = r - LAGS[s]
            if 0 <= i < GROUPS:
                event(LINE[i], s)
                if s == 1:
                    freed.add(LINE[i])
        if r < GROUPS:
            while LINE[r] not in made:
                assert may_run()
                run_piece()
            event(LINE[r], 0)
        while done < len(pieces) and clock < PACE * (r + 1) and may_run():
            run_piece()
        if done == len(pieces):
            if stage is None:
                stage = 0
            elif stage < 4:
                for copy in acc_copies(stage):
                    copy.wait()
                for n in ((0,), (1, 2, 3), (4,), (5,))[stage]:
                    acc[...] += acc_in[n]
                stage += 1
                if stage < 4:
                    for copy in acc_copies(stage):
                        copy.start()
    assert done == len(pieces) and stage == 4 and got[0] == GROUPS
    offset = (lax.axis_index("dp") * 4 + lax.axis_index("fsdp")) * 24
    sum_out[:, 0:WIDTH] = pltpu.roll(acc[:, 0:WIDTH], WIDTH - offset, 1)
    sum_out[:, WIDTH:] = acc[:, WIDTH:]
    put(10).start()
    for n in range(11):
        put(n).wait()
    pltpu.make_async_copy(mem_grad, memory_out, out_sem.at[0]).wait()
    pltpu.make_async_copy(total, input_out, out_sem.at[1]).wait()


BACKWARD_OUT = (
    (((512, 768), WIDE), ((256, 768), WIDE)),
    (((24, 768), WIDE),) * 8 + (((24, 3072), WIDE), ((96, 768), WIDE), ((16, 896), WIDE)),
)


def backward_call(gains, lens, *arrays):
    shape = lambda s: jax.ShapeDtypeStruct(*s)
    vmem = lambda *s: pltpu.VMEM(s, LOW)
    return pl.pallas_call(
        backward_kernel,
        out_shape=tuple(shape(s) for s in BACKWARD_OUT[0] + BACKWARD_OUT[1]),
        in_specs=[pl.BlockSpec(memory_space=pltpu.VMEM), pl.BlockSpec(memory_space=pltpu.SMEM)]
        + [pl.BlockSpec(memory_space=pl.ANY)] * len(arrays),
        out_specs=[pl.BlockSpec(memory_space=pl.ANY)] * 13,
        scratch_shapes=[
            *[pltpu.VMEM(*s) for s in BACKWARD_OUT[1]],
            vmem(SLOTS, 4, 4, 48, 768),
            vmem(512, 3072), vmem(512, 3072), pltpu.VMEM((256, 768), WIDE), vmem(512, 768),
            pltpu.VMEM((512, 768), WIDE),
            vmem(512, 768), vmem(512, 768), vmem(512, 768), vmem(256, 768), vmem(256, 768), vmem(256, 768),
            vmem(512, 1536),
            vmem(512, 768), vmem(512, 768),
            pltpu.VMEM((512, 768), WIDE), pltpu.VMEM((512, 768), WIDE),
            vmem(512, 768), vmem(512, 768), vmem(512, 768),
            vmem(512, 768), vmem(512, 768), vmem(512, 768),
            pltpu.VMEM((16, LENGTH), WIDE),
            vmem(4, 4, 4, 48, 768),
            vmem(GROUPS, 4, 4, 48, 384), vmem(GROUPS, 2, 4, 48, 384), vmem(GROUPS, 9, 48, 384),
            pltpu.VMEM((2, 48, 384), WIDE),
            pltpu.VMEM((12, 48, 384), WIDE), pltpu.VMEM((4, 48, 384), WIDE),
            pltpu.VMEM((12, 24, 384), WIDE), pltpu.VMEM((2, 48, 384), WIDE),
            pltpu.VMEM((16, 896), WIDE), pltpu.VMEM((6, 16, 896), WIDE),
            pltpu.SemaphoreType.DMA((GROUPS, 13)), pltpu.SemaphoreType.DMA((GROUPS, 13)),
            pltpu.SemaphoreType.DMA((6,)), pltpu.SemaphoreType.DMA((6,)),
            pltpu.SemaphoreType.DMA((28,)), pltpu.SemaphoreType.DMA((GROUPS,)), pltpu.SemaphoreType.DMA((2,)),
            pltpu.SemaphoreType.DMA((11,)),
        ],
        compiler_params=pltpu.CompilerParams(collective_id=1, has_side_effects=True, vmem_limit_bytes=62 * 2**20),
    )(gains, lens, *arrays)


def place_kernel(*refs):
    arrays, outs, held, own, sems = refs[:14], refs[14:31], refs[31:45], refs[45:49], refs[49]
    copies = [pltpu.make_async_copy(src, dst, sems.at[0, n]) for n, (src, dst) in enumerate(zip(arrays, held))]
    for copy in copies:
        copy.start()
    copies[13].wait()
    small = held[13]
    for n in range(3):
        own[n][...] = small[n : n + 1, 0:24]
    own[3][...] = small[0:HEADS, WIDTH : WIDTH + BUCKETS]
    sources = list(held[:13]) + list(own)
    onward = [pltpu.make_async_copy(src, dst, sems.at[1, n]) for n, (src, dst) in enumerate(zip(sources, outs))]
    for copy in onward[13:]:
        copy.start()
    for n in range(13):
        copies[n].wait()
        onward[n].start()
    for copy in onward:
        copy.wait()


def place_call(small, *arrays):
    last = [((1, 24), WIDE)] * 3 + [((HEADS, BUCKETS), WIDE)]
    shapes = [(a.shape, a.dtype) for a in arrays] + last
    return pl.pallas_call(
        place_kernel,
        out_shape=tuple(jax.ShapeDtypeStruct(*s) for s in shapes),
        in_specs=[pl.BlockSpec(memory_space=pl.ANY)] * 14,
        out_specs=[pl.BlockSpec(memory_space=pl.ANY)] * 17,
        scratch_shapes=[pltpu.VMEM(a.shape, a.dtype) for a in arrays]
        + [pltpu.VMEM(small.shape, small.dtype)]
        + [pltpu.VMEM(*s) for s in last]
        + [pltpu.SemaphoreType.DMA((2, 17))],
    )(*arrays, small)


def layer_kernels(decoder_in, memory, out_grad, lengths, *params):
    shards, table = params[:13], params[13]
    (
        w, gains, normed, q, k, v, ctx, p, after_self, ncross, cq, mk, mv, cctx, pc, after_cross, nff, act, slope, layer,
    ) = forward(shards, decoder_in, memory, table, lengths)
    rows = decoder_in.reshape(ROWS, WIDTH)
    input_grad, memory_grad, *pieces, in_piece, out_piece, small = backward_call(
        gains, lengths.reshape(2), w, act, slope, nff, after_cross, cctx, ncross, cq, mk, mv,
        memory.reshape(2 * MEMORY, WIDTH), pc, after_self, p, normed, q, k, v, ctx, rows, out_grad.reshape(ROWS, WIDTH),
    )
    layer, input_grad, memory_grad, *rest = place_call(small, layer, input_grad, memory_grad, *pieces, in_piece, out_piece)
    return (
        layer.reshape(decoder_in.shape),
        input_grad.reshape(decoder_in.shape),
        memory_grad.reshape(memory.shape),
        *rest[:10],
        *[part.reshape(24) for part in rest[10:13]],
        rest[13].T,
    )


def body(decoder_in, memory, out_grad, lengths, *params):
    sizes = (lax.axis_size("dp"), lax.axis_size("fsdp"))
    if sizes == (8, 4) and decoder_in.shape == (2, 1, LENGTH, WIDTH) and params[0].shape == (24, WIDTH):
        return layer_kernels(decoder_in, memory, out_grad, lengths, *params)
    return plain_body(decoder_in, memory, out_grad, lengths, *params)


def solution(mesh):
    return jax.shard_map(
        body,
        mesh=mesh,
        in_specs=(
            P(None, ("dp", "fsdp"), None, None),
            P(None, ("dp", "fsdp"), None, None),
            P(None, ("dp", "fsdp"), None, None),
            P(None, ("dp", "fsdp")),
            P(("dp", "fsdp"), None),
            P(("dp", "fsdp"), None),
            P(("dp", "fsdp"), None),
            P(("dp", "fsdp"), None),
            P(("dp", "fsdp"), None),
            P(("dp", "fsdp"), None),
            P(("dp", "fsdp"), None),
            P(("dp", "fsdp"), None),
            P(("dp", "fsdp"), None),
            P(("dp", "fsdp"), None),
            P(("dp", "fsdp")),
            P(("dp", "fsdp")),
            P(("dp", "fsdp")),
            P(),
        ),
        out_specs=(
            P(None, ("dp", "fsdp"), None, None),
            P(None, ("dp", "fsdp"), None, None),
            P(None, ("dp", "fsdp"), None, None),
            P(("dp", "fsdp"), None),
            P(("dp", "fsdp"), None),
            P(("dp", "fsdp"), None),
            P(("dp", "fsdp"), None),
            P(("dp", "fsdp"), None),
            P(("dp", "fsdp"), None),
            P(("dp", "fsdp"), None),
            P(("dp", "fsdp"), None),
            P(("dp", "fsdp"), None),
            P(("dp", "fsdp"), None),
            P(("dp", "fsdp")),
            P(("dp", "fsdp")),
            P(("dp", "fsdp")),
            P(),
        ),
        check_vma=False,
    )
```
